128 devices in a mesh: section: 2 (over y_lo), expert: 16 (over y_hi, z, core), shard: 4 (over x).
Axes of the slice: x: 4, y: 4 (y_hi: 2, y_lo: 2; y = y_hi * 2 + y_lo), z: 4, core: 2. Of those that a mesh axis runs over, the one named last changes fastest.
Arguments:
- tokens: bfloat16 [2, 8192, 1536], P(None, ('expert', 'shard')), may hold values from -6 to 6
- routes: int32 [2, 2, 8192, 4], P('section', None, ('expert', 'shard')), may hold values from 0 to 31, all different within a row; in each aligned block of 128 rows (0 to 127, 128 to 255, ..., all dimensions but the last counted through in order) at most 18 rows name the same one
- lengths: int32 [2, 16, 2], P(None, 'expert'), may hold values from 1 to 385, 512 in all within a row
- gain_attn: bfloat16 [2, 1536], P('section', ('expert', 'shard')), may hold values from 0.5 to 1.5
- w_query: bfloat16 [2, 1536, 1536], P('section', ('expert', 'shard')), may hold values from -0.15625 to 0.15625
- w_key: bfloat16 [2, 1536, 256], P('section', ('expert', 'shard')), may hold values from -0.15625 to 0.15625
- w_value: bfloat16 [2, 1536, 256], P('section', ('expert', 'shard')), may hold values from -0.15625 to 0.15625
- w_out: bfloat16 [2, 1536, 1536], P('section', ('expert', 'shard')), may hold values from -0.625 to 0.625
- gain_moe: bfloat16 [2, 1536], P('section', ('expert', 'shard')), may hold values from 0.5 to 1.5
- w_router: bfloat16 [2, 1536, 32], P('section', ('expert', 'shard')), may hold values from -0.078125 to 0.078125
- w_gate: bfloat16 [2, 32, 1536, 768], P('section', 'expert', 'shard'), may hold values from -0.15625 to 0.15625
- w_up: bfloat16 [2, 32, 1536, 768], P('section', 'expert', 'shard'), may hold values from -0.15625 to 0.15625
- w_down: bfloat16 [2, 32, 768, 1536], P('section', 'expert', None, 'shard'), may hold values from -0.625 to 0.625
- cotangent: bfloat16 [2, 8192, 1536], P(None, ('expert', 'shard')), may hold values from -6 to 6
Outputs:
- mixed: bfloat16 [2, 8192, 1536], P(None, ('expert', 'shard'))
- grad_tokens: bfloat16 [2, 8192, 1536], P('section', ('expert', 'shard'))
- grad_gain_attn: float32 [2, 1536], P('section', ('expert', 'shard'))
- grad_w_query: float32 [2, 1536, 1536], P('section', ('expert', 'shard'))
- grad_w_key: float32 [2, 1536, 256], P('section', ('expert', 'shard'))
- grad_w_value: float32 [2, 1536, 256], P('section', ('expert', 'shard'))
- grad_w_out: float32 [2, 1536, 1536], P('section', ('expert', 'shard'))
- grad_gain_moe: float32 [2, 1536], P('section', ('expert', 'shard'))
- grad_w_router: float32 [2, 1536, 32], P('section', ('expert', 'shard'))
- grad_w_gate: float32 [2, 32, 1536, 768], P('section', 'expert', 'shard')
- grad_w_up: float32 [2, 32, 1536, 768], P('section', 'expert', 'shard')
- grad_w_down: float32 [2, 32, 768, 1536], P('section', 'expert', None, 'shard')
The draws below stay inside these ranges and needn't reach their ends.
Inputs may be any that keep to these rules, and one draw needn't show every extreme that they name: `routes`: the 4 experts of a token differ. Of one device's 128 rows of one micro-batch and one layer (aligned blocks of 128 rows), at most 18 name the same expert, and in some blocks an expert is named by exactly 18. Each group's 2 lengths sum to 512; none is longer than 385.
All inputs are finite; a program needn't handle non-finite values.
Results may differ from the reference program's by a relative error of at most 0.028.
Values may be sent and summed in bfloat16 or wider, within the bound.
A program may use at most 384 MiB of HBM per device.

```python
import math
import jax
import jax.numpy as jnp
import numpy as np
from jax import lax

D = 1536
HEADS = 12
KV_HEADS = 2
HEAD_DIM = 128
FF = 768
EXPERTS = 32
TOPK = 4
TOK_MB = 128
MB = 2
SEQS = 2
LAYERS = 2
CAP = 18
GROUP = 512
LONGEST = 385
GROUPS = 16
ROWS = 8192
QW = 1536
KVW = 256


def steps_of(key, shape, cuts, least, high):
    factor_of = 1.0
    for axis_at, shards_of in cuts:
        draws = jax.random.uniform(jax.random.fold_in(jax.random.fold_in(key, 6), axis_at), (shards_of,), jnp.float32, least / len(cuts), high / len(cuts))
        factor_of = factor_of * jnp.repeat(jnp.exp(draws), shape[axis_at] // shards_of).reshape((-1,) + (1,) * (len(shape) - 1 - axis_at))
    return factor_of


def split_up(number_of, total, reach, slope):
    portions = [(1 << 20) // math.isqrt(grade ** slope) + 1 for grade in range(2, number_of + 1)]
    rest, holding = total - reach - (number_of - 1), [1] * (number_of - 1)
    while rest > 0:
        candidates = [i for i in range(number_of - 1) if holding[i] < reach]
        pool, left = sum([portions[i] for i in candidates]), rest
        for i in candidates:
            addition = min(reach - holding[i], max(1, left * portions[i] // pool), rest)
            holding[i] = holding[i] + addition
            rest = rest - addition
    return np.array([reach] + holding)


def uneven_parts(stream_key, count, total, limit, slope):
    if count == 2:
        one = jax.random.randint(stream_key, (), max(1, total - limit), min(limit, total - 1) + 1)
        return jnp.stack([one, total - one])
    tallies = jnp.asarray(split_up(count, total, limit, slope), jnp.int32)
    pairs = (count - 1) // 2
    giver, taker = tallies[1:1 + 2 * pairs:2], tallies[2:2 + 2 * pairs:2]
    slack = jnp.minimum(giver - 1, limit - taker)
    shifted = jax.random.randint(jax.random.fold_in(stream_key, 1), (pairs,), 0, 1 << 20) % (slack + 1)
    tallies = tallies.at[1:1 + 2 * pairs:2].set(giver - shifted).at[2:2 + 2 * pairs:2].set(taker + shifted)
    return tallies[jax.random.permutation(jax.random.fold_in(stream_key, 2), count)]


def routed_block(stream_key, own, number, rows, number_of, top, bound, skew):
    order = jax.random.permutation(stream_key, number_of)
    heavy_load, ordinary = shares(number_of, rows * top, bound, skew, True), shares(number_of, rows * top, bound, skew, False)
    places = jnp.arange(number_of)

    def named(sizes, offset_by):
        used = int((sizes > 0).sum())
        fixed = max(1, used // 4)
        moved = fixed + (places - fixed + offset_by * (used - fixed)) % max(1, number_of - fixed)
        return jnp.zeros((number_of,), jnp.int32).at[order[jnp.where(places < fixed, places, moved)]].set(jnp.asarray(sizes, jnp.int32))

    sizes = jnp.where(number % 4 == 0, named(heavy_load, number // 4), named(ordinary, number - number // 4 - 1))
    mixed = jax.random.permutation(jax.random.fold_in(own, 3), number_of)
    donor, receiver = mixed[0:number_of // 2 * 2:2], mixed[1:number_of // 2 * 2:2]
    margin = jnp.minimum(sizes[donor] - 1, bound - sizes[receiver]) // 2
    margin = jnp.where((donor == order[0]) | (receiver == order[0]) | (sizes[receiver] == 0), 0, jnp.maximum(margin, 0))
    moved = jax.random.randint(jax.random.fold_in(own, 4), (number_of // 2,), 0, 1 << 20) % (margin + 1)
    sizes = sizes.at[donor].add(-moved).at[receiver].add(moved)
    items = jnp.searchsorted(jnp.cumsum(sizes), jnp.arange(rows * top), side="right").astype(jnp.int32)
    grid = items.reshape(top, rows).T
    grid = grid[jax.random.permutation(jax.random.fold_in(own, 1), rows)]
    offset_by = jax.random.randint(jax.random.fold_in(own, 2), (rows, 1), 0, top)
    return jnp.take_along_axis(grid, (jnp.arange(top)[None, :] + offset_by) % top, axis=1)


def shares(number_of, total, reach, skew, full):
    loads = [(1 << 20) // math.isqrt(standing ** skew) + 1 for standing in range(1, number_of + 1)]
    largest = reach if full else min(reach, max(-(-total // number_of), total * loads[0] // sum(loads)))
    least = 1 if total - largest >= number_of - 1 else 0
    given, rest = [largest] + [least] * (number_of - 1), total - largest - least * (number_of - 1)
    while rest > 0:
        free = [i for i in range(1, number_of) if given[i] < largest] or [i for i in range(1, number_of) if given[i] < reach]
        whole, remaining = sum([loads[i] for i in free]), rest
        for i in free:
            addition = min(reach - given[i], max(1, remaining * loads[i] // whole), rest)
            given[i] = given[i] + addition
            rest = rest - addition
    return np.array(given)


def bell_draw(own_key, shape, spread, bound, shards=(), kind=jnp.bfloat16):
    values = jax.random.normal(own_key, shape, jnp.float32) * spread
    if len(shards) > 0:
        values = steps_of(own_key, shape, shards, -0.22, 0.18) * values
    return jnp.clip(values, min=-bound, max=bound).astype(kind)


def setup_inputs(seed: int = 0) -> dict:
    splits = jax.random.split(jax.random.key(seed), 15)
    tokens = bell_draw(splits[0], (MB, ROWS, D), 1.0, 6.0, ((1, 64),))
    routes_keys = jax.random.split(jax.random.fold_in(splits[1], 1), LAYERS * MB * ROWS // TOK_MB)
    routes_turns = jax.random.permutation(jax.random.fold_in(splits[1], 3), LAYERS * MB * ROWS // TOK_MB)
    routes = jax.vmap(lambda own, number: routed_block(jax.random.fold_in(splits[1], 2), own, number, TOK_MB, EXPERTS, TOPK, CAP, 2))(routes_keys, routes_turns).reshape((LAYERS, MB, ROWS, TOPK))
    lengths = jax.vmap(lambda own: uneven_parts(own, SEQS, GROUP, LONGEST, 2))(jax.random.split(splits[2], MB * GROUPS)).reshape((MB, GROUPS, SEQS)).astype(jnp.int32)
    gain_attn = jnp.clip(1.0 + 0.1 * jax.random.normal(splits[3], (LAYERS, D), jnp.float32), 0.5, 1.5).astype(jnp.bfloat16)
    w_query = bell_draw(splits[4], (LAYERS, D, QW), D ** -0.5, 0.15625, ((0, 2), (1, 64)))
    w_key = bell_draw(splits[5], (LAYERS, D, KVW), D ** -0.5, 0.15625, ((0, 2), (1, 64)))
    w_value = bell_draw(splits[6], (LAYERS, D, KVW), D ** -0.5, 0.15625, ((0, 2), (1, 64)))
    w_out = bell_draw(splits[7], (LAYERS, QW, D), (QW // 16) ** -0.5, 0.625, ((0, 2), (1, 64)))
    gain_moe = jnp.clip(1.0 + 0.1 * jax.random.normal(splits[8], (LAYERS, D), jnp.float32), 0.5, 1.5).astype(jnp.bfloat16)
    w_router = bell_draw(splits[9], (LAYERS, D, EXPERTS), (4 * D) ** -0.5, 0.078125, ((0, 2), (1, 64)))
    w_gate = bell_draw(splits[10], (LAYERS, EXPERTS, D, FF), D ** -0.5, 0.15625, ((0, 2), (1, 16), (2, 4)))
    w_up = bell_draw(splits[11], (LAYERS, EXPERTS, D, FF), D ** -0.5, 0.15625, ((0, 2), (1, 16), (2, 4)))
    w_down = bell_draw(splits[12], (LAYERS, EXPERTS, FF, D), (FF // 8) ** -0.5, 0.625, ((0, 2), (1, 16), (3, 4)))
    cotangent = bell_draw(splits[13], (MB, ROWS, D), 1.0, 6.0, ((1, 64),))
    return {"tokens": tokens, "routes": routes, "lengths": lengths, "gain_attn": gain_attn, "w_query": w_query, "w_key": w_key, "w_value": w_value, "w_out": w_out, "gain_moe": gain_moe, "w_router": w_router, "w_gate": w_gate, "w_up": w_up, "w_down": w_down, "cotangent": cotangent}


@jax.custom_vjp
def low(v):
    return lax.optimization_barrier(v.astype(jnp.bfloat16)).astype(jnp.float32)

@jax.custom_vjp
def low_back(v):
    return v

def low_keep(v):
    return (low(v), None)

def low_pass(kept, grad):
    return (grad,)

def back_keep(v):
    return (v, None)

def back_low(kept, grad):
    return (low(grad),)
low.defvjp(low_keep, low_pass)
low_back.defvjp(back_keep, back_low)
epsilon = 1e-06
rope_base = 1000000.0
masked_score = -1e+30
highest = lax.Precision.HIGHEST

def norm_rows(field, gain_row):
    return field * lax.rsqrt(lax.optimization_barrier(jnp.mean(field * field, axis=-1, keepdims=True)) + epsilon) * gain_row

def document_layout(doc_lengths, group_rows):
    doc_ends = jnp.cumsum(doc_lengths).astype(jnp.int32)
    starts = doc_ends - doc_lengths
    row_index = jnp.arange(group_rows, dtype=jnp.int32)
    segment = lax.optimization_barrier(jnp.sum((row_index[:, None] >= doc_ends[None, :]).astype(jnp.int32), axis=1))
    member = segment[:, None] == jnp.arange(doc_lengths.shape[0], dtype=jnp.int32)[None, :]
    position = row_index - lax.optimization_barrier(jnp.sum(jnp.where(member, starts[None, :], 0), axis=1))
    return (segment, position)

def rotary_tables(position, head_size):
    half_dim = head_size // 2
    frequency = rope_base ** (-2.0 * jnp.arange(half_dim, dtype=jnp.float32) / head_size)
    angles = position.astype(jnp.float32)[:, None] * frequency[None, :]
    return (jnp.cos(angles)[:, None, :], jnp.sin(angles)[:, None, :])

def rotate(field, cosine, sine_table):
    half_dim = field.shape[-1] // 2
    first_half = field[..., :half_dim]
    second_half = field[..., half_dim:]
    return jnp.concatenate([first_half * cosine - second_half * sine_table, second_half * cosine + first_half * sine_table], axis=-1)

def attend_group(inputs):
    query_rows, key_rows, value_rows, segment = inputs
    row_index = jnp.arange(GROUP, dtype=jnp.int32)
    allowed = (segment[:, None] == segment[None, :]) & (row_index[:, None] >= row_index[None, :])
    scores = low_back(jnp.einsum('qgrd,kgd->grqk', query_rows, key_rows, precision=highest) * HEAD_DIM ** (-0.5))
    scores = jnp.where(allowed[None, None], scores, masked_score)
    largest = lax.optimization_barrier(jnp.max(scores, axis=-1, keepdims=True))
    exponent = jnp.exp(scores - largest)
    attn_probs = low(exponent / lax.optimization_barrier(jnp.sum(exponent, axis=-1, keepdims=True)))
    return jnp.einsum('grqk,kgd->qgrd', attn_probs, value_rows, precision=highest)

def expert_term(h_moe, column, gate_w, up_w, down_w):
    rows_in = low_back(h_moe)
    gate_pre = low_back(jnp.dot(rows_in, gate_w, precision=highest))
    up_pre = low_back(jnp.dot(rows_in, up_w, precision=highest))
    hidden = low(jax.nn.silu(gate_pre) * up_pre)
    result = low_back(low(jnp.dot(hidden, down_w, precision=highest)))
    return column[:, None] * result

def layer(layer_in, gain_a, query_w, key_w, value_w, out_w, gain_m, router_w, gate_w, up_w, down_w, route_rows, doc_lengths):
    group_ratio = HEADS // KV_HEADS
    h_attn = low(norm_rows(layer_in, gain_a))
    query_pre = low_back(jnp.dot(h_attn, query_w, precision=highest))
    key_pre = low_back(jnp.dot(h_attn, key_w, precision=highest))
    value_all = low_back(low(jnp.dot(h_attn, value_w, precision=highest)))
    segment, position = jax.vmap(lambda lens_row: document_layout(lens_row, GROUP))(doc_lengths)
    cosine, sine_table = rotary_tables(position.reshape(-1), HEAD_DIM)
    query_all = low(rotate(query_pre.reshape(ROWS, HEADS, HEAD_DIM), cosine, sine_table))
    key_all = low(rotate(key_pre.reshape(ROWS, KV_HEADS, HEAD_DIM), cosine, sine_table))
    attended = lax.map(jax.checkpoint(attend_group), (query_all.reshape(GROUPS, GROUP, KV_HEADS, group_ratio, HEAD_DIM), key_all.reshape(GROUPS, GROUP, KV_HEADS, HEAD_DIM), value_all.reshape(GROUPS, GROUP, KV_HEADS, HEAD_DIM), segment))
    attended = low_back(low(attended.reshape(ROWS, HEADS * HEAD_DIM)))
    x_mid = layer_in + low_back(jnp.dot(attended, out_w, precision=highest))
    h_moe = low(norm_rows(x_mid, gain_m))
    logits = low_back(jnp.dot(h_moe, router_w, precision=highest))
    choose = route_rows[:, :, None] == jnp.arange(EXPERTS, dtype=jnp.int32)[None, None, :]
    chosen = lax.optimization_barrier(jnp.sum(jnp.where(choose, logits[:, None, :], 0.0), axis=2))
    chosen_top = lax.optimization_barrier(jnp.max(chosen, axis=1, keepdims=True))
    gate_exp = jnp.exp(chosen - chosen_top)
    gate_probs = gate_exp / lax.optimization_barrier(jnp.sum(gate_exp, axis=1, keepdims=True))
    table = lax.optimization_barrier(jnp.sum(jnp.where(choose, gate_probs[:, :, None], 0.0), axis=1))
    step_term = jax.checkpoint(expert_term)

    def accumulate(total, inputs):
        return (total + step_term(h_moe, *inputs), None)
    total, _ = lax.scan(accumulate, jnp.zeros_like(x_mid), (table.T, gate_w, up_w, down_w))
    return x_mid + total

def forward_all(tokens, gain_attn, w_query, w_key, w_value, w_out, gain_moe, w_router, w_gate, w_up, w_down, routes, lengths):
    results = []
    for micro_index in range(MB):
        current = tokens[micro_index]
        for level in range(LAYERS):
            if level > 0:
                current = low_back(low(current))
            current = layer(current, gain_attn[level], w_query[level], w_key[level], w_value[level], w_out[level], gain_moe[level], w_router[level], w_gate[level], w_up[level], w_down[level], routes[level, micro_index], lengths[micro_index])
        results.append(current)
    return jnp.stack(results)

def reference(tokens, routes, lengths, gain_attn, w_query, w_key, w_value, w_out, gain_moe, w_router, w_gate, w_up, w_down, cotangent):
    floats = tuple((array.astype(jnp.float32) for array in (tokens, gain_attn, w_query, w_key, w_value, w_out, gain_moe, w_router, w_gate, w_up, w_down)))

    def run(*inputs):
        return forward_all(*inputs, routes, lengths)
    mixed, pullback = jax.vjp(run, *floats)
    grads = pullback(cotangent.astype(jnp.float32))
    return (mixed.astype(jnp.bfloat16), grads[0].astype(jnp.bfloat16), grads[1], grads[2], grads[3], grads[4], grads[5], grads[6], grads[7], grads[8], grads[9], grads[10])
```

```python
import jax
import jax.numpy as jnp
from jax import lax
from jax.sharding import Mesh
from jax.sharding import PartitionSpec as P

HEADS = 12
HEAD_DIM = 128
EXPERTS = 32
MAIN = 16
EXTRA = 2
CHUNKS = 6

epsilon = 1e-06
rope_base = 1000000.0
masked_score = -1e30

BF = jnp.bfloat16
F32 = jnp.float32
CHIPS = ("yh", "z", "shard")
DEVICES = ("yh", "z", "core", "shard")


def dot(a, b, dims=((1,), (0,))):
    return lax.dot_general(a, b, (dims, ((), ())), preferred_element_type=F32)


def norm_rows(field, gain_row):
    return field * lax.rsqrt(jnp.mean(field * field, axis=-1, keepdims=True) + epsilon) * gain_row


def norm_back(field, gain_row, grad):
    scale = lax.rsqrt(jnp.mean(field * field, axis=-1, keepdims=True) + epsilon)
    scaled = grad * gain_row
    grad_gain = jnp.sum(grad * field * scale, axis=0)
    centre = jnp.mean(scaled * field, axis=-1, keepdims=True)
    return scale * scaled - field * (scale * scale * scale) * centre, grad_gain


def document_layout(doc_lengths, group_rows):
    doc_ends = jnp.cumsum(doc_lengths)
    starts = doc_ends - doc_lengths
    row_index = jnp.arange(group_rows, dtype=jnp.int32)
    segment = jnp.sum((row_index[:, None] >= doc_ends[None, :]).astype(jnp.int32), axis=1)
    member = segment[:, None] == jnp.arange(doc_lengths.shape[0], dtype=jnp.int32)[None, :]
    position = row_index - jnp.sum(jnp.where(member, starts[None, :], 0), axis=1)
    return (segment, position)


def rotary_tables(position, head_size):
    half_dim = head_size // 2
    frequency = rope_base ** (-2.0 * jnp.arange(half_dim, dtype=F32) / head_size)
    angles = position.astype(F32)[:, None] * frequency[None, :]
    return (jnp.cos(angles)[:, None, :], jnp.sin(angles)[:, None, :])


def rotate(field, cosine, sine):
    half_dim = field.shape[-1] // 2
    first, second = field[..., :half_dim], field[..., half_dim:]
    return jnp.concatenate(
        [first * cosine - second * sine, second * cosine + first * sine], axis=-1
    )


def rotate_back(field, cosine, sine):
    half_dim = field.shape[-1] // 2
    first, second = field[..., :half_dim], field[..., half_dim:]
    return jnp.concatenate(
        [first * cosine + second * sine, second * cosine - first * sine], axis=-1
    )


def swap(value, axis):
    return lax.ppermute(value, axis, [(0, 1), (1, 0)])


def slot_tables(route_rows):
    rows = route_rows.shape[0]
    chosen = route_rows.T[None, :, :] == jnp.arange(EXPERTS, dtype=jnp.int32)[:, None, None]
    hot = jnp.any(chosen, axis=1)
    index = jnp.arange(rows, dtype=jnp.int32)
    before = (index[:, None] < index[None, :]).astype(BF)
    rank = jnp.where(hot, dot(hot.astype(BF), before), -1.0)
    place = jnp.arange(MAIN, dtype=jnp.int32)
    main = rank[:, None, :] == place.astype(F32)[None, :, None]
    extra = rank[:, None, :] == (MAIN + place % EXTRA).astype(F32)[None, :, None]
    extra = extra & (place < EXTRA * CHUNKS)[None, :, None]
    piece = place[:, None] // EXTRA == jnp.arange(CHUNKS, dtype=jnp.int32)[None, :]
    return hot, main, extra, piece


def pieces_side(extra, piece):
    count, place, rows = extra.shape
    wide = jnp.where(piece[None, :, :, None], extra[:, :, None, :], 0)
    return wide.reshape(count * place, CHUNKS * rows)


def stacked(field):
    return jnp.concatenate(jnp.split(field, CHUNKS, axis=1), axis=0)


def unstacked(field):
    return jnp.concatenate(jnp.split(field, CHUNKS, axis=0), axis=1)


def unfold_table(sources):
    row = jnp.arange(CHUNKS * sources * EXTRA, dtype=jnp.int32)
    piece, source, extra = row // (sources * EXTRA), row // EXTRA % sources, row % EXTRA
    column = jnp.arange(sources * MAIN, dtype=jnp.int32)
    return (
        (source * MAIN + piece * EXTRA + extra)[:, None] == column[None, :]
    ).astype(BF)


def exchange(message):
    return lax.all_to_all(message, CHIPS, split_axis=0, concat_axis=0, tiled=True)


def pick_rows(field, tables):
    main, side = tables["main"], tables["side"]
    return dot(main, field), dot(side, stacked(field))


def arrived_rows(message, unfold):
    width = message.shape[1] - 256
    extra = unstacked(dot(unfold, message[:, width:]).astype(BF))
    return jnp.concatenate([message[:, :width], extra], axis=0)


def fold_rows(rows, unfold, sources):
    main = rows[: sources * MAIN]
    extra = dot(unfold, stacked(rows[sources * MAIN :]), ((0,), (0,))).astype(BF)
    return jnp.concatenate([main, extra], axis=1)


def tables_of(route_rows):
    hot, main, extra, piece = slot_tables(route_rows)
    count, place, rows = main.shape
    return {
        "hot": hot,
        "main3": main,
        "extra3": extra,
        "piece": piece,
        "main": main.reshape(count * place, rows).astype(BF),
        "side": pieces_side(extra.astype(BF), piece),
    }


def low_pair(value):
    high = value.astype(BF)
    return high, (value - high.astype(F32)).astype(BF)


def forward_layer(layer_in, mixer, experts, tables, unfold, layout):
    qkv_w, out_w, router_w, gain_a, gain_m = mixer
    gate_w, up_w, down_w = experts()
    tok_rows, model_width = layer_in.shape
    query_width = HEADS * HEAD_DIM
    kv_width = (qkv_w.shape[1] - query_width) // 2
    kv_heads = kv_width // HEAD_DIM
    cosine, sine, allowed = layout
    h_attn = norm_rows(layer_in, gain_a).astype(BF)
    qkv = dot(h_attn, qkv_w)
    query = rotate(qkv[:, :query_width].reshape(tok_rows, HEADS, HEAD_DIM), cosine, sine)
    query = query.astype(BF).reshape(tok_rows, kv_heads, HEADS // kv_heads, HEAD_DIM)
    key = rotate(
        qkv[:, query_width : query_width + kv_width].reshape(tok_rows, kv_heads, HEAD_DIM),
        cosine,
        sine,
    ).astype(BF)
    value = qkv[:, query_width + kv_width :].astype(BF).reshape(tok_rows, kv_heads, HEAD_DIM)
    both = lax.all_gather(jnp.concatenate([key, value], axis=1), "shard", axis=0, tiled=True)
    key_all, value_all = both[:, :kv_heads], both[:, kv_heads:]
    scores = jnp.einsum("qgrd,kgd->grqk", query, key_all, preferred_element_type=F32)
    scores = jnp.where(allowed[None, None], scores * HEAD_DIM ** (-0.5), masked_score)
    exponent = jnp.exp(scores - jnp.max(scores, axis=-1, keepdims=True))
    probs = exponent / jnp.sum(exponent, axis=-1, keepdims=True)
    attended = jnp.einsum(
        "grqk,kgd->qgrd", probs.astype(BF), value_all, preferred_element_type=F32
    )
    attended = attended.reshape(tok_rows, query_width).astype(BF)
    x_mid = layer_in + dot(attended, out_w)
    h_moe = norm_rows(x_mid, gain_m).astype(BF)
    logits = dot(router_w, h_moe, ((0,), (1,)))
    hot = tables["hot"]
    top = jnp.max(jnp.where(hot, logits, masked_score), axis=0, keepdims=True)
    gate_exp = jnp.where(hot, jnp.exp(jnp.where(hot, logits, masked_score) - top), 0.0)
    gates = gate_exp / jnp.sum(gate_exp, axis=0, keepdims=True)
    main, side = pick_rows(h_moe, tables)
    message = jnp.concatenate([main, side], axis=1).astype(BF)
    arrived = arrived_rows(exchange(message), unfold)
    gate_pre = dot(arrived, gate_w)
    up_pre = dot(arrived, up_w)
    hidden = (jax.nn.silu(gate_pre) * up_pre).astype(BF)
    produced = dot(hidden, down_w).astype(BF)
    returned = exchange(fold_rows(produced, unfold, EXPERTS))
    gates_main = jnp.where(tables["main3"], gates[:, None, :], 0.0)
    gates_extra = jnp.where(tables["extra3"], gates[:, None, :], 0.0)
    back_main, back_side = returned[:, :model_width], returned[:, model_width:]
    rows_first = ((0,), (0,))
    block_out = x_mid
    for part in low_pair(gates_main.reshape(-1, tok_rows)):
        block_out = block_out + dot(part, back_main, rows_first)
    for part in low_pair(pieces_side(gates_extra, tables["piece"])):
        block_out = block_out + unstacked(dot(part, back_side, rows_first))
    stored = {
        "layer_in": layer_in,
        "h_attn": h_attn,
        "query": query,
        "key_all": key_all,
        "value_all": value_all,
        "probs": probs,
        "attended": attended,
        "x_mid": x_mid,
        "h_moe": h_moe,
        "gates": gates,
        "slot_main": jnp.sum(gates_main, axis=2).reshape(-1, 1),
        "slot_side": jnp.sum(gates_extra, axis=2).reshape(-1, 1),
        "back_main": back_main,
        "back_side": back_side,
        "arrived": arrived,
        "gate_pre": gate_pre,
        "up_pre": up_pre,
        "hidden": hidden,
    }
    return (block_out, stored)


def backward_layer(grad_out, stored, mixer, experts, tables, unfold, layout):
    qkv_w, out_w, router_w, gain_a, gain_m = mixer
    gate_w, up_w, down_w = experts()
    cosine, sine, _ = layout
    tok_rows, model_width = grad_out.shape
    query_width = HEADS * HEAD_DIM
    kv_width = (qkv_w.shape[1] - query_width) // 2
    kv_heads = kv_width // HEAD_DIM
    score_scale = HEAD_DIM ** (-0.5)
    rows_first, both_last = ((0,), (0,)), ((1,), (1,))
    gates, hot = stored["gates"], tables["hot"]
    main, side = pick_rows(grad_out.astype(BF), tables)
    message = jnp.concatenate(
        [main * stored["slot_main"], side * stored["slot_side"]], axis=1
    ).astype(BF)
    dgate_main = jnp.sum(main * stored["back_main"].astype(F32), axis=1)
    dgate_side = jnp.sum(side * stored["back_side"].astype(F32), axis=1)
    came = arrived_rows(exchange(message), unfold)
    gate_pre, up_pre = stored["gate_pre"], stored["up_pre"]
    grad_down = dot(stored["hidden"], came, rows_first)
    grad_hidden = dot(came, down_w, both_last)
    logistic = jax.nn.sigmoid(gate_pre)
    grad_gate_pre = (
        grad_hidden * up_pre * (logistic * (1.0 + gate_pre * (1.0 - logistic)))
    ).astype(BF)
    grad_up_pre = (grad_hidden * (gate_pre * logistic)).astype(BF)
    grad_rows = dot(grad_gate_pre, gate_w, both_last) + dot(grad_up_pre, up_w, both_last)
    returned = exchange(fold_rows(grad_rows.astype(BF), unfold, EXPERTS))
    grad_gate = dot(stored["arrived"], grad_gate_pre, rows_first)
    grad_up = dot(stored["arrived"], grad_up_pre, rows_first)
    dgate = jnp.sum(
        jnp.where(tables["main3"], dgate_main.reshape(EXPERTS, MAIN, 1), 0.0), axis=1
    ) + jnp.sum(jnp.where(tables["extra3"], dgate_side.reshape(EXPERTS, MAIN, 1), 0.0), axis=1)
    dlogits = jnp.where(
        hot, gates * (dgate - jnp.sum(gates * dgate, axis=0, keepdims=True)), 0.0
    ).astype(BF)
    h_moe = stored["h_moe"]
    grad_router = dot(h_moe, dlogits, ((0,), (1,)))
    grad_h_moe = (
        dot(tables["main"], returned[:, :model_width], rows_first)
        + unstacked(dot(tables["side"], returned[:, model_width:], rows_first))
        + dot(dlogits, router_w, ((0,), (1,)))
    )
    grad_x_mid, grad_gain_m = norm_back(stored["x_mid"], gain_m, grad_h_moe)
    grad_x_mid = grad_x_mid + grad_out
    grad_branch = grad_x_mid.astype(BF)
    grad_wout = dot(stored["attended"], grad_branch, rows_first)
    query = stored["query"]
    grad_att = dot(grad_branch, out_w, both_last).astype(BF).reshape(query.shape)
    probs, key_all, value_all = stored["probs"], stored["key_all"], stored["value_all"]
    grad_probs = jnp.einsum("qgrd,kgd->grqk", grad_att, value_all, preferred_element_type=F32)
    grad_value_all = jnp.einsum(
        "grqk,qgrd->kgd", probs.astype(BF), grad_att, preferred_element_type=F32
    )
    centre = jnp.sum(grad_probs * probs, axis=-1, keepdims=True)
    grad_scores = (probs * (grad_probs - centre)).astype(BF)
    grad_query = (
        jnp.einsum("grqk,kgd->qgrd", grad_scores, key_all, preferred_element_type=F32)
        * score_scale
    )
    grad_key_all = (
        jnp.einsum("grqk,qgrd->kgd", grad_scores, query, preferred_element_type=F32)
        * score_scale
    )
    both = jnp.concatenate([grad_key_all, grad_value_all], axis=1).astype(BF)
    parts = lax.all_to_all(
        both.reshape(-1, tok_rows, *both.shape[1:]), "shard", split_axis=0, concat_axis=0, tiled=True
    )
    both = parts.astype(F32).sum(axis=0)
    grad_query_pre = rotate_back(grad_query.reshape(tok_rows, HEADS, HEAD_DIM), cosine, sine)
    grad_key_pre = rotate_back(both[:, :kv_heads], cosine, sine)
    grad_qkv = jnp.concatenate(
        [
            grad_query_pre.reshape(tok_rows, query_width),
            grad_key_pre.reshape(tok_rows, kv_width),
            both[:, kv_heads:].reshape(tok_rows, kv_width),
        ],
        axis=1,
    ).astype(BF)
    grad_wqkv = dot(stored["h_attn"], grad_qkv, rows_first)
    grad_h_attn = dot(grad_qkv, qkv_w, both_last)
    grad_in, grad_gain_a = norm_back(stored["layer_in"], gain_a, grad_h_attn)
    grad_in = grad_in + grad_x_mid
    narrow = jnp.concatenate(
        [
            grad_wqkv[:, query_width:],
            grad_router,
            grad_gain_a[:, None],
            grad_gain_m[:, None],
            jnp.zeros((model_width, 94), F32),
        ],
        axis=1,
    )
    return (
        grad_in,
        (grad_wqkv[:, :query_width], grad_wout, narrow),
        (grad_gate, grad_up, grad_down),
    )


def collect_mixer(local):
    whole = lax.all_gather(local, DEVICES, axis=0, tiled=True)
    return (
        whole[:, :2048],
        whole[:, 2048:3584],
        whole[:, 3584:3616],
        whole[:, 3616].astype(F32),
        whole[:, 3617].astype(F32),
    )


def pack_experts(gate, up, down):
    count, depth, width = gate.shape
    half = depth // 2
    across = down.reshape(count, 2, 2, half, depth)
    across = jnp.concatenate([across[:, :, 0], across[:, :, 1]], axis=-1)
    return jnp.stack(
        [gate.reshape(count, 2, half, width), up.reshape(count, 2, half, width), across], axis=2
    )


def unpack_halves(pieces):
    halves, shards, _, half, width = pieces.shape
    depth = shards * halves * half
    gate = pieces[:, :, 0].transpose(1, 0, 2, 3).reshape(depth, width)
    up = pieces[:, :, 1].transpose(1, 0, 2, 3).reshape(depth, width)
    down = pieces[:, :, 2].reshape(halves, shards, half, 2, width // 2)
    down = down.transpose(0, 3, 2, 1, 4).reshape(width, depth)
    return gate, up, down


def pack_halves(gate, up, down):
    depth, width = gate.shape
    half = depth // 8
    gate = gate.reshape(4, 2, half, width).transpose(1, 0, 2, 3)
    up = up.reshape(4, 2, half, width).transpose(1, 0, 2, 3)
    down = down.reshape(2, 2, half, 4, width // 2).transpose(0, 3, 2, 1, 4)
    return jnp.stack([gate, up, down.reshape(2, 4, half, width)], axis=2)


def own_half(gate, up, down):
    pieces = pack_experts(gate, up, down)
    pieces = lax.all_to_all(pieces, "core", split_axis=1, concat_axis=0, tiled=True)[:, 0]
    return lax.all_to_all(pieces, "shard", split_axis=0, concat_axis=0, tiled=True)


def both_halves(piece):
    return unpack_halves(lax.all_gather(piece, "core", axis=0, tiled=False))


def sum_over_cores(grads):
    pieces = pack_halves(*grads).astype(BF)
    arrived = lax.all_to_all(pieces, "core", split_axis=0, concat_axis=0, tiled=True)
    return arrived[0].astype(F32) + arrived[1].astype(F32)


def to_owners(piece):
    pieces = lax.all_to_all(piece.astype(BF), "shard", split_axis=0, concat_axis=0, tiled=True)
    pieces = pieces.reshape(2, 2, *pieces.shape[1:])
    pieces = lax.all_to_all(pieces, "core", split_axis=0, concat_axis=0, tiled=True)
    halves, count, _, half, width = pieces.shape
    pieces = pieces.transpose(1, 0, 2, 3, 4).astype(F32)
    gate = pieces[:, :, 0].reshape(count, halves * half, width)
    up = pieces[:, :, 1].reshape(count, halves * half, width)
    down = pieces[:, :, 2].reshape(count, halves, half, 2, width // 2)
    down = down.transpose(0, 1, 3, 2, 4).reshape(count, width, width // 2)
    return gate, up, down


def scatter_mixer(grads):
    return tuple(
        lax.psum_scatter(g.astype(BF), DEVICES, scatter_dimension=0, tiled=True) for g in grads
    )


def per_device(
    tokens,
    routes,
    lengths,
    gain_attn,
    w_query,
    w_key,
    w_value,
    w_out,
    gain_moe,
    w_router,
    w_gate,
    w_up,
    w_down,
    cotangent,
):
    section = lax.axis_index("section")
    shard = lax.axis_index("shard")
    first = section == 0
    tok_rows, model_width = tokens.shape[1:]
    group_rows = tok_rows * lax.axis_size("shard")

    def mine(a):
        return lax.dynamic_index_in_dim(a, section, 0, keepdims=False)

    def by_layer(own, other):
        return jnp.where(first, own, other), jnp.where(first, other, own)

    local = jnp.concatenate(
        [
            w_query[0],
            w_key[0],
            w_value[0],
            w_out[0],
            w_router[0],
            gain_attn[0][:, None],
            gain_moe[0][:, None],
            jnp.zeros((w_query.shape[1], 94), BF),
        ],
        axis=1,
    )
    local_0, local_1 = by_layer(local, swap(local, "section"))
    mixers = [collect_mixer(local_0), collect_mixer(local_1)]
    route_other = swap(lax.dynamic_index_in_dim(routes[0], 1 - section, 0, keepdims=False), "section")
    tables = [tables_of(r) for r in by_layer(mine(routes[0]), route_other)]
    own_piece = own_half(w_gate[0], w_up[0], w_down[0])
    pieces = by_layer(own_piece, swap(own_piece, "section"))
    experts = [both_halves(p) for p in pieces]
    unfold = unfold_table(EXPERTS)

    segment, position = document_layout(mine(lengths[:, 0]), group_rows)
    row_start = shard * tok_rows
    own_segment = lax.dynamic_slice_in_dim(segment, row_start, tok_rows)
    cosine, sine = rotary_tables(
        lax.dynamic_slice_in_dim(position, row_start, tok_rows), HEAD_DIM
    )
    query_index = row_start + jnp.arange(tok_rows, dtype=jnp.int32)
    allowed = (own_segment[:, None] == segment[None, :]) & (
        query_index[:, None] >= jnp.arange(group_rows, dtype=jnp.int32)[None, :]
    )
    layout = (cosine, sine, allowed)

    current = mine(tokens).astype(F32)
    saved = []
    for layer in range(2):
        out, stored = forward_layer(
            current, mixers[layer], lambda: experts[layer], tables[layer], unfold, layout
        )
        saved.append(stored)
        low = out.astype(BF)
        current = low.astype(F32)
    other = swap(low, "section")
    mixed = jnp.where(first, jnp.stack([low, other]), jnp.stack([other, low]))

    grad = mine(cotangent).astype(F32)
    mixer_parts, expert_parts = [None, None], [None, None]
    for layer in (1, 0):
        grad, mixer_grad, expert_grad = backward_layer(
            grad, saved[layer], mixers[layer], lambda: experts[layer], tables[layer], unfold, layout
        )
        grad_low = grad.astype(BF)
        grad = grad_low.astype(F32)
        mixer_parts[layer] = scatter_mixer(mixer_grad)
        cores = sum_over_cores(expert_grad)
        got = lax.ppermute(cores.astype(BF), "section", [(1 - layer, layer)])
        expert_parts[layer] = cores + got.astype(F32)

    sums = []
    for part_0, part_1 in zip(*mixer_parts):
        keep, give = by_layer(part_0, part_1)
        sums.append(keep.astype(F32) + swap(give, "section").astype(F32))
    grad_wq, grad_wo, narrow = sums
    experts_sum = jnp.where(first, expert_parts[0], expert_parts[1])
    grad_gate, grad_up, grad_down = to_owners(experts_sum)
    return (
        mixed,
        grad_low[None],
        narrow[:, 544][None],
        grad_wq[None],
        narrow[:, :256][None],
        narrow[:, 256:512][None],
        grad_wo[None],
        narrow[:, 545][None],
        narrow[:, 512:544][None],
        grad_gate[None],
        grad_up[None],
        grad_down[None],
    )


def solution(mesh):
    fine = Mesh(mesh.devices.reshape(2, 2, 4, 2, 4), ("section", *DEVICES))
    expert = ("yh", "z", "core")
    return jax.shard_map(
        per_device,
        mesh=fine,
        in_specs=(
            P(None, DEVICES, None),
            P("section", None, DEVICES, None),
            P(None, expert, None),
            P("section", DEVICES),
            P("section", DEVICES, None),
            P("section", DEVICES, None),
            P("section", DEVICES, None),
            P("section", DEVICES, None),
            P("section", DEVICES),
            P("section", DEVICES, None),
            P("section", expert, "shard", None),
            P("section", expert, "shard", None),
            P("section", expert, None, "shard"),
            P(None, DEVICES, None),
        ),
        out_specs=(
            P(None, DEVICES, None),
            P("section", DEVICES, None),
            P("section", DEVICES),
            P("section", DEVICES, None),
            P("section", DEVICES, None),
            P("section", DEVICES, None),
            P("section", DEVICES, None),
            P("section", DEVICES),
            P("section", DEVICES, None),
            P("section", expert, "shard", None),
            P("section", expert, "shard", None),
            P("section", expert, None, "shard"),
        ),
        check_vma=False,
    )
```

```python
import jax
import jax.numpy as jnp
from jax import lax
from jax.experimental import pallas as pl
from jax.experimental.pallas import tpu as pltpu
from jax.sharding import Mesh
from jax.sharding import PartitionSpec as P

HEADS = 12
HEAD_DIM = 128
EXPERTS = 32
MAIN = 16
EXTRA = 2
CHUNKS = 6

epsilon = 1e-06
rope_base = 1000000.0
masked_score = -1e30

BF = jnp.bfloat16
F32 = jnp.float32
CHIPS = ("yh", "z", "shard")
DEVICES = ("yh", "z", "core", "shard")


def dot(a, b, dims=((1,), (0,))):
    return lax.dot_general(a, b, (dims, ((), ())), preferred_element_type=F32)


def norm_rows(field, gain_row):
    return field * lax.rsqrt(jnp.mean(field * field, axis=-1, keepdims=True) + epsilon) * gain_row


def norm_back(field, gain_row, grad):
    scale = lax.rsqrt(jnp.mean(field * field, axis=-1, keepdims=True) + epsilon)
    scaled = grad * gain_row
    grad_gain = jnp.sum(grad * field * scale, axis=0)
    centre = jnp.mean(scaled * field, axis=-1, keepdims=True)
    return scale * scaled - field * (scale * scale * scale) * centre, grad_gain


def document_layout(doc_lengths, group_rows):
    doc_ends = jnp.cumsum(doc_lengths)
    starts = doc_ends - doc_lengths
    row_index = jnp.arange(group_rows, dtype=jnp.int32)
    segment = jnp.sum((row_index[:, None] >= doc_ends[None, :]).astype(jnp.int32), axis=1)
    member = segment[:, None] == jnp.arange(doc_lengths.shape[0], dtype=jnp.int32)[None, :]
    position = row_index - jnp.sum(jnp.where(member, starts[None, :], 0), axis=1)
    return (segment, position)


def rotary_tables(position, head_size):
    half_dim = head_size // 2
    frequency = rope_base ** (-2.0 * jnp.arange(half_dim, dtype=F32) / head_size)
    angles = position.astype(F32)[:, None] * frequency[None, :]
    return (jnp.cos(angles)[:, None, :], jnp.sin(angles)[:, None, :])


def rotate(field, cosine, sine):
    half_dim = field.shape[-1] // 2
    first, second = field[..., :half_dim], field[..., half_dim:]
    return jnp.concatenate(
        [first * cosine - second * sine, second * cosine + first * sine], axis=-1
    )


def rotate_back(field, cosine, sine):
    half_dim = field.shape[-1] // 2
    first, second = field[..., :half_dim], field[..., half_dim:]
    return jnp.concatenate(
        [first * cosine + second * sine, second * cosine - first * sine], axis=-1
    )


def swap(value, axis):
    return lax.ppermute(value, axis, [(0, 1), (1, 0)])


def around(axis, size):
    here = lax.axis_index(axis)
    return [lax.rem(here + step, size) for step in range(1, size)]


def move(name, number, arrays, shapes, peers, copies):
    count = len(arrays)
    total = 40

    def kernel(*refs):
        ins, outs = refs[:count], refs[count : count + len(shapes)]
        sent, got = refs[count + len(shapes) :]
        barrier = pltpu.get_barrier_semaphore()
        near = peers()
        for peer in near:
            pl.semaphore_signal(
                barrier, inc=1, device_id=peer, device_id_type=pl.DeviceIdType.MESH
            )
        pl.semaphore_wait(barrier, len(near))
        started = []
        for k, (source, target, device) in enumerate(copies(ins, outs)):
            if device is None:
                copy = pltpu.make_async_copy(source, target, got.at[k])
            else:
                copy = pltpu.make_async_remote_copy(
                    src_ref=source,
                    dst_ref=target,
                    send_sem=sent.at[k],
                    recv_sem=got.at[k],
                    device_id=device,
                    device_id_type=pl.DeviceIdType.MESH,
                )
            copy.start()
            started.append(copy)
        for copy in started:
            copy.wait()

    space = pl.BlockSpec(memory_space=pltpu.HBM)
    return pl.pallas_call(
        kernel,
        out_shape=[jax.ShapeDtypeStruct(s, BF) for s in shapes],
        in_specs=[space] * count,
        out_specs=[space] * len(shapes),
        scratch_shapes=[pltpu.SemaphoreType.DMA((total,)), pltpu.SemaphoreType.DMA((total,))],
        compiler_params=pltpu.CompilerParams(collective_id=number, has_side_effects=True),
        name=name,
    )(*arrays)


def total(*parts):
    out = parts[0].astype(F32)
    for part in parts[1:]:
        out = out + part.astype(F32)
    return out


def reduce_all(mixer_grads, expert_grads, section):
    core, shard, z = (lax.axis_index(a) for a in ("core", "shard", "z"))
    at = lambda a, i, axis: lax.dynamic_index_in_dim(a, i, axis, keepdims=False)
    widths = [g.shape[1] for g in mixer_grads[0]]
    mix = [g.reshape(8, 2, 4, 24, w) for grads in mixer_grads for g, w in zip(grads, widths)]
    exp = []
    for gate, up, down in expert_grads:
        exp += [gate.reshape(4, 2, 192, 768), up.reshape(4, 2, 192, 768)]
        exp += [down.reshape(2, 384, 1536)]

    def copies(ins, outs):
        other = lax.rem(core_index() + 1, 2)
        views = [r.at[:, other] for r in ins[:6]]
        views += [r.at[other] if k % 3 == 2 else r.at[:, other] for k, r in enumerate(ins[6:])]
        return [(v, o, {"core": other}) for v, o in zip(views, outs)]

    core_index = lambda: lax.axis_index("core")
    shapes = [(8, 4, 24, w) for w in widths] * 2 + [(4, 192, 768), (4, 192, 768), (384, 1536)] * 2
    got = move(
        "cores", 1, mix + exp, shapes, lambda: [{"core": lax.rem(core_index() + 1, 2)}], copies
    )
    mix = [total(at(m, core, 1), g).astype(BF) for m, g in zip(mix, got[:6])]
    exp = [
        total(at(e, core, 0 if k % 3 == 2 else 1), g).astype(BF)
        for k, (e, g) in enumerate(zip(exp, got[6:]))
    ]

    first = section == 0
    give = [jnp.where(first, b, a) for a, b in zip(exp[:3], exp[3:])]
    keep = [jnp.where(first, a, b) for a, b in zip(exp[:3], exp[3:])]
    mix = [m if k % 3 == 0 else m.reshape(2, 4, 4, 24, -1) for k, m in enumerate(mix)]

    def peers():
        out = [{"section": lax.rem(lax.axis_index("section") + 1, 2)}]
        out += [{"shard": x} for x in around("shard", 4)]
        return out + [{"z": i} for i in around("z", 4)]

    def copies_2(ins, outs):
        out = []
        for k in range(3):
            out.append((ins[6 + k], outs[6 + k], peers()[0]))
        for step, (x, i) in enumerate(zip(around("shard", 4), around("z", 4))):
            for k in range(6):
                if k % 3 == 0:
                    out.append((ins[k].at[:, x], outs[k].at[step], {"shard": x}))
                else:
                    out.append((ins[k].at[:, i], outs[k].at[step], {"z": i}))
        return out

    shapes = [(3, 8, 24, widths[0]), (3, 2, 4, 24, widths[1]), (3, 2, 4, 24, widths[2])] * 2
    shapes += [(4, 192, 768), (4, 192, 768), (384, 1536)]
    got = move("first_axis", 2, mix + give, shapes, peers, copies_2)
    mix = [
        total(at(m, shard if k % 3 == 0 else z, 1), *g).astype(BF)
        for k, (m, g) in enumerate(zip(mix, got[:6]))
    ]
    exp = [total(e, g).astype(BF) for e, g in zip(keep, got[6:])]

    mix = [m.reshape(2, 4, 24, -1) for m in mix]

    def peers_3():
        return [{"shard": x} for x in around("shard", 4)] + [{"z": i} for i in around("z", 4)]

    def copies_3(ins, outs):
        here = lax.axis_index("shard")
        out = []

        def shard_of(k, x):
            if k % 3 == 2:
                return ins[6 + k].at[:, pl.ds(pl.multiple_of(x * 384, 128), 384)]
            return ins[6 + k].at[x]

        for step, (x, i) in enumerate(zip(around("shard", 4), around("z", 4))):
            for k in range(3):
                out.append((shard_of(k, x), outs[6 + k].at[here], {"shard": x}))
            for k in range(6):
                if k % 3 == 0:
                    out.append((ins[k].at[:, i], outs[k].at[step], {"z": i}))
                else:
                    out.append((ins[k].at[:, x], outs[k].at[step], {"shard": x}))
        for k in range(3):
            out.append((shard_of(k, here), outs[6 + k].at[here], None))
        return out

    shapes = [(3, 2, 24, w) for w in widths] * 2 + [(4, 192, 768), (4, 192, 768), (4, 384, 384)]
    got = move("other_axis", 3, mix + exp, shapes, peers_3, copies_3)
    mix = [
        total(at(m, z if k % 3 == 0 else shard, 1), *g).astype(BF)
        for k, (m, g) in enumerate(zip(mix, got[:6]))
    ]
    exp = got[6:]

    def places():
        here = 2 * lax.axis_index("yh") + lax.axis_index("section")
        out = []
        for step in range(1, 4):
            there = lax.rem(here + step, 4)
            out.append((there // 2, lax.rem(there, 2)))
        return out

    def peers_4():
        out = [{"yh": y, "section": s} for y, s in places()]
        return out + [{"core": lax.rem(core_index() + 1, 2)}]

    def copies_4(ins, outs):
        out = []
        core = core_index()
        other = lax.rem(core + 1, 2)
        for k in range(3):
            half = ins[3 + k]
            out.append((half.at[pl.ds(2 * other, 2)], outs[3 + k].at[:, core], {"core": other}))
        for step, (y, s) in enumerate(places()):
            for k in range(3):
                out.append((ins[k].at[s, y], outs[k].at[step], {"yh": y, "section": s}))
        for k in range(3):
            half = ins[3 + k]
            out.append((half.at[pl.ds(2 * core, 2)], outs[3 + k].at[:, core], None))
        return out

    pairs = [jnp.stack([a, b]) for a, b in zip(mix[:3], mix[3:])]
    shapes = [(3, 24, w) for w in widths]
    shapes += [(2, 2, 192, 768), (2, 2, 192, 768), (2, 2, 384, 384)]
    got = move("last_axis", 4, pairs + list(exp), shapes, peers_4, copies_4)
    yh = lax.axis_index("yh")
    sums = [total(at(at(p, section, 0), yh, 0), *g) for p, g in zip(pairs, got[:3])]
    gate, up, down = (g.astype(F32) for g in got[3:])
    return sums, (gate.reshape(2, 384, 768), up.reshape(2, 384, 768), down.reshape(2, 768, 384))


def slot_tables(route_rows):
    rows = route_rows.shape[0]
    chosen = route_rows.T[None, :, :] == jnp.arange(EXPERTS, dtype=jnp.int32)[:, None, None]
    hot = jnp.any(chosen, axis=1)
    index = jnp.arange(rows, dtype=jnp.int32)
    before = (index[:, None] < index[None, :]).astype(BF)
    rank = jnp.where(hot, dot(hot.astype(BF), before), -1.0)
    place = jnp.arange(MAIN, dtype=jnp.int32)
    main = rank[:, None, :] == place.astype(F32)[None, :, None]
    extra = rank[:, None, :] == (MAIN + place % EXTRA).astype(F32)[None, :, None]
    extra = extra & (place < EXTRA * CHUNKS)[None, :, None]
    piece = place[:, None] // EXTRA == jnp.arange(CHUNKS, dtype=jnp.int32)[None, :]
    return hot, main, extra, piece


def pieces_side(extra, piece):
    count, place, rows = extra.shape
    wide = jnp.where(piece[None, :, :, None], extra[:, :, None, :], 0)
    return wide.reshape(count * place, CHUNKS * rows)


def stacked(field):
    return jnp.concatenate(jnp.split(field, CHUNKS, axis=1), axis=0)


def unstacked(field):
    return jnp.concatenate(jnp.split(field, CHUNKS, axis=0), axis=1)


def unfold_table(sources):
    row = jnp.arange(CHUNKS * sources * EXTRA, dtype=jnp.int32)
    piece, source, extra = row // (sources * EXTRA), row // EXTRA % sources, row % EXTRA
    column = jnp.arange(sources * MAIN, dtype=jnp.int32)
    return (
        (source * MAIN + piece * EXTRA + extra)[:, None] == column[None, :]
    ).astype(BF)


def exchange(message):
    return lax.all_to_all(message, CHIPS, split_axis=0, concat_axis=0, tiled=True)


def pick_rows(field, tables):
    main, side = tables["main"], tables["side"]
    return dot(main, field), dot(side, stacked(field))


def arrived_rows(message, unfold):
    width = message.shape[1] - 256
    extra = unstacked(dot(unfold, message[:, width:]).astype(BF))
    return jnp.concatenate([message[:, :width], extra], axis=0)


def fold_rows(rows, unfold, sources):
    main = rows[: sources * MAIN]
    extra = dot(unfold, stacked(rows[sources * MAIN :]), ((0,), (0,))).astype(BF)
    return jnp.concatenate([main, extra], axis=1)


def tables_of(route_rows):
    hot, main, extra, piece = slot_tables(route_rows)
    count, place, rows = main.shape
    return {
        "hot": hot,
        "main3": main,
        "extra3": extra,
        "piece": piece,
        "main": main.reshape(count * place, rows).astype(BF),
        "side": pieces_side(extra.astype(BF), piece),
    }


def low_pair(value):
    high = value.astype(BF)
    return high, (value - high.astype(F32)).astype(BF)


def forward_layer(layer_in, mixer, experts, tables, unfold, layout):
    qkv_w, out_w, router_w, gain_a, gain_m = mixer
    gate_w, up_w, down_w = experts()
    tok_rows, model_width = layer_in.shape
    query_width = HEADS * HEAD_DIM
    kv_width = (qkv_w.shape[1] - query_width) // 2
    kv_heads = kv_width // HEAD_DIM
    cosine, sine, allowed = layout
    h_attn = norm_rows(layer_in, gain_a).astype(BF)
    qkv = dot(h_attn, qkv_w)
    query = rotate(qkv[:, :query_width].reshape(tok_rows, HEADS, HEAD_DIM), cosine, sine)
    query = query.astype(BF).reshape(tok_rows, kv_heads, HEADS // kv_heads, HEAD_DIM)
    key = rotate(
        qkv[:, query_width : query_width + kv_width].reshape(tok_rows, kv_heads, HEAD_DIM),
        cosine,
        sine,
    ).astype(BF)
    value = qkv[:, query_width + kv_width :].astype(BF).reshape(tok_rows, kv_heads, HEAD_DIM)
    both = lax.all_gather(jnp.concatenate([key, value], axis=1), "shard", axis=0, tiled=True)
    key_all, value_all = both[:, :kv_heads], both[:, kv_heads:]
    scores = jnp.einsum("qgrd,kgd->grqk", query, key_all, preferred_element_type=F32)
    scores = jnp.where(allowed[None, None], scores * HEAD_DIM ** (-0.5), masked_score)
    exponent = jnp.exp(scores - jnp.max(scores, axis=-1, keepdims=True))
    probs = exponent / jnp.sum(exponent, axis=-1, keepdims=True)
    attended = jnp.einsum(
        "grqk,kgd->qgrd", probs.astype(BF), value_all, preferred_element_type=F32
    )
    attended = attended.reshape(tok_rows, query_width).astype(BF)
    x_mid = layer_in + dot(attended, out_w)
    h_moe = norm_rows(x_mid, gain_m).astype(BF)
    logits = dot(router_w, h_moe, ((0,), (1,)))
    hot = tables["hot"]
    top = jnp.max(jnp.where(hot, logits, masked_score), axis=0, keepdims=True)
    gate_exp = jnp.where(hot, jnp.exp(jnp.where(hot, logits, masked_score) - top), 0.0)
    gates = gate_exp / jnp.sum(gate_exp, axis=0, keepdims=True)
    main, side = pick_rows(h_moe, tables)
    message = jnp.concatenate([main, side], axis=1).astype(BF)
    arrived = arrived_rows(exchange(message), unfold)
    gate_pre = dot(arrived, gate_w)
    up_pre = dot(arrived, up_w)
    hidden = (jax.nn.silu(gate_pre) * up_pre).astype(BF)
    produced = dot(hidden, down_w).astype(BF)
    returned = exchange(fold_rows(produced, unfold, EXPERTS))
    gates_main = jnp.where(tables["main3"], gates[:, None, :], 0.0)
    gates_extra = jnp.where(tables["extra3"], gates[:, None, :], 0.0)
    back_main, back_side = returned[:, :model_width], returned[:, model_width:]
    rows_first = ((0,), (0,))
    block_out = x_mid
    for part in low_pair(gates_main.reshape(-1, tok_rows)):
        block_out = block_out + dot(part, back_main, rows_first)
    for part in low_pair(pieces_side(gates_extra, tables["piece"])):
        block_out = block_out + unstacked(dot(part, back_side, rows_first))
    stored = {
        "layer_in": layer_in,
        "h_attn": h_attn,
        "query": query,
        "key_all": key_all,
        "value_all": value_all,
        "probs": probs,
        "attended": attended,
        "x_mid": x_mid,
        "h_moe": h_moe,
        "gates": gates,
        "slot_main": jnp.sum(gates_main, axis=2).reshape(-1, 1),
        "slot_side": jnp.sum(gates_extra, axis=2).reshape(-1, 1),
        "back_main": back_main,
        "back_side": back_side,
        "arrived": arrived,
        "gate_pre": gate_pre,
        "up_pre": up_pre,
        "hidden": hidden,
    }
    return (block_out, stored)


def backward_layer(grad_out, stored, mixer, experts, tables, unfold, layout):
    qkv_w, out_w, router_w, gain_a, gain_m = mixer
    gate_w, up_w, down_w = experts()
    cosine, sine, _ = layout
    tok_rows, model_width = grad_out.shape
    query_width = HEADS * HEAD_DIM
    kv_width = (qkv_w.shape[1] - query_width) // 2
    kv_heads = kv_width // HEAD_DIM
    score_scale = HEAD_DIM ** (-0.5)
    rows_first, both_last = ((0,), (0,)), ((1,), (1,))
    gates, hot = stored["gates"], tables["hot"]
    main, side = pick_rows(grad_out.astype(BF), tables)
    message = jnp.concatenate(
        [main * stored["slot_main"], side * stored["slot_side"]], axis=1
    ).astype(BF)
    dgate_main = jnp.sum(main * stored["back_main"].astype(F32), axis=1)
    dgate_side = jnp.sum(side * stored["back_side"].astype(F32), axis=1)
    came = arrived_rows(exchange(message), unfold)
    gate_pre, up_pre = stored["gate_pre"], stored["up_pre"]
    grad_down = dot(stored["hidden"], came, rows_first).astype(BF)
    grad_hidden = dot(came, down_w, both_last)
    logistic = jax.nn.sigmoid(gate_pre)
    grad_gate_pre = (
        grad_hidden * up_pre * (logistic * (1.0 + gate_pre * (1.0 - logistic)))
    ).astype(BF)
    grad_up_pre = (grad_hidden * (gate_pre * logistic)).astype(BF)
    grad_rows = dot(grad_gate_pre, gate_w, both_last) + dot(grad_up_pre, up_w, both_last)
    returned = exchange(fold_rows(grad_rows.astype(BF), unfold, EXPERTS))
    grad_gate = dot(stored["arrived"], grad_gate_pre, rows_first).astype(BF)
    grad_up = dot(stored["arrived"], grad_up_pre, rows_first).astype(BF)
    dgate = jnp.sum(
        jnp.where(tables["main3"], dgate_main.reshape(EXPERTS, MAIN, 1), 0.0), axis=1
    ) + jnp.sum(jnp.where(tables["extra3"], dgate_side.reshape(EXPERTS, MAIN, 1), 0.0), axis=1)
    dlogits = jnp.where(
        hot, gates * (dgate - jnp.sum(gates * dgate, axis=0, keepdims=True)), 0.0
    ).astype(BF)
    h_moe = stored["h_moe"]
    grad_router = dot(h_moe, dlogits, ((0,), (1,)))
    grad_h_moe = (
        dot(tables["main"], returned[:, :model_width], rows_first)
        + unstacked(dot(tables["side"], returned[:, model_width:], rows_first))
        + dot(dlogits, router_w, ((0,), (1,)))
    )
    grad_x_mid, grad_gain_m = norm_back(stored["x_mid"], gain_m, grad_h_moe)
    grad_x_mid = grad_x_mid + grad_out
    grad_branch = grad_x_mid.astype(BF)
    grad_wout = dot(stored["attended"], grad_branch, rows_first).astype(BF)
    query = stored["query"]
    grad_att = dot(grad_branch, out_w, both_last).astype(BF).reshape(query.shape)
    probs, key_all, value_all = stored["probs"], stored["key_all"], stored["value_all"]
    grad_probs = jnp.einsum("qgrd,kgd->grqk", grad_att, value_all, preferred_element_type=F32)
    grad_value_all = jnp.einsum(
        "grqk,qgrd->kgd", probs.astype(BF), grad_att, preferred_element_type=F32
    )
    centre = jnp.sum(grad_probs * probs, axis=-1, keepdims=True)
    grad_scores = (probs * (grad_probs - centre)).astype(BF)
    grad_query = (
        jnp.einsum("grqk,kgd->qgrd", grad_scores, key_all, preferred_element_type=F32)
        * score_scale
    )
    grad_key_all = (
        jnp.einsum("grqk,qgrd->kgd", grad_scores, query, preferred_element_type=F32)
        * score_scale
    )
    both = jnp.concatenate([grad_key_all, grad_value_all], axis=1).astype(BF)
    parts = lax.all_to_all(
        both.reshape(-1, tok_rows, *both.shape[1:]), "shard", split_axis=0, concat_axis=0, tiled=True
    )
    both = parts.astype(F32).sum(axis=0)
    grad_query_pre = rotate_back(grad_query.reshape(tok_rows, HEADS, HEAD_DIM), cosine, sine)
    grad_key_pre = rotate_back(both[:, :kv_heads], cosine, sine)
    grad_qkv = jnp.concatenate(
        [
            grad_query_pre.reshape(tok_rows, query_width),
            grad_key_pre.reshape(tok_rows, kv_width),
            both[:, kv_heads:].reshape(tok_rows, kv_width),
        ],
        axis=1,
    ).astype(BF)
    grad_wqkv = dot(stored["h_attn"], grad_qkv, rows_first).astype(BF)
    grad_h_attn = dot(grad_qkv, qkv_w, both_last)
    grad_in, grad_gain_a = norm_back(stored["layer_in"], gain_a, grad_h_attn)
    grad_in = grad_in + grad_x_mid
    narrow = jnp.concatenate(
        [
            grad_router,
            grad_gain_a[:, None],
            grad_gain_m[:, None],
            jnp.zeros((model_width, 94), F32),
        ],
        axis=1,
    ).astype(BF)
    return (
        grad_in,
        (grad_wqkv, grad_wout, narrow),
        (grad_gate, grad_up, grad_down),
    )


def collect_mixer(local):
    whole = lax.all_gather(local, DEVICES, axis=0, tiled=True)
    return (
        whole[:, :2048],
        whole[:, 2048:3584],
        whole[:, 3584:3616],
        whole[:, 3616].astype(F32),
        whole[:, 3617].astype(F32),
    )


def pack_experts(gate, up, down):
    count, depth, width = gate.shape
    half = depth // 2
    across = down.reshape(count, 2, 2, half, depth)
    across = jnp.concatenate([across[:, :, 0], across[:, :, 1]], axis=-1)
    return jnp.stack(
        [gate.reshape(count, 2, half, width), up.reshape(count, 2, half, width), across], axis=2
    )


def unpack_halves(pieces):
    halves, shards, _, half, width = pieces.shape
    depth = shards * halves * half
    gate = pieces[:, :, 0].transpose(1, 0, 2, 3).reshape(depth, width)
    up = pieces[:, :, 1].transpose(1, 0, 2, 3).reshape(depth, width)
    down = pieces[:, :, 2].reshape(halves, shards, half, 2, width // 2)
    down = down.transpose(0, 3, 2, 1, 4).reshape(width, depth)
    return gate, up, down


def own_half(gate, up, down):
    pieces = pack_experts(gate, up, down)
    pieces = lax.all_to_all(pieces, "core", split_axis=1, concat_axis=0, tiled=True)[:, 0]
    return lax.all_to_all(pieces, "shard", split_axis=0, concat_axis=0, tiled=True)


def both_halves(piece):
    return unpack_halves(lax.all_gather(piece, "core", axis=0, tiled=False))


def per_device(
    tokens,
    routes,
    lengths,
    gain_attn,
    w_query,
    w_key,
    w_value,
    w_out,
    gain_moe,
    w_router,
    w_gate,
    w_up,
    w_down,
    cotangent,
):
    section = lax.axis_index("section")
    shard = lax.axis_index("shard")
    first = section == 0
    tok_rows, model_width = tokens.shape[1:]
    group_rows = tok_rows * lax.axis_size("shard")

    def mine(a):
        return lax.dynamic_index_in_dim(a, section, 0, keepdims=False)

    def by_layer(own, other):
        return jnp.where(first, own, other), jnp.where(first, other, own)

    local = jnp.concatenate(
        [
            w_query[0],
            w_key[0],
            w_value[0],
            w_out[0],
            w_router[0],
            gain_attn[0][:, None],
            gain_moe[0][:, None],
            jnp.zeros((w_query.shape[1], 94), BF),
        ],
        axis=1,
    )
    local_0, local_1 = by_layer(local, swap(local, "section"))
    mixers = [collect_mixer(local_0), collect_mixer(local_1)]
    route_other = swap(lax.dynamic_index_in_dim(routes[0], 1 - section, 0, keepdims=False), "section")
    tables = [tables_of(r) for r in by_layer(mine(routes[0]), route_other)]
    own_piece = own_half(w_gate[0], w_up[0], w_down[0])
    pieces = by_layer(own_piece, swap(own_piece, "section"))
    experts = [both_halves(p) for p in pieces]
    unfold = unfold_table(EXPERTS)

    segment, position = document_layout(mine(lengths[:, 0]), group_rows)
    row_start = shard * tok_rows
    own_segment = lax.dynamic_slice_in_dim(segment, row_start, tok_rows)
    cosine, sine = rotary_tables(
        lax.dynamic_slice_in_dim(position, row_start, tok_rows), HEAD_DIM
    )
    query_index = row_start + jnp.arange(tok_rows, dtype=jnp.int32)
    allowed = (own_segment[:, None] == segment[None, :]) & (
        query_index[:, None] >= jnp.arange(group_rows, dtype=jnp.int32)[None, :]
    )
    layout = (cosine, sine, allowed)

    current = mine(tokens).astype(F32)
    saved = []
    for layer in range(2):
        out, stored = forward_layer(
            current, mixers[layer], lambda: experts[layer], tables[layer], unfold, layout
        )
        saved.append(stored)
        low = out.astype(BF)
        current = low.astype(F32)
    other = swap(low, "section")
    mixed = jnp.where(first, jnp.stack([low, other]), jnp.stack([other, low]))

    grad = mine(cotangent).astype(F32)
    mixer_parts, expert_parts = [None, None], [None, None]
    for layer in (1, 0):
        grad, mixer_grad, expert_grad = backward_layer(
            grad, saved[layer], mixers[layer], lambda: experts[layer], tables[layer], unfold, layout
        )
        grad_low = grad.astype(BF)
        grad = grad_low.astype(F32)
        mixer_parts[layer] = mixer_grad
        expert_parts[layer] = expert_grad

    sums, (grad_gate, grad_up, grad_down) = reduce_all(mixer_parts, expert_parts, section)
    qkv, grad_wo, narrow = sums
    return (
        mixed,
        grad_low[None],
        narrow[:, 32][None],
        qkv[:, :1536][None],
        qkv[:, 1536:1792][None],
        qkv[:, 1792:][None],
        grad_wo[None],
        narrow[:, 33][None],
        narrow[:, :32][None],
        grad_gate[None],
        grad_up[None],
        grad_down[None],
    )


def solution(mesh):
    fine = Mesh(mesh.devices.reshape(2, 2, 4, 2, 4), ("section", *DEVICES))
    expert = ("yh", "z", "core")
    return jax.shard_map(
        per_device,
        mesh=fine,
        in_specs=(
            P(None, DEVICES, None),
            P("section", None, DEVICES, None),
            P(None, expert, None),
            P("section", DEVICES),
            P("section", DEVICES, None),
            P("section", DEVICES, None),
            P("section", DEVICES, None),
            P("section", DEVICES, None),
            P("section", DEVICES),
            P("section", DEVICES, None),
            P("section", expert, "shard", None),
            P("section", expert, "shard", None),
            P("section", expert, None, "shard"),
            P(None, DEVICES, None),
        ),
        out_specs=(
            P(None, DEVICES, None),
            P("section", DEVICES, None),
            P("section", DEVICES),
            P("section", DEVICES, None),
            P("section", DEVICES, None),
            P("section", DEVICES, None),
            P("section", DEVICES, None),
            P("section", DEVICES),
            P("section", DEVICES, None),
            P("section", expert, "shard", None),
            P("section", expert, "shard", None),
            P("section", expert, None, "shard"),
        ),
        check_vma=False,
    )
```

```python
import jax
import jax.numpy as jnp
from jax import lax
from jax.experimental import pallas as pl
from jax.experimental.pallas import tpu as pltpu
from jax.sharding import Mesh
from jax.sharding import PartitionSpec as P

HEADS = 12
HEAD_DIM = 128
EXPERTS = 32
MAIN = 16
EXTRA = 2
CHUNKS = 6

epsilon = 1e-06
rope_base = 1000000.0
masked_score = -1e30

BF = jnp.bfloat16
F32 = jnp.float32
CHIPS = ("yh", "z", "shard")
DEVICES = ("yh", "z", "core", "shard")


def dot(a, b, dims=((1,), (0,))):
    return lax.dot_general(a, b, (dims, ((), ())), preferred_element_type=F32)


def norm_rows(field, gain_row):
    return field * lax.rsqrt(jnp.mean(field * field, axis=-1, keepdims=True) + epsilon) * gain_row


def norm_back(field, gain_row, grad):
    scale = lax.rsqrt(jnp.mean(field * field, axis=-1, keepdims=True) + epsilon)
    scaled = grad * gain_row
    grad_gain = jnp.sum(grad * field * scale, axis=0)
    centre = jnp.mean(scaled * field, axis=-1, keepdims=True)
    return scale * scaled - field * (scale * scale * scale) * centre, grad_gain


def document_layout(doc_lengths, group_rows):
    doc_ends = jnp.cumsum(doc_lengths)
    starts = doc_ends - doc_lengths
    row_index = jnp.arange(group_rows, dtype=jnp.int32)
    segment = jnp.sum((row_index[:, None] >= doc_ends[None, :]).astype(jnp.int32), axis=1)
    member = segment[:, None] == jnp.arange(doc_lengths.shape[0], dtype=jnp.int32)[None, :]
    position = row_index - jnp.sum(jnp.where(member, starts[None, :], 0), axis=1)
    return (segment, position)


def rotary_tables(position, head_size):
    half_dim = head_size // 2
    frequency = rope_base ** (-2.0 * jnp.arange(half_dim, dtype=F32) / head_size)
    angles = position.astype(F32)[:, None] * frequency[None, :]
    return (jnp.cos(angles)[:, None, :], jnp.sin(angles)[:, None, :])


def rotate(field, cosine, sine):
    half_dim = field.shape[-1] // 2
    first, second = field[..., :half_dim], field[..., half_dim:]
    return jnp.concatenate(
        [first * cosine - second * sine, second * cosine + first * sine], axis=-1
    )


def rotate_back(field, cosine, sine):
    half_dim = field.shape[-1] // 2
    first, second = field[..., :half_dim], field[..., half_dim:]
    return jnp.concatenate(
        [first * cosine + second * sine, second * cosine - first * sine], axis=-1
    )


def swap(value, axis):
    return lax.ppermute(value, axis, [(0, 1), (1, 0)])


def around(axis, size):
    here = lax.axis_index(axis)
    return [lax.rem(here + step, size) for step in range(1, size)]


def move(name, number, arrays, shapes, peers, copies):
    count = len(arrays)
    total = 40

    def kernel(*refs):
        ins, outs = refs[:count], refs[count : count + len(shapes)]
        sent, got = refs[count + len(shapes) :]
        barrier = pltpu.get_barrier_semaphore()
        near = peers()
        for peer in near:
            pl.semaphore_signal(
                barrier, inc=1, device_id=peer, device_id_type=pl.DeviceIdType.MESH
            )
        pl.semaphore_wait(barrier, len(near))
        started = []
        for k, (source, target, device) in enumerate(copies(ins, outs)):
            if device is None:
                copy = pltpu.make_async_copy(source, target, got.at[k])
            else:
                copy = pltpu.make_async_remote_copy(
                    src_ref=source,
                    dst_ref=target,
                    send_sem=sent.at[k],
                    recv_sem=got.at[k],
                    device_id=device,
                    device_id_type=pl.DeviceIdType.MESH,
                )
            copy.start()
            started.append(copy)
        for copy in started:
            copy.wait()

    space = pl.BlockSpec(memory_space=pltpu.HBM)
    return pl.pallas_call(
        kernel,
        out_shape=[jax.ShapeDtypeStruct(s, BF) for s in shapes],
        in_specs=[space] * count,
        out_specs=[space] * len(shapes),
        scratch_shapes=[pltpu.SemaphoreType.DMA((total,)), pltpu.SemaphoreType.DMA((total,))],
        compiler_params=pltpu.CompilerParams(collective_id=number, has_side_effects=True),
        name=name,
    )(*arrays)


def total(*parts):
    out = parts[0].astype(F32)
    for part in parts[1:]:
        out = out + part.astype(F32)
    return out


def at(array, index, axis):
    return lax.dynamic_index_in_dim(array, index, axis, keepdims=False)


def other(axis):
    return lax.rem(lax.axis_index(axis) + 1, 2)


def sum_over_cores(grads, number):
    gate, up, down = grads
    halves = [gate.reshape(4, 2, 192, 768), up.reshape(4, 2, 192, 768), down.reshape(2, 384, 1536)]

    def copies(ins, outs):
        there = other("core")
        views = [ins[0].at[:, there], ins[1].at[:, there], ins[2].at[there]]
        return [(v, o, {"core": there}) for v, o in zip(views, outs)]

    shapes = [(4, 192, 768), (4, 192, 768), (384, 1536)]
    got = move("expert_cores", number, halves, shapes, lambda: [{"core": other("core")}], copies)
    core = lax.axis_index("core")
    return [total(at(h, core, 0 if k == 2 else 1), g) for k, (h, g) in enumerate(zip(halves, got))]


def reduce_all(mixer_grads, late, exp):
    core, shard, z, yh, section = (
        lax.axis_index(a) for a in ("core", "shard", "z", "yh", "section")
    )
    widths = [g.shape[1] for g in mixer_grads]
    mix = [g.reshape(8, 2, 4, 24, w) for g, w in zip(mixer_grads, widths)]

    got = move(
        "cores",
        1,
        mix,
        [(8, 4, 24, w) for w in widths],
        lambda: [{"core": other("core")}],
        lambda ins, outs: [
            (r.at[:, other("core")], o, {"core": other("core")}) for r, o in zip(ins, outs)
        ],
    )
    mix = [total(at(m, core, 1), g).astype(BF) for m, g in zip(mix, got)]

    mix = [m.reshape(2, 4, 4, 24, -1) for m in mix]

    def peers_2():
        return [{"shard": x} for x in around("shard", 4)] + [{"z": i} for i in around("z", 4)]

    def copies_2(ins, outs):
        here = lax.axis_index("shard")
        out = []
        for step, (x, i) in enumerate(zip(around("shard", 4), around("z", 4))):
            for k in range(3):
                out.append((ins[k].at[:, i], outs[k].at[step], {"z": i}))
            for k in range(3, 6):
                if k == 5:
                    source = ins[k].at[:, pl.ds(pl.multiple_of(x * 384, 128), 384)]
                else:
                    source = ins[k].at[x]
                out.append((source, outs[k].at[here], {"shard": x}))
        return out

    shapes = [(3, 2, 4, 24, w) for w in widths] + [(4, 192, 768), (4, 192, 768), (4, 384, 384)]
    got = move("first_axis", 2, mix + exp, shapes, peers_2, copies_2)
    mix = [total(at(m, z, 1), *g).astype(BF) for m, g in zip(mix, got[:3])]
    own = [at(exp[0], shard, 0), at(exp[1], shard, 0)]
    own.append(lax.dynamic_slice_in_dim(exp[2], shard * 384, 384, 1))
    exp = [lax.dynamic_update_index_in_dim(g, o, shard, 0) for g, o in zip(got[3:], own)]

    got = move(
        "other_axis",
        3,
        mix,
        [(3, 2, 24, w) for w in widths],
        lambda: [{"shard": x} for x in around("shard", 4)],
        lambda ins, outs: [
            (ins[k].at[:, x], outs[k].at[step], {"shard": x})
            for step, x in enumerate(around("shard", 4))
            for k in range(3)
        ],
    )
    mix = [total(at(m, shard, 1), *g).astype(BF) for m, g in zip(mix, got)]

    def places():
        here = 2 * lax.axis_index("yh") + lax.axis_index("section")
        there = [lax.rem(here + step, 4) for step in range(1, 4)]
        return [(t // 2, lax.rem(t, 2)) for t in there]

    def peers_4():
        return [{"yh": y, "section": s} for y, s in places()] + [{"core": other("core")}]

    def copies_4(ins, outs):
        there = other("core")
        out = []
        for k in range(3, 6):
            out.append((ins[k].at[pl.ds(2 * there, 2)], outs[k], {"core": there}))
        for step, (y, s) in enumerate(places()):
            for k in range(3):
                out.append((ins[k].at[s, y], outs[k].at[step], {"yh": y, "section": s}))
        return out

    mine = (jnp.arange(2) == yh)[:, None, None]
    late = [jnp.where(mine, part[None], jnp.zeros((), BF)) for part in late]
    pairs = [jnp.stack([a, b]) for a, b in zip(mix, late)]
    shapes = [(3, 24, w) for w in widths] + [(2, 192, 768), (2, 192, 768), (2, 384, 384)]
    got = move("last_axis", 4, pairs + exp, shapes, peers_4, copies_4)
    sums = [total(at(at(p, section, 0), yh, 0), *g) for p, g in zip(pairs, got[:3])]
    kept = [lax.dynamic_slice_in_dim(e, 2 * core, 2, 0) for e in exp]
    grads = []
    for k, g in zip(kept, got[3:]):
        low = jnp.where(core == 0, k, g)
        high = jnp.where(core == 0, g, k)
        grads.append(jnp.concatenate([low, high], axis=1).astype(F32))
    return sums, grads


def gather_weights(local, experts):
    widths = [a.shape[1] for a in local]

    def kernel(*refs):
        mine, shards = refs[:3], refs[3:6]
        full, whole = refs[6:9], refs[9:12]
        stage = refs[12:15]
        sent, got, sent_x, got_e, sent_c, got_c, sent_y, sent_o, local_sem = refs[15:]
        s, yh, z, c, x = (lax.axis_index(a) for a in ("section", "yh", "z", "core", "shard"))
        place = 2 * yh + s
        ys = [lax.rem(place + k, 4) for k in (1, 2, 3)]
        ys = [{"yh": y // 2, "section": lax.rem(y, 2)} for y in ys]
        xs = [{"shard": lax.rem(x + k, 4)} for k in (1, 2, 3)]
        z_up, z_down = lax.rem(z + 1, 4), lax.rem(z + 3, 4)
        sibling, partner = {"core": 1 - c}, {"section": 1 - s}

        def piece(k, i, h):
            if k == 2:
                return shards[2].at[i, pl.ds(pl.multiple_of(h * 384, 128), 384)]
            return shards[k].at[i, pl.ds(pl.multiple_of(h * 192, 64), 192)]

        def landing(k, layer, source, half):
            if k == 2:
                return whole[2].at[layer, half, :, pl.ds(pl.multiple_of(source * 384, 128), 384)]
            return whole[k].at[layer, source, half]

        def remote(source, target, send, receive, device):
            return pltpu.make_async_remote_copy(
                src_ref=source,
                dst_ref=target,
                send_sem=send,
                recv_sem=receive,
                device_id=device,
                device_id_type=pl.DeviceIdType.MESH,
            )

        def start(copies):
            for copy in copies:
                copy.start()
            return copies

        def finish(copies):
            for copy in copies:
                copy.wait()

        has_own = x // 2 == c
        own = lax.rem(x, 2)
        staged = start(
            [pltpu.make_async_copy(piece(k, own, c), stage[k], local_sem.at[k]) for k in range(3)]
        )
        barrier = pltpu.get_barrier_semaphore()
        near = ys + xs + [{"z": z_up}, {"z": z_down}, sibling]
        near += [{"shard": lax.rem(x + k, 4), "core": 1 - c} for k in (1, 2, 3)]
        for peer in near:
            pl.semaphore_signal(
                barrier, inc=1, device_id=peer, device_id_type=pl.DeviceIdType.MESH
            )
        pl.semaphore_wait(barrier, len(near))

        here = [f.at[s, yh, z, c, x] for f in full]
        kept = start(
            [pltpu.make_async_copy(mine[j], here[j], local_sem.at[3 + j]) for j in range(3)]
        )
        along_y = start(
            [
                remote(mine[j], here[j], sent.at[k * 3 + j], got.at[k * 3 + j], device)
                for k, device in enumerate(ys)
                for j in range(3)
            ]
        )
        finish(staged)

        @pl.when(has_own)
        def _():
            for k in range(3):
                remote(
                    piece(k, own, 1 - c),
                    landing(k, s, x, 1 - c),
                    sent_o.at[k],
                    got_e.at[s, x, k],
                    sibling,
                ).start()
                pltpu.make_async_copy(stage[k], landing(k, s, x, c), got_e.at[s, x, k]).start()

        def pass_on(layer, distance, to_partner):
            source = lax.rem(x + distance, 4)
            for k in range(3):
                view = landing(k, layer, source, c)
                receive = got_e.at[layer, source, k]
                remote(view, view, sent_o.at[k], receive, sibling).wait_recv()
                if to_partner:
                    remote(view, view, sent_y.at[distance, k], receive, partner).start()
                across = got_c.at[layer, source, k]
                remote(view, view, sent_c.at[layer, source, k], across, sibling).start()

        finish(along_y)
        finish(kept)
        views = [f.at[0, :, z, c, x] for f in full]
        along_x = start(
            [
                remote(v, v, sent.at[9 + k * 3 + j], got.at[9 + k * 3 + j], device)
                for k, device in enumerate(xs)
                for j, v in enumerate(views)
            ]
        )
        pass_on(s, 0, True)
        finish(along_x)

        def ring(base, up_views, down_views):
            out = []
            for j in range(3):
                n = base + 2 * j
                out.append(remote(up_views[j], up_views[j], sent.at[n], got.at[n], {"z": z_up}))
                n = n + 1
                out.append(
                    remote(down_views[j], down_views[j], sent.at[n], got.at[n], {"z": z_down})
                )
            return start(out)

        views = [f.at[0, :, z, c] for f in full]
        along_z = ring(18, views, views)
        for i in range(2):

            @pl.when(x != 2 * c + i)
            def _():
                for h in range(2):
                    for k in range(3):
                        remote(
                            piece(k, i, h),
                            landing(k, s, x, h),
                            sent_x.at[(i * 2 + h) * 3 + k],
                            got_e.at[s, x, k],
                            {"shard": 2 * c + i, "core": h},
                        ).start()

        finish(along_z)
        along_z = ring(
            24, [f.at[0, 0, z_down, c] for f in full], [f.at[0, 1, z_up, c] for f in full]
        )
        for distance in (1, 3, 2):
            pass_on(s, distance, True)
        finish(along_z)
        views = [f.at[0, :, :, c] for f in full]
        across = start(
            [remote(v, v, sent.at[30 + j], got.at[30 + j], sibling) for j, v in enumerate(views)]
        )
        for distance in (0, 1, 3, 2):
            pass_on(1 - s, distance, False)

        finish(across)
        for i in range(2):

            @pl.when(x != 2 * c + i)
            def _():
                for h in range(2):
                    for k in range(3):
                        view = piece(k, i, h)
                        n = (i * 2 + h) * 3 + k
                        remote(view, view, sent_x.at[n], got_e.at[0, 0, k], sibling).wait_send()

        @pl.when(has_own)
        def _():
            for k in range(3):
                view = piece(k, own, 1 - c)
                remote(view, view, sent_o.at[k], got_e.at[0, 0, k], sibling).wait_send()

        for source in range(4):
            for k in range(3):
                view = landing(k, s, source, c)
                send = sent_y.at[source, k]
                remote(view, view, send, got_e.at[0, 0, k], partner).wait_send()
                for layer in range(2):
                    view = landing(k, layer, source, c)
                    arrived = landing(k, layer, source, 1 - c)
                    send, receive = sent_c.at[layer, source, k], got_c.at[layer, source, k]
                    remote(view, view, send, receive, sibling).wait_send()
                    remote(arrived, arrived, send, receive, sibling).wait_recv()

    space = pl.BlockSpec(memory_space=pltpu.HBM)
    near_space = pl.BlockSpec(memory_space=pltpu.VMEM)
    shapes = [(2, 2, 4, 2, 4, 24, w) for w in widths]
    shapes += [(2, 4, 2, 192, 768), (2, 4, 2, 192, 768), (2, 2, 384, 1536)]
    dma = pltpu.SemaphoreType.DMA
    return pl.pallas_call(
        kernel,
        out_shape=[jax.ShapeDtypeStruct(shape, BF) for shape in shapes],
        in_specs=[near_space] * 3 + [space] * 3,
        out_specs=[space] * 6,
        scratch_shapes=[
            pltpu.VMEM((192, 768), BF),
            pltpu.VMEM((192, 768), BF),
            pltpu.VMEM((384, 384), BF),
            dma((33,)),
            dma((33,)),
            dma((12,)),
            dma((2, 4, 3)),
            dma((2, 4, 3)),
            dma((2, 4, 3)),
            dma((4, 3)),
            dma((3,)),
            dma((6,)),
        ],
        compiler_params=pltpu.CompilerParams(collective_id=0, has_side_effects=True),
        name="gather_weights",
    )(*local, *experts)


def slot_tables(route_rows):
    rows = route_rows.shape[0]
    chosen = route_rows.T[None, :, :] == jnp.arange(EXPERTS, dtype=jnp.int32)[:, None, None]
    hot = jnp.any(chosen, axis=1)
    index = jnp.arange(rows, dtype=jnp.int32)
    before = (index[:, None] < index[None, :]).astype(BF)
    rank = jnp.where(hot, dot(hot.astype(BF), before), -1.0)
    place = jnp.arange(MAIN, dtype=jnp.int32)
    main = rank[:, None, :] == place.astype(F32)[None, :, None]
    extra = rank[:, None, :] == (MAIN + place % EXTRA).astype(F32)[None, :, None]
    extra = extra & (place < EXTRA * CHUNKS)[None, :, None]
    piece = place[:, None] // EXTRA == jnp.arange(CHUNKS, dtype=jnp.int32)[None, :]
    return hot, main, extra, piece


def pieces_side(extra, piece):
    count, place, rows = extra.shape
    wide = jnp.where(piece[None, :, :, None], extra[:, :, None, :], 0)
    return wide.reshape(count * place, CHUNKS * rows)


def stacked(field):
    return jnp.concatenate(jnp.split(field, CHUNKS, axis=1), axis=0)


def unstacked(field):
    return jnp.concatenate(jnp.split(field, CHUNKS, axis=0), axis=1)


def unfold_table(sources):
    row = jnp.arange(CHUNKS * sources * EXTRA, dtype=jnp.int32)
    piece, source, extra = row // (sources * EXTRA), row // EXTRA % sources, row % EXTRA
    column = jnp.arange(sources * MAIN, dtype=jnp.int32)
    return (
        (source * MAIN + piece * EXTRA + extra)[:, None] == column[None, :]
    ).astype(BF)


def exchange(message):
    return lax.all_to_all(message, CHIPS, split_axis=0, concat_axis=0, tiled=True)


def pick_rows(field, tables):
    main, side = tables["main"], tables["side"]
    return dot(main, field), dot(side, stacked(field))


def arrived_rows(message, unfold):
    width = message.shape[1] - 256
    extra = unstacked(dot(unfold, message[:, width:]).astype(BF))
    return jnp.concatenate([message[:, :width], extra], axis=0)


def fold_rows(rows, unfold, sources):
    main = rows[: sources * MAIN]
    extra = dot(unfold, stacked(rows[sources * MAIN :]), ((0,), (0,))).astype(BF)
    return jnp.concatenate([main, extra], axis=1)


def tables_of(route_rows):
    hot, main, extra, piece = slot_tables(route_rows)
    count, place, rows = main.shape
    return {
        "hot": hot,
        "main3": main,
        "extra3": extra,
        "piece": piece,
        "main": main.reshape(count * place, rows).astype(BF),
        "side": pieces_side(extra.astype(BF), piece),
    }


def low_pair(value):
    high = value.astype(BF)
    return high, (value - high.astype(F32)).astype(BF)


def forward_layer(layer_in, mixer, experts, tables, unfold, layout):
    qkv_w, out_w, router_w, gain_a, gain_m = mixer
    gate_w, up_w, down_w = experts()
    tok_rows, model_width = layer_in.shape
    query_width = HEADS * HEAD_DIM
    kv_width = (qkv_w.shape[1] - query_width) // 2
    kv_heads = kv_width // HEAD_DIM
    cosine, sine, allowed = layout
    h_attn = norm_rows(layer_in, gain_a).astype(BF)
    qkv = dot(h_attn, qkv_w)
    query = rotate(qkv[:, :query_width].reshape(tok_rows, HEADS, HEAD_DIM), cosine, sine)
    query = query.astype(BF).reshape(tok_rows, kv_heads, HEADS // kv_heads, HEAD_DIM)
    key = rotate(
        qkv[:, query_width : query_width + kv_width].reshape(tok_rows, kv_heads, HEAD_DIM),
        cosine,
        sine,
    ).astype(BF)
    value = qkv[:, query_width + kv_width :].astype(BF).reshape(tok_rows, kv_heads, HEAD_DIM)
    both = lax.all_gather(jnp.concatenate([key, value], axis=1), "shard", axis=0, tiled=True)
    key_all, value_all = both[:, :kv_heads], both[:, kv_heads:]
    scores = jnp.einsum("qgrd,kgd->grqk", query, key_all, preferred_element_type=F32)
    scores = jnp.where(allowed[None, None], scores * HEAD_DIM ** (-0.5), masked_score)
    exponent = jnp.exp(scores - jnp.max(scores, axis=-1, keepdims=True))
    probs = exponent / jnp.sum(exponent, axis=-1, keepdims=True)
    attended = jnp.einsum(
        "grqk,kgd->qgrd", probs.astype(BF), value_all, preferred_element_type=F32
    )
    attended = attended.reshape(tok_rows, query_width).astype(BF)
    x_mid = layer_in + dot(attended, out_w)
    h_moe = norm_rows(x_mid, gain_m).astype(BF)
    logits = dot(router_w, h_moe, ((0,), (1,)))
    hot = tables["hot"]
    top = jnp.max(jnp.where(hot, logits, masked_score), axis=0, keepdims=True)
    gate_exp = jnp.where(hot, jnp.exp(jnp.where(hot, logits, masked_score) - top), 0.0)
    gates = gate_exp / jnp.sum(gate_exp, axis=0, keepdims=True)
    main, side = pick_rows(h_moe, tables)
    message = jnp.concatenate([main, side], axis=1).astype(BF)
    arrived = arrived_rows(exchange(message), unfold)
    gate_pre = dot(arrived, gate_w)
    up_pre = dot(arrived, up_w)
    hidden = (jax.nn.silu(gate_pre) * up_pre).astype(BF)
    produced = dot(hidden, down_w).astype(BF)
    returned = exchange(fold_rows(produced, unfold, EXPERTS))
    gates_main = jnp.where(tables["main3"], gates[:, None, :], 0.0)
    gates_extra = jnp.where(tables["extra3"], gates[:, None, :], 0.0)
    back_main, back_side = returned[:, :model_width], returned[:, model_width:]
    rows_first = ((0,), (0,))
    block_out = x_mid
    for part in low_pair(gates_main.reshape(-1, tok_rows)):
        block_out = block_out + dot(part, back_main, rows_first)
    for part in low_pair(pieces_side(gates_extra, tables["piece"])):
        block_out = block_out + unstacked(dot(part, back_side, rows_first))
    stored = {
        "layer_in": layer_in,
        "h_attn": h_attn,
        "query": query,
        "key_all": key_all,
        "value_all": value_all,
        "probs": probs,
        "attended": attended,
        "x_mid": x_mid,
        "h_moe": h_moe,
        "gates": gates,
        "slot_main": jnp.sum(gates_main, axis=2).reshape(-1, 1),
        "slot_side": jnp.sum(gates_extra, axis=2).reshape(-1, 1),
        "back_main": back_main,
        "back_side": back_side,
        "arrived": arrived,
        "gate_pre": gate_pre,
        "up_pre": up_pre,
        "hidden": hidden,
    }
    return (block_out, stored)


def backward_layer(grad_out, stored, mixer, experts, tables, unfold, layout, number):
    qkv_w, out_w, router_w, gain_a, gain_m = mixer
    gate_w, up_w, down_w = experts()
    cosine, sine, _ = layout
    tok_rows, model_width = grad_out.shape
    query_width = HEADS * HEAD_DIM
    kv_width = (qkv_w.shape[1] - query_width) // 2
    kv_heads = kv_width // HEAD_DIM
    score_scale = HEAD_DIM ** (-0.5)
    rows_first, both_last = ((0,), (0,)), ((1,), (1,))
    gates, hot = stored["gates"], tables["hot"]
    main, side = pick_rows(grad_out.astype(BF), tables)
    message = jnp.concatenate(
        [main * stored["slot_main"], side * stored["slot_side"]], axis=1
    ).astype(BF)
    dgate_main = jnp.sum(main * stored["back_main"].astype(F32), axis=1)
    dgate_side = jnp.sum(side * stored["back_side"].astype(F32), axis=1)
    came = arrived_rows(exchange(message), unfold)
    gate_pre, up_pre = stored["gate_pre"], stored["up_pre"]
    grad_down = dot(stored["hidden"], came, rows_first).astype(BF)
    grad_hidden = dot(came, down_w, both_last)
    logistic = jax.nn.sigmoid(gate_pre)
    grad_gate_pre = (
        grad_hidden * up_pre * (logistic * (1.0 + gate_pre * (1.0 - logistic)))
    ).astype(BF)
    grad_up_pre = (grad_hidden * (gate_pre * logistic)).astype(BF)
    grad_rows = dot(grad_gate_pre, gate_w, both_last) + dot(grad_up_pre, up_w, both_last)
    returned = exchange(fold_rows(grad_rows.astype(BF), unfold, EXPERTS))
    grad_gate = dot(stored["arrived"], grad_gate_pre, rows_first).astype(BF)
    grad_up = dot(stored["arrived"], grad_up_pre, rows_first).astype(BF)
    halves = [h.astype(BF) for h in sum_over_cores((grad_gate, grad_up, grad_down), number)]
    returned, *halves = lax.optimization_barrier((returned, *halves))
    dgate = jnp.sum(
        jnp.where(tables["main3"], dgate_main.reshape(EXPERTS, MAIN, 1), 0.0), axis=1
    ) + jnp.sum(jnp.where(tables["extra3"], dgate_side.reshape(EXPERTS, MAIN, 1), 0.0), axis=1)
    dlogits = jnp.where(
        hot, gates * (dgate - jnp.sum(gates * dgate, axis=0, keepdims=True)), 0.0
    ).astype(BF)
    h_moe = stored["h_moe"]
    grad_router = dot(h_moe, dlogits, ((0,), (1,)))
    grad_h_moe = (
        dot(tables["main"], returned[:, :model_width], rows_first)
        + unstacked(dot(tables["side"], returned[:, model_width:], rows_first))
        + dot(dlogits, router_w, ((0,), (1,)))
    )
    grad_x_mid, grad_gain_m = norm_back(stored["x_mid"], gain_m, grad_h_moe)
    grad_x_mid = grad_x_mid + grad_out
    grad_branch = grad_x_mid.astype(BF)
    grad_wout = dot(stored["attended"], grad_branch, rows_first).astype(BF)
    query = stored["query"]
    grad_att = dot(grad_branch, out_w, both_last).astype(BF).reshape(query.shape)
    probs, key_all, value_all = stored["probs"], stored["key_all"], stored["value_all"]
    grad_probs = jnp.einsum("qgrd,kgd->grqk", grad_att, value_all, preferred_element_type=F32)
    grad_value_all = jnp.einsum(
        "grqk,qgrd->kgd", probs.astype(BF), grad_att, preferred_element_type=F32
    )
    centre = jnp.sum(grad_probs * probs, axis=-1, keepdims=True)
    grad_scores = (probs * (grad_probs - centre)).astype(BF)
    grad_query = (
        jnp.einsum("grqk,kgd->qgrd", grad_scores, key_all, preferred_element_type=F32)
        * score_scale
    )
    grad_key_all = (
        jnp.einsum("grqk,qgrd->kgd", grad_scores, query, preferred_element_type=F32)
        * score_scale
    )
    both = jnp.concatenate([grad_key_all, grad_value_all], axis=1).astype(BF)
    parts = lax.all_to_all(
        both.reshape(-1, tok_rows, *both.shape[1:]), "shard", split_axis=0, concat_axis=0, tiled=True
    )
    both = parts.astype(F32).sum(axis=0)
    grad_query_pre = rotate_back(grad_query.reshape(tok_rows, HEADS, HEAD_DIM), cosine, sine)
    grad_key_pre = rotate_back(both[:, :kv_heads], cosine, sine)
    grad_qkv = jnp.concatenate(
        [
            grad_query_pre.reshape(tok_rows, query_width),
            grad_key_pre.reshape(tok_rows, kv_width),
            both[:, kv_heads:].reshape(tok_rows, kv_width),
        ],
        axis=1,
    ).astype(BF)
    grad_wqkv = dot(stored["h_attn"], grad_qkv, rows_first).astype(BF)
    grad_h_attn = dot(grad_qkv, qkv_w, both_last)
    grad_in, grad_gain_a = norm_back(stored["layer_in"], gain_a, grad_h_attn)
    grad_in = grad_in + grad_x_mid
    narrow = jnp.concatenate(
        [
            grad_router,
            grad_gain_a[:, None],
            grad_gain_m[:, None],
            jnp.zeros((model_width, 94), F32),
        ],
        axis=1,
    ).astype(BF)
    return (
        grad_in,
        (grad_wqkv, grad_wout, narrow),
        halves,
    )


def split_mixer(qkv, out, narrow):
    return qkv, out, narrow[:, :32], narrow[:, 32].astype(F32), narrow[:, 33].astype(F32)


def per_device(
    tokens,
    routes,
    lengths,
    gain_attn,
    w_query,
    w_key,
    w_value,
    w_out,
    gain_moe,
    w_router,
    w_gate,
    w_up,
    w_down,
    cotangent,
):
    section, yh, z, core, shard = (
        lax.axis_index(a) for a in ("section", "yh", "z", "core", "shard")
    )
    first = section == 0
    tok_rows, model_width = tokens.shape[1:]
    group_rows = tok_rows * lax.axis_size("shard")

    def mine(a):
        return lax.dynamic_index_in_dim(a, section, 0, keepdims=False)

    def by_layer(own, other):
        return jnp.where(first, own, other), jnp.where(first, other, own)

    local = [
        jnp.concatenate([w_query[0], w_key[0], w_value[0]], axis=1),
        w_out[0],
        jnp.concatenate(
            [
                w_router[0],
                gain_attn[0][:, None],
                gain_moe[0][:, None],
                jnp.zeros((w_query.shape[1], 94), BF),
            ],
            axis=1,
        ),
    ]
    weights = gather_weights(local, (w_gate[0], w_up[0], w_down[0]))
    full, whole = weights[:3], weights[3:]
    index = ((yh * 4 + z) * 2 + core) * 4 + shard
    late = jnp.concatenate([at(f[1].reshape(64, 24, -1), index, 0) for f in full], axis=1)
    late = lax.all_gather(late, DEVICES, axis=0, tiled=True)
    mixers = [
        split_mixer(*(f[0].reshape(model_width, -1) for f in full)),
        split_mixer(late[:, :2048], late[:, 2048:3584], late[:, 3584:]),
    ]
    route_other = swap(at(routes[0], 1 - section, 0), "section")
    tables = [tables_of(r) for r in by_layer(mine(routes[0]), route_other)]
    experts = [
        (
            whole[0][layer].reshape(model_width, 768),
            whole[1][layer].reshape(model_width, 768),
            whole[2][layer].reshape(768, model_width),
        )
        for layer in range(2)
    ]
    unfold = unfold_table(EXPERTS)

    segment, position = document_layout(mine(lengths[:, 0]), group_rows)
    row_start = shard * tok_rows
    own_segment = lax.dynamic_slice_in_dim(segment, row_start, tok_rows)
    cosine, sine = rotary_tables(
        lax.dynamic_slice_in_dim(position, row_start, tok_rows), HEAD_DIM
    )
    query_index = row_start + jnp.arange(tok_rows, dtype=jnp.int32)
    allowed = (own_segment[:, None] == segment[None, :]) & (
        query_index[:, None] >= jnp.arange(group_rows, dtype=jnp.int32)[None, :]
    )
    layout = (cosine, sine, allowed)

    current = mine(tokens).astype(F32)
    saved = []
    for layer in range(2):
        out, stored = forward_layer(
            current, mixers[layer], lambda: experts[layer], tables[layer], unfold, layout
        )
        saved.append(stored)
        low = out.astype(BF)
        current = low.astype(F32)
    other = swap(low, "section")
    mixed = jnp.where(first, jnp.stack([low, other]), jnp.stack([other, low]))

    grad = mine(cotangent).astype(F32)
    expert_sums = [None, None]
    for layer in (1, 0):
        grad, mixer_grad, expert_half = backward_layer(
            grad,
            saved[layer],
            mixers[layer],
            lambda: experts[layer],
            tables[layer],
            unfold,
            layout,
            5 + layer,
        )
        grad_low = grad.astype(BF)
        grad = grad_low.astype(F32)
        given = [lax.ppermute(h, "section", [(1 - layer, layer)]) for h in expert_half]
        expert_sums[layer] = [(h, g) for h, g in zip(expert_half, given)]
        if layer == 1:
            late = lax.optimization_barrier(jnp.concatenate(mixer_grad, axis=1))
            late = lax.psum_scatter(late, DEVICES, scatter_dimension=0, tiled=True)
            late = lax.optimization_barrier(late)
    late = [late[:, :2048], late[:, 2048:3584], late[:, 3584:]]
    halves = [
        jnp.where(first, total(*a), total(*b)).astype(BF) for a, b in zip(*expert_sums)
    ]
    sums, (grad_gate, grad_up, grad_down) = reduce_all(mixer_grad, late, halves)
    qkv, grad_wo, narrow = sums
    return (
        mixed,
        grad_low[None],
        narrow[:, 32][None],
        qkv[:, :1536][None],
        qkv[:, 1536:1792][None],
        qkv[:, 1792:][None],
        grad_wo[None],
        narrow[:, 33][None],
        narrow[:, :32][None],
        grad_gate[None],
        grad_up[None],
        grad_down[None],
    )


def solution(mesh):
    fine = Mesh(mesh.devices.reshape(2, 2, 4, 2, 4), ("section", *DEVICES))
    expert = ("yh", "z", "core")
    return jax.shard_map(
        per_device,
        mesh=fine,
        in_specs=(
            P(None, DEVICES, None),
            P("section", None, DEVICES, None),
            P(None, expert, None),
            P("section", DEVICES),
            P("section", DEVICES, None),
            P("section", DEVICES, None),
            P("section", DEVICES, None),
            P("section", DEVICES, None),
            P("section", DEVICES),
            P("section", DEVICES, None),
            P("section", expert, "shard", None),
            P("section", expert, "shard", None),
            P("section", expert, None, "shard"),
            P(None, DEVICES, None),
        ),
        out_specs=(
            P(None, DEVICES, None),
            P("section", DEVICES, None),
            P("section", DEVICES),
            P("section", DEVICES, None),
            P("section", DEVICES, None),
            P("section", DEVICES, None),
            P("section", DEVICES, None),
            P("section", DEVICES),
            P("section", DEVICES, None),
            P("section", expert, "shard", None),
            P("section", expert, "shard", None),
            P("section", expert, None, "shard"),
        ),
        check_vma=False,
    )
```

```python
import jax
import jax.numpy as jnp
from jax import lax
from jax.experimental import pallas as pl
from jax.experimental.pallas import tpu as pltpu
from jax.sharding import Mesh
from jax.sharding import PartitionSpec as P

HEADS = 12
HEAD_DIM = 128
EXPERTS = 32
MAIN = 16
EXTRA = 2
CHUNKS = 6

epsilon = 1e-06
rope_base = 1000000.0
masked_score = -1e30

BF = jnp.bfloat16
F32 = jnp.float32
CHIPS = ("yh", "z", "shard")
DEVICES = ("yh", "z", "core", "shard")


def dot(a, b, dims=((1,), (0,))):
    return lax.dot_general(a, b, (dims, ((), ())), preferred_element_type=F32)


def document_layout(doc_lengths, group_rows):
    doc_ends = jnp.cumsum(doc_lengths)
    starts = doc_ends - doc_lengths
    row_index = jnp.arange(group_rows, dtype=jnp.int32)
    segment = jnp.sum((row_index[:, None] >= doc_ends[None, :]).astype(jnp.int32), axis=1)
    member = segment[:, None] == jnp.arange(doc_lengths.shape[0], dtype=jnp.int32)[None, :]
    position = row_index - jnp.sum(jnp.where(member, starts[None, :], 0), axis=1)
    return (segment, position)


def rotary_tables(position, head_size):
    half_dim = head_size // 2
    frequency = rope_base ** (-2.0 * jnp.arange(half_dim, dtype=F32) / head_size)
    angles = position.astype(F32)[:, None] * frequency[None, :]
    cosine, sine = jnp.cos(angles), jnp.sin(angles)
    return jnp.concatenate([cosine, cosine], axis=1), jnp.concatenate([-sine, sine], axis=1)


def swap(value, axis):
    return lax.ppermute(value, axis, [(0, 1), (1, 0)])


def around(axis, size):
    here = lax.axis_index(axis)
    return [lax.rem(here + step, size) for step in range(1, size)]


def move(name, number, arrays, shapes, peers, copies):
    count = len(arrays)
    total = 40

    def kernel(*refs):
        ins, outs = refs[:count], refs[count : count + len(shapes)]
        sent, got = refs[count + len(shapes) :]
        barrier = pltpu.get_barrier_semaphore()
        near = peers()
        for peer in near:
            pl.semaphore_signal(
                barrier, inc=1, device_id=peer, device_id_type=pl.DeviceIdType.MESH
            )
        pl.semaphore_wait(barrier, len(near))
        started = []
        for k, (source, target, device) in enumerate(copies(ins, outs)):
            if device is None:
                copy = pltpu.make_async_copy(source, target, got.at[k])
            else:
                copy = pltpu.make_async_remote_copy(
                    src_ref=source,
                    dst_ref=target,
                    send_sem=sent.at[k],
                    recv_sem=got.at[k],
                    device_id=device,
                    device_id_type=pl.DeviceIdType.MESH,
                )
            copy.start()
            started.append(copy)
        for copy in started:
            copy.wait()

    space = pl.BlockSpec(memory_space=pltpu.HBM)
    return pl.pallas_call(
        kernel,
        out_shape=[jax.ShapeDtypeStruct(s, BF) for s in shapes],
        in_specs=[space] * count,
        out_specs=[space] * len(shapes),
        scratch_shapes=[pltpu.SemaphoreType.DMA((total,)), pltpu.SemaphoreType.DMA((total,))],
        compiler_params=pltpu.CompilerParams(collective_id=number, has_side_effects=True),
        name=name,
    )(*arrays)


def total(*parts):
    out = parts[0].astype(F32)
    for part in parts[1:]:
        out = out + part.astype(F32)
    return out


def at(array, index, axis):
    return lax.dynamic_index_in_dim(array, index, axis, keepdims=False)


def other(axis):
    return lax.rem(lax.axis_index(axis) + 1, 2)


def sum_over_cores(grads, number):
    gate, up, down = grads
    halves = [gate.reshape(4, 2, 192, 768), up.reshape(4, 2, 192, 768), down.reshape(2, 384, 1536)]

    def copies(ins, outs):
        there = other("core")
        views = [ins[0].at[:, there], ins[1].at[:, there], ins[2].at[there]]
        return [(v, o, {"core": there}) for v, o in zip(views, outs)]

    shapes = [(4, 192, 768), (4, 192, 768), (384, 1536)]
    got = move("expert_cores", number, halves, shapes, lambda: [{"core": other("core")}], copies)
    core = lax.axis_index("core")
    gate, up, down = (
        total(at(h, core, 0 if k == 2 else 1), g).astype(BF)
        for k, (h, g) in enumerate(zip(halves, got))
    )
    return jnp.concatenate(
        [gate.reshape(768, 768), up.reshape(768, 768), down[:, :768], down[:, 768:]], axis=0
    )


def reduce_all(grads, late, exp):
    core, shard, z, yh, section = (
        lax.axis_index(a) for a in ("core", "shard", "z", "yh", "section")
    )
    width = grads.shape[1]
    mix = grads.reshape(8, 2, 4, 24, width)

    got = move(
        "cores",
        1,
        [mix],
        [(8, 4, 24, width)],
        lambda: [{"core": other("core")}],
        lambda ins, outs: [(ins[0].at[:, other("core")], outs[0], {"core": other("core")})],
    )[0]
    mix = total(at(mix, core, 1), got).astype(BF).reshape(2, 4, 4, 24, width)

    def shards_of(ref, x):
        down = ref.at[
            pl.ds(pl.multiple_of(1536 + x // 2 * 384, 128), 384),
            pl.ds(pl.multiple_of(lax.rem(x, 2) * 384, 128), 384),
        ]
        gate = ref.at[pl.ds(pl.multiple_of(x * 192, 64), 192)]
        up = ref.at[pl.ds(pl.multiple_of(768 + x * 192, 64), 192)]
        return gate, up, down

    def copies_2(ins, outs):
        here = lax.axis_index("shard")
        out = []
        for step, (x, i) in enumerate(zip(around("shard", 4), around("z", 4))):
            out.append((ins[0].at[:, i], outs[0].at[step], {"z": i}))
            for k, source in enumerate(shards_of(ins[1], x)):
                out.append((source, outs[1 + k].at[here], {"shard": x}))
        return out

    shapes = [(3, 2, 4, 24, width), (4, 192, 768), (4, 192, 768), (4, 384, 384)]
    got = move(
        "first_axis",
        2,
        [mix, exp],
        shapes,
        lambda: [{"shard": x} for x in around("shard", 4)] + [{"z": i} for i in around("z", 4)],
        copies_2,
    )
    mix = total(at(mix, z, 1), *got[0]).astype(BF)
    rows = [
        lax.dynamic_slice(exp, (shard * 192, 0), (192, 768)),
        lax.dynamic_slice(exp, (768 + shard * 192, 0), (192, 768)),
        lax.dynamic_slice(exp, (1536 + shard // 2 * 384, shard % 2 * 384), (384, 384)),
    ]
    exp = [lax.dynamic_update_index_in_dim(g, o, shard, 0) for g, o in zip(got[1:], rows)]

    got = move(
        "other_axis",
        3,
        [mix],
        [(3, 2, 24, width)],
        lambda: [{"shard": x} for x in around("shard", 4)],
        lambda ins, outs: [
            (ins[0].at[:, x], outs[0].at[step], {"shard": x})
            for step, x in enumerate(around("shard", 4))
        ],
    )[0]
    mix = total(at(mix, shard, 1), *got).astype(BF)

    def places():
        here = 2 * lax.axis_index("yh") + lax.axis_index("section")
        there = [lax.rem(here + step, 4) for step in range(1, 4)]
        return [(t // 2, lax.rem(t, 2)) for t in there]

    def copies_4(ins, outs):
        there = other("core")
        out = [
            (ins[1 + k].at[pl.ds(2 * there, 2)], outs[1 + k], {"core": there}) for k in range(3)
        ]
        for step, (y, s) in enumerate(places()):
            out.append((ins[0].at[s, y], outs[0].at[step], {"yh": y, "section": s}))
        return out

    mine = (jnp.arange(2) == yh)[:, None, None]
    pairs = jnp.stack([mix, jnp.where(mine, late[None], jnp.zeros((), BF))])
    got = move(
        "last_axis",
        4,
        [pairs, *exp],
        [(3, 24, width), (2, 192, 768), (2, 192, 768), (2, 384, 384)],
        lambda: [{"yh": y, "section": s} for y, s in places()] + [{"core": other("core")}],
        copies_4,
    )
    sums = total(at(at(pairs, section, 0), yh, 0), *got[0])
    out = []
    for e, g in zip(exp, got[1:]):
        kept = lax.dynamic_slice_in_dim(e, 2 * core, 2, 0)
        low, high = jnp.where(core == 0, kept, g), jnp.where(core == 0, g, kept)
        out.append(jnp.concatenate([low, high], axis=1).astype(F32))
    return sums, out


def gather_weights(local, experts):
    rows, width = local.shape

    def kernel(*refs):
        mine, shards = refs[0], refs[1:4]
        full, late, whole = refs[4], refs[5], refs[6:9]
        stage = refs[9:12]
        sent, got, sent_x, got_e, sent_c, got_c, sent_y, sent_o, local_sem = refs[12:]
        s, yh, z, c, x = (lax.axis_index(a) for a in ("section", "yh", "z", "core", "shard"))
        place = 2 * yh + s
        ys = [lax.rem(place + k, 4) for k in (1, 2, 3)]
        ys = [{"yh": y // 2, "section": lax.rem(y, 2)} for y in ys]
        xs = [{"shard": lax.rem(x + k, 4)} for k in (1, 2, 3)]
        z_up, z_down = lax.rem(z + 1, 4), lax.rem(z + 3, 4)
        sibling, partner = {"core": 1 - c}, {"section": 1 - s}

        def piece(k, i, h):
            if k == 2:
                return shards[2].at[i, pl.ds(pl.multiple_of(h * 384, 128), 384)]
            return shards[k].at[i, pl.ds(pl.multiple_of(h * 192, 64), 192)]

        def landing(k, layer, source, half):
            if k == 2:
                return whole[2].at[layer, half, :, pl.ds(pl.multiple_of(source * 384, 128), 384)]
            return whole[k].at[layer, source, half]

        def remote(source, target, send, receive, device):
            return pltpu.make_async_remote_copy(
                src_ref=source,
                dst_ref=target,
                send_sem=send,
                recv_sem=receive,
                device_id=device,
                device_id_type=pl.DeviceIdType.MESH,
            )

        def start(copies):
            for copy in copies:
                copy.start()
            return copies

        def finish(copies):
            for copy in copies:
                copy.wait()

        has_own = x // 2 == c
        own = lax.rem(x, 2)
        staged = start(
            [pltpu.make_async_copy(piece(k, own, c), stage[k], local_sem.at[k]) for k in range(3)]
        )
        barrier = pltpu.get_barrier_semaphore()
        near = ys + xs + [{"z": z_up}, {"z": z_down}, sibling]
        near += [{"shard": lax.rem(x + k, 4), "core": 1 - c} for k in (1, 2, 3)]
        for peer in near:
            pl.semaphore_signal(
                barrier, inc=1, device_id=peer, device_id_type=pl.DeviceIdType.MESH
            )
        pl.semaphore_wait(barrier, len(near))

        here = full.at[yh, z, c, x]

        def along_y(target):
            out = [pltpu.make_async_copy(mine, target, local_sem.at[3])]
            for k, device in enumerate(ys):
                out.append(remote(mine, target, sent.at[k], got.at[k], device))
            return out

        @pl.when(s == 0)
        def _():
            start(along_y(here))

        @pl.when(s == 1)
        def _():
            start(along_y(late.at[yh]))

        finish(staged)

        @pl.when(has_own)
        def _():
            for k in range(3):
                remote(
                    piece(k, own, 1 - c),
                    landing(k, s, x, 1 - c),
                    sent_o.at[k],
                    got_e.at[s, x, k],
                    sibling,
                ).start()
                pltpu.make_async_copy(stage[k], landing(k, s, x, c), got_e.at[s, x, k]).start()

        def pass_on(layer, distance, to_partner):
            source = lax.rem(x + distance, 4)
            for k in range(3):
                view = landing(k, layer, source, c)
                receive = got_e.at[layer, source, k]
                remote(view, view, sent_o.at[k], receive, sibling).wait_recv()
                if to_partner:
                    remote(view, view, sent_y.at[distance, k], receive, partner).start()
                across = got_c.at[layer, source, k]
                remote(view, view, sent_c.at[layer, source, k], across, sibling).start()

        finish(along_y(here))
        view = full.at[:, z, c, x]
        along_x = start(
            [remote(view, view, sent.at[3 + k], got.at[3 + k], xs[k]) for k in range(3)]
        )
        pass_on(s, 0, True)
        finish(along_x)

        def ring(base, up, down):
            return start(
                [
                    remote(up, up, sent.at[base], got.at[base], {"z": z_up}),
                    remote(down, down, sent.at[base + 1], got.at[base + 1], {"z": z_down}),
                ]
            )

        view = full.at[:, z, c]
        along_z = ring(6, view, view)
        for i in range(2):

            @pl.when(x != 2 * c + i)
            def _():
                for h in range(2):
                    for k in range(3):
                        remote(
                            piece(k, i, h),
                            landing(k, s, x, h),
                            sent_x.at[(i * 2 + h) * 3 + k],
                            got_e.at[s, x, k],
                            {"shard": 2 * c + i, "core": h},
                        ).start()

        finish(along_z)
        along_z = ring(8, full.at[0, z_down, c], full.at[1, z_up, c])
        for distance in (1, 3, 2):
            pass_on(s, distance, True)
        finish(along_z)
        view = full.at[:, :, c]
        across = start([remote(view, view, sent.at[10], got.at[10], sibling)])
        for distance in (0, 1, 3, 2):
            pass_on(1 - s, distance, False)

        finish(across)
        for i in range(2):

            @pl.when(x != 2 * c + i)
            def _():
                for h in range(2):
                    for k in range(3):
                        view = piece(k, i, h)
                        n = (i * 2 + h) * 3 + k
                        remote(view, view, sent_x.at[n], got_e.at[0, 0, k], sibling).wait_send()

        @pl.when(has_own)
        def _():
            for k in range(3):
                view = piece(k, own, 1 - c)
                remote(view, view, sent_o.at[k], got_e.at[0, 0, k], sibling).wait_send()

        for source in range(4):
            for k in range(3):
                view = landing(k, s, source, c)
                send = sent_y.at[source, k]
                remote(view, view, send, got_e.at[0, 0, k], partner).wait_send()
                for layer in range(2):
                    view = landing(k, layer, source, c)
                    arrived = landing(k, layer, source, 1 - c)
                    send, receive = sent_c.at[layer, source, k], got_c.at[layer, source, k]
                    remote(view, view, send, receive, sibling).wait_send()
                    remote(arrived, arrived, send, receive, sibling).wait_recv()

    space = pl.BlockSpec(memory_space=pltpu.HBM)
    near_space = pl.BlockSpec(memory_space=pltpu.VMEM)
    shapes = [(2, 4, 2, 4, rows, width), (2, rows, width)]
    shapes += [(2, 4, 2, 192, 768), (2, 4, 2, 192, 768), (2, 2, 384, 1536)]
    dma = pltpu.SemaphoreType.DMA
    return pl.pallas_call(
        kernel,
        out_shape=[jax.ShapeDtypeStruct(shape, BF) for shape in shapes],
        in_specs=[near_space] + [space] * 3,
        out_specs=[space] * 5,
        scratch_shapes=[
            pltpu.VMEM((192, 768), BF),
            pltpu.VMEM((192, 768), BF),
            pltpu.VMEM((384, 384), BF),
            dma((11,)),
            dma((11,)),
            dma((12,)),
            dma((2, 4, 3)),
            dma((2, 4, 3)),
            dma((2, 4, 3)),
            dma((4, 3)),
            dma((3,)),
            dma((4,)),
        ],
        compiler_params=pltpu.CompilerParams(collective_id=0, has_side_effects=True),
        name="gather_weights",
    )(local, *experts)


def rank_of(route_rows):
    rows = route_rows.shape[0]
    chosen = route_rows.T[None, :, :] == jnp.arange(EXPERTS, dtype=jnp.int32)[:, None, None]
    hot = jnp.any(chosen, axis=1)
    index = jnp.arange(rows, dtype=jnp.int32)
    before = (index[:, None] < index[None, :]).astype(BF)
    return jnp.where(hot, dot(hot.astype(BF), before), -1.0)


def stacked(field):
    return jnp.concatenate(jnp.split(field, CHUNKS, axis=1), axis=0)


def unstacked(field):
    return jnp.concatenate(jnp.split(field, CHUNKS, axis=0), axis=1)


def unfold_table(sources):
    row = jnp.arange(CHUNKS * sources * EXTRA, dtype=jnp.int32)
    piece, source, extra = row // (sources * EXTRA), row // EXTRA % sources, row % EXTRA
    column = jnp.arange(sources * MAIN, dtype=jnp.int32)
    return (
        (source * MAIN + piece * EXTRA + extra)[:, None] == column[None, :]
    ).astype(BF)


def exchange(message):
    return lax.all_to_all(message, CHIPS, split_axis=0, concat_axis=0, tiled=True)


def arrived_rows(message, unfold):
    width = message.shape[1] - 256
    extra = unstacked(dot(unfold, message[:, width:]).astype(BF))
    return jnp.concatenate([message[:, :width], extra], axis=0)


def fold_rows(rows, unfold, sources):
    main = rows[: sources * MAIN]
    extra = dot(unfold, stacked(rows[sources * MAIN :]), ((0,), (0,))).astype(BF)
    return jnp.concatenate([main, extra], axis=1)


def low_pair(value):
    high = value.astype(BF)
    return high, (value - high.astype(F32)).astype(BF)


OUT_COLUMNS, QKV_STEP = 1536, 512


def columns(width, place):
    return lambda rows: pl.BlockSpec((rows, width), lambda i: (0, place), memory_space=pltpu.VMEM)


OUT_BLOCK = [columns(OUT_COLUMNS, 0)]
QKV_BLOCKS = [columns(QKV_STEP, 3 + k) for k in range(4)]
NARROW_BLOCK = [columns(128, 28)]


def fused(name, body, shapes, *arrays):
    near = pl.BlockSpec(memory_space=pltpu.VMEM)
    specs, given = [], []
    for array in arrays:
        if isinstance(array, tuple):
            array, blocks = array
            specs += [block(array.shape[0]) for block in blocks]
            given += [array] * len(blocks)
        else:
            specs.append(near)
            given.append(array)
    return pl.pallas_call(
        body,
        grid=(1,),
        out_shape=[jax.ShapeDtypeStruct(shape, kind) for shape, kind in shapes],
        in_specs=specs,
        out_specs=[near] * len(shapes),
        compiler_params=pltpu.CompilerParams(vmem_limit_bytes=48 << 20),
        name=name,
    )(*given)


TN, NT = ((0,), (0,)), ((1,), (1,))


def slots(rank):
    count, rows = rank.shape
    place = lax.broadcasted_iota(jnp.int32, (count, MAIN, rows), 1)
    wide = jnp.broadcast_to(rank[:, None, :], (count, MAIN, rows))
    main = jnp.where(wide == place.astype(F32), 1.0, 0.0)
    extra = (MAIN + lax.rem(place, EXTRA)).astype(F32)
    extra = jnp.where((wide == extra) & (place < EXTRA * CHUNKS), 1.0, 0.0)
    return main, extra


def per_piece(table):
    piece = lax.rem(lax.broadcasted_iota(jnp.int32, table.shape, 0), MAIN) // EXTRA
    return [jnp.where(piece == j, table, 0.0) for j in range(CHUNKS)]


def flat(table):
    return table.reshape(table.shape[0] * table.shape[1], table.shape[2])


def send_table(main, extra, field):
    width = field.shape[1] // CHUNKS
    side = None
    for j, table in enumerate(per_piece(flat(extra))):
        part = dot(table.astype(BF), field[:, j * width : (j + 1) * width])
        side = part if side is None else side + part
    return dot(flat(main).astype(BF), field), side


def bring_back(main, extra, rows, exact):
    parts = low_pair if exact else (lambda t: (t.astype(BF),))
    model_width = rows.shape[1] - 256
    total_main = None
    for table in parts(main):
        part = dot(table, rows[:, :model_width], TN)
        total_main = part if total_main is None else total_main + part
    side = []
    for table in per_piece(extra):
        total_side = None
        for t in parts(table):
            part = dot(t, rows[:, model_width:], TN)
            total_side = part if total_side is None else total_side + part
        side.append(total_side)
    return total_main + jnp.concatenate(side, axis=1)


def gain_rows(narrow):
    row = lax.broadcasted_iota(jnp.int32, (8, narrow.shape[1]), 0)
    column = lax.broadcasted_iota(jnp.int32, (8, narrow.shape[1]), 1)
    pick = jnp.where(column == row + EXPERTS, 1.0, 0.0).astype(BF)
    rows = dot(pick, narrow, NT)
    return rows[0:1], rows[1:2]


def turn(field, cosine, sine):
    return field * cosine + pltpu.roll(field, HEAD_DIM // 2, 1) * sine


def turn_back(field, cosine, sine):
    return field * cosine - pltpu.roll(field, HEAD_DIM // 2, 1) * sine


def combined(x_mid, rank, gates, rows):
    main, extra = slots(rank)
    wide = jnp.broadcast_to(gates[:, None, :], main.shape)
    return x_mid + bring_back(flat(main * wide), flat(extra * wide), rows, True)


def project_body(combine):
    def body(*refs):
        if combine:
            mid_ref, rank_ref, gates_ref, rows_ref = refs[:4]
            refs = refs[4:]
            low = combined(mid_ref[...], rank_ref[...], gates_ref[...], rows_ref[...]).astype(BF)
        else:
            low = refs[0][...]
            refs = refs[1:]
        weights, refs = refs[:4], refs[4:]
        narrow, cos_ref, sin_ref, low_ref, h_ref, q_ref, kv_ref = refs
        field = low.astype(F32)
        low_ref[...] = low
        gain, _ = gain_rows(narrow[...])
        scale = lax.rsqrt(jnp.mean(field * field, axis=1, keepdims=True) + epsilon)
        h = (field * scale * gain).astype(BF)
        h_ref[...] = h
        cosine, sine = cos_ref[...], sin_ref[...]
        query_width = q_ref.shape[1]
        for at_column in range(0, 4 * QKV_STEP, 256):
            inside = at_column % QKV_STEP
            part = dot(h, weights[at_column // QKV_STEP][:, inside : inside + 256])
            if at_column < query_width + kv_ref.shape[1] // 2:
                part = jnp.concatenate(
                    [turn(part[:, k : k + HEAD_DIM], cosine, sine) for k in (0, HEAD_DIM)], axis=1
                )
            if at_column < query_width:
                q_ref[:, at_column : at_column + 256] = part.astype(BF)
            else:
                at_kv = at_column - query_width
                kv_ref[:, at_kv : at_kv + 256] = part.astype(BF)

    return body


def project(source, weights, tables):
    combine = len(source) > 1
    tok_rows, model_width = source[0].shape
    shapes = [((tok_rows, model_width), BF)] * 2
    shapes += [((tok_rows, HEADS * HEAD_DIM), BF)]
    shapes += [((tok_rows, 4 * QKV_STEP - HEADS * HEAD_DIM), BF)]
    return fused(
        "project_combined" if combine else "project",
        project_body(combine),
        shapes,
        *source,
        (weights, QKV_BLOCKS + NARROW_BLOCK),
        *tables,
    )


def finish_body(mid_ref, rank_ref, gates_ref, rows_ref, out_ref):
    out = combined(mid_ref[...], rank_ref[...], gates_ref[...], rows_ref[...])
    out_ref[...] = out.astype(BF)


def heads_of(kv_ref):
    kv_heads = kv_ref.shape[2] // 2 // HEAD_DIM
    parts = []
    for k in range(2 * kv_heads):
        part = kv_ref[:, :, k * HEAD_DIM : (k + 1) * HEAD_DIM]
        parts.append(part.reshape(part.shape[0] * part.shape[1], HEAD_DIM))
    return parts[:kv_heads], parts[kv_heads:]


def attend_body(
    low_ref, q_ref, kv_ref, allowed_ref, weight, narrow, rank_ref,
    mid_ref, h_ref, att_ref, probs_ref, gates_ref, out_ref,
):
    keys, values = heads_of(kv_ref)
    allowed = allowed_ref[...] > 0.0
    ratio = HEADS // len(keys)
    for head in range(HEADS):
        lanes = slice(head * HEAD_DIM, (head + 1) * HEAD_DIM)
        scores = dot(q_ref[:, lanes], keys[head // ratio], NT) * HEAD_DIM ** (-0.5)
        scores = jnp.where(allowed, scores, masked_score)
        exponent = jnp.exp(scores - jnp.max(scores, axis=1, keepdims=True))
        probs = exponent / jnp.sum(exponent, axis=1, keepdims=True)
        probs_ref[head] = probs
        att_ref[:, lanes] = dot(probs.astype(BF), values[head // ratio]).astype(BF)
    mid = low_ref[...].astype(F32) + dot(att_ref[...], weight[...])
    mid_ref[...] = mid
    _, gain = gain_rows(narrow[...])
    scale = lax.rsqrt(jnp.mean(mid * mid, axis=1, keepdims=True) + epsilon)
    h = (mid * scale * gain).astype(BF)
    h_ref[...] = h
    rank = rank_ref[...]
    logits = jnp.transpose(dot(h, narrow[...]))[:EXPERTS]
    logits = jnp.where(rank >= 0.0, logits, masked_score)
    gate_exp = jnp.exp(logits - jnp.max(logits, axis=0, keepdims=True))
    gate_exp = jnp.where(rank >= 0.0, gate_exp, 0.0)
    gates_ref[...] = gate_exp / jnp.sum(gate_exp, axis=0, keepdims=True)
    main, side = send_table(*slots(rank), h)
    width = main.shape[1]
    out_ref[:, :width] = main.astype(BF)
    out_ref[:, width:] = side.astype(BF)


def attend(low, q, kv, allowed, weights, rank):
    tok_rows, model_width = low.shape
    shapes = [
        ((tok_rows, model_width), F32),
        ((tok_rows, model_width), BF),
        ((tok_rows, HEADS * HEAD_DIM), BF),
        ((HEADS, tok_rows, allowed.shape[1]), F32),
        (rank.shape, F32),
        ((EXPERTS * MAIN, model_width + 256), BF),
    ]
    return fused(
        "attend", attend_body, shapes,
        low, q, kv, allowed, (weights, OUT_BLOCK + NARROW_BLOCK), rank,
    )


def grad_slots_body(grad_ref, rank_ref, gates_ref, rows_ref, out_ref, dlogits_ref):
    gates = gates_ref[...]
    main, extra = slots(rank_ref[...])
    wide = jnp.broadcast_to(gates[:, None, :], main.shape)
    grad_main, grad_side = send_table(main, extra, grad_ref[...])
    width = grad_main.shape[1]
    dgate = None
    for table, grad, columns in (
        (main, grad_main, slice(0, width)),
        (extra, grad_side, slice(width, width + 256)),
    ):
        slot_gate = jnp.sum(flat(table * wide), axis=1, keepdims=True)
        out_ref[:, columns] = (grad * slot_gate).astype(BF)
        slot_dgate = jnp.sum(grad * rows_ref[:, columns].astype(F32), axis=1, keepdims=True)
        part = jnp.sum((flat(table) * slot_dgate).reshape(table.shape), axis=1)
        dgate = part if dgate is None else dgate + part
    dlogits = gates * (dgate - jnp.sum(gates * dgate, axis=0, keepdims=True))
    pad = jnp.zeros((dlogits_ref.shape[1] - EXPERTS, dlogits.shape[1]), F32)
    dlogits_ref[...] = jnp.transpose(jnp.concatenate([dlogits, pad], axis=0)).astype(BF)


def grad_slots(grad, rank, gates, rows):
    shapes = [(rows.shape, BF), ((grad.shape[0], 128), BF)]
    return fused("grad_slots", grad_slots_body, shapes, grad, rank, gates, rows)


def norm_grads(field, gain, grad):
    scale = lax.rsqrt(jnp.mean(field * field, axis=1, keepdims=True) + epsilon)
    scaled = grad * gain
    centre = jnp.mean(scaled * field, axis=1, keepdims=True)
    dgain = jnp.sum(grad * field * scale, axis=0, keepdims=True)
    return scale * scaled - field * (scale * scale * scale) * centre, dgain


def grad_attend_body(
    grad_ref, rows_ref, rank_ref, dlogits_ref, weight, narrow, mid_ref, q_ref, kv_ref, probs_ref,
    cos_ref, sin_ref,
    dmid_ref, dbr_ref, dq_ref, dkv_ref, dgain_ref, datt_ref,
):
    main, extra = slots(rank_ref[...])
    dh = bring_back(flat(main), flat(extra), rows_ref[...], False)
    dh = dh + dot(dlogits_ref[...], narrow[...], NT)
    _, gain = gain_rows(narrow[...])
    dmid, dgain = norm_grads(mid_ref[...], gain, dh)
    dmid = dmid + grad_ref[...].astype(F32)
    dgain_ref[...] = dgain
    dmid_ref[...] = dmid
    dbr_ref[...] = dmid.astype(BF)
    datt_ref[...] = dot(dbr_ref[...], weight[...], NT).astype(BF)
    keys, values = heads_of(kv_ref)
    ratio = HEADS // len(keys)
    cosine, sine = cos_ref[...], sin_ref[...]
    count, tok_rows = kv_ref.shape[0], kv_ref.shape[1]
    scale = HEAD_DIM ** (-0.5)
    for k in range(len(keys)):
        dkey, dvalue = None, None
        for head in range(k * ratio, (k + 1) * ratio):
            lanes = slice(head * HEAD_DIM, (head + 1) * HEAD_DIM)
            probs, datt = probs_ref[head], datt_ref[:, lanes]
            dprobs = dot(datt, values[k], NT)
            centre = jnp.sum(dprobs * probs, axis=1, keepdims=True)
            dscores = (probs * (dprobs - centre)).astype(BF)
            part = dot(probs.astype(BF), datt, TN)
            dvalue = part if dvalue is None else dvalue + part
            part = dot(dscores, q_ref[:, lanes], TN)
            dkey = part if dkey is None else dkey + part
            dquery = dot(dscores, keys[k]) * scale
            dq_ref[:, lanes] = turn_back(dquery, cosine, sine).astype(BF)
        at_key, at_value = k * HEAD_DIM, (len(keys) + k) * HEAD_DIM
        shape = (count, tok_rows, HEAD_DIM)
        dkv_ref[:, :, at_key : at_key + HEAD_DIM] = (dkey * scale).astype(BF).reshape(shape)
        dkv_ref[:, :, at_value : at_value + HEAD_DIM] = dvalue.astype(BF).reshape(shape)


def grad_attend(grad, rows, rank, dlogits, weights, mid, q, kv, probs, tables):
    tok_rows, model_width = mid.shape
    shapes = [
        ((tok_rows, model_width), F32),
        ((tok_rows, model_width), BF),
        (q.shape, BF),
        (kv.shape, BF),
        ((1, model_width), F32),
        (q.shape, BF),
    ]
    return fused(
        "grad_attend", grad_attend_body, shapes,
        grad, rows, rank, dlogits, (weights, OUT_BLOCK + NARROW_BLOCK), mid, q, kv, probs, *tables,
    )[:5]


def grad_project_body(
    dq_ref, dkv_ref, dmid_ref, low_ref, weight_0, weight_1, weight_2, weight_3, narrow, cos_ref,
    sin_ref,
    dqkv_ref, grad_ref, dgain_ref,
):
    query_width, kv_width = dq_ref.shape[1], dkv_ref.shape[1] // 2
    cosine, sine = cos_ref[...], sin_ref[...]
    dqkv_ref[:, :query_width] = dq_ref[...]
    for k in range(0, kv_width, HEAD_DIM):
        part = turn_back(dkv_ref[:, k : k + HEAD_DIM], cosine, sine)
        dqkv_ref[:, query_width + k : query_width + k + HEAD_DIM] = part.astype(BF)
    dqkv_ref[:, query_width + kv_width :] = dkv_ref[:, kv_width:].astype(BF)
    dh = None
    for k, weight in enumerate((weight_0, weight_1, weight_2, weight_3)):
        part = dot(dqkv_ref[:, k * QKV_STEP : (k + 1) * QKV_STEP], weight[...], NT)
        dh = part if dh is None else dh + part
    gain, _ = gain_rows(narrow[...])
    dlow, dgain = norm_grads(low_ref[...].astype(F32), gain, dh)
    dgain_ref[...] = dgain
    grad_ref[...] = (dlow + dmid_ref[...]).astype(BF)


def grad_project(dq, dkv, dmid, low, weights, tables):
    tok_rows, model_width = low.shape
    shapes = [
        ((tok_rows, 4 * QKV_STEP), BF),
        ((tok_rows, model_width), BF),
        ((1, model_width), F32),
    ]
    return fused(
        "grad_project", grad_project_body, shapes,
        dq, dkv, dmid, low, (weights, QKV_BLOCKS + NARROW_BLOCK), *tables,
    )


def weight_grads_body(
    h_ref, dqkv_ref, att_ref, dbr_ref, h2_ref, dlogits_ref, dgain_a_ref, dgain_m_ref, out_ref
):
    step = 512
    place = 0
    for left, right in ((att_ref, dbr_ref), (h_ref, dqkv_ref)):
        for k in range(0, right.shape[1], step):
            part = dot(left[...], right[:, k : k + step], TN)
            out_ref[:, place : place + step] = part.astype(BF)
            place += step
    narrow = dot(h2_ref[...], dlogits_ref[...], TN)
    rows = jnp.concatenate(
        [dgain_a_ref[...], dgain_m_ref[...], jnp.zeros((126, h_ref.shape[1]), F32)], axis=0
    )
    columns = pltpu.roll(jnp.transpose(rows), EXPERTS, 1)
    out_ref[:, place:] = (narrow + columns).astype(BF)


def weight_grads(h, dqkv, att, dbr, h2, dlogits, dgain_a, dgain_m):
    columns = dqkv.shape[1] + dbr.shape[1] + 128
    return fused(
        "weight_grads", weight_grads_body, [((h.shape[1], columns), BF)],
        h, dqkv, att, dbr, h2, dlogits, dgain_a, dgain_m,
    )[0]


def greet(peers):
    barrier = pltpu.get_barrier_semaphore()
    for peer in peers:
        pl.semaphore_signal(barrier, inc=1, device_id=peer, device_id_type=pl.DeviceIdType.MESH)
    pl.semaphore_wait(barrier, len(peers))


def small_exchange(name, number, array, shape, scratch, before, after):
    def kernel(in_ref, out_ref, *rest):
        here = lax.axis_index("shard")
        held = rest[0] if scratch else out_ref
        sent, got = rest[-2:]
        peers = [{"shard": x} for x in around("shard", 4)]
        greet(peers)
        copies = []
        for k, peer in enumerate(peers):
            source, target = before(in_ref, held, here, peer["shard"], k)
            copies.append(
                pltpu.make_async_remote_copy(
                    src_ref=source,
                    dst_ref=target,
                    send_sem=sent.at[k],
                    recv_sem=got.at[k],
                    device_id=peer,
                    device_id_type=pl.DeviceIdType.MESH,
                )
            )
            copies[-1].start()
        if not scratch:
            after(in_ref, held, out_ref, here)
        for copy in copies:
            copy.wait()
        if scratch:
            after(in_ref, held, out_ref, here)

    near = pl.BlockSpec(memory_space=pltpu.VMEM)
    dma = pltpu.SemaphoreType.DMA
    return pl.pallas_call(
        kernel,
        out_shape=jax.ShapeDtypeStruct(*shape),
        in_specs=[near],
        out_specs=near,
        scratch_shapes=scratch + [dma((3,)), dma((3,))],
        compiler_params=pltpu.CompilerParams(collective_id=number, has_side_effects=True),
        name=name,
    )(array)


def gather_group(kv, number):
    def before(in_ref, held, here, there, k):
        return in_ref, held.at[here]

    def after(in_ref, held, out_ref, here):
        out_ref[here] = in_ref[...]

    return small_exchange("gather_group", number, kv, ((4, *kv.shape), BF), [], before, after)


def sum_group(dkv, number):
    def before(in_ref, held, here, there, k):
        return in_ref.at[there], held.at[k]

    def after(in_ref, held, out_ref, here):
        out = in_ref[here].astype(F32)
        for k in range(3):
            out = out + held[k].astype(F32)
        out_ref[...] = out

    held = [pltpu.VMEM((3, *dkv.shape[1:]), BF)]
    return small_exchange("sum_group", number, dkv, (dkv.shape[1:], F32), held, before, after)


def forward_layer(source, weights, experts, rank, unfold, tables, allowed, number):
    gate_w, up_w, down_w = experts
    low, h_attn, query, kv = project(source, weights, tables)
    kv_all = gather_group(kv, number)
    x_mid, h_moe, attended, probs, gates, message = attend(low, query, kv_all, allowed, weights, rank)
    arrived = arrived_rows(exchange(message), unfold)
    gate_pre = dot(arrived, gate_w)
    up_pre = dot(arrived, up_w)
    hidden = (jax.nn.silu(gate_pre) * up_pre).astype(BF)
    produced = dot(hidden, down_w).astype(BF)
    returned = exchange(fold_rows(produced, unfold, EXPERTS))
    stored = {
        "low": low,
        "h_attn": h_attn,
        "query": query,
        "kv_all": kv_all,
        "probs": probs,
        "attended": attended,
        "x_mid": x_mid,
        "h_moe": h_moe,
        "gates": gates,
        "returned": returned,
        "arrived": arrived,
        "gate_pre": gate_pre,
        "up_pre": up_pre,
        "hidden": hidden,
    }
    return (x_mid, rank, gates, returned), stored


def backward_layer(grad, stored, weights, experts, rank, unfold, tables, numbers):
    gate_w, up_w, down_w = experts
    message, dlogits = grad_slots(grad, rank, stored["gates"], stored["returned"])
    came = arrived_rows(exchange(message), unfold)
    gate_pre, up_pre = stored["gate_pre"], stored["up_pre"]
    grad_down = dot(stored["hidden"], came, TN).astype(BF)
    grad_hidden = dot(came, down_w, NT)
    logistic = jax.nn.sigmoid(gate_pre)
    grad_gate_pre = (
        grad_hidden * up_pre * (logistic * (1.0 + gate_pre * (1.0 - logistic)))
    ).astype(BF)
    grad_up_pre = (grad_hidden * (gate_pre * logistic)).astype(BF)
    grad_rows = dot(grad_gate_pre, gate_w, NT) + dot(grad_up_pre, up_w, NT)
    returned = exchange(fold_rows(grad_rows.astype(BF), unfold, EXPERTS))
    grad_gate = dot(stored["arrived"], grad_gate_pre, TN).astype(BF)
    grad_up = dot(stored["arrived"], grad_up_pre, TN).astype(BF)
    half = sum_over_cores((grad_gate, grad_up, grad_down), numbers[0])
    returned, half = lax.optimization_barrier((returned, half))
    kv_all = stored["kv_all"]
    dmid, dbr, dquery, dkv, dgain_m = grad_attend(
        grad, returned, rank, dlogits, weights, stored["x_mid"], stored["query"], kv_all,
        stored["probs"], tables,
    )
    dkv = sum_group(dkv, numbers[1])
    dqkv, grad_in, dgain_a = grad_project(dquery, dkv, dmid, stored["low"], weights, tables)
    grads = weight_grads(
        stored["h_attn"], dqkv, stored["attended"], dbr, stored["h_moe"], dlogits, dgain_a, dgain_m
    )
    return grad_in, grads, half


def per_device(
    tokens,
    routes,
    lengths,
    gain_attn,
    w_query,
    w_key,
    w_value,
    w_out,
    gain_moe,
    w_router,
    w_gate,
    w_up,
    w_down,
    cotangent,
):
    section, yh, z, core, shard = (
        lax.axis_index(a) for a in ("section", "yh", "z", "core", "shard")
    )
    first = section == 0
    tok_rows, model_width = tokens.shape[1:]
    group_rows = tok_rows * lax.axis_size("shard")

    def mine(a):
        return lax.dynamic_index_in_dim(a, section, 0, keepdims=False)

    def by_layer(own, other):
        return jnp.where(first, own, other), jnp.where(first, other, own)

    local = jnp.concatenate(
        [
            w_out[0],
            w_query[0],
            w_key[0],
            w_value[0],
            w_router[0],
            gain_attn[0][:, None],
            gain_moe[0][:, None],
            jnp.zeros((w_query.shape[1], 94), BF),
        ],
        axis=1,
    )
    full, late, *whole = gather_weights(local, (w_gate[0], w_up[0], w_down[0]))
    weights = [
        full.reshape(model_width, -1),
        lax.all_gather(at(late, yh, 0), DEVICES, axis=0, tiled=True),
    ]
    route_other = swap(at(routes[0], 1 - section, 0), "section")
    ranks = [rank_of(r) for r in by_layer(mine(routes[0]), route_other)]
    experts = [
        (
            whole[0][layer].reshape(model_width, 768),
            whole[1][layer].reshape(model_width, 768),
            whole[2][layer].reshape(768, model_width),
        )
        for layer in range(2)
    ]
    unfold = unfold_table(EXPERTS)

    segment, position = document_layout(mine(lengths[:, 0]), group_rows)
    row_start = shard * tok_rows
    own_segment = lax.dynamic_slice_in_dim(segment, row_start, tok_rows)
    tables = rotary_tables(lax.dynamic_slice_in_dim(position, row_start, tok_rows), HEAD_DIM)
    query_index = row_start + jnp.arange(tok_rows, dtype=jnp.int32)
    allowed = (own_segment[:, None] == segment[None, :]) & (
        query_index[:, None] >= jnp.arange(group_rows, dtype=jnp.int32)[None, :]
    )
    allowed = allowed.astype(F32)

    source, saved = (mine(tokens),), []
    for layer in range(2):
        source, stored = forward_layer(
            source, weights[layer], experts[layer], ranks[layer], unfold, tables, allowed, 7 + layer
        )
        saved.append(stored)
    low = fused("finish", finish_body, [((tok_rows, model_width), BF)], *source)[0]
    away = swap(low, "section")
    mixed = jnp.where(first, jnp.stack([low, away]), jnp.stack([away, low]))

    grad = mine(cotangent)
    sums = [None, None]
    for layer in (1, 0):
        grad, mixer_grad, half = backward_layer(
            grad,
            saved[layer],
            weights[layer],
            experts[layer],
            ranks[layer],
            unfold,
            tables,
            (5 + layer, 9 + layer),
        )
        given = lax.ppermute(half, "section", [(1 - layer, layer)])
        sums[layer] = (half, given)
        if layer == 1:
            late = lax.psum_scatter(mixer_grad, DEVICES, scatter_dimension=0, tiled=True)
            late = lax.optimization_barrier(late)
    halves = jnp.where(first, total(*sums[0]), total(*sums[1])).astype(BF)
    mix, (grad_gate, grad_up, grad_down) = reduce_all(mixer_grad, late, halves)
    return (
        mixed,
        grad[None],
        mix[:, 3616][None],
        mix[:, 1536:3072][None],
        mix[:, 3072:3328][None],
        mix[:, 3328:3584][None],
        mix[:, :1536][None],
        mix[:, 3617][None],
        mix[:, 3584:3616][None],
        grad_gate[None],
        grad_up[None],
        grad_down[None],
    )


def solution(mesh):
    fine = Mesh(mesh.devices.reshape(2, 2, 4, 2, 4), ("section", *DEVICES))
    expert = ("yh", "z", "core")
    return jax.shard_map(
        per_device,
        mesh=fine,
        in_specs=(
            P(None, DEVICES, None),
            P("section", None, DEVICES, None),
            P(None, expert, None),
            P("section", DEVICES),
            P("section", DEVICES, None),
            P("section", DEVICES, None),
            P("section", DEVICES, None),
            P("section", DEVICES, None),
            P("section", DEVICES),
            P("section", DEVICES, None),
            P("section", expert, "shard", None),
            P("section", expert, "shard", None),
            P("section", expert, None, "shard"),
            P(None, DEVICES, None),
        ),
        out_specs=(
            P(None, DEVICES, None),
            P("section", DEVICES, None),
            P("section", DEVICES),
            P("section", DEVICES, None),
            P("section", DEVICES, None),
            P("section", DEVICES, None),
            P("section", DEVICES, None),
            P("section", DEVICES),
            P("section", DEVICES, None),
            P("section", expert, "shard", None),
            P("section", expert, "shard", None),
            P("section", expert, None, "shard"),
        ),
        check_vma=False,
    )
```

```python
import jax
import jax.numpy as jnp
from jax import lax
from jax.experimental import pallas as pl
from jax.experimental.pallas import tpu as pltpu
from jax.sharding import Mesh
from jax.sharding import PartitionSpec as P

HEADS = 12
HEAD_DIM = 128
EXPERTS = 32
MAIN = 16
EXTRA = 2
CHUNKS = 6

epsilon = 1e-06
rope_base = 1000000.0
masked_score = -1e30

BF = jnp.bfloat16
F32 = jnp.float32
CHIPS = ("yh", "z", "shard")
DEVICES = ("yh", "z", "core", "shard")


def dot(a, b, dims=((1,), (0,))):
    return lax.dot_general(a, b, (dims, ((), ())), preferred_element_type=F32)


def document_layout(doc_lengths, group_rows):
    doc_ends = jnp.cumsum(doc_lengths)
    starts = doc_ends - doc_lengths
    row_index = jnp.arange(group_rows, dtype=jnp.int32)
    segment = jnp.sum((row_index[:, None] >= doc_ends[None, :]).astype(jnp.int32), axis=1)
    member = segment[:, None] == jnp.arange(doc_lengths.shape[0], dtype=jnp.int32)[None, :]
    position = row_index - jnp.sum(jnp.where(member, starts[None, :], 0), axis=1)
    return (segment, position)


def rotary_tables(position, head_size):
    half_dim = head_size // 2
    frequency = rope_base ** (-2.0 * jnp.arange(half_dim, dtype=F32) / head_size)
    angles = position.astype(F32)[:, None] * frequency[None, :]
    cosine, sine = jnp.cos(angles), jnp.sin(angles)
    return jnp.concatenate([cosine, cosine], axis=1), jnp.concatenate([-sine, sine], axis=1)


def swap(value, axis):
    return lax.ppermute(value, axis, [(0, 1), (1, 0)])


def around(axis, size):
    here = lax.axis_index(axis)
    return [lax.rem(here + step, size) for step in range(1, size)]


def move(name, number, arrays, shapes, peers, copies):
    count = len(arrays)
    total = 40

    def kernel(*refs):
        ins, outs = refs[:count], refs[count : count + len(shapes)]
        sent, got = refs[count + len(shapes) :]
        barrier = pltpu.get_barrier_semaphore()
        near = peers()
        for peer in near:
            pl.semaphore_signal(
                barrier, inc=1, device_id=peer, device_id_type=pl.DeviceIdType.MESH
            )
        pl.semaphore_wait(barrier, len(near))
        started = []
        for k, (source, target, device) in enumerate(copies(ins, outs)):
            if device is None:
                copy = pltpu.make_async_copy(source, target, got.at[k])
            else:
                copy = pltpu.make_async_remote_copy(
                    src_ref=source,
                    dst_ref=target,
                    send_sem=sent.at[k],
                    recv_sem=got.at[k],
                    device_id=device,
                    device_id_type=pl.DeviceIdType.MESH,
                )
            copy.start()
            started.append(copy)
        for copy in started:
            copy.wait()

    space = pl.BlockSpec(memory_space=pltpu.HBM)
    return pl.pallas_call(
        kernel,
        out_shape=[jax.ShapeDtypeStruct(s, BF) for s in shapes],
        in_specs=[space] * count,
        out_specs=[space] * len(shapes),
        scratch_shapes=[pltpu.SemaphoreType.DMA((total,)), pltpu.SemaphoreType.DMA((total,))],
        compiler_params=pltpu.CompilerParams(collective_id=number, has_side_effects=True),
        name=name,
    )(*arrays)


def total(*parts):
    out = parts[0].astype(F32)
    for part in parts[1:]:
        out = out + part.astype(F32)
    return out


def at(array, index, axis):
    return lax.dynamic_index_in_dim(array, index, axis, keepdims=False)


def other(axis):
    return lax.rem(lax.axis_index(axis) + 1, 2)


def sum_over_cores(grads, number):
    gate, up, down = grads
    halves = [gate.reshape(4, 2, 192, 768), up.reshape(4, 2, 192, 768), down.reshape(2, 384, 1536)]

    def copies(ins, outs):
        there = other("core")
        views = [ins[0].at[:, there], ins[1].at[:, there], ins[2].at[there]]
        return [(v, o, {"core": there}) for v, o in zip(views, outs)]

    shapes = [(4, 192, 768), (4, 192, 768), (384, 1536)]
    got = move("expert_cores", number, halves, shapes, lambda: [{"core": other("core")}], copies)
    core = lax.axis_index("core")
    gate, up, down = (
        total(at(h, core, 0 if k == 2 else 1), g).astype(BF)
        for k, (h, g) in enumerate(zip(halves, got))
    )
    return jnp.concatenate(
        [gate.reshape(768, 768), up.reshape(768, 768), down[:, :768], down[:, 768:]], axis=0
    )


def reduce_all(grads, late, exp):
    core, shard, z, yh, section = (
        lax.axis_index(a) for a in ("core", "shard", "z", "yh", "section")
    )
    width = grads.shape[1]
    mix = grads.reshape(8, 2, 4, 24, width)

    got = move(
        "cores",
        1,
        [mix],
        [(8, 4, 24, width)],
        lambda: [{"core": other("core")}],
        lambda ins, outs: [(ins[0].at[:, other("core")], outs[0], {"core": other("core")})],
    )[0]
    mix = total(at(mix, core, 1), got).astype(BF).reshape(2, 4, 4, 24, width)

    def shards_of(ref, x):
        down = ref.at[
            pl.ds(pl.multiple_of(1536 + x // 2 * 384, 128), 384),
            pl.ds(pl.multiple_of(lax.rem(x, 2) * 384, 128), 384),
        ]
        gate = ref.at[pl.ds(pl.multiple_of(x * 192, 64), 192)]
        up = ref.at[pl.ds(pl.multiple_of(768 + x * 192, 64), 192)]
        return gate, up, down

    def copies_2(ins, outs):
        here = lax.axis_index("shard")
        out = []
        for step, (x, i) in enumerate(zip(around("shard", 4), around("z", 4))):
            out.append((ins[0].at[:, i], outs[0].at[step], {"z": i}))
            for k, source in enumerate(shards_of(ins[1], x)):
                out.append((source, outs[1 + k].at[here], {"shard": x}))
        return out

    shapes = [(3, 2, 4, 24, width), (4, 192, 768), (4, 192, 768), (4, 384, 384)]
    got = move(
        "first_axis",
        2,
        [mix, exp],
        shapes,
        lambda: [{"shard": x} for x in around("shard", 4)] + [{"z": i} for i in around("z", 4)],
        copies_2,
    )
    mix = total(at(mix, z, 1), *got[0]).astype(BF)
    rows = [
        lax.dynamic_slice(exp, (shard * 192, 0), (192, 768)),
        lax.dynamic_slice(exp, (768 + shard * 192, 0), (192, 768)),
        lax.dynamic_slice(exp, (1536 + shard // 2 * 384, shard % 2 * 384), (384, 384)),
    ]
    exp = [lax.dynamic_update_index_in_dim(g, o, shard, 0) for g, o in zip(got[1:], rows)]

    got = move(
        "other_axis",
        3,
        [mix],
        [(3, 2, 24, width)],
        lambda: [{"shard": x} for x in around("shard", 4)],
        lambda ins, outs: [
            (ins[0].at[:, x], outs[0].at[step], {"shard": x})
            for step, x in enumerate(around("shard", 4))
        ],
    )[0]
    mix = total(at(mix, shard, 1), *got).astype(BF)

    def places():
        here = 2 * lax.axis_index("yh") + lax.axis_index("section")
        there = [lax.rem(here + step, 4) for step in range(1, 4)]
        return [(t // 2, lax.rem(t, 2)) for t in there]

    def copies_4(ins, outs):
        there = other("core")
        out = [
            (ins[1 + k].at[pl.ds(2 * there, 2)], outs[1 + k], {"core": there}) for k in range(3)
        ]
        for step, (y, s) in enumerate(places()):
            out.append((ins[0].at[s, y], outs[0].at[step], {"yh": y, "section": s}))
        return out

    mine = (jnp.arange(2) == yh)[:, None, None]
    pairs = jnp.stack([mix, jnp.where(mine, late[None], jnp.zeros((), BF))])
    got = move(
        "last_axis",
        4,
        [pairs, *exp],
        [(3, 24, width), (2, 192, 768), (2, 192, 768), (2, 384, 384)],
        lambda: [{"yh": y, "section": s} for y, s in places()] + [{"core": other("core")}],
        copies_4,
    )
    sums = total(at(at(pairs, section, 0), yh, 0), *got[0])
    out = []
    for e, g in zip(exp, got[1:]):
        kept = lax.dynamic_slice_in_dim(e, 2 * core, 2, 0)
        low, high = jnp.where(core == 0, kept, g), jnp.where(core == 0, g, kept)
        out.append(jnp.concatenate([low, high], axis=1).astype(F32))
    return sums, out


def gather_weights(local, experts):
    rows, width = local.shape

    def kernel(*refs):
        mine, shards = refs[0], refs[1:4]
        full, late, whole = refs[4], refs[5], refs[6:9]
        stage = refs[9:12]
        sent, got, sent_x, got_e, sent_c, got_c, sent_y, sent_o, local_sem = refs[12:]
        s, yh, z, c, x = (lax.axis_index(a) for a in ("section", "yh", "z", "core", "shard"))
        place = 2 * yh + s
        ys = [lax.rem(place + k, 4) for k in (1, 2, 3)]
        ys = [{"yh": y // 2, "section": lax.rem(y, 2)} for y in ys]
        xs = [{"shard": lax.rem(x + k, 4)} for k in (1, 2, 3)]
        z_up, z_down = lax.rem(z + 1, 4), lax.rem(z + 3, 4)
        sibling, partner = {"core": 1 - c}, {"section": 1 - s}

        def piece(k, i, h):
            if k == 2:
                return shards[2].at[i, pl.ds(pl.multiple_of(h * 384, 128), 384)]
            return shards[k].at[i, pl.ds(pl.multiple_of(h * 192, 64), 192)]

        def landing(k, layer, source, half):
            if k == 2:
                return whole[2].at[layer, half, :, pl.ds(pl.multiple_of(source * 384, 128), 384)]
            return whole[k].at[layer, source, half]

        def remote(source, target, send, receive, device):
            return pltpu.make_async_remote_copy(
                src_ref=source,
                dst_ref=target,
                send_sem=send,
                recv_sem=receive,
                device_id=device,
                device_id_type=pl.DeviceIdType.MESH,
            )

        def start(copies):
            for copy in copies:
                copy.start()
            return copies

        def finish(copies):
            for copy in copies:
                copy.wait()

        has_own = x // 2 == c
        own = lax.rem(x, 2)
        staged = start(
            [pltpu.make_async_copy(piece(k, own, c), stage[k], local_sem.at[k]) for k in range(3)]
        )
        barrier = pltpu.get_barrier_semaphore()
        near = ys + xs + [{"z": z_up}, {"z": z_down}, sibling]
        near += [{"shard": lax.rem(x + k, 4), "core": 1 - c} for k in (1, 2, 3)]
        for peer in near:
            pl.semaphore_signal(
                barrier, inc=1, device_id=peer, device_id_type=pl.DeviceIdType.MESH
            )
        pl.semaphore_wait(barrier, len(near))

        for i in range(2):

            @pl.when(x != 2 * c + i)
            def _():
                for h in range(2):
                    for k in range(3):
                        remote(
                            piece(k, i, h),
                            landing(k, s, x, h),
                            sent_x.at[(i * 2 + h) * 3 + k],
                            got_e.at[s, x, k],
                            {"shard": 2 * c + i, "core": h},
                        ).start()

        here = full.at[yh, z, c, x]

        def along_y(target):
            out = [pltpu.make_async_copy(mine, target, local_sem.at[3])]
            for k, device in enumerate(ys):
                out.append(remote(mine, target, sent.at[k], got.at[k], device))
            return out

        @pl.when(s == 0)
        def _():
            start(along_y(here))

        @pl.when(s == 1)
        def _():
            start(along_y(late.at[yh]))

        finish(staged)

        @pl.when(has_own)
        def _():
            for k in range(3):
                remote(
                    piece(k, own, 1 - c),
                    landing(k, s, x, 1 - c),
                    sent_o.at[k],
                    got_e.at[s, x, k],
                    sibling,
                ).start()
                pltpu.make_async_copy(stage[k], landing(k, s, x, c), got_e.at[s, x, k]).start()

        def pass_on(layer, distance, to_partner):
            source = lax.rem(x + distance, 4)
            for k in range(3):
                view = landing(k, layer, source, c)
                receive = got_e.at[layer, source, k]
                remote(view, view, sent_o.at[k], receive, sibling).wait_recv()
                if to_partner:
                    remote(view, view, sent_y.at[distance, k], receive, partner).start()
                across = got_c.at[layer, source, k]
                remote(view, view, sent_c.at[layer, source, k], across, sibling).start()

        finish(along_y(here))
        view = full.at[:, z, c, x]
        along_x = start(
            [remote(view, view, sent.at[3 + k], got.at[3 + k], xs[k]) for k in range(3)]
        )
        pass_on(s, 0, True)
        finish(along_x)

        def ring(base, up, down):
            return start(
                [
                    remote(up, up, sent.at[base], got.at[base], {"z": z_up}),
                    remote(down, down, sent.at[base + 1], got.at[base + 1], {"z": z_down}),
                ]
            )

        view = full.at[:, z, c]
        along_z = ring(6, view, view)
        finish(along_z)
        along_z = ring(8, full.at[0, z_down, c], full.at[1, z_up, c])
        for distance in (1, 3, 2):
            pass_on(s, distance, True)
        finish(along_z)
        view = full.at[:, :, c]
        across = start([remote(view, view, sent.at[10], got.at[10], sibling)])
        for distance in (0, 1, 3, 2):
            pass_on(1 - s, distance, False)

        finish(across)
        for i in range(2):

            @pl.when(x != 2 * c + i)
            def _():
                for h in range(2):
                    for k in range(3):
                        view = piece(k, i, h)
                        n = (i * 2 + h) * 3 + k
                        remote(view, view, sent_x.at[n], got_e.at[0, 0, k], sibling).wait_send()

        @pl.when(has_own)
        def _():
            for k in range(3):
                view = piece(k, own, 1 - c)
                remote(view, view, sent_o.at[k], got_e.at[0, 0, k], sibling).wait_send()

        for source in range(4):
            for k in range(3):
                view = landing(k, s, source, c)
                send = sent_y.at[source, k]
                remote(view, view, send, got_e.at[0, 0, k], partner).wait_send()
                for layer in range(2):
                    view = landing(k, layer, source, c)
                    arrived = landing(k, layer, source, 1 - c)
                    send, receive = sent_c.at[layer, source, k], got_c.at[layer, source, k]
                    remote(view, view, send, receive, sibling).wait_send()
                    remote(arrived, arrived, send, receive, sibling).wait_recv()

    space = pl.BlockSpec(memory_space=pltpu.HBM)
    near_space = pl.BlockSpec(memory_space=pltpu.VMEM)
    shapes = [(2, 4, 2, 4, rows, width), (2, rows, width)]
    shapes += [(2, 4, 2, 192, 768), (2, 4, 2, 192, 768), (2, 2, 384, 1536)]
    dma = pltpu.SemaphoreType.DMA
    return pl.pallas_call(
        kernel,
        out_shape=[jax.ShapeDtypeStruct(shape, BF) for shape in shapes],
        in_specs=[near_space] + [space] * 3,
        out_specs=[space] * 5,
        scratch_shapes=[
            pltpu.VMEM((192, 768), BF),
            pltpu.VMEM((192, 768), BF),
            pltpu.VMEM((384, 384), BF),
            dma((11,)),
            dma((11,)),
            dma((12,)),
            dma((2, 4, 3)),
            dma((2, 4, 3)),
            dma((2, 4, 3)),
            dma((4, 3)),
            dma((3,)),
            dma((4,)),
        ],
        compiler_params=pltpu.CompilerParams(collective_id=0, has_side_effects=True),
        name="gather_weights",
    )(local, *experts)


def rank_of(route_rows):
    rows = route_rows.shape[0]
    chosen = route_rows.T[None, :, :] == jnp.arange(EXPERTS, dtype=jnp.int32)[:, None, None]
    hot = jnp.any(chosen, axis=1)
    index = jnp.arange(rows, dtype=jnp.int32)
    before = (index[:, None] < index[None, :]).astype(BF)
    return jnp.where(hot, dot(hot.astype(BF), before), -1.0)


def stacked(field):
    return jnp.concatenate(jnp.split(field, CHUNKS, axis=1), axis=0)


def unstacked(field):
    return jnp.concatenate(jnp.split(field, CHUNKS, axis=0), axis=1)


def unfold_table(sources):
    row = jnp.arange(CHUNKS * sources * EXTRA, dtype=jnp.int32)
    piece, source, extra = row // (sources * EXTRA), row // EXTRA % sources, row % EXTRA
    column = jnp.arange(sources * MAIN, dtype=jnp.int32)
    return (
        (source * MAIN + piece * EXTRA + extra)[:, None] == column[None, :]
    ).astype(BF)


def exchange(message):
    return lax.all_to_all(message, CHIPS, split_axis=0, concat_axis=0, tiled=True)


def arrived_rows(message, unfold):
    width = message.shape[1] - 256
    extra = unstacked(dot(unfold, message[:, width:]).astype(BF))
    return jnp.concatenate([message[:, :width], extra], axis=0)


def fold_rows(rows, unfold, sources):
    main = rows[: sources * MAIN]
    extra = dot(unfold, stacked(rows[sources * MAIN :]), ((0,), (0,))).astype(BF)
    return jnp.concatenate([main, extra], axis=1)


def low_pair(value):
    high = value.astype(BF)
    return high, (value - high.astype(F32)).astype(BF)


OUT_COLUMNS, QKV_STEP = 1536, 512


def columns(width, place):
    return lambda rows: pl.BlockSpec((rows, width), lambda i: (0, place), memory_space=pltpu.VMEM)


OUT_BLOCK = [columns(OUT_COLUMNS, 0)]
QKV_BLOCKS = [columns(QKV_STEP, 3 + k) for k in range(4)]
NARROW_BLOCK = [columns(128, 28)]


def fused(name, body, shapes, *arrays):
    near = pl.BlockSpec(memory_space=pltpu.VMEM)
    specs, given = [], []
    for array in arrays:
        if isinstance(array, tuple):
            array, blocks = array
            specs += [block(array.shape[0]) for block in blocks]
            given += [array] * len(blocks)
        else:
            specs.append(near)
            given.append(array)
    return pl.pallas_call(
        body,
        grid=(1,),
        out_shape=[jax.ShapeDtypeStruct(shape, kind) for shape, kind in shapes],
        in_specs=specs,
        out_specs=[near] * len(shapes),
        compiler_params=pltpu.CompilerParams(vmem_limit_bytes=48 << 20),
        name=name,
    )(*given)


TN, NT = ((0,), (0,)), ((1,), (1,))


def slots(rank):
    count, rows = rank.shape
    place = lax.broadcasted_iota(jnp.int32, (count, MAIN, rows), 1)
    wide = jnp.broadcast_to(rank[:, None, :], (count, MAIN, rows))
    main = jnp.where(wide == place.astype(F32), 1.0, 0.0)
    extra = (MAIN + lax.rem(place, EXTRA)).astype(F32)
    extra = jnp.where((wide == extra) & (place < EXTRA * CHUNKS), 1.0, 0.0)
    return main, extra


def per_piece(table):
    piece = lax.rem(lax.broadcasted_iota(jnp.int32, table.shape, 0), MAIN) // EXTRA
    return [jnp.where(piece == j, table, 0.0) for j in range(CHUNKS)]


def flat(table):
    return table.reshape(table.shape[0] * table.shape[1], table.shape[2])


def send_table(main, extra, field):
    width = field.shape[1] // CHUNKS
    side = None
    for j, table in enumerate(per_piece(flat(extra))):
        part = dot(table.astype(BF), field[:, j * width : (j + 1) * width])
        side = part if side is None else side + part
    return dot(flat(main).astype(BF), field), side


def bring_back(main, extra, rows, exact):
    parts = low_pair if exact else (lambda t: (t.astype(BF),))
    model_width = rows.shape[1] - 256
    total_main = None
    for table in parts(main):
        part = dot(table, rows[:, :model_width], TN)
        total_main = part if total_main is None else total_main + part
    side = []
    for table in per_piece(extra):
        total_side = None
        for t in parts(table):
            part = dot(t, rows[:, model_width:], TN)
            total_side = part if total_side is None else total_side + part
        side.append(total_side)
    return total_main + jnp.concatenate(side, axis=1)


def gain_rows(narrow):
    row = lax.broadcasted_iota(jnp.int32, (8, narrow.shape[1]), 0)
    column = lax.broadcasted_iota(jnp.int32, (8, narrow.shape[1]), 1)
    pick = jnp.where(column == row + EXPERTS, 1.0, 0.0).astype(BF)
    rows = dot(pick, narrow, NT)
    return rows[0:1], rows[1:2]


def turn(field, cosine, sine):
    return field * cosine + pltpu.roll(field, HEAD_DIM // 2, 1) * sine


def turn_back(field, cosine, sine):
    return field * cosine - pltpu.roll(field, HEAD_DIM // 2, 1) * sine


def combined(x_mid, rank, gates, rows):
    main, extra = slots(rank)
    wide = jnp.broadcast_to(gates[:, None, :], main.shape)
    return x_mid + bring_back(flat(main * wide), flat(extra * wide), rows, True)


def project_body(combine):
    def body(*refs):
        if combine:
            mid_ref, rank_ref, gates_ref, rows_ref = refs[:4]
            refs = refs[4:]
            low = combined(mid_ref[...], rank_ref[...], gates_ref[...], rows_ref[...]).astype(BF)
        else:
            low = refs[0][...]
            refs = refs[1:]
        weights, refs = refs[:4], refs[4:]
        narrow, cos_ref, sin_ref, low_ref, h_ref, q_ref, kv_ref = refs
        field = low.astype(F32)
        low_ref[...] = low
        gain, _ = gain_rows(narrow[...])
        scale = lax.rsqrt(jnp.mean(field * field, axis=1, keepdims=True) + epsilon)
        h = (field * scale * gain).astype(BF)
        h_ref[...] = h
        cosine, sine = cos_ref[...], sin_ref[...]
        query_width = q_ref.shape[1]
        for at_column in range(0, 4 * QKV_STEP, 256):
            inside = at_column % QKV_STEP
            part = dot(h, weights[at_column // QKV_STEP][:, inside : inside + 256])
            if at_column < query_width + kv_ref.shape[1] // 2:
                part = jnp.concatenate(
                    [turn(part[:, k : k + HEAD_DIM], cosine, sine) for k in (0, HEAD_DIM)], axis=1
                )
            if at_column < query_width:
                q_ref[:, at_column : at_column + 256] = part.astype(BF)
            else:
                at_kv = at_column - query_width
                kv_ref[:, at_kv : at_kv + 256] = part.astype(BF)

    return body


def project(source, weights, tables):
    combine = len(source) > 1
    tok_rows, model_width = source[0].shape
    shapes = [((tok_rows, model_width), BF)] * 2
    shapes += [((tok_rows, HEADS * HEAD_DIM), BF)]
    shapes += [((tok_rows, 4 * QKV_STEP - HEADS * HEAD_DIM), BF)]
    return fused(
        "project_combined" if combine else "project",
        project_body(combine),
        shapes,
        *source,
        (weights, QKV_BLOCKS + NARROW_BLOCK),
        *tables,
    )


def finish_body(mid_ref, rank_ref, gates_ref, rows_ref, out_ref):
    out = combined(mid_ref[...], rank_ref[...], gates_ref[...], rows_ref[...])
    out_ref[...] = out.astype(BF)


def heads_of(kv_ref):
    kv_heads = kv_ref.shape[2] // 2 // HEAD_DIM
    parts = []
    for k in range(2 * kv_heads):
        part = kv_ref[:, :, k * HEAD_DIM : (k + 1) * HEAD_DIM]
        parts.append(part.reshape(part.shape[0] * part.shape[1], HEAD_DIM))
    return parts[:kv_heads], parts[kv_heads:]


def attend_body(
    low_ref, q_ref, kv_ref, allowed_ref, weight, narrow, rank_ref,
    mid_ref, h_ref, att_ref, probs_ref, gates_ref, out_ref,
):
    keys, values = heads_of(kv_ref)
    allowed = allowed_ref[...] > 0.0
    ratio = HEADS // len(keys)
    for head in range(HEADS):
        lanes = slice(head * HEAD_DIM, (head + 1) * HEAD_DIM)
        scores = dot(q_ref[:, lanes], keys[head // ratio], NT) * HEAD_DIM ** (-0.5)
        scores = jnp.where(allowed, scores, masked_score)
        exponent = jnp.exp(scores - jnp.max(scores, axis=1, keepdims=True))
        probs = exponent / jnp.sum(exponent, axis=1, keepdims=True)
        probs_ref[head] = probs
        att_ref[:, lanes] = dot(probs.astype(BF), values[head // ratio]).astype(BF)
    mid = low_ref[...].astype(F32) + dot(att_ref[...], weight[...])
    mid_ref[...] = mid
    _, gain = gain_rows(narrow[...])
    scale = lax.rsqrt(jnp.mean(mid * mid, axis=1, keepdims=True) + epsilon)
    h = (mid * scale * gain).astype(BF)
    h_ref[...] = h
    rank = rank_ref[...]
    logits = jnp.transpose(dot(h, narrow[...]))[:EXPERTS]
    logits = jnp.where(rank >= 0.0, logits, masked_score)
    gate_exp = jnp.exp(logits - jnp.max(logits, axis=0, keepdims=True))
    gate_exp = jnp.where(rank >= 0.0, gate_exp, 0.0)
    gates_ref[...] = gate_exp / jnp.sum(gate_exp, axis=0, keepdims=True)
    main, side = send_table(*slots(rank), h)
    width = main.shape[1]
    out_ref[:, :width] = main.astype(BF)
    out_ref[:, width:] = side.astype(BF)


def attend(low, q, kv, allowed, weights, rank):
    tok_rows, model_width = low.shape
    shapes = [
        ((tok_rows, model_width), F32),
        ((tok_rows, model_width), BF),
        ((tok_rows, HEADS * HEAD_DIM), BF),
        ((HEADS, tok_rows, allowed.shape[1]), F32),
        (rank.shape, F32),
        ((EXPERTS * MAIN, model_width + 256), BF),
    ]
    return fused(
        "attend", attend_body, shapes,
        low, q, kv, allowed, (weights, OUT_BLOCK + NARROW_BLOCK), rank,
    )


def grad_slots_body(grad_ref, rank_ref, gates_ref, rows_ref, out_ref, dlogits_ref):
    gates = gates_ref[...]
    main, extra = slots(rank_ref[...])
    wide = jnp.broadcast_to(gates[:, None, :], main.shape)
    grad_main, grad_side = send_table(main, extra, grad_ref[...])
    width = grad_main.shape[1]
    dgate = None
    for table, grad, columns in (
        (main, grad_main, slice(0, width)),
        (extra, grad_side, slice(width, width + 256)),
    ):
        slot_gate = jnp.sum(flat(table * wide), axis=1, keepdims=True)
        out_ref[:, columns] = (grad * slot_gate).astype(BF)
        slot_dgate = jnp.sum(grad * rows_ref[:, columns].astype(F32), axis=1, keepdims=True)
        part = jnp.sum((flat(table) * slot_dgate).reshape(table.shape), axis=1)
        dgate = part if dgate is None else dgate + part
    dlogits = gates * (dgate - jnp.sum(gates * dgate, axis=0, keepdims=True))
    pad = jnp.zeros((dlogits_ref.shape[1] - EXPERTS, dlogits.shape[1]), F32)
    dlogits_ref[...] = jnp.transpose(jnp.concatenate([dlogits, pad], axis=0)).astype(BF)


def grad_slots(grad, rank, gates, rows):
    shapes = [(rows.shape, BF), ((grad.shape[0], 128), BF)]
    return fused("grad_slots", grad_slots_body, shapes, grad, rank, gates, rows)


def norm_grads(field, gain, grad):
    scale = lax.rsqrt(jnp.mean(field * field, axis=1, keepdims=True) + epsilon)
    scaled = grad * gain
    centre = jnp.mean(scaled * field, axis=1, keepdims=True)
    dgain = jnp.sum(grad * field * scale, axis=0, keepdims=True)
    return scale * scaled - field * (scale * scale * scale) * centre, dgain


def grad_attend_body(
    grad_ref, rows_ref, rank_ref, dlogits_ref, weight, narrow, mid_ref, q_ref, kv_ref, probs_ref,
    cos_ref, sin_ref,
    dmid_ref, dbr_ref, dq_ref, dkv_ref, dgain_ref, datt_ref,
):
    main, extra = slots(rank_ref[...])
    dh = bring_back(flat(main), flat(extra), rows_ref[...], False)
    dh = dh + dot(dlogits_ref[...], narrow[...], NT)
    _, gain = gain_rows(narrow[...])
    dmid, dgain = norm_grads(mid_ref[...], gain, dh)
    dmid = dmid + grad_ref[...].astype(F32)
    dgain_ref[...] = dgain
    dmid_ref[...] = dmid
    dbr_ref[...] = dmid.astype(BF)
    datt_ref[...] = dot(dbr_ref[...], weight[...], NT).astype(BF)
    keys, values = heads_of(kv_ref)
    ratio = HEADS // len(keys)
    cosine, sine = cos_ref[...], sin_ref[...]
    count, tok_rows = kv_ref.shape[0], kv_ref.shape[1]
    scale = HEAD_DIM ** (-0.5)
    for k in range(len(keys)):
        dkey, dvalue = None, None
        for head in range(k * ratio, (k + 1) * ratio):
            lanes = slice(head * HEAD_DIM, (head + 1) * HEAD_DIM)
            probs, datt = probs_ref[head], datt_ref[:, lanes]
            dprobs = dot(datt, values[k], NT)
            centre = jnp.sum(dprobs * probs, axis=1, keepdims=True)
            dscores = (probs * (dprobs - centre)).astype(BF)
            part = dot(probs.astype(BF), datt, TN)
            dvalue = part if dvalue is None else dvalue + part
            part = dot(dscores, q_ref[:, lanes], TN)
            dkey = part if dkey is None else dkey + part
            dquery = dot(dscores, keys[k]) * scale
            dq_ref[:, lanes] = turn_back(dquery, cosine, sine).astype(BF)
        at_key, at_value = k * HEAD_DIM, (len(keys) + k) * HEAD_DIM
        shape = (count, tok_rows, HEAD_DIM)
        dkv_ref[:, :, at_key : at_key + HEAD_DIM] = (dkey * scale).astype(BF).reshape(shape)
        dkv_ref[:, :, at_value : at_value + HEAD_DIM] = dvalue.astype(BF).reshape(shape)


def grad_attend(grad, rows, rank, dlogits, weights, mid, q, kv, probs, tables):
    tok_rows, model_width = mid.shape
    shapes = [
        ((tok_rows, model_width), F32),
        ((tok_rows, model_width), BF),
        (q.shape, BF),
        (kv.shape, BF),
        ((1, model_width), F32),
        (q.shape, BF),
    ]
    return fused(
        "grad_attend", grad_attend_body, shapes,
        grad, rows, rank, dlogits, (weights, OUT_BLOCK + NARROW_BLOCK), mid, q, kv, probs, *tables,
    )[:5]


def grad_project_body(
    dq_ref, dkv_ref, dmid_ref, low_ref, weight_0, weight_1, weight_2, weight_3, narrow, cos_ref,
    sin_ref,
    dqkv_ref, grad_ref, dgain_ref,
):
    query_width, kv_width = dq_ref.shape[1], dkv_ref.shape[1] // 2
    cosine, sine = cos_ref[...], sin_ref[...]
    dqkv_ref[:, :query_width] = dq_ref[...]
    for k in range(0, kv_width, HEAD_DIM):
        part = turn_back(dkv_ref[:, k : k + HEAD_DIM], cosine, sine)
        dqkv_ref[:, query_width + k : query_width + k + HEAD_DIM] = part.astype(BF)
    dqkv_ref[:, query_width + kv_width :] = dkv_ref[:, kv_width:].astype(BF)
    dh = None
    for k, weight in enumerate((weight_0, weight_1, weight_2, weight_3)):
        part = dot(dqkv_ref[:, k * QKV_STEP : (k + 1) * QKV_STEP], weight[...], NT)
        dh = part if dh is None else dh + part
    gain, _ = gain_rows(narrow[...])
    dlow, dgain = norm_grads(low_ref[...].astype(F32), gain, dh)
    dgain_ref[...] = dgain
    grad_ref[...] = (dlow + dmid_ref[...]).astype(BF)


def grad_project(dq, dkv, dmid, low, weights, tables):
    tok_rows, model_width = low.shape
    shapes = [
        ((tok_rows, 4 * QKV_STEP), BF),
        ((tok_rows, model_width), BF),
        ((1, model_width), F32),
    ]
    return fused(
        "grad_project", grad_project_body, shapes,
        dq, dkv, dmid, low, (weights, QKV_BLOCKS + NARROW_BLOCK), *tables,
    )


def weight_grads_body(
    h_ref, dqkv_ref, att_ref, dbr_ref, h2_ref, dlogits_ref, dgain_a_ref, dgain_m_ref, out_ref
):
    step = 512
    place = 0
    for left, right in ((att_ref, dbr_ref), (h_ref, dqkv_ref)):
        for k in range(0, right.shape[1], step):
            part = dot(left[...], right[:, k : k + step], TN)
            out_ref[:, place : place + step] = part.astype(BF)
            place += step
    narrow = dot(h2_ref[...], dlogits_ref[...], TN)
    rows = jnp.concatenate(
        [dgain_a_ref[...], dgain_m_ref[...], jnp.zeros((126, h_ref.shape[1]), F32)], axis=0
    )
    columns = pltpu.roll(jnp.transpose(rows), EXPERTS, 1)
    out_ref[:, place:] = (narrow + columns).astype(BF)


def weight_grads(h, dqkv, att, dbr, h2, dlogits, dgain_a, dgain_m):
    columns = dqkv.shape[1] + dbr.shape[1] + 128
    return fused(
        "weight_grads", weight_grads_body, [((h.shape[1], columns), BF)],
        h, dqkv, att, dbr, h2, dlogits, dgain_a, dgain_m,
    )[0]


def greet(peers):
    barrier = pltpu.get_barrier_semaphore()
    for peer in peers:
        pl.semaphore_signal(barrier, inc=1, device_id=peer, device_id_type=pl.DeviceIdType.MESH)
    pl.semaphore_wait(barrier, len(peers))


def small_exchange(name, number, array, shape, scratch, before, after):
    def kernel(in_ref, out_ref, *rest):
        here = lax.axis_index("shard")
        held = rest[0] if scratch else out_ref
        sent, got = rest[-2:]
        peers = [{"shard": x} for x in around("shard", 4)]
        greet(peers)
        copies = []
        for k, peer in enumerate(peers):
            source, target = before(in_ref, held, here, peer["shard"], k)
            copies.append(
                pltpu.make_async_remote_copy(
                    src_ref=source,
                    dst_ref=target,
                    send_sem=sent.at[k],
                    recv_sem=got.at[k],
                    device_id=peer,
                    device_id_type=pl.DeviceIdType.MESH,
                )
            )
            copies[-1].start()
        if not scratch:
            after(in_ref, held, out_ref, here)
        for copy in copies:
            copy.wait()
        if scratch:
            after(in_ref, held, out_ref, here)

    near = pl.BlockSpec(memory_space=pltpu.VMEM)
    dma = pltpu.SemaphoreType.DMA
    return pl.pallas_call(
        kernel,
        out_shape=jax.ShapeDtypeStruct(*shape),
        in_specs=[near],
        out_specs=near,
        scratch_shapes=scratch + [dma((3,)), dma((3,))],
        compiler_params=pltpu.CompilerParams(collective_id=number, has_side_effects=True),
        name=name,
    )(array)


def gather_group(kv, number):
    def before(in_ref, held, here, there, k):
        return in_ref, held.at[here]

    def after(in_ref, held, out_ref, here):
        out_ref[here] = in_ref[...]

    return small_exchange("gather_group", number, kv, ((4, *kv.shape), BF), [], before, after)


def sum_group(dkv, number):
    def before(in_ref, held, here, there, k):
        return in_ref.at[there], held.at[k]

    def after(in_ref, held, out_ref, here):
        out = in_ref[here].astype(F32)
        for k in range(3):
            out = out + held[k].astype(F32)
        out_ref[...] = out

    held = [pltpu.VMEM((3, *dkv.shape[1:]), BF)]
    return small_exchange("sum_group", number, dkv, (dkv.shape[1:], F32), held, before, after)


def forward_layer(source, weights, experts, rank, unfold, tables, allowed, number):
    gate_w, up_w, down_w = experts
    low, h_attn, query, kv = project(source, weights, tables)
    kv_all = gather_group(kv, number)
    x_mid, h_moe, attended, probs, gates, message = attend(low, query, kv_all, allowed, weights, rank)
    arrived = arrived_rows(exchange(message), unfold)
    gate_pre = dot(arrived, gate_w)
    up_pre = dot(arrived, up_w)
    hidden = (jax.nn.silu(gate_pre) * up_pre).astype(BF)
    produced = dot(hidden, down_w).astype(BF)
    returned = exchange(fold_rows(produced, unfold, EXPERTS))
    stored = {
        "low": low,
        "h_attn": h_attn,
        "query": query,
        "kv_all": kv_all,
        "probs": probs,
        "attended": attended,
        "x_mid": x_mid,
        "h_moe": h_moe,
        "gates": gates,
        "returned": returned,
        "arrived": arrived,
        "gate_pre": gate_pre,
        "up_pre": up_pre,
        "hidden": hidden,
    }
    return (x_mid, rank, gates, returned), stored


def backward_layer(grad, ready, stored, weights, experts, rank, unfold, tables, numbers):
    gate_w, up_w, down_w = experts
    message, dlogits = grad_slots(grad, rank, stored["gates"], stored["returned"])
    came, *ready = lax.optimization_barrier((exchange(message), *ready))
    came = arrived_rows(came, unfold)
    gate_pre, up_pre = stored["gate_pre"], stored["up_pre"]
    grad_down = dot(stored["hidden"], came, TN).astype(BF)
    grad_hidden = dot(came, down_w, NT)
    logistic = jax.nn.sigmoid(gate_pre)
    grad_gate_pre = (
        grad_hidden * up_pre * (logistic * (1.0 + gate_pre * (1.0 - logistic)))
    ).astype(BF)
    grad_up_pre = (grad_hidden * (gate_pre * logistic)).astype(BF)
    grad_rows = dot(grad_gate_pre, gate_w, NT) + dot(grad_up_pre, up_w, NT)
    returned = exchange(fold_rows(grad_rows.astype(BF), unfold, EXPERTS))
    grad_gate = dot(stored["arrived"], grad_gate_pre, TN).astype(BF)
    grad_up = dot(stored["arrived"], grad_up_pre, TN).astype(BF)
    half = sum_over_cores((grad_gate, grad_up, grad_down), numbers[0])
    returned, half = lax.optimization_barrier((returned, half))
    kv_all = stored["kv_all"]
    dmid, dbr, dquery, dkv, dgain_m = grad_attend(
        grad, returned, rank, dlogits, weights, stored["x_mid"], stored["query"], kv_all,
        stored["probs"], tables,
    )
    dkv = sum_group(dkv, numbers[1])
    dqkv, grad_in, dgain_a = grad_project(dquery, dkv, dmid, stored["low"], weights, tables)
    grads = weight_grads(
        stored["h_attn"], dqkv, stored["attended"], dbr, stored["h_moe"], dlogits, dgain_a, dgain_m
    )
    return grad_in, grads, half, ready


def per_device(
    tokens,
    routes,
    lengths,
    gain_attn,
    w_query,
    w_key,
    w_value,
    w_out,
    gain_moe,
    w_router,
    w_gate,
    w_up,
    w_down,
    cotangent,
):
    section, yh, z, core, shard = (
        lax.axis_index(a) for a in ("section", "yh", "z", "core", "shard")
    )
    first = section == 0
    tok_rows, model_width = tokens.shape[1:]
    group_rows = tok_rows * lax.axis_size("shard")

    def mine(a):
        return lax.dynamic_index_in_dim(a, section, 0, keepdims=False)

    def by_layer(own, other):
        return jnp.where(first, own, other), jnp.where(first, other, own)

    local = jnp.concatenate(
        [
            w_out[0],
            w_query[0],
            w_key[0],
            w_value[0],
            w_router[0],
            gain_attn[0][:, None],
            gain_moe[0][:, None],
            jnp.zeros((w_query.shape[1], 94), BF),
        ],
        axis=1,
    )
    full, late, *whole = gather_weights(local, (w_gate[0], w_up[0], w_down[0]))
    weights = [
        full.reshape(model_width, -1),
        lax.all_gather(at(late, yh, 0), DEVICES, axis=0, tiled=True),
    ]
    route_other = swap(at(routes[0], 1 - section, 0), "section")
    ranks = [rank_of(r) for r in by_layer(mine(routes[0]), route_other)]
    experts = [
        (
            whole[0][layer].reshape(model_width, 768),
            whole[1][layer].reshape(model_width, 768),
            whole[2][layer].reshape(768, model_width),
        )
        for layer in range(2)
    ]
    unfold = unfold_table(EXPERTS)

    segment, position = document_layout(mine(lengths[:, 0]), group_rows)
    row_start = shard * tok_rows
    own_segment = lax.dynamic_slice_in_dim(segment, row_start, tok_rows)
    tables = rotary_tables(lax.dynamic_slice_in_dim(position, row_start, tok_rows), HEAD_DIM)
    query_index = row_start + jnp.arange(tok_rows, dtype=jnp.int32)
    allowed = (own_segment[:, None] == segment[None, :]) & (
        query_index[:, None] >= jnp.arange(group_rows, dtype=jnp.int32)[None, :]
    )
    allowed = allowed.astype(F32)

    source, saved = (mine(tokens),), []
    for layer in range(2):
        source, stored = forward_layer(
            source, weights[layer], experts[layer], ranks[layer], unfold, tables, allowed, 7 + layer
        )
        saved.append(stored)
    low = fused("finish", finish_body, [((tok_rows, model_width), BF)], *source)[0]
    grad, low = lax.optimization_barrier((mine(cotangent), low))
    away = swap(low, "section")

    sums, ready = [None, None], (away,)
    for layer in (1, 0):
        grad, mixer_grad, half, ready = backward_layer(
            grad,
            ready,
            saved[layer],
            weights[layer],
            experts[layer],
            ranks[layer],
            unfold,
            tables,
            (5 + layer, 9 + layer),
        )
        given = lax.ppermute(half, "section", [(1 - layer, layer)])
        sums[layer] = (half, given)
        if layer == 1:
            (away,), ready = ready, (given,)
            late = lax.psum_scatter(mixer_grad, DEVICES, scatter_dimension=0, tiled=True)
            late = lax.optimization_barrier(late)
    mixed = jnp.where(first, jnp.stack([low, away]), jnp.stack([away, low]))
    halves = jnp.where(first, total(*sums[0]), total(sums[1][0], *ready)).astype(BF)
    mix, (grad_gate, grad_up, grad_down) = reduce_all(mixer_grad, late, halves)
    return (
        mixed,
        grad[None],
        mix[:, 3616][None],
        mix[:, 1536:3072][None],
        mix[:, 3072:3328][None],
        mix[:, 3328:3584][None],
        mix[:, :1536][None],
        mix[:, 3617][None],
        mix[:, 3584:3616][None],
        grad_gate[None],
        grad_up[None],
        grad_down[None],
    )


def solution(mesh):
    fine = Mesh(mesh.devices.reshape(2, 2, 4, 2, 4), ("section", *DEVICES))
    expert = ("yh", "z", "core")
    return jax.shard_map(
        per_device,
        mesh=fine,
        in_specs=(
            P(None, DEVICES, None),
            P("section", None, DEVICES, None),
            P(None, expert, None),
            P("section", DEVICES),
            P("section", DEVICES, None),
            P("section", DEVICES, None),
            P("section", DEVICES, None),
            P("section", DEVICES, None),
            P("section", DEVICES),
            P("section", DEVICES, None),
            P("section", expert, "shard", None),
            P("section", expert, "shard", None),
            P("section", expert, None, "shard"),
            P(None, DEVICES, None),
        ),
        out_specs=(
            P(None, DEVICES, None),
            P("section", DEVICES, None),
            P("section", DEVICES),
            P("section", DEVICES, None),
            P("section", DEVICES, None),
            P("section", DEVICES, None),
            P("section", DEVICES, None),
            P("section", DEVICES),
            P("section", DEVICES, None),
            P("section", expert, "shard", None),
            P("section", expert, "shard", None),
            P("section", expert, None, "shard"),
        ),
        check_vma=False,
    )
```

```python
import jax
import jax.numpy as jnp
from jax import lax
from jax.experimental import pallas as pl
from jax.experimental.pallas import tpu as pltpu
from jax.sharding import Mesh
from jax.sharding import PartitionSpec as P

HEADS = 12
HEAD_DIM = 128
EXPERTS = 32
MAIN = 16
EXTRA = 2
CHUNKS = 6

epsilon = 1e-06
rope_base = 1000000.0
masked_score = -1e30

BF = jnp.bfloat16
F32 = jnp.float32
CHIPS = ("yh", "z", "shard")
DEVICES = ("yh", "z", "core", "shard")


def dot(a, b, dims=((1,), (0,))):
    return lax.dot_general(a, b, (dims, ((), ())), preferred_element_type=F32)


def document_layout(doc_lengths, group_rows):
    doc_ends = jnp.cumsum(doc_lengths)
    starts = doc_ends - doc_lengths
    row_index = jnp.arange(group_rows, dtype=jnp.int32)
    segment = jnp.sum((row_index[:, None] >= doc_ends[None, :]).astype(jnp.int32), axis=1)
    member = segment[:, None] == jnp.arange(doc_lengths.shape[0], dtype=jnp.int32)[None, :]
    position = row_index - jnp.sum(jnp.where(member, starts[None, :], 0), axis=1)
    return (segment, position)


def rotary_tables(position, head_size):
    half_dim = head_size // 2
    frequency = rope_base ** (-2.0 * jnp.arange(half_dim, dtype=F32) / head_size)
    angles = position.astype(F32)[:, None] * frequency[None, :]
    cosine, sine = jnp.cos(angles), jnp.sin(angles)
    return jnp.concatenate([cosine, cosine], axis=1), jnp.concatenate([-sine, sine], axis=1)


def swap(value, axis):
    return lax.ppermute(value, axis, [(0, 1), (1, 0)])


def around(axis, size):
    here = lax.axis_index(axis)
    return [lax.rem(here + step, size) for step in range(1, size)]


def move(name, number, arrays, shapes, peers, copies):
    count = len(arrays)
    total = 40

    def kernel(*refs):
        ins, outs = refs[:count], refs[count : count + len(shapes)]
        sent, got = refs[count + len(shapes) :]
        barrier = pltpu.get_barrier_semaphore()
        near = peers()
        for peer in near:
            pl.semaphore_signal(
                barrier, inc=1, device_id=peer, device_id_type=pl.DeviceIdType.MESH
            )
        pl.semaphore_wait(barrier, len(near))
        started = []
        for k, (source, target, device) in enumerate(copies(ins, outs)):
            if device is None:
                copy = pltpu.make_async_copy(source, target, got.at[k])
            else:
                copy = pltpu.make_async_remote_copy(
                    src_ref=source,
                    dst_ref=target,
                    send_sem=sent.at[k],
                    recv_sem=got.at[k],
                    device_id=device,
                    device_id_type=pl.DeviceIdType.MESH,
                )
            copy.start()
            started.append(copy)
        for copy in started:
            copy.wait()

    space = pl.BlockSpec(memory_space=pltpu.HBM)
    return pl.pallas_call(
        kernel,
        out_shape=[jax.ShapeDtypeStruct(s, BF) for s in shapes],
        in_specs=[space] * count,
        out_specs=[space] * len(shapes),
        scratch_shapes=[pltpu.SemaphoreType.DMA((total,)), pltpu.SemaphoreType.DMA((total,))],
        compiler_params=pltpu.CompilerParams(collective_id=number, has_side_effects=True),
        name=name,
    )(*arrays)


def total(*parts):
    out = parts[0].astype(F32)
    for part in parts[1:]:
        out = out + part.astype(F32)
    return out


def at(array, index, axis):
    return lax.dynamic_index_in_dim(array, index, axis, keepdims=False)


def other(axis):
    return lax.rem(lax.axis_index(axis) + 1, 2)


def sum_over_cores(grads, number):
    gate, up, down = grads
    halves = [gate.reshape(4, 2, 192, 768), up.reshape(4, 2, 192, 768), down.reshape(2, 384, 1536)]

    def copies(ins, outs):
        there = other("core")
        views = [ins[0].at[:, there], ins[1].at[:, there], ins[2].at[there]]
        return [(v, o, {"core": there}) for v, o in zip(views, outs)]

    shapes = [(4, 192, 768), (4, 192, 768), (384, 1536)]
    got = move("expert_cores", number, halves, shapes, lambda: [{"core": other("core")}], copies)
    core = lax.axis_index("core")
    gate, up, down = (
        total(at(h, core, 0 if k == 2 else 1), g).astype(BF)
        for k, (h, g) in enumerate(zip(halves, got))
    )
    return jnp.concatenate(
        [gate.reshape(768, 768), up.reshape(768, 768), down[:, :768], down[:, 768:]], axis=0
    )


def reduce_all(grads, late, finish_experts):
    core, shard, z, yh, section = (
        lax.axis_index(a) for a in ("core", "shard", "z", "yh", "section")
    )
    width = grads.shape[1]
    mix = grads.reshape(8, 2, 4, 24, width)

    got = move(
        "cores",
        1,
        [mix],
        [(8, 4, 24, width)],
        lambda: [{"core": other("core")}],
        lambda ins, outs: [(ins[0].at[:, other("core")], outs[0], {"core": other("core")})],
    )[0]
    mix = total(at(mix, core, 1), got).astype(BF).reshape(2, 4, 4, 24, width)

    cut = 1792
    sizes = (cut, width - cut)

    def peers_2():
        return [{"shard": x} for x in around("shard", 4)] + [{"z": i} for i in around("z", 4)]

    def copies_2(ins, outs):
        out = []
        for step, (x, i) in enumerate(zip(around("shard", 4), around("z", 4))):
            out.append((ins[0].at[:, :, x, :, pl.ds(0, cut)], outs[0].at[step], {"shard": x}))
            out.append((ins[0].at[:, i, :, :, pl.ds(cut, width - cut)], outs[1].at[step], {"z": i}))
        return out

    shapes = [(3, 2, 4, 24, size) for size in sizes]
    got = move("first_axis", 2, [mix], shapes, peers_2, copies_2)
    mix = [
        total(at(mix[..., :cut], shard, 2), *got[0]).astype(BF),
        total(at(mix[..., cut:], z, 1), *got[1]).astype(BF),
    ]

    exp = finish_experts()

    def shards_of(ref, x):
        down = ref.at[
            pl.ds(pl.multiple_of(1536 + x // 2 * 384, 128), 384),
            pl.ds(pl.multiple_of(lax.rem(x, 2) * 384, 128), 384),
        ]
        gate = ref.at[pl.ds(pl.multiple_of(x * 192, 64), 192)]
        up = ref.at[pl.ds(pl.multiple_of(768 + x * 192, 64), 192)]
        return gate, up, down

    def copies_3(ins, outs):
        here = lax.axis_index("shard")
        out = []
        for step, (x, i) in enumerate(zip(around("shard", 4), around("z", 4))):
            out.append((ins[0].at[:, i], outs[0].at[step], {"z": i}))
            out.append((ins[1].at[:, x], outs[1].at[step], {"shard": x}))
            for k, source in enumerate(shards_of(ins[2], x)):
                out.append((source, outs[2 + k].at[here], {"shard": x}))
        return out

    shapes = [(3, 2, 24, size) for size in sizes] + [(4, 192, 768), (4, 192, 768), (4, 384, 384)]
    got = move("other_axis", 3, [*mix, exp], shapes, peers_2, copies_3)
    mix = jnp.concatenate(
        [
            total(at(mix[0], z, 1), *got[0]).astype(BF),
            total(at(mix[1], shard, 1), *got[1]).astype(BF),
        ],
        axis=-1,
    )
    rows = [
        lax.dynamic_slice(exp, (shard * 192, 0), (192, 768)),
        lax.dynamic_slice(exp, (768 + shard * 192, 0), (192, 768)),
        lax.dynamic_slice(exp, (1536 + shard // 2 * 384, shard % 2 * 384), (384, 384)),
    ]
    exp = [lax.dynamic_update_index_in_dim(g, o, shard, 0) for g, o in zip(got[2:], rows)]

    def places():
        here = 2 * lax.axis_index("yh") + lax.axis_index("section")
        there = [lax.rem(here + step, 4) for step in range(1, 4)]
        return [(t // 2, lax.rem(t, 2)) for t in there]

    def copies_4(ins, outs):
        there = other("core")
        out = [
            (ins[1 + k].at[pl.ds(2 * there, 2)], outs[1 + k], {"core": there}) for k in range(3)
        ]
        for step, (y, s) in enumerate(places()):
            out.append((ins[0].at[s, y], outs[0].at[step], {"yh": y, "section": s}))
        return out

    mine = (jnp.arange(2) == yh)[:, None, None]
    pairs = jnp.stack([mix, jnp.where(mine, late[None], jnp.zeros((), BF))])
    got = move(
        "last_axis",
        4,
        [pairs, *exp],
        [(3, 24, width), (2, 192, 768), (2, 192, 768), (2, 384, 384)],
        lambda: [{"yh": y, "section": s} for y, s in places()] + [{"core": other("core")}],
        copies_4,
    )
    sums = total(at(at(pairs, section, 0), yh, 0), *got[0])
    out = []
    for e, g in zip(exp, got[1:]):
        kept = lax.dynamic_slice_in_dim(e, 2 * core, 2, 0)
        low, high = jnp.where(core == 0, kept, g), jnp.where(core == 0, g, kept)
        out.append(jnp.concatenate([low, high], axis=1).astype(F32))
    return sums, out


def gather_weights(local, experts):
    rows, width = local.shape

    def kernel(*refs):
        mine, shards = refs[0], refs[1:4]
        full, late, whole = refs[4], refs[5], refs[6:9]
        stage = refs[9:12]
        sent, got, sent_x, got_e, sent_c, got_c, sent_y, sent_o, local_sem = refs[12:]
        s, yh, z, c, x = (lax.axis_index(a) for a in ("section", "yh", "z", "core", "shard"))
        place = 2 * yh + s
        ys = [lax.rem(place + k, 4) for k in (1, 2, 3)]
        ys = [{"yh": y // 2, "section": lax.rem(y, 2)} for y in ys]
        xs = [{"shard": lax.rem(x + k, 4)} for k in (1, 2, 3)]
        z_up, z_down = lax.rem(z + 1, 4), lax.rem(z + 3, 4)
        sibling, partner = {"core": 1 - c}, {"section": 1 - s}

        def piece(k, i, h):
            if k == 2:
                return shards[2].at[i, pl.ds(pl.multiple_of(h * 384, 128), 384)]
            return shards[k].at[i, pl.ds(pl.multiple_of(h * 192, 64), 192)]

        def landing(k, layer, source, half):
            if k == 2:
                return whole[2].at[layer, half, :, pl.ds(pl.multiple_of(source * 384, 128), 384)]
            return whole[k].at[layer, source, half]

        def remote(source, target, send, receive, device):
            return pltpu.make_async_remote_copy(
                src_ref=source,
                dst_ref=target,
                send_sem=send,
                recv_sem=receive,
                device_id=device,
                device_id_type=pl.DeviceIdType.MESH,
            )

        def start(copies):
            for copy in copies:
                copy.start()
            return copies

        def finish(copies):
            for copy in copies:
                copy.wait()

        has_own = x // 2 == c
        own = lax.rem(x, 2)
        staged = start(
            [pltpu.make_async_copy(piece(k, own, c), stage[k], local_sem.at[k]) for k in range(3)]
        )
        barrier = pltpu.get_barrier_semaphore()
        near = ys + xs + [{"z": z_up}, {"z": z_down}, sibling]
        near += [{"shard": lax.rem(x + k, 4), "core": 1 - c} for k in (1, 2, 3)]
        for peer in near:
            pl.semaphore_signal(
                barrier, inc=1, device_id=peer, device_id_type=pl.DeviceIdType.MESH
            )
        pl.semaphore_wait(barrier, len(near))

        here = full.at[yh, z, c, x]

        def along_y(target):
            out = [pltpu.make_async_copy(mine, target, local_sem.at[3])]
            for k, device in enumerate(ys):
                out.append(remote(mine, target, sent.at[k], got.at[k], device))
            return out

        @pl.when(s == 0)
        def _():
            start(along_y(here))

        @pl.when(s == 1)
        def _():
            start(along_y(late.at[yh]))

        finish(staged)

        @pl.when(has_own)
        def _():
            for k in range(3):
                remote(
                    piece(k, own, 1 - c),
                    landing(k, s, x, 1 - c),
                    sent_o.at[k],
                    got_e.at[s, x, k],
                    sibling,
                ).start()
                pltpu.make_async_copy(stage[k], landing(k, s, x, c), got_e.at[s, x, k]).start()

        def pass_on(layer, distance, to_partner):
            source = lax.rem(x + distance, 4)
            for k in range(3):
                view = landing(k, layer, source, c)
                receive = got_e.at[layer, source, k]
                remote(view, view, sent_o.at[k], receive, sibling).wait_recv()
                if to_partner:
                    remote(view, view, sent_y.at[distance, k], receive, partner).start()
                across = got_c.at[layer, source, k]
                remote(view, view, sent_c.at[layer, source, k], across, sibling).start()

        finish(along_y(here))
        view = full.at[:, z, c, x]
        along_x = start(
            [remote(view, view, sent.at[3 + k], got.at[3 + k], xs[k]) for k in range(3)]
        )
        pass_on(s, 0, True)
        finish(along_x)

        def ring(base, up, down):
            return start(
                [
                    remote(up, up, sent.at[base], got.at[base], {"z": z_up}),
                    remote(down, down, sent.at[base + 1], got.at[base + 1], {"z": z_down}),
                ]
            )

        view = full.at[:, z, c]
        along_z = ring(6, view, view)
        for i in range(2):

            @pl.when(x != 2 * c + i)
            def _():
                for h in range(2):
                    for k in range(3):
                        remote(
                            piece(k, i, h),
                            landing(k, s, x, h),
                            sent_x.at[(i * 2 + h) * 3 + k],
                            got_e.at[s, x, k],
                            {"shard": 2 * c + i, "core": h},
                        ).start()

        finish(along_z)
        along_z = ring(8, full.at[0, z_down, c], full.at[1, z_up, c])
        for distance in (1, 3, 2):
            pass_on(s, distance, True)
        finish(along_z)
        view = full.at[:, :, c]
        across = start([remote(view, view, sent.at[10], got.at[10], sibling)])
        for distance in (0, 1, 3, 2):
            pass_on(1 - s, distance, False)

        finish(across)
        for i in range(2):

            @pl.when(x != 2 * c + i)
            def _():
                for h in range(2):
                    for k in range(3):
                        view = piece(k, i, h)
                        n = (i * 2 + h) * 3 + k
                        remote(view, view, sent_x.at[n], got_e.at[0, 0, k], sibling).wait_send()

        @pl.when(has_own)
        def _():
            for k in range(3):
                view = piece(k, own, 1 - c)
                remote(view, view, sent_o.at[k], got_e.at[0, 0, k], sibling).wait_send()

        for source in range(4):
            for k in range(3):
                view = landing(k, s, source, c)
                send = sent_y.at[source, k]
                remote(view, view, send, got_e.at[0, 0, k], partner).wait_send()
                for layer in range(2):
                    view = landing(k, layer, source, c)
                    arrived = landing(k, layer, source, 1 - c)
                    send, receive = sent_c.at[layer, source, k], got_c.at[layer, source, k]
                    remote(view, view, send, receive, sibling).wait_send()
                    remote(arrived, arrived, send, receive, sibling).wait_recv()

    space = pl.BlockSpec(memory_space=pltpu.HBM)
    near_space = pl.BlockSpec(memory_space=pltpu.VMEM)
    shapes = [(2, 4, 2, 4, rows, width), (2, rows, width)]
    shapes += [(2, 4, 2, 192, 768), (2, 4, 2, 192, 768), (2, 2, 384, 1536)]
    dma = pltpu.SemaphoreType.DMA
    return pl.pallas_call(
        kernel,
        out_shape=[jax.ShapeDtypeStruct(shape, BF) for shape in shapes],
        in_specs=[near_space] + [space] * 3,
        out_specs=[space] * 5,
        scratch_shapes=[
            pltpu.VMEM((192, 768), BF),
            pltpu.VMEM((192, 768), BF),
            pltpu.VMEM((384, 384), BF),
            dma((11,)),
            dma((11,)),
            dma((12,)),
            dma((2, 4, 3)),
            dma((2, 4, 3)),
            dma((2, 4, 3)),
            dma((4, 3)),
            dma((3,)),
            dma((4,)),
        ],
        compiler_params=pltpu.CompilerParams(collective_id=0, has_side_effects=True),
        name="gather_weights",
    )(local, *experts)


def rank_of(route_rows):
    rows = route_rows.shape[0]
    chosen = route_rows.T[None, :, :] == jnp.arange(EXPERTS, dtype=jnp.int32)[:, None, None]
    hot = jnp.any(chosen, axis=1)
    index = jnp.arange(rows, dtype=jnp.int32)
    before = (index[:, None] < index[None, :]).astype(BF)
    return jnp.where(hot, dot(hot.astype(BF), before), -1.0)


def stacked(field):
    return jnp.concatenate(jnp.split(field, CHUNKS, axis=1), axis=0)


def unstacked(field):
    return jnp.concatenate(jnp.split(field, CHUNKS, axis=0), axis=1)


def unfold_table(sources):
    row = jnp.arange(CHUNKS * sources * EXTRA, dtype=jnp.int32)
    piece, source, extra = row // (sources * EXTRA), row // EXTRA % sources, row % EXTRA
    column = jnp.arange(sources * MAIN, dtype=jnp.int32)
    return (
        (source * MAIN + piece * EXTRA + extra)[:, None] == column[None, :]
    ).astype(BF)


def arrived_rows(message, unfold):
    width = message.shape[1] - 256
    extra = unstacked(dot(unfold, message[:, width:]).astype(BF))
    return jnp.concatenate([message[:, :width], extra], axis=0)


def fold_rows(rows, unfold, sources):
    main = rows[: sources * MAIN]
    extra = dot(unfold, stacked(rows[sources * MAIN :]), ((0,), (0,))).astype(BF)
    return jnp.concatenate([main, extra], axis=1)


def low_pair(value):
    high = value.astype(BF)
    return high, (value - high.astype(F32)).astype(BF)


OUT_COLUMNS, QKV_STEP = 1536, 512


def columns(width, place):
    return lambda rows: pl.BlockSpec((rows, width), lambda i: (0, place), memory_space=pltpu.VMEM)


OUT_BLOCK = [columns(OUT_COLUMNS, 0)]
QKV_BLOCKS = [columns(QKV_STEP, 3 + k) for k in range(4)]
NARROW_BLOCK = [columns(128, 28)]


def fused(name, body, shapes, *arrays):
    near = pl.BlockSpec(memory_space=pltpu.VMEM)
    specs, given = [], []
    for array in arrays:
        if isinstance(array, tuple):
            array, blocks = array
            specs += [block(array.shape[0]) for block in blocks]
            given += [array] * len(blocks)
        else:
            specs.append(near)
            given.append(array)
    return pl.pallas_call(
        body,
        grid=(1,),
        out_shape=[jax.ShapeDtypeStruct(shape, kind) for shape, kind in shapes],
        in_specs=specs,
        out_specs=[near] * len(shapes),
        compiler_params=pltpu.CompilerParams(vmem_limit_bytes=48 << 20),
        name=name,
    )(*given)


TN, NT = ((0,), (0,)), ((1,), (1,))


def slots(rank):
    count, rows = rank.shape
    place = lax.broadcasted_iota(jnp.int32, (count, MAIN, rows), 1)
    wide = jnp.broadcast_to(rank[:, None, :], (count, MAIN, rows))
    main = jnp.where(wide == place.astype(F32), 1.0, 0.0)
    extra = (MAIN + lax.rem(place, EXTRA)).astype(F32)
    extra = jnp.where((wide == extra) & (place < EXTRA * CHUNKS), 1.0, 0.0)
    return main, extra


def per_piece(table):
    piece = lax.rem(lax.broadcasted_iota(jnp.int32, table.shape, 0), MAIN) // EXTRA
    return [jnp.where(piece == j, table, 0.0) for j in range(CHUNKS)]


def flat(table):
    return table.reshape(table.shape[0] * table.shape[1], table.shape[2])


def send_table(main, extra, field):
    width = field.shape[1] // CHUNKS
    side = None
    for j, table in enumerate(per_piece(flat(extra))):
        part = dot(table.astype(BF), field[:, j * width : (j + 1) * width])
        side = part if side is None else side + part
    return dot(flat(main).astype(BF), field), side


def bring_back(main, extra, rows, exact):
    parts = low_pair if exact else (lambda t: (t.astype(BF),))
    model_width = rows.shape[1] - 256
    total_main = None
    for table in parts(main):
        part = dot(table, rows[:, :model_width], TN)
        total_main = part if total_main is None else total_main + part
    side = []
    for table in per_piece(extra):
        total_side = None
        for t in parts(table):
            part = dot(t, rows[:, model_width:], TN)
            total_side = part if total_side is None else total_side + part
        side.append(total_side)
    return total_main + jnp.concatenate(side, axis=1)


def gain_rows(narrow):
    row = lax.broadcasted_iota(jnp.int32, (8, narrow.shape[1]), 0)
    column = lax.broadcasted_iota(jnp.int32, (8, narrow.shape[1]), 1)
    pick = jnp.where(column == row + EXPERTS, 1.0, 0.0).astype(BF)
    rows = dot(pick, narrow, NT)
    return rows[0:1], rows[1:2]


def turn(field, cosine, sine):
    return field * cosine + pltpu.roll(field, HEAD_DIM // 2, 1) * sine


def turn_back(field, cosine, sine):
    return field * cosine - pltpu.roll(field, HEAD_DIM // 2, 1) * sine


def combined(x_mid, rank, gates, rows):
    main, extra = slots(rank)
    wide = jnp.broadcast_to(gates[:, None, :], main.shape)
    return x_mid + bring_back(flat(main * wide), flat(extra * wide), rows, True)


def project_body(combine):
    def body(*refs):
        if combine:
            mid_ref, rank_ref, gates_ref, rows_ref = refs[:4]
            refs = refs[4:]
            low = combined(mid_ref[...], rank_ref[...], gates_ref[...], rows_ref[...]).astype(BF)
        else:
            low = refs[0][...]
            refs = refs[1:]
        weights, refs = refs[:4], refs[4:]
        narrow, cos_ref, sin_ref, low_ref, h_ref, q_ref, kv_ref = refs
        field = low.astype(F32)
        low_ref[...] = low
        gain, _ = gain_rows(narrow[...])
        scale = lax.rsqrt(jnp.mean(field * field, axis=1, keepdims=True) + epsilon)
        h = (field * scale * gain).astype(BF)
        h_ref[...] = h
        cosine, sine = cos_ref[...], sin_ref[...]
        query_width = q_ref.shape[1]
        for at_column in range(0, 4 * QKV_STEP, 256):
            inside = at_column % QKV_STEP
            part = dot(h, weights[at_column // QKV_STEP][:, inside : inside + 256])
            if at_column < query_width + kv_ref.shape[1] // 2:
                part = jnp.concatenate(
                    [turn(part[:, k : k + HEAD_DIM], cosine, sine) for k in (0, HEAD_DIM)], axis=1
                )
            if at_column < query_width:
                q_ref[:, at_column : at_column + 256] = part.astype(BF)
            else:
                at_kv = at_column - query_width
                kv_ref[:, at_kv : at_kv + 256] = part.astype(BF)

    return body


def project(source, weights, tables):
    combine = len(source) > 1
    tok_rows, model_width = source[0].shape
    shapes = [((tok_rows, model_width), BF)] * 2
    shapes += [((tok_rows, HEADS * HEAD_DIM), BF)]
    shapes += [((tok_rows, 4 * QKV_STEP - HEADS * HEAD_DIM), BF)]
    return fused(
        "project_combined" if combine else "project",
        project_body(combine),
        shapes,
        *source,
        (weights, QKV_BLOCKS + NARROW_BLOCK),
        *tables,
    )


def finish_body(mid_ref, rank_ref, gates_ref, rows_ref, out_ref):
    out = combined(mid_ref[...], rank_ref[...], gates_ref[...], rows_ref[...])
    out_ref[...] = out.astype(BF)


def heads_of(kv_ref):
    kv_heads = kv_ref.shape[2] // 2 // HEAD_DIM
    parts = []
    for k in range(2 * kv_heads):
        part = kv_ref[:, :, k * HEAD_DIM : (k + 1) * HEAD_DIM]
        parts.append(part.reshape(part.shape[0] * part.shape[1], HEAD_DIM))
    return parts[:kv_heads], parts[kv_heads:]


def attend_body(
    low_ref, q_ref, kv_ref, allowed_ref, weight, narrow, rank_ref,
    mid_ref, h_ref, att_ref, probs_ref, gates_ref, out_ref,
):
    keys, values = heads_of(kv_ref)
    allowed = allowed_ref[...] > 0.0
    ratio = HEADS // len(keys)
    for head in range(HEADS):
        lanes = slice(head * HEAD_DIM, (head + 1) * HEAD_DIM)
        scores = dot(q_ref[:, lanes], keys[head // ratio], NT) * HEAD_DIM ** (-0.5)
        scores = jnp.where(allowed, scores, masked_score)
        exponent = jnp.exp(scores - jnp.max(scores, axis=1, keepdims=True))
        probs = exponent / jnp.sum(exponent, axis=1, keepdims=True)
        probs_ref[head] = probs
        att_ref[:, lanes] = dot(probs.astype(BF), values[head // ratio]).astype(BF)
    mid = low_ref[...].astype(F32) + dot(att_ref[...], weight[...])
    mid_ref[...] = mid
    _, gain = gain_rows(narrow[...])
    scale = lax.rsqrt(jnp.mean(mid * mid, axis=1, keepdims=True) + epsilon)
    h = (mid * scale * gain).astype(BF)
    h_ref[...] = h
    rank = rank_ref[...]
    logits = jnp.transpose(dot(h, narrow[...]))[:EXPERTS]
    logits = jnp.where(rank >= 0.0, logits, masked_score)
    gate_exp = jnp.exp(logits - jnp.max(logits, axis=0, keepdims=True))
    gate_exp = jnp.where(rank >= 0.0, gate_exp, 0.0)
    gates_ref[...] = gate_exp / jnp.sum(gate_exp, axis=0, keepdims=True)
    main, side = send_table(*slots(rank), h)
    width = main.shape[1]
    out_ref[:, :width] = main.astype(BF)
    out_ref[:, width:] = side.astype(BF)


def attend(low, q, kv, allowed, weights, rank):
    tok_rows, model_width = low.shape
    shapes = [
        ((tok_rows, model_width), F32),
        ((tok_rows, model_width), BF),
        ((tok_rows, HEADS * HEAD_DIM), BF),
        ((HEADS, tok_rows, allowed.shape[1]), F32),
        (rank.shape, F32),
        ((EXPERTS * MAIN, model_width + 256), BF),
    ]
    return fused(
        "attend", attend_body, shapes,
        low, q, kv, allowed, (weights, OUT_BLOCK + NARROW_BLOCK), rank,
    )


def grad_slots_body(grad_ref, rank_ref, gates_ref, rows_ref, out_ref, dlogits_ref):
    gates = gates_ref[...]
    main, extra = slots(rank_ref[...])
    wide = jnp.broadcast_to(gates[:, None, :], main.shape)
    grad_main, grad_side = send_table(main, extra, grad_ref[...])
    width = grad_main.shape[1]
    dgate = None
    for table, grad, columns in (
        (main, grad_main, slice(0, width)),
        (extra, grad_side, slice(width, width + 256)),
    ):
        slot_gate = jnp.sum(flat(table * wide), axis=1, keepdims=True)
        out_ref[:, columns] = (grad * slot_gate).astype(BF)
        slot_dgate = jnp.sum(grad * rows_ref[:, columns].astype(F32), axis=1, keepdims=True)
        part = jnp.sum((flat(table) * slot_dgate).reshape(table.shape), axis=1)
        dgate = part if dgate is None else dgate + part
    dlogits = gates * (dgate - jnp.sum(gates * dgate, axis=0, keepdims=True))
    pad = jnp.zeros((dlogits_ref.shape[1] - EXPERTS, dlogits.shape[1]), F32)
    dlogits_ref[...] = jnp.transpose(jnp.concatenate([dlogits, pad], axis=0)).astype(BF)


def grad_slots(grad, rank, gates, rows):
    shapes = [(rows.shape, BF), ((grad.shape[0], 128), BF)]
    return fused("grad_slots", grad_slots_body, shapes, grad, rank, gates, rows)


def norm_grads(field, gain, grad):
    scale = lax.rsqrt(jnp.mean(field * field, axis=1, keepdims=True) + epsilon)
    scaled = grad * gain
    centre = jnp.mean(scaled * field, axis=1, keepdims=True)
    dgain = jnp.sum(grad * field * scale, axis=0, keepdims=True)
    return scale * scaled - field * (scale * scale * scale) * centre, dgain


def grad_attend_body(
    grad_ref, rows_ref, rank_ref, dlogits_ref, weight, narrow, mid_ref, q_ref, kv_ref, probs_ref,
    cos_ref, sin_ref,
    dmid_ref, dbr_ref, dq_ref, dkv_ref, dgain_ref, datt_ref,
):
    main, extra = slots(rank_ref[...])
    dh = bring_back(flat(main), flat(extra), rows_ref[...], False)
    dh = dh + dot(dlogits_ref[...], narrow[...], NT)
    _, gain = gain_rows(narrow[...])
    dmid, dgain = norm_grads(mid_ref[...], gain, dh)
    dmid = dmid + grad_ref[...].astype(F32)
    dgain_ref[...] = dgain
    dmid_ref[...] = dmid
    dbr_ref[...] = dmid.astype(BF)
    datt_ref[...] = dot(dbr_ref[...], weight[...], NT).astype(BF)
    keys, values = heads_of(kv_ref)
    ratio = HEADS // len(keys)
    cosine, sine = cos_ref[...], sin_ref[...]
    count, tok_rows = kv_ref.shape[0], kv_ref.shape[1]
    scale = HEAD_DIM ** (-0.5)
    for k in range(len(keys)):
        dkey, dvalue = None, None
        for head in range(k * ratio, (k + 1) * ratio):
            lanes = slice(head * HEAD_DIM, (head + 1) * HEAD_DIM)
            probs, datt = probs_ref[head], datt_ref[:, lanes]
            dprobs = dot(datt, values[k], NT)
            centre = jnp.sum(dprobs * probs, axis=1, keepdims=True)
            dscores = (probs * (dprobs - centre)).astype(BF)
            part = dot(probs.astype(BF), datt, TN)
            dvalue = part if dvalue is None else dvalue + part
            part = dot(dscores, q_ref[:, lanes], TN)
            dkey = part if dkey is None else dkey + part
            dquery = dot(dscores, keys[k]) * scale
            dq_ref[:, lanes] = turn_back(dquery, cosine, sine).astype(BF)
        at_key, at_value = k * HEAD_DIM, (len(keys) + k) * HEAD_DIM
        shape = (count, tok_rows, HEAD_DIM)
        dkv_ref[:, :, at_key : at_key + HEAD_DIM] = (dkey * scale).astype(BF).reshape(shape)
        dkv_ref[:, :, at_value : at_value + HEAD_DIM] = dvalue.astype(BF).reshape(shape)


def grad_attend(grad, rows, rank, dlogits, weights, mid, q, kv, probs, tables):
    tok_rows, model_width = mid.shape
    shapes = [
        ((tok_rows, model_width), F32),
        ((tok_rows, model_width), BF),
        (q.shape, BF),
        (kv.shape, BF),
        ((1, model_width), F32),
        (q.shape, BF),
    ]
    return fused(
        "grad_attend", grad_attend_body, shapes,
        grad, rows, rank, dlogits, (weights, OUT_BLOCK + NARROW_BLOCK), mid, q, kv, probs, *tables,
    )[:5]


def grad_project_body(
    dq_ref, dkv_ref, dmid_ref, low_ref, weight_0, weight_1, weight_2, weight_3, narrow, cos_ref,
    sin_ref,
    dqkv_ref, grad_ref, dgain_ref,
):
    query_width, kv_width = dq_ref.shape[1], dkv_ref.shape[1] // 2
    cosine, sine = cos_ref[...], sin_ref[...]
    dqkv_ref[:, :query_width] = dq_ref[...]
    for k in range(0, kv_width, HEAD_DIM):
        part = turn_back(dkv_ref[:, k : k + HEAD_DIM], cosine, sine)
        dqkv_ref[:, query_width + k : query_width + k + HEAD_DIM] = part.astype(BF)
    dqkv_ref[:, query_width + kv_width :] = dkv_ref[:, kv_width:].astype(BF)
    dh = None
    for k, weight in enumerate((weight_0, weight_1, weight_2, weight_3)):
        part = dot(dqkv_ref[:, k * QKV_STEP : (k + 1) * QKV_STEP], weight[...], NT)
        dh = part if dh is None else dh + part
    gain, _ = gain_rows(narrow[...])
    dlow, dgain = norm_grads(low_ref[...].astype(F32), gain, dh)
    dgain_ref[...] = dgain
    grad_ref[...] = (dlow + dmid_ref[...]).astype(BF)


def grad_project(dq, dkv, dmid, low, weights, tables):
    tok_rows, model_width = low.shape
    shapes = [
        ((tok_rows, 4 * QKV_STEP), BF),
        ((tok_rows, model_width), BF),
        ((1, model_width), F32),
    ]
    return fused(
        "grad_project", grad_project_body, shapes,
        dq, dkv, dmid, low, (weights, QKV_BLOCKS + NARROW_BLOCK), *tables,
    )


def weight_grads_body(
    h_ref, dqkv_ref, att_ref, dbr_ref, h2_ref, dlogits_ref, dgain_a_ref, dgain_m_ref, out_ref
):
    step = 512
    place = 0
    for left, right in ((att_ref, dbr_ref), (h_ref, dqkv_ref)):
        for k in range(0, right.shape[1], step):
            part = dot(left[...], right[:, k : k + step], TN)
            out_ref[:, place : place + step] = part.astype(BF)
            place += step
    narrow = dot(h2_ref[...], dlogits_ref[...], TN)
    rows = jnp.concatenate(
        [dgain_a_ref[...], dgain_m_ref[...], jnp.zeros((126, h_ref.shape[1]), F32)], axis=0
    )
    columns = pltpu.roll(jnp.transpose(rows), EXPERTS, 1)
    out_ref[:, place:] = (narrow + columns).astype(BF)


def weight_grads(h, dqkv, att, dbr, h2, dlogits, dgain_a, dgain_m):
    columns = dqkv.shape[1] + dbr.shape[1] + 128
    return fused(
        "weight_grads", weight_grads_body, [((h.shape[1], columns), BF)],
        h, dqkv, att, dbr, h2, dlogits, dgain_a, dgain_m,
    )[0]


def greet(peers):
    barrier = pltpu.get_barrier_semaphore()
    for peer in peers:
        pl.semaphore_signal(barrier, inc=1, device_id=peer, device_id_type=pl.DeviceIdType.MESH)
    pl.semaphore_wait(barrier, len(peers))


def small_exchange(name, number, array, shape, scratch, before, after):
    def kernel(in_ref, out_ref, *rest):
        here = lax.axis_index("shard")
        held = rest[0] if scratch else out_ref
        sent, got = rest[-2:]
        peers = [{"shard": x} for x in around("shard", 4)]
        greet(peers)
        copies = []
        for k, peer in enumerate(peers):
            source, target = before(in_ref, held, here, peer["shard"], k)
            copies.append(
                pltpu.make_async_remote_copy(
                    src_ref=source,
                    dst_ref=target,
                    send_sem=sent.at[k],
                    recv_sem=got.at[k],
                    device_id=peer,
                    device_id_type=pl.DeviceIdType.MESH,
                )
            )
            copies[-1].start()
        if not scratch:
            after(in_ref, held, out_ref, here)
        for copy in copies:
            copy.wait()
        if scratch:
            after(in_ref, held, out_ref, here)

    near = pl.BlockSpec(memory_space=pltpu.VMEM)
    dma = pltpu.SemaphoreType.DMA
    return pl.pallas_call(
        kernel,
        out_shape=jax.ShapeDtypeStruct(*shape),
        in_specs=[near],
        out_specs=near,
        scratch_shapes=scratch + [dma((3,)), dma((3,))],
        compiler_params=pltpu.CompilerParams(collective_id=number, has_side_effects=True),
        name=name,
    )(array)


def gather_group(kv, number):
    def before(in_ref, held, here, there, k):
        return in_ref, held.at[here]

    def after(in_ref, held, out_ref, here):
        out_ref[here] = in_ref[...]

    return small_exchange("gather_group", number, kv, ((4, *kv.shape), BF), [], before, after)


def sum_group(dkv, number):
    def before(in_ref, held, here, there, k):
        return in_ref.at[there], held.at[k]

    def after(in_ref, held, out_ref, here):
        out = in_ref[here].astype(F32)
        for k in range(3):
            out = out + held[k].astype(F32)
        out_ref[...] = out

    held = [pltpu.VMEM((3, *dkv.shape[1:]), BF)]
    return small_exchange("sum_group", number, dkv, (dkv.shape[1:], F32), held, before, after)


PARTNERS = [(dy, dz, (dz + k) % 4) for k in range(4) for dy in range(2) for dz in range(4)]
GROUP = 8
GROUPS = len(PARTNERS) // GROUP


def facing(n):
    k, dy, dz = n // GROUP, n // 4 % 2, n % 4
    return -k % GROUPS * GROUP + dy * 4 + -dz % 4


def partners():
    s, yh, z, x = (lax.axis_index(a) for a in ("section", "yh", "z", "shard"))
    out = []
    for dy, dz, dx in PARTNERS:
        there = {
            "section": lax.rem(s + dy, 2),
            "yh": lax.rem(yh + dy, 2),
            "z": lax.rem(z + dz, 4),
            "shard": lax.rem(x + dx, 4),
        }
        out.append((there, (there["yh"] * 4 + there["z"]) * 4 + there["shard"]))
    return out


def exchange_rows(message, returned, arrived, produced, sems, work, after):
    sent, got, sent_back, got_back = sems
    near = partners()
    own = near[0][1]
    greet([device for device, _ in near[1:]])

    def remote(source, target, send, receive, device):
        return pltpu.make_async_remote_copy(
            src_ref=source,
            dst_ref=target,
            send_sem=send,
            recv_sem=receive,
            device_id=device,
            device_id_type=pl.DeviceIdType.MESH,
        )

    def out(n):
        device, expert = near[n]
        f = facing(n)
        return remote(message.at[expert], arrived.at[f], sent.at[n], got.at[f], device)

    def back(n):
        return remote(
            produced.at[n], returned.at[own], sent_back.at[n], got_back.at[facing(n)], near[n][0]
        )

    for k in range(GROUPS):
        for n in range(-k % GROUPS * GROUP, -k % GROUPS * GROUP + GROUP):
            if n:
                out(n).start()
    arrived[0] = message[own]
    for k in range(GROUPS):
        members = range(k * GROUP, (k + 1) * GROUP)
        for n in members:
            if n:
                remote(arrived.at[n], arrived.at[n], sent.at[n], got.at[n], near[n][0]).wait_recv()
        rows = arrived[k * GROUP : (k + 1) * GROUP]
        result = work(k, rows.reshape(GROUP * MAIN, rows.shape[2]))
        produced[k * GROUP : (k + 1) * GROUP] = result.reshape(rows.shape)
        for n in members:
            if n:
                back(n).start()
    returned[own] = produced[0]
    after()
    for n in range(1, len(near)):
        device, expert = near[n]
        out(n).wait_send()
        back(n).wait_send()
        view = returned.at[expert]
        remote(view, view, sent_back.at[n], got_back.at[n], device).wait_recv()


def exchange_call(name, number, body, inputs, shapes, message_shape, scratch):
    near = pl.BlockSpec(memory_space=pltpu.VMEM)
    dma = pltpu.SemaphoreType.DMA
    count = message_shape[0]
    return pl.pallas_call(
        body,
        out_shape=[jax.ShapeDtypeStruct(shape, kind) for shape, kind in shapes],
        in_specs=[near] * len(inputs),
        out_specs=[near] * len(shapes),
        scratch_shapes=[pltpu.VMEM(message_shape, BF), pltpu.VMEM(message_shape, BF)]
        + [dma((count,)) for _ in range(4)]
        + scratch,
        compiler_params=pltpu.CompilerParams(
            collective_id=number, has_side_effects=True, vmem_limit_bytes=56 << 20
        ),
        name=name,
    )(*inputs)


def expert_forward(message, experts, unfold, number):
    message = message.reshape(EXPERTS, MAIN, message.shape[1])
    rows = GROUP * (MAIN + EXTRA)
    depth, width = experts[0].shape

    def body(message_ref, gate_w, up_w, down_w, unfold_ref, *refs):
        returned, rows_ref, gate_ref, up_ref, hidden_ref = refs[:5]
        arrived, produced, *sems = refs[5:]

        def work(k, came):
            field = arrived_rows(came, unfold_ref[...])
            rows_ref[k] = field
            gate = dot(field, gate_w[...])
            up = dot(field, up_w[...])
            gate_ref[k] = gate
            up_ref[k] = up
            hidden = (gate / (1.0 + jnp.exp(-gate)) * up).astype(BF)
            hidden_ref[k] = hidden
            return fold_rows(dot(hidden, down_w[...]).astype(BF), unfold_ref[...], GROUP)

        exchange_rows(message_ref, returned, arrived, produced, sems, work, lambda: None)

    shapes = [
        (message.shape, BF),
        ((GROUPS, rows, depth), BF),
        ((GROUPS, rows, width), F32),
        ((GROUPS, rows, width), F32),
        ((GROUPS, rows, width), BF),
    ]
    returned, *kept = exchange_call(
        "expert_forward", number, body, [message, *experts, unfold], shapes, message.shape, []
    )
    return returned.reshape(-1, message.shape[2]), kept


def expert_backward(message, experts, kept, unfold, number):
    message = message.reshape(EXPERTS, MAIN, message.shape[1])
    rows = GROUP * (MAIN + EXTRA)
    depth, width = experts[0].shape

    def body(message_ref, gate_w, up_w, down_w, rows_ref, gate_ref, up_ref, hidden_ref, *refs):
        unfold_ref, returned, dgate_w, dup_w, ddown_w = refs[:5]
        arrived, produced = refs[5:7]
        sems, (came_ref, dgate_ref, dup_ref) = refs[7:11], refs[11:]

        def work(k, came):
            field = arrived_rows(came, unfold_ref[...])
            came_ref[k] = field
            dhidden = dot(field, down_w[...], NT)
            gate = gate_ref[k]
            logistic = 1.0 / (1.0 + jnp.exp(-gate))
            dgate = dhidden * up_ref[k] * (logistic * (1.0 + gate * (1.0 - logistic)))
            dgate_ref[k] = dgate.astype(BF)
            dup_ref[k] = (dhidden * (gate * logistic)).astype(BF)
            out = dot(dgate_ref[k], gate_w[...], NT) + dot(dup_ref[k], up_w[...], NT)
            return fold_rows(out.astype(BF), unfold_ref[...], GROUP)

        def after():
            field = rows_ref[...].reshape(GROUPS * rows, depth)
            step = 256
            for column in range(0, width, step):
                lanes = slice(column, column + step)
                for source, target in ((dgate_ref, dgate_w), (dup_ref, dup_w)):
                    part = source[:, :, lanes].reshape(GROUPS * rows, step)
                    target[:, lanes] = dot(field, part, TN).astype(BF)
            field = hidden_ref[...].reshape(GROUPS * rows, width)
            for column in range(0, depth, step):
                lanes = slice(column, column + step)
                part = came_ref[:, :, lanes].reshape(GROUPS * rows, step)
                ddown_w[:, lanes] = dot(field, part, TN).astype(BF)

        exchange_rows(message_ref, returned, arrived, produced, sems, work, after)

    shapes = [(message.shape, BF), ((depth, width), BF), ((depth, width), BF), ((width, depth), BF)]
    scratch = [
        pltpu.VMEM((GROUPS, rows, depth), BF),
        pltpu.VMEM((GROUPS, rows, width), BF),
        pltpu.VMEM((GROUPS, rows, width), BF),
    ]
    returned, *grads = exchange_call(
        "expert_backward",
        number,
        body,
        [message, *experts, *kept, unfold],
        shapes,
        message.shape,
        scratch,
    )
    return returned.reshape(-1, message.shape[2]), grads


def forward_layer(source, weights, experts, rank, unfold, tables, allowed, numbers):
    low, h_attn, query, kv = project(source, weights, tables)
    kv_all = gather_group(kv, numbers[0])
    x_mid, h_moe, attended, probs, gates, message = attend(low, query, kv_all, allowed, weights, rank)
    returned, kept = expert_forward(message, experts, unfold, numbers[1])
    stored = {
        "low": low,
        "h_attn": h_attn,
        "query": query,
        "kv_all": kv_all,
        "probs": probs,
        "attended": attended,
        "x_mid": x_mid,
        "h_moe": h_moe,
        "gates": gates,
        "returned": returned,
        "kept": kept,
    }
    return (x_mid, rank, gates, returned), stored


def backward_layer(grad, ready, stored, weights, experts, rank, unfold, tables, numbers):
    message, dlogits = grad_slots(grad, rank, stored["gates"], stored["returned"])
    returned, expert_grads = expert_backward(message, experts, stored["kept"], unfold, numbers[2])
    returned, *ready = lax.optimization_barrier((returned, *ready))
    half = sum_over_cores(expert_grads, numbers[0])
    returned, half = lax.optimization_barrier((returned, half))
    kv_all = stored["kv_all"]
    dmid, dbr, dquery, dkv, dgain_m = grad_attend(
        grad, returned, rank, dlogits, weights, stored["x_mid"], stored["query"], kv_all,
        stored["probs"], tables,
    )
    dkv = sum_group(dkv, numbers[1])
    dqkv, grad_in, dgain_a = grad_project(dquery, dkv, dmid, stored["low"], weights, tables)
    grads = weight_grads(
        stored["h_attn"], dqkv, stored["attended"], dbr, stored["h_moe"], dlogits, dgain_a, dgain_m
    )
    return grad_in, grads, half, ready


def per_device(
    tokens,
    routes,
    lengths,
    gain_attn,
    w_query,
    w_key,
    w_value,
    w_out,
    gain_moe,
    w_router,
    w_gate,
    w_up,
    w_down,
    cotangent,
):
    section, yh, z, core, shard = (
        lax.axis_index(a) for a in ("section", "yh", "z", "core", "shard")
    )
    first = section == 0
    tok_rows, model_width = tokens.shape[1:]
    group_rows = tok_rows * lax.axis_size("shard")

    def mine(a):
        return lax.dynamic_index_in_dim(a, section, 0, keepdims=False)

    def by_layer(own, other):
        return jnp.where(first, own, other), jnp.where(first, other, own)

    local = jnp.concatenate(
        [
            w_out[0],
            w_query[0],
            w_key[0],
            w_value[0],
            w_router[0],
            gain_attn[0][:, None],
            gain_moe[0][:, None],
            jnp.zeros((w_query.shape[1], 94), BF),
        ],
        axis=1,
    )
    full, late, *whole = gather_weights(local, (w_gate[0], w_up[0], w_down[0]))
    weights = [
        full.reshape(model_width, -1),
        lax.all_gather(at(late, yh, 0), DEVICES, axis=0, tiled=True),
    ]
    route_other = swap(at(routes[0], 1 - section, 0), "section")
    ranks = [rank_of(r) for r in by_layer(mine(routes[0]), route_other)]
    experts = [
        (
            whole[0][layer].reshape(model_width, 768),
            whole[1][layer].reshape(model_width, 768),
            whole[2][layer].reshape(768, model_width),
        )
        for layer in range(2)
    ]
    unfold = unfold_table(GROUP)

    segment, position = document_layout(mine(lengths[:, 0]), group_rows)
    row_start = shard * tok_rows
    own_segment = lax.dynamic_slice_in_dim(segment, row_start, tok_rows)
    tables = rotary_tables(lax.dynamic_slice_in_dim(position, row_start, tok_rows), HEAD_DIM)
    query_index = row_start + jnp.arange(tok_rows, dtype=jnp.int32)
    allowed = (own_segment[:, None] == segment[None, :]) & (
        query_index[:, None] >= jnp.arange(group_rows, dtype=jnp.int32)[None, :]
    )
    allowed = allowed.astype(F32)

    source, saved = (mine(tokens),), []
    for layer in range(2):
        source, stored = forward_layer(
            source, weights[layer], experts[layer], ranks[layer], unfold, tables, allowed,
            (7 + layer, 11 + layer),
        )
        saved.append(stored)
    low = fused("finish", finish_body, [((tok_rows, model_width), BF)], *source)[0]
    grad, low = lax.optimization_barrier((mine(cotangent), low))
    away = swap(low, "section")

    sums, ready = [None, None], (away,)
    for layer in (1, 0):
        grad, mixer_grad, half, ready = backward_layer(
            grad,
            ready,
            saved[layer],
            weights[layer],
            experts[layer],
            ranks[layer],
            unfold,
            tables,
            (5 + layer, 9 + layer, 13 + layer),
        )
        given = lax.ppermute(half, "section", [(1 - layer, layer)])
        sums[layer] = (half, given)
        if layer == 1:
            (away,), ready = ready, (given,)
            late = lax.psum_scatter(mixer_grad, DEVICES, scatter_dimension=0, tiled=True)
            late = lax.optimization_barrier(late)
    mixed = jnp.where(first, jnp.stack([low, away]), jnp.stack([away, low]))

    def finish_experts():
        return jnp.where(first, total(*sums[0]), total(sums[1][0], *ready)).astype(BF)

    mix, (grad_gate, grad_up, grad_down) = reduce_all(mixer_grad, late, finish_experts)
    return (
        mixed,
        grad[None],
        mix[:, 3616][None],
        mix[:, 1536:3072][None],
        mix[:, 3072:3328][None],
        mix[:, 3328:3584][None],
        mix[:, :1536][None],
        mix[:, 3617][None],
        mix[:, 3584:3616][None],
        grad_gate[None],
        grad_up[None],
        grad_down[None],
    )


def solution(mesh):
    fine = Mesh(mesh.devices.reshape(2, 2, 4, 2, 4), ("section", *DEVICES))
    expert = ("yh", "z", "core")
    return jax.shard_map(
        per_device,
        mesh=fine,
        in_specs=(
            P(None, DEVICES, None),
            P("section", None, DEVICES, None),
            P(None, expert, None),
            P("section", DEVICES),
            P("section", DEVICES, None),
            P("section", DEVICES, None),
            P("section", DEVICES, None),
            P("section", DEVICES, None),
            P("section", DEVICES),
            P("section", DEVICES, None),
            P("section", expert, "shard", None),
            P("section", expert, "shard", None),
            P("section", expert, None, "shard"),
            P(None, DEVICES, None),
        ),
        out_specs=(
            P(None, DEVICES, None),
            P("section", DEVICES, None),
            P("section", DEVICES),
            P("section", DEVICES, None),
            P("section", DEVICES, None),
            P("section", DEVICES, None),
            P("section", DEVICES, None),
            P("section", DEVICES),
            P("section", DEVICES, None),
            P("section", expert, "shard", None),
            P("section", expert, "shard", None),
            P("section", expert, None, "shard"),
        ),
        check_vma=False,
    )
```

```python
import jax
import jax.numpy as jnp
from jax import lax
from jax.experimental import pallas as pl
from jax.experimental.pallas import tpu as pltpu
from jax.sharding import Mesh
from jax.sharding import PartitionSpec as P

HEADS = 12
HEAD_DIM = 128
EXPERTS = 32
MAIN = 16
EXTRA = 2
CHUNKS = 6

epsilon = 1e-06
rope_base = 1000000.0
masked_score = -1e30

BF = jnp.bfloat16
F32 = jnp.float32
CHIPS = ("yh", "z", "shard")
DEVICES = ("yh", "z", "core", "shard")


def dot(a, b, dims=((1,), (0,))):
    return lax.dot_general(a, b, (dims, ((), ())), preferred_element_type=F32)


def document_layout(doc_lengths, group_rows):
    doc_ends = jnp.cumsum(doc_lengths)
    starts = doc_ends - doc_lengths
    row_index = jnp.arange(group_rows, dtype=jnp.int32)
    segment = jnp.sum((row_index[:, None] >= doc_ends[None, :]).astype(jnp.int32), axis=1)
    member = segment[:, None] == jnp.arange(doc_lengths.shape[0], dtype=jnp.int32)[None, :]
    position = row_index - jnp.sum(jnp.where(member, starts[None, :], 0), axis=1)
    return (segment, position)


def rotary_tables(position, head_size):
    half_dim = head_size // 2
    frequency = rope_base ** (-2.0 * jnp.arange(half_dim, dtype=F32) / head_size)
    angles = position.astype(F32)[:, None] * frequency[None, :]
    cosine, sine = jnp.cos(angles), jnp.sin(angles)
    return jnp.concatenate([cosine, cosine], axis=1), jnp.concatenate([-sine, sine], axis=1)


def swap(value, axis):
    return lax.ppermute(value, axis, [(0, 1), (1, 0)])


def around(axis, size):
    here = lax.axis_index(axis)
    return [lax.rem(here + step, size) for step in range(1, size)]


def move(name, number, arrays, shapes, peers, copies):
    count = len(arrays)
    total = 40

    def kernel(*refs):
        ins, outs = refs[:count], refs[count : count + len(shapes)]
        sent, got = refs[count + len(shapes) :]
        barrier = pltpu.get_barrier_semaphore()
        near = peers()
        for peer in near:
            pl.semaphore_signal(
                barrier, inc=1, device_id=peer, device_id_type=pl.DeviceIdType.MESH
            )
        pl.semaphore_wait(barrier, len(near))
        started = []
        for k, (source, target, device) in enumerate(copies(ins, outs)):
            if device is None:
                copy = pltpu.make_async_copy(source, target, got.at[k])
            else:
                copy = pltpu.make_async_remote_copy(
                    src_ref=source,
                    dst_ref=target,
                    send_sem=sent.at[k],
                    recv_sem=got.at[k],
                    device_id=device,
                    device_id_type=pl.DeviceIdType.MESH,
                )
            copy.start()
            started.append(copy)
        for copy in started:
            copy.wait()

    space = pl.BlockSpec(memory_space=pltpu.HBM)
    return pl.pallas_call(
        kernel,
        out_shape=[jax.ShapeDtypeStruct(s, BF) for s in shapes],
        in_specs=[space] * count,
        out_specs=[space] * len(shapes),
        scratch_shapes=[pltpu.SemaphoreType.DMA((total,)), pltpu.SemaphoreType.DMA((total,))],
        compiler_params=pltpu.CompilerParams(collective_id=number, has_side_effects=True),
        name=name,
    )(*arrays)


def total(*parts):
    out = parts[0].astype(F32)
    for part in parts[1:]:
        out = out + part.astype(F32)
    return out


def at(array, index, axis):
    return lax.dynamic_index_in_dim(array, index, axis, keepdims=False)


def other(axis):
    return lax.rem(lax.axis_index(axis) + 1, 2)


def sum_over_cores(grads, number):
    gate, up, down = grads
    halves = [gate.reshape(4, 2, 192, 768), up.reshape(4, 2, 192, 768), down.reshape(2, 384, 1536)]

    def copies(ins, outs):
        there = other("core")
        views = [ins[0].at[:, there], ins[1].at[:, there], ins[2].at[there]]
        return [(v, o, {"core": there}) for v, o in zip(views, outs)]

    shapes = [(4, 192, 768), (4, 192, 768), (384, 1536)]
    got = move("expert_cores", number, halves, shapes, lambda: [{"core": other("core")}], copies)
    core = lax.axis_index("core")
    gate, up, down = (
        total(at(h, core, 0 if k == 2 else 1), g).astype(BF)
        for k, (h, g) in enumerate(zip(halves, got))
    )
    down = down.reshape(2, 192, 4, 384).transpose(2, 1, 0, 3).reshape(4, 192, 768)
    return jnp.concatenate([gate, up, down], axis=1)


def reduce_all(grads, late, finish_experts):
    core, shard, z, yh, section = (
        lax.axis_index(a) for a in ("core", "shard", "z", "yh", "section")
    )
    width = grads.shape[1]
    mix = grads.reshape(8, 2, 4, 24, width)

    got = move(
        "cores",
        1,
        [mix],
        [(8, 4, 24, width)],
        lambda: [{"core": other("core")}],
        lambda ins, outs: [(ins[0].at[:, other("core")], outs[0], {"core": other("core")})],
    )[0]
    mix = total(at(mix, core, 1), got).astype(BF).reshape(2, 4, 4, 24, width)

    cut = 1792
    sizes = (cut, width - cut)

    def peers_2():
        return [{"shard": x} for x in around("shard", 4)] + [{"z": i} for i in around("z", 4)]

    def copies_2(ins, outs):
        out = []
        for step, (x, i) in enumerate(zip(around("shard", 4), around("z", 4))):
            out.append((ins[0].at[:, :, x, :, pl.ds(0, cut)], outs[0].at[step], {"shard": x}))
            out.append((ins[0].at[:, i, :, :, pl.ds(cut, width - cut)], outs[1].at[step], {"z": i}))
        return out

    shapes = [(3, 2, 4, 24, size) for size in sizes]
    got = move("first_axis", 2, [mix], shapes, peers_2, copies_2)
    own = [
        lax.dynamic_slice(mix, (0, 0, shard, 0, 0), (2, 4, 1, 24, cut))[:, :, 0],
        lax.dynamic_slice(mix, (0, z, 0, 0, cut), (2, 1, 4, 24, width - cut))[:, 0],
    ]
    mix = [total(m, *g).astype(BF) for m, g in zip(own, got)]

    def copies_3(ins, outs):
        out = []
        for step, (x, i) in enumerate(zip(around("shard", 4), around("z", 4))):
            out.append((ins[0].at[:, i], outs[0].at[step], {"z": i}))
            out.append((ins[1].at[:, x], outs[1].at[step], {"shard": x}))
        return out

    shapes = [(3, 2, 24, size) for size in sizes]
    got = move("other_axis", 3, mix, shapes, peers_2, copies_3)
    mix = jnp.concatenate(
        [
            total(at(mix[0], z, 1), *got[0]).astype(BF),
            total(at(mix[1], shard, 1), *got[1]).astype(BF),
        ],
        axis=-1,
    )
    exp = finish_experts()

    def places():
        here = 2 * lax.axis_index("yh") + lax.axis_index("section")
        there = [lax.rem(here + step, 4) for step in range(1, 4)]
        return [(t // 2, lax.rem(t, 2)) for t in there]

    def copies_4(ins, outs):
        there = other("core")
        out = [(ins[1].at[pl.ds(2 * there, 2)], outs[1], {"core": there})]
        for step, (y, s) in enumerate(places()):
            out.append((ins[0].at[s, y], outs[0].at[step], {"yh": y, "section": s}))
        return out

    mine = (jnp.arange(2) == yh)[:, None, None]
    pairs = jnp.stack([mix, jnp.where(mine, late[None], jnp.zeros((), BF))])
    got = move(
        "last_axis",
        4,
        [pairs, exp],
        [(3, 24, width), (2, 576, 768)],
        lambda: [{"yh": y, "section": s} for y, s in places()] + [{"core": other("core")}],
        copies_4,
    )
    sums = total(at(at(pairs, section, 0), yh, 0), *got[0])
    kept = lax.dynamic_slice_in_dim(exp, 2 * core, 2, 0)
    halves = jnp.where(core == 0, kept, got[1]), jnp.where(core == 0, got[1], kept)
    gate, up = (
        jnp.concatenate([h[:, k : k + 192] for h in halves], axis=1).astype(F32) for k in (0, 192)
    )
    down = [h[:, 384:, k : k + 384] for h in halves for k in (0, 384)]
    return sums, (gate, up, jnp.concatenate(down, axis=1).astype(F32))


def gather_weights(local, experts):
    rows, width = local.shape

    def kernel(*refs):
        mine, shards = refs[0], refs[1:4]
        full, late, whole = refs[4], refs[5], refs[6:9]
        stage = refs[9:12]
        sent, got, sent_x, got_e, sent_c, got_c, sent_y, sent_o, local_sem = refs[12:]
        s, yh, z, c, x = (lax.axis_index(a) for a in ("section", "yh", "z", "core", "shard"))
        place = 2 * yh + s
        ys = [lax.rem(place + k, 4) for k in (1, 2, 3)]
        ys = [{"yh": y // 2, "section": lax.rem(y, 2)} for y in ys]
        xs = [{"shard": lax.rem(x + k, 4)} for k in (1, 2, 3)]
        z_up, z_down = lax.rem(z + 1, 4), lax.rem(z + 3, 4)
        sibling, partner = {"core": 1 - c}, {"section": 1 - s}

        def piece(k, i, h):
            if k == 2:
                return shards[2].at[i, pl.ds(pl.multiple_of(h * 384, 128), 384)]
            return shards[k].at[i, pl.ds(pl.multiple_of(h * 192, 64), 192)]

        def landing(k, layer, source, half):
            if k == 2:
                return whole[2].at[layer, half, :, pl.ds(pl.multiple_of(source * 384, 128), 384)]
            return whole[k].at[layer, source, half]

        def remote(source, target, send, receive, device):
            return pltpu.make_async_remote_copy(
                src_ref=source,
                dst_ref=target,
                send_sem=send,
                recv_sem=receive,
                device_id=device,
                device_id_type=pl.DeviceIdType.MESH,
            )

        def start(copies):
            for copy in copies:
                copy.start()
            return copies

        def finish(copies):
            for copy in copies:
                copy.wait()

        has_own = x // 2 == c
        own = lax.rem(x, 2)
        staged = start(
            [pltpu.make_async_copy(piece(k, own, c), stage[k], local_sem.at[k]) for k in range(3)]
        )
        barrier = pltpu.get_barrier_semaphore()
        zs = [{"z": lax.rem(z + k, 4)} for k in (1, 2, 3)]
        x_up, x_down = xs[0]["shard"], xs[2]["shard"]
        near = ys + xs + zs + [sibling]
        near += [{"shard": lax.rem(x + k, 4), "core": 1 - c} for k in (1, 2, 3)]
        for peer in near:
            pl.semaphore_signal(
                barrier, inc=1, device_id=peer, device_id_type=pl.DeviceIdType.MESH
            )
        pl.semaphore_wait(barrier, len(near))

        here = full.at[yh, z, c, x]

        def along_y(target):
            out = [pltpu.make_async_copy(mine, target, local_sem.at[3])]
            for k, device in enumerate(ys):
                out.append(remote(mine, target, sent.at[k], got.at[k], device))
            return out

        @pl.when(s == 0)
        def _():
            start(along_y(here))

        @pl.when(s == 1)
        def _():
            start(along_y(late.at[yh, z, c, x]))

        finish(staged)

        @pl.when(has_own)
        def _():
            for k in range(3):
                remote(
                    piece(k, own, 1 - c),
                    landing(k, s, x, 1 - c),
                    sent_o.at[k],
                    got_e.at[s, x, k],
                    sibling,
                ).start()
                pltpu.make_async_copy(stage[k], landing(k, s, x, c), got_e.at[s, x, k]).start()

        def pass_on(layer, distance, to_partner):
            source = lax.rem(x + distance, 4)
            for k in range(3):
                view = landing(k, layer, source, c)
                receive = got_e.at[layer, source, k]
                remote(view, view, sent_o.at[k], receive, sibling).wait_recv()
                if to_partner:
                    remote(view, view, sent_y.at[distance, k], receive, partner).start()
                across = got_c.at[layer, source, k]
                remote(view, view, sent_c.at[layer, source, k], across, sibling).start()

        finish(along_y(here))
        view, view_late = full.at[:, z, c, x], late.at[:, z, c, x]
        along_x = start(
            [remote(view, view, sent.at[3 + k], got.at[3 + k], xs[k]) for k in range(3)]
        )
        late_z = start(
            [
                remote(view_late, view_late, sent.at[11 + k], got.at[11 + k], zs[k])
                for k in range(3)
            ]
        )
        pass_on(s, 0, True)
        finish(along_x)

        def ring(base, axis, places, up, down):
            return start(
                [
                    remote(up, up, sent.at[base], got.at[base], {axis: places[0]}),
                    remote(down, down, sent.at[base + 1], got.at[base + 1], {axis: places[1]}),
                ]
            )

        view = full.at[:, z, c]
        along_z = ring(6, "z", (z_up, z_down), view, view)
        for i in range(2):

            @pl.when(x != 2 * c + i)
            def _():
                for h in range(2):
                    for k in range(3):
                        remote(
                            piece(k, i, h),
                            landing(k, s, x, h),
                            sent_x.at[(i * 2 + h) * 3 + k],
                            got_e.at[s, x, k],
                            {"shard": 2 * c + i, "core": h},
                        ).start()

        finish(late_z)
        view = late.at[:, :, c, x]
        late_x = ring(14, "shard", (x_up, x_down), view, view)
        finish(along_z)
        along_z = ring(8, "z", (z_up, z_down), full.at[0, z_down, c], full.at[1, z_up, c])
        for distance in (1, 3, 2):
            pass_on(s, distance, True)
        finish(along_z)
        view = full.at[:, :, c]
        across = start([remote(view, view, sent.at[10], got.at[10], sibling)])
        finish(late_x)
        late_x = ring(
            16, "shard", (x_up, x_down), late.at[0, :, c, x_down], late.at[1, :, c, x_up]
        )
        for distance in (0, 1):
            pass_on(1 - s, distance, False)
        finish(late_x)
        view = late.at[:, :, c]
        across += start([remote(view, view, sent.at[18], got.at[18], sibling)])
        for distance in (3, 2):
            pass_on(1 - s, distance, False)

        finish(across)
        for i in range(2):

            @pl.when(x != 2 * c + i)
            def _():
                for h in range(2):
                    for k in range(3):
                        view = piece(k, i, h)
                        n = (i * 2 + h) * 3 + k
                        remote(view, view, sent_x.at[n], got_e.at[0, 0, k], sibling).wait_send()

        @pl.when(has_own)
        def _():
            for k in range(3):
                view = piece(k, own, 1 - c)
                remote(view, view, sent_o.at[k], got_e.at[0, 0, k], sibling).wait_send()

        for source in range(4):
            for k in range(3):
                view = landing(k, s, source, c)
                send = sent_y.at[source, k]
                remote(view, view, send, got_e.at[0, 0, k], partner).wait_send()
                for layer in range(2):
                    view = landing(k, layer, source, c)
                    arrived = landing(k, layer, source, 1 - c)
                    send, receive = sent_c.at[layer, source, k], got_c.at[layer, source, k]
                    remote(view, view, send, receive, sibling).wait_send()
                    remote(arrived, arrived, send, receive, sibling).wait_recv()

    space = pl.BlockSpec(memory_space=pltpu.HBM)
    near_space = pl.BlockSpec(memory_space=pltpu.VMEM)
    shapes = [(2, 4, 2, 4, rows, width)] * 2
    shapes += [(2, 4, 2, 192, 768), (2, 4, 2, 192, 768), (2, 2, 384, 1536)]
    dma = pltpu.SemaphoreType.DMA
    return pl.pallas_call(
        kernel,
        out_shape=[jax.ShapeDtypeStruct(shape, BF) for shape in shapes],
        in_specs=[near_space] + [space] * 3,
        out_specs=[space] * 5,
        scratch_shapes=[
            pltpu.VMEM((192, 768), BF),
            pltpu.VMEM((192, 768), BF),
            pltpu.VMEM((384, 384), BF),
            dma((19,)),
            dma((19,)),
            dma((12,)),
            dma((2, 4, 3)),
            dma((2, 4, 3)),
            dma((2, 4, 3)),
            dma((4, 3)),
            dma((3,)),
            dma((4,)),
        ],
        compiler_params=pltpu.CompilerParams(collective_id=0, has_side_effects=True),
        name="gather_weights",
    )(local, *experts)


def rank_of(route_rows):
    rows = route_rows.shape[0]
    chosen = route_rows.T[None, :, :] == jnp.arange(EXPERTS, dtype=jnp.int32)[:, None, None]
    hot = jnp.any(chosen, axis=1)
    index = jnp.arange(rows, dtype=jnp.int32)
    before = (index[:, None] < index[None, :]).astype(BF)
    return jnp.where(hot, dot(hot.astype(BF), before), -1.0)


def stacked(field):
    return jnp.concatenate(jnp.split(field, CHUNKS, axis=1), axis=0)


def unstacked(field):
    return jnp.concatenate(jnp.split(field, CHUNKS, axis=0), axis=1)


def unfold_table(sources):
    row = jnp.arange(CHUNKS * sources * EXTRA, dtype=jnp.int32)
    piece, source, extra = row // (sources * EXTRA), row // EXTRA % sources, row % EXTRA
    column = jnp.arange(sources * MAIN, dtype=jnp.int32)
    return (
        (source * MAIN + piece * EXTRA + extra)[:, None] == column[None, :]
    ).astype(BF)


def arrived_rows(message, unfold):
    width = message.shape[1] - 256
    extra = unstacked(dot(unfold, message[:, width:]).astype(BF))
    return jnp.concatenate([message[:, :width], extra], axis=0)


def fold_rows(rows, unfold, sources):
    main = rows[: sources * MAIN]
    extra = dot(unfold, stacked(rows[sources * MAIN :]), ((0,), (0,))).astype(BF)
    return jnp.concatenate([main, extra], axis=1)


def low_pair(value):
    high = value.astype(BF)
    return high, (value - high.astype(F32)).astype(BF)


OUT_COLUMNS, QKV_STEP = 1536, 512


def columns(width, place):
    return lambda rows: pl.BlockSpec((rows, width), lambda i: (0, place), memory_space=pltpu.VMEM)


OUT_BLOCK = [columns(OUT_COLUMNS, 0)]
QKV_BLOCKS = [columns(QKV_STEP, 3 + k) for k in range(4)]
NARROW_BLOCK = [columns(128, 28)]


def fused(name, body, shapes, *arrays):
    near = pl.BlockSpec(memory_space=pltpu.VMEM)
    specs, given = [], []
    for array in arrays:
        if isinstance(array, tuple):
            array, blocks = array
            specs += [block(array.shape[0]) for block in blocks]
            given += [array] * len(blocks)
        else:
            specs.append(near)
            given.append(array)
    return pl.pallas_call(
        body,
        grid=(1,),
        out_shape=[jax.ShapeDtypeStruct(shape, kind) for shape, kind in shapes],
        in_specs=specs,
        out_specs=[near] * len(shapes),
        compiler_params=pltpu.CompilerParams(vmem_limit_bytes=48 << 20),
        name=name,
    )(*given)


TN, NT = ((0,), (0,)), ((1,), (1,))


def slots(rank):
    count, rows = rank.shape
    place = lax.broadcasted_iota(jnp.int32, (count, MAIN, rows), 1)
    wide = jnp.broadcast_to(rank[:, None, :], (count, MAIN, rows))
    main = jnp.where(wide == place.astype(F32), 1.0, 0.0)
    extra = (MAIN + lax.rem(place, EXTRA)).astype(F32)
    extra = jnp.where((wide == extra) & (place < EXTRA * CHUNKS), 1.0, 0.0)
    return main, extra


def per_piece(table):
    piece = lax.rem(lax.broadcasted_iota(jnp.int32, table.shape, 0), MAIN) // EXTRA
    return [jnp.where(piece == j, table, 0.0) for j in range(CHUNKS)]


def flat(table):
    return table.reshape(table.shape[0] * table.shape[1], table.shape[2])


def send_table(main, extra, field):
    width = field.shape[1] // CHUNKS
    side = None
    for j, table in enumerate(per_piece(flat(extra))):
        part = dot(table.astype(BF), field[:, j * width : (j + 1) * width])
        side = part if side is None else side + part
    return dot(flat(main).astype(BF), field), side


def bring_back(main, extra, rows, exact):
    parts = low_pair if exact else (lambda t: (t.astype(BF),))
    model_width = rows.shape[1] - 256
    total_main = None
    for table in parts(main):
        part = dot(table, rows[:, :model_width], TN)
        total_main = part if total_main is None else total_main + part
    side = []
    for table in per_piece(extra):
        total_side = None
        for t in parts(table):
            part = dot(t, rows[:, model_width:], TN)
            total_side = part if total_side is None else total_side + part
        side.append(total_side)
    return total_main + jnp.concatenate(side, axis=1)


def gain_rows(narrow):
    row = lax.broadcasted_iota(jnp.int32, (8, narrow.shape[1]), 0)
    column = lax.broadcasted_iota(jnp.int32, (8, narrow.shape[1]), 1)
    pick = jnp.where(column == row + EXPERTS, 1.0, 0.0).astype(BF)
    rows = dot(pick, narrow, NT)
    return rows[0:1], rows[1:2]


def turn(field, cosine, sine):
    return field * cosine + pltpu.roll(field, HEAD_DIM // 2, 1) * sine


def turn_back(field, cosine, sine):
    return field * cosine - pltpu.roll(field, HEAD_DIM // 2, 1) * sine


def combined(x_mid, rank, gates, rows):
    main, extra = slots(rank)
    wide = jnp.broadcast_to(gates[:, None, :], main.shape)
    return x_mid + bring_back(flat(main * wide), flat(extra * wide), rows, True)


def project_body(combine):
    def body(*refs):
        if combine:
            mid_ref, rank_ref, gates_ref, rows_ref = refs[:4]
            refs = refs[4:]
            low = combined(mid_ref[...], rank_ref[...], gates_ref[...], rows_ref[...]).astype(BF)
        else:
            low = refs[0][...]
            refs = refs[1:]
        weights, refs = refs[:4], refs[4:]
        narrow, cos_ref, sin_ref, low_ref, h_ref, q_ref, kv_ref = refs
        field = low.astype(F32)
        low_ref[...] = low
        gain, _ = gain_rows(narrow[...])
        scale = lax.rsqrt(jnp.mean(field * field, axis=1, keepdims=True) + epsilon)
        h = (field * scale * gain).astype(BF)
        h_ref[...] = h
        cosine, sine = cos_ref[...], sin_ref[...]
        query_width = q_ref.shape[1]
        for at_column in range(0, 4 * QKV_STEP, 256):
            inside = at_column % QKV_STEP
            part = dot(h, weights[at_column // QKV_STEP][:, inside : inside + 256])
            if at_column < query_width + kv_ref.shape[1] // 2:
                part = jnp.concatenate(
                    [turn(part[:, k : k + HEAD_DIM], cosine, sine) for k in (0, HEAD_DIM)], axis=1
                )
            if at_column < query_width:
                q_ref[:, at_column : at_column + 256] = part.astype(BF)
            else:
                at_kv = at_column - query_width
                kv_ref[:, at_kv : at_kv + 256] = part.astype(BF)

    return body


def project(source, weights, tables):
    combine = len(source) > 1
    tok_rows, model_width = source[0].shape
    shapes = [((tok_rows, model_width), BF)] * 2
    shapes += [((tok_rows, HEADS * HEAD_DIM), BF)]
    shapes += [((tok_rows, 4 * QKV_STEP - HEADS * HEAD_DIM), BF)]
    return fused(
        "project_combined" if combine else "project",
        project_body(combine),
        shapes,
        *source,
        (weights, QKV_BLOCKS + NARROW_BLOCK),
        *tables,
    )


def finish_body(mid_ref, rank_ref, gates_ref, rows_ref, out_ref):
    out = combined(mid_ref[...], rank_ref[...], gates_ref[...], rows_ref[...])
    out_ref[...] = out.astype(BF)


def heads_of(kv_ref):
    kv_heads = kv_ref.shape[2] // 2 // HEAD_DIM
    parts = []
    for k in range(2 * kv_heads):
        part = kv_ref[:, :, k * HEAD_DIM : (k + 1) * HEAD_DIM]
        parts.append(part.reshape(part.shape[0] * part.shape[1], HEAD_DIM))
    return parts[:kv_heads], parts[kv_heads:]


def attend_body(
    low_ref, q_ref, kv_ref, allowed_ref, weight, narrow, rank_ref,
    mid_ref, h_ref, att_ref, probs_ref, gates_ref, out_ref,
):
    keys, values = heads_of(kv_ref)
    allowed = allowed_ref[...] > 0.0
    ratio = HEADS // len(keys)
    for head in range(HEADS):
        lanes = slice(head * HEAD_DIM, (head + 1) * HEAD_DIM)
        scores = dot(q_ref[:, lanes], keys[head // ratio], NT) * HEAD_DIM ** (-0.5)
        scores = jnp.where(allowed, scores, masked_score)
        exponent = jnp.exp(scores - jnp.max(scores, axis=1, keepdims=True))
        probs = exponent / jnp.sum(exponent, axis=1, keepdims=True)
        probs_ref[head] = probs
        att_ref[:, lanes] = dot(probs.astype(BF), values[head // ratio]).astype(BF)
    mid = low_ref[...].astype(F32) + dot(att_ref[...], weight[...])
    mid_ref[...] = mid
    _, gain = gain_rows(narrow[...])
    scale = lax.rsqrt(jnp.mean(mid * mid, axis=1, keepdims=True) + epsilon)
    h = (mid * scale * gain).astype(BF)
    h_ref[...] = h
    rank = rank_ref[...]
    logits = jnp.transpose(dot(h, narrow[...]))[:EXPERTS]
    logits = jnp.where(rank >= 0.0, logits, masked_score)
    gate_exp = jnp.exp(logits - jnp.max(logits, axis=0, keepdims=True))
    gate_exp = jnp.where(rank >= 0.0, gate_exp, 0.0)
    gates_ref[...] = gate_exp / jnp.sum(gate_exp, axis=0, keepdims=True)
    main, side = send_table(*slots(rank), h)
    width = main.shape[1]
    out_ref[:, :width] = main.astype(BF)
    out_ref[:, width:] = side.astype(BF)


def attend(low, q, kv, allowed, weights, rank):
    tok_rows, model_width = low.shape
    shapes = [
        ((tok_rows, model_width), F32),
        ((tok_rows, model_width), BF),
        ((tok_rows, HEADS * HEAD_DIM), BF),
        ((HEADS, tok_rows, allowed.shape[1]), F32),
        (rank.shape, F32),
        ((EXPERTS * MAIN, model_width + 256), BF),
    ]
    return fused(
        "attend", attend_body, shapes,
        low, q, kv, allowed, (weights, OUT_BLOCK + NARROW_BLOCK), rank,
    )


def grad_slots_body(grad_ref, rank_ref, gates_ref, rows_ref, out_ref, dlogits_ref):
    gates = gates_ref[...]
    main, extra = slots(rank_ref[...])
    wide = jnp.broadcast_to(gates[:, None, :], main.shape)
    grad_main, grad_side = send_table(main, extra, grad_ref[...])
    width = grad_main.shape[1]
    dgate = None
    for table, grad, columns in (
        (main, grad_main, slice(0, width)),
        (extra, grad_side, slice(width, width + 256)),
    ):
        slot_gate = jnp.sum(flat(table * wide), axis=1, keepdims=True)
        out_ref[:, columns] = (grad * slot_gate).astype(BF)
        slot_dgate = jnp.sum(grad * rows_ref[:, columns].astype(F32), axis=1, keepdims=True)
        part = jnp.sum((flat(table) * slot_dgate).reshape(table.shape), axis=1)
        dgate = part if dgate is None else dgate + part
    dlogits = gates * (dgate - jnp.sum(gates * dgate, axis=0, keepdims=True))
    pad = jnp.zeros((dlogits_ref.shape[1] - EXPERTS, dlogits.shape[1]), F32)
    dlogits_ref[...] = jnp.transpose(jnp.concatenate([dlogits, pad], axis=0)).astype(BF)


def grad_slots(grad, rank, gates, rows):
    shapes = [(rows.shape, BF), ((grad.shape[0], 128), BF)]
    return fused("grad_slots", grad_slots_body, shapes, grad, rank, gates, rows)


def norm_grads(field, gain, grad):
    scale = lax.rsqrt(jnp.mean(field * field, axis=1, keepdims=True) + epsilon)
    scaled = grad * gain
    centre = jnp.mean(scaled * field, axis=1, keepdims=True)
    dgain = jnp.sum(grad * field * scale, axis=0, keepdims=True)
    return scale * scaled - field * (scale * scale * scale) * centre, dgain


def grad_attend_body(
    grad_ref, rows_ref, rank_ref, dlogits_ref, weight, narrow, mid_ref, q_ref, kv_ref, probs_ref,
    cos_ref, sin_ref,
    dmid_ref, dbr_ref, dq_ref, dkv_ref, dgain_ref, datt_ref,
):
    main, extra = slots(rank_ref[...])
    dh = bring_back(flat(main), flat(extra), rows_ref[...], False)
    dh = dh + dot(dlogits_ref[...], narrow[...], NT)
    _, gain = gain_rows(narrow[...])
    dmid, dgain = norm_grads(mid_ref[...], gain, dh)
    dmid = dmid + grad_ref[...].astype(F32)
    dgain_ref[...] = dgain
    dmid_ref[...] = dmid
    dbr_ref[...] = dmid.astype(BF)
    datt_ref[...] = dot(dbr_ref[...], weight[...], NT).astype(BF)
    keys, values = heads_of(kv_ref)
    ratio = HEADS // len(keys)
    cosine, sine = cos_ref[...], sin_ref[...]
    count, tok_rows = kv_ref.shape[0], kv_ref.shape[1]
    scale = HEAD_DIM ** (-0.5)
    for k in range(len(keys)):
        dkey, dvalue = None, None
        for head in range(k * ratio, (k + 1) * ratio):
            lanes = slice(head * HEAD_DIM, (head + 1) * HEAD_DIM)
            probs, datt = probs_ref[head], datt_ref[:, lanes]
            dprobs = dot(datt, values[k], NT)
            centre = jnp.sum(dprobs * probs, axis=1, keepdims=True)
            dscores = (probs * (dprobs - centre)).astype(BF)
            part = dot(probs.astype(BF), datt, TN)
            dvalue = part if dvalue is None else dvalue + part
            part = dot(dscores, q_ref[:, lanes], TN)
            dkey = part if dkey is None else dkey + part
            dquery = dot(dscores, keys[k]) * scale
            dq_ref[:, lanes] = turn_back(dquery, cosine, sine).astype(BF)
        at_key, at_value = k * HEAD_DIM, (len(keys) + k) * HEAD_DIM
        shape = (count, tok_rows, HEAD_DIM)
        dkv_ref[:, :, at_key : at_key + HEAD_DIM] = (dkey * scale).astype(BF).reshape(shape)
        dkv_ref[:, :, at_value : at_value + HEAD_DIM] = dvalue.astype(BF).reshape(shape)


def grad_attend(grad, rows, rank, dlogits, weights, mid, q, kv, probs, tables):
    tok_rows, model_width = mid.shape
    shapes = [
        ((tok_rows, model_width), F32),
        ((tok_rows, model_width), BF),
        (q.shape, BF),
        (kv.shape, BF),
        ((1, model_width), F32),
        (q.shape, BF),
    ]
    return fused(
        "grad_attend", grad_attend_body, shapes,
        grad, rows, rank, dlogits, (weights, OUT_BLOCK + NARROW_BLOCK), mid, q, kv, probs, *tables,
    )[:5]


def grad_project_body(
    dq_ref, dkv_ref, dmid_ref, low_ref, weight_0, weight_1, weight_2, weight_3, narrow, cos_ref,
    sin_ref,
    dqkv_ref, grad_ref, dgain_ref,
):
    query_width, kv_width = dq_ref.shape[1], dkv_ref.shape[1] // 2
    cosine, sine = cos_ref[...], sin_ref[...]
    dqkv_ref[:, :query_width] = dq_ref[...]
    for k in range(0, kv_width, HEAD_DIM):
        part = turn_back(dkv_ref[:, k : k + HEAD_DIM], cosine, sine)
        dqkv_ref[:, query_width + k : query_width + k + HEAD_DIM] = part.astype(BF)
    dqkv_ref[:, query_width + kv_width :] = dkv_ref[:, kv_width:].astype(BF)
    dh = None
    for k, weight in enumerate((weight_0, weight_1, weight_2, weight_3)):
        part = dot(dqkv_ref[:, k * QKV_STEP : (k + 1) * QKV_STEP], weight[...], NT)
        dh = part if dh is None else dh + part
    gain, _ = gain_rows(narrow[...])
    dlow, dgain = norm_grads(low_ref[...].astype(F32), gain, dh)
    dgain_ref[...] = dgain
    grad_ref[...] = (dlow + dmid_ref[...]).astype(BF)


def grad_project(dq, dkv, dmid, low, weights, tables):
    tok_rows, model_width = low.shape
    shapes = [
        ((tok_rows, 4 * QKV_STEP), BF),
        ((tok_rows, model_width), BF),
        ((1, model_width), F32),
    ]
    return fused(
        "grad_project", grad_project_body, shapes,
        dq, dkv, dmid, low, (weights, QKV_BLOCKS + NARROW_BLOCK), *tables,
    )


def weight_grads_body(
    h_ref, dqkv_ref, att_ref, dbr_ref, h2_ref, dlogits_ref, dgain_a_ref, dgain_m_ref, out_ref
):
    step = 512
    place = 0
    for left, right in ((att_ref, dbr_ref), (h_ref, dqkv_ref)):
        for k in range(0, right.shape[1], step):
            part = dot(left[...], right[:, k : k + step], TN)
            out_ref[:, place : place + step] = part.astype(BF)
            place += step
    narrow = dot(h2_ref[...], dlogits_ref[...], TN)
    rows = jnp.concatenate(
        [dgain_a_ref[...], dgain_m_ref[...], jnp.zeros((126, h_ref.shape[1]), F32)], axis=0
    )
    columns = pltpu.roll(jnp.transpose(rows), EXPERTS, 1)
    out_ref[:, place:] = (narrow + columns).astype(BF)


def weight_grads(h, dqkv, att, dbr, h2, dlogits, dgain_a, dgain_m):
    columns = dqkv.shape[1] + dbr.shape[1] + 128
    return fused(
        "weight_grads", weight_grads_body, [((h.shape[1], columns), BF)],
        h, dqkv, att, dbr, h2, dlogits, dgain_a, dgain_m,
    )[0]


def greet(peers):
    barrier = pltpu.get_barrier_semaphore()
    for peer in peers:
        pl.semaphore_signal(barrier, inc=1, device_id=peer, device_id_type=pl.DeviceIdType.MESH)
    pl.semaphore_wait(barrier, len(peers))


def small_exchange(name, number, array, shape, scratch, before, after):
    def kernel(in_ref, out_ref, *rest):
        here = lax.axis_index("shard")
        held = rest[0] if scratch else out_ref
        sent, got = rest[-2:]
        peers = [{"shard": x} for x in around("shard", 4)]
        greet(peers)
        copies = []
        for k, peer in enumerate(peers):
            source, target = before(in_ref, held, here, peer["shard"], k)
            copies.append(
                pltpu.make_async_remote_copy(
                    src_ref=source,
                    dst_ref=target,
                    send_sem=sent.at[k],
                    recv_sem=got.at[k],
                    device_id=peer,
                    device_id_type=pl.DeviceIdType.MESH,
                )
            )
            copies[-1].start()
        if not scratch:
            after(in_ref, held, out_ref, here)
        for copy in copies:
            copy.wait()
        if scratch:
            after(in_ref, held, out_ref, here)

    near = pl.BlockSpec(memory_space=pltpu.VMEM)
    dma = pltpu.SemaphoreType.DMA
    return pl.pallas_call(
        kernel,
        out_shape=jax.ShapeDtypeStruct(*shape),
        in_specs=[near],
        out_specs=near,
        scratch_shapes=scratch + [dma((3,)), dma((3,))],
        compiler_params=pltpu.CompilerParams(collective_id=number, has_side_effects=True),
        name=name,
    )(array)


def gather_group(kv, number):
    def before(in_ref, held, here, there, k):
        return in_ref, held.at[here]

    def after(in_ref, held, out_ref, here):
        out_ref[here] = in_ref[...]

    return small_exchange("gather_group", number, kv, ((4, *kv.shape), BF), [], before, after)


def sum_group(dkv, number):
    def before(in_ref, held, here, there, k):
        return in_ref.at[there], held.at[k]

    def after(in_ref, held, out_ref, here):
        out = in_ref[here].astype(F32)
        for k in range(3):
            out = out + held[k].astype(F32)
        out_ref[...] = out

    held = [pltpu.VMEM((3, *dkv.shape[1:]), BF)]
    return small_exchange("sum_group", number, dkv, (dkv.shape[1:], F32), held, before, after)


PARTNERS = [(dy, dz, (dz + k) % 4) for k in range(4) for dy in range(2) for dz in range(4)]
GROUP = 8
GROUPS = len(PARTNERS) // GROUP


def facing(n):
    k, dy, dz = n // GROUP, n // 4 % 2, n % 4
    return -k % GROUPS * GROUP + dy * 4 + -dz % 4


def partners():
    s, yh, z, x = (lax.axis_index(a) for a in ("section", "yh", "z", "shard"))
    out = []
    for dy, dz, dx in PARTNERS:
        there = {
            "section": lax.rem(s + dy, 2),
            "yh": lax.rem(yh + dy, 2),
            "z": lax.rem(z + dz, 4),
            "shard": lax.rem(x + dx, 4),
        }
        out.append((there, (there["yh"] * 4 + there["z"]) * 4 + there["shard"]))
    return out


def exchange_rows(message, returned, arrived, produced, sems, work, after):
    sent, got, sent_back, got_back = sems
    near = partners()
    own = near[0][1]
    greet([device for device, _ in near[1:]])

    def remote(source, target, send, receive, device):
        return pltpu.make_async_remote_copy(
            src_ref=source,
            dst_ref=target,
            send_sem=send,
            recv_sem=receive,
            device_id=device,
            device_id_type=pl.DeviceIdType.MESH,
        )

    def out(n):
        device, expert = near[n]
        f = facing(n)
        return remote(message.at[expert], arrived.at[f], sent.at[n], got.at[f], device)

    def back(n):
        return remote(
            produced.at[n], returned.at[own], sent_back.at[n], got_back.at[facing(n)], near[n][0]
        )

    for k in range(GROUPS):
        for n in range(-k % GROUPS * GROUP, -k % GROUPS * GROUP + GROUP):
            if n:
                out(n).start()
    arrived[0] = message[own]
    for k in range(GROUPS):
        members = range(k * GROUP, (k + 1) * GROUP)
        for n in members:
            if n:
                remote(arrived.at[n], arrived.at[n], sent.at[n], got.at[n], near[n][0]).wait_recv()
        rows = arrived[k * GROUP : (k + 1) * GROUP]
        result = work(k, rows.reshape(GROUP * MAIN, rows.shape[2]))
        produced[k * GROUP : (k + 1) * GROUP] = result.reshape(rows.shape)
        for n in members:
            if n:
                back(n).start()
    returned[own] = produced[0]
    after()
    for n in range(1, len(near)):
        device, expert = near[n]
        out(n).wait_send()
        back(n).wait_send()
        view = returned.at[expert]
        remote(view, view, sent_back.at[n], got_back.at[n], device).wait_recv()


def exchange_call(name, number, body, inputs, shapes, message_shape, scratch):
    near = pl.BlockSpec(memory_space=pltpu.VMEM)
    dma = pltpu.SemaphoreType.DMA
    count = message_shape[0]
    return pl.pallas_call(
        body,
        out_shape=[jax.ShapeDtypeStruct(shape, kind) for shape, kind in shapes],
        in_specs=[near] * len(inputs),
        out_specs=[near] * len(shapes),
        scratch_shapes=[pltpu.VMEM(message_shape, BF), pltpu.VMEM(message_shape, BF)]
        + [dma((count,)) for _ in range(4)]
        + scratch,
        compiler_params=pltpu.CompilerParams(
            collective_id=number, has_side_effects=True, vmem_limit_bytes=56 << 20
        ),
        name=name,
    )(*inputs)


def expert_forward(message, experts, unfold, number):
    message = message.reshape(EXPERTS, MAIN, message.shape[1])
    rows = GROUP * (MAIN + EXTRA)
    depth, width = experts[0].shape

    def body(message_ref, gate_w, up_w, down_w, unfold_ref, *refs):
        returned, rows_ref, gate_ref, up_ref, hidden_ref = refs[:5]
        arrived, produced, *sems = refs[5:]

        def work(k, came):
            field = arrived_rows(came, unfold_ref[...])
            rows_ref[k] = field
            gate = dot(field, gate_w[...])
            up = dot(field, up_w[...])
            gate_ref[k] = gate
            up_ref[k] = up
            hidden = (gate / (1.0 + jnp.exp(-gate)) * up).astype(BF)
            hidden_ref[k] = hidden
            return fold_rows(dot(hidden, down_w[...]).astype(BF), unfold_ref[...], GROUP)

        exchange_rows(message_ref, returned, arrived, produced, sems, work, lambda: None)

    shapes = [
        (message.shape, BF),
        ((GROUPS, rows, depth), BF),
        ((GROUPS, rows, width), F32),
        ((GROUPS, rows, width), F32),
        ((GROUPS, rows, width), BF),
    ]
    returned, *kept = exchange_call(
        "expert_forward", number, body, [message, *experts, unfold], shapes, message.shape, []
    )
    return returned.reshape(-1, message.shape[2]), kept


def expert_backward(message, experts, kept, unfold, number):
    message = message.reshape(EXPERTS, MAIN, message.shape[1])
    rows = GROUP * (MAIN + EXTRA)
    depth, width = experts[0].shape

    def body(message_ref, gate_w, up_w, down_w, rows_ref, gate_ref, up_ref, hidden_ref, *refs):
        unfold_ref, returned, dgate_w, dup_w, ddown_w = refs[:5]
        arrived, produced = refs[5:7]
        sems, (came_ref, dgate_ref, dup_ref) = refs[7:11], refs[11:]

        def work(k, came):
            field = arrived_rows(came, unfold_ref[...])
            came_ref[k] = field
            dhidden = dot(field, down_w[...], NT)
            gate = gate_ref[k]
            logistic = 1.0 / (1.0 + jnp.exp(-gate))
            dgate = dhidden * up_ref[k] * (logistic * (1.0 + gate * (1.0 - logistic)))
            dgate_ref[k] = dgate.astype(BF)
            dup_ref[k] = (dhidden * (gate * logistic)).astype(BF)
            out = dot(dgate_ref[k], gate_w[...], NT) + dot(dup_ref[k], up_w[...], NT)
            return fold_rows(out.astype(BF), unfold_ref[...], GROUP)

        def after():
            field = rows_ref[...].reshape(GROUPS * rows, depth)
            step = 256
            for column in range(0, width, step):
                lanes = slice(column, column + step)
                for source, target in ((dgate_ref, dgate_w), (dup_ref, dup_w)):
                    part = source[:, :, lanes].reshape(GROUPS * rows, step)
                    target[:, lanes] = dot(field, part, TN).astype(BF)
            field = hidden_ref[...].reshape(GROUPS * rows, width)
            for column in range(0, depth, step):
                lanes = slice(column, column + step)
                part = came_ref[:, :, lanes].reshape(GROUPS * rows, step)
                ddown_w[:, lanes] = dot(field, part, TN).astype(BF)

        exchange_rows(message_ref, returned, arrived, produced, sems, work, after)

    shapes = [(message.shape, BF), ((depth, width), BF), ((depth, width), BF), ((width, depth), BF)]
    scratch = [
        pltpu.VMEM((GROUPS, rows, depth), BF),
        pltpu.VMEM((GROUPS, rows, width), BF),
        pltpu.VMEM((GROUPS, rows, width), BF),
    ]
    returned, *grads = exchange_call(
        "expert_backward",
        number,
        body,
        [message, *experts, *kept, unfold],
        shapes,
        message.shape,
        scratch,
    )
    return returned.reshape(-1, message.shape[2]), grads


def forward_layer(source, weights, experts, rank, unfold, tables, allowed, numbers):
    low, h_attn, query, kv = project(source, weights, tables)
    kv_all = gather_group(kv, numbers[0])
    x_mid, h_moe, attended, probs, gates, message = attend(low, query, kv_all, allowed, weights, rank)
    returned, kept = expert_forward(message, experts, unfold, numbers[1])
    stored = {
        "low": low,
        "h_attn": h_attn,
        "query": query,
        "kv_all": kv_all,
        "probs": probs,
        "attended": attended,
        "x_mid": x_mid,
        "h_moe": h_moe,
        "gates": gates,
        "returned": returned,
        "kept": kept,
    }
    return (x_mid, rank, gates, returned), stored


def backward_layer(grad, ready, stored, weights, experts, rank, unfold, tables, numbers):
    message, dlogits = grad_slots(grad, rank, stored["gates"], stored["returned"])
    returned, expert_grads = expert_backward(message, experts, stored["kept"], unfold, numbers[2])
    half = sum_over_cores(expert_grads, numbers[0])
    returned, half = lax.optimization_barrier((returned, half))
    kv_all = stored["kv_all"]
    dmid, dbr, dquery, dkv, dgain_m = grad_attend(
        grad, returned, rank, dlogits, weights, stored["x_mid"], stored["query"], kv_all,
        stored["probs"], tables,
    )
    dkv, *ready = lax.optimization_barrier((dkv, *ready))
    dkv = sum_group(dkv, numbers[1])
    dqkv, grad_in, dgain_a = grad_project(dquery, dkv, dmid, stored["low"], weights, tables)
    grads = weight_grads(
        stored["h_attn"], dqkv, stored["attended"], dbr, stored["h_moe"], dlogits, dgain_a, dgain_m
    )
    return grad_in, grads, half, ready


def per_device(
    tokens,
    routes,
    lengths,
    gain_attn,
    w_query,
    w_key,
    w_value,
    w_out,
    gain_moe,
    w_router,
    w_gate,
    w_up,
    w_down,
    cotangent,
):
    section, yh, z, core, shard = (
        lax.axis_index(a) for a in ("section", "yh", "z", "core", "shard")
    )
    first = section == 0
    tok_rows, model_width = tokens.shape[1:]
    group_rows = tok_rows * lax.axis_size("shard")

    def mine(a):
        return lax.dynamic_index_in_dim(a, section, 0, keepdims=False)

    def by_layer(own, other):
        return jnp.where(first, own, other), jnp.where(first, other, own)

    local = jnp.concatenate(
        [
            w_out[0],
            w_query[0],
            w_key[0],
            w_value[0],
            w_router[0],
            gain_attn[0][:, None],
            gain_moe[0][:, None],
            jnp.zeros((w_query.shape[1], 94), BF),
        ],
        axis=1,
    )
    full, late, *whole = gather_weights(local, (w_gate[0], w_up[0], w_down[0]))
    weights = [full.reshape(model_width, -1), late.reshape(model_width, -1)]
    route_other = swap(at(routes[0], 1 - section, 0), "section")
    ranks = [rank_of(r) for r in by_layer(mine(routes[0]), route_other)]
    experts = [
        (
            whole[0][layer].reshape(model_width, 768),
            whole[1][layer].reshape(model_width, 768),
            whole[2][layer].reshape(768, model_width),
        )
        for layer in range(2)
    ]
    unfold = unfold_table(GROUP)

    segment, position = document_layout(mine(lengths[:, 0]), group_rows)
    row_start = shard * tok_rows
    own_segment = lax.dynamic_slice_in_dim(segment, row_start, tok_rows)
    tables = rotary_tables(lax.dynamic_slice_in_dim(position, row_start, tok_rows), HEAD_DIM)
    query_index = row_start + jnp.arange(tok_rows, dtype=jnp.int32)
    allowed = (own_segment[:, None] == segment[None, :]) & (
        query_index[:, None] >= jnp.arange(group_rows, dtype=jnp.int32)[None, :]
    )
    allowed = allowed.astype(F32)

    source, saved = (mine(tokens),), []
    for layer in range(2):
        source, stored = forward_layer(
            source, weights[layer], experts[layer], ranks[layer], unfold, tables, allowed,
            (7 + layer, 11 + layer),
        )
        saved.append(stored)
    low = fused("finish", finish_body, [((tok_rows, model_width), BF)], *source)[0]
    grad, low = lax.optimization_barrier((mine(cotangent), low))
    away = swap(low, "section")

    sums, ready = [None, None], (away,)
    for layer in (1, 0):
        grad, mixer_grad, half, ready = backward_layer(
            grad,
            ready,
            saved[layer],
            weights[layer],
            experts[layer],
            ranks[layer],
            unfold,
            tables,
            (5 + layer, 9 + layer, 13 + layer),
        )
        half = lax.all_to_all(half, "shard", split_axis=0, concat_axis=0, tiled=True)
        given = lax.ppermute(half, "section", [(1 - layer, layer)])
        sums[layer] = (half, given)
        if layer == 1:
            (away,), ready = ready, (given,)
            late = lax.psum_scatter(mixer_grad, DEVICES, scatter_dimension=0, tiled=True)
            late = lax.optimization_barrier(late)
    mixed = jnp.where(first, jnp.stack([low, away]), jnp.stack([away, low]))

    def finish_experts():
        return jnp.where(first, total(*sums[0]), total(sums[1][0], *ready)).astype(BF)

    mix, (grad_gate, grad_up, grad_down) = reduce_all(mixer_grad, late, finish_experts)
    return (
        mixed,
        grad[None],
        mix[:, 3616][None],
        mix[:, 1536:3072][None],
        mix[:, 3072:3328][None],
        mix[:, 3328:3584][None],
        mix[:, :1536][None],
        mix[:, 3617][None],
        mix[:, 3584:3616][None],
        grad_gate[None],
        grad_up[None],
        grad_down[None],
    )


def solution(mesh):
    fine = Mesh(mesh.devices.reshape(2, 2, 4, 2, 4), ("section", *DEVICES))
    expert = ("yh", "z", "core")
    return jax.shard_map(
        per_device,
        mesh=fine,
        in_specs=(
            P(None, DEVICES, None),
            P("section", None, DEVICES, None),
            P(None, expert, None),
            P("section", DEVICES),
            P("section", DEVICES, None),
            P("section", DEVICES, None),
            P("section", DEVICES, None),
            P("section", DEVICES, None),
            P("section", DEVICES),
            P("section", DEVICES, None),
            P("section", expert, "shard", None),
            P("section", expert, "shard", None),
            P("section", expert, None, "shard"),
            P(None, DEVICES, None),
        ),
        out_specs=(
            P(None, DEVICES, None),
            P("section", DEVICES, None),
            P("section", DEVICES),
            P("section", DEVICES, None),
            P("section", DEVICES, None),
            P("section", DEVICES, None),
            P("section", DEVICES, None),
            P("section", DEVICES),
            P("section", DEVICES, None),
            P("section", expert, "shard", None),
            P("section", expert, "shard", None),
            P("section", expert, None, "shard"),
        ),
        check_vma=False,
    )
```

```python
import jax
import jax.numpy as jnp
from jax import lax
from jax.experimental import pallas as pl
from jax.experimental.pallas import tpu as pltpu
from jax.sharding import Mesh
from jax.sharding import PartitionSpec as P

HEADS = 12
HEAD_DIM = 128
EXPERTS = 32
MAIN = 16
EXTRA = 2
CHUNKS = 6

epsilon = 1e-06
rope_base = 1000000.0
masked_score = -1e30

BF = jnp.bfloat16
F32 = jnp.float32
CHIPS = ("yh", "z", "shard")
DEVICES = ("yh", "z", "core", "shard")


def dot(a, b, dims=((1,), (0,))):
    return lax.dot_general(a, b, (dims, ((), ())), preferred_element_type=F32)


def document_layout(doc_lengths, group_rows):
    doc_ends = jnp.cumsum(doc_lengths)
    starts = doc_ends - doc_lengths
    row_index = jnp.arange(group_rows, dtype=jnp.int32)
    segment = jnp.sum((row_index[:, None] >= doc_ends[None, :]).astype(jnp.int32), axis=1)
    member = segment[:, None] == jnp.arange(doc_lengths.shape[0], dtype=jnp.int32)[None, :]
    position = row_index - jnp.sum(jnp.where(member, starts[None, :], 0), axis=1)
    return (segment, position)


def rotary_tables(position, head_size):
    half_dim = head_size // 2
    frequency = rope_base ** (-2.0 * jnp.arange(half_dim, dtype=F32) / head_size)
    angles = position.astype(F32)[:, None] * frequency[None, :]
    cosine, sine = jnp.cos(angles), jnp.sin(angles)
    return jnp.concatenate([cosine, cosine], axis=1), jnp.concatenate([-sine, sine], axis=1)


def swap(value, axis):
    return lax.ppermute(value, axis, [(0, 1), (1, 0)])


def around(axis, size):
    here = lax.axis_index(axis)
    return [lax.rem(here + step, size) for step in range(1, size)]


def move(name, number, arrays, shapes, peers, copies):
    count = len(arrays)
    total = 40

    def kernel(*refs):
        ins, outs = refs[:count], refs[count : count + len(shapes)]
        sent, got = refs[count + len(shapes) :]
        barrier = pltpu.get_barrier_semaphore()
        near = peers()
        for peer in near:
            pl.semaphore_signal(
                barrier, inc=1, device_id=peer, device_id_type=pl.DeviceIdType.MESH
            )
        pl.semaphore_wait(barrier, len(near))
        started = []
        for k, (source, target, device) in enumerate(copies(ins, outs)):
            if device is None:
                copy = pltpu.make_async_copy(source, target, got.at[k])
            else:
                copy = pltpu.make_async_remote_copy(
                    src_ref=source,
                    dst_ref=target,
                    send_sem=sent.at[k],
                    recv_sem=got.at[k],
                    device_id=device,
                    device_id_type=pl.DeviceIdType.MESH,
                )
            copy.start()
            started.append(copy)
        for copy in started:
            copy.wait()

    space = pl.BlockSpec(memory_space=pltpu.HBM)
    return pl.pallas_call(
        kernel,
        out_shape=[jax.ShapeDtypeStruct(s, BF) for s in shapes],
        in_specs=[space] * count,
        out_specs=[space] * len(shapes),
        scratch_shapes=[pltpu.SemaphoreType.DMA((total,)), pltpu.SemaphoreType.DMA((total,))],
        compiler_params=pltpu.CompilerParams(collective_id=number, has_side_effects=True),
        name=name,
    )(*arrays)


def total(*parts):
    out = parts[0].astype(F32)
    for part in parts[1:]:
        out = out + part.astype(F32)
    return out


def at(array, index, axis):
    return lax.dynamic_index_in_dim(array, index, axis, keepdims=False)


def other(axis):
    return lax.rem(lax.axis_index(axis) + 1, 2)


def reduce_all(grads, late, finish_experts):
    core, shard, z, yh, section = (
        lax.axis_index(a) for a in ("core", "shard", "z", "yh", "section")
    )
    width = grads.shape[1]
    mix = grads.reshape(8, 2, 4, 24, width)

    got = move(
        "cores",
        1,
        [mix],
        [(8, 4, 24, width)],
        lambda: [{"core": other("core")}],
        lambda ins, outs: [(ins[0].at[:, other("core")], outs[0], {"core": other("core")})],
    )[0]
    mix = total(at(mix, core, 1), got).astype(BF).reshape(2, 4, 4, 24, width)

    cut = 1792
    sizes = (cut, width - cut)

    def peers_2():
        return [{"shard": x} for x in around("shard", 4)] + [{"z": i} for i in around("z", 4)]

    def copies_2(ins, outs):
        out = []
        for step, (x, i) in enumerate(zip(around("shard", 4), around("z", 4))):
            out.append((ins[0].at[:, :, x, :, pl.ds(0, cut)], outs[0].at[step], {"shard": x}))
            out.append((ins[0].at[:, i, :, :, pl.ds(cut, width - cut)], outs[1].at[step], {"z": i}))
        return out

    shapes = [(3, 2, 4, 24, size) for size in sizes]
    got = move("first_axis", 2, [mix], shapes, peers_2, copies_2)
    own = [
        lax.dynamic_slice(mix, (0, 0, shard, 0, 0), (2, 4, 1, 24, cut))[:, :, 0],
        lax.dynamic_slice(mix, (0, z, 0, 0, cut), (2, 1, 4, 24, width - cut))[:, 0],
    ]
    mix = [total(m, *g).astype(BF) for m, g in zip(own, got)]

    exp = finish_experts()

    def shards_of(ref, x):
        down = ref.at[
            pl.ds(pl.multiple_of(1536 + x // 2 * 384, 128), 384),
            pl.ds(pl.multiple_of(lax.rem(x, 2) * 384, 128), 384),
        ]
        gate = ref.at[pl.ds(pl.multiple_of(x * 192, 64), 192)]
        up = ref.at[pl.ds(pl.multiple_of(768 + x * 192, 64), 192)]
        return gate, up, down

    def copies_3(ins, outs):
        here = lax.axis_index("shard")
        out = []
        for step, (x, i) in enumerate(zip(around("shard", 4), around("z", 4))):
            out.append((ins[0].at[:, i], outs[0].at[step], {"z": i}))
            out.append((ins[1].at[:, x], outs[1].at[step], {"shard": x}))
            for k, source in enumerate(shards_of(ins[2], x)):
                out.append((source, outs[2 + k].at[here], {"shard": x}))
        return out

    shapes = [(3, 2, 24, size) for size in sizes] + [(4, 192, 768), (4, 192, 768), (4, 384, 384)]
    got = move("other_axis", 3, [*mix, exp], shapes, peers_2, copies_3)
    mix = jnp.concatenate(
        [
            total(at(mix[0], z, 1), *got[0]).astype(BF),
            total(at(mix[1], shard, 1), *got[1]).astype(BF),
        ],
        axis=-1,
    )
    rows = [
        lax.dynamic_slice(exp, (shard * 192, 0), (192, 768)),
        lax.dynamic_slice(exp, (768 + shard * 192, 0), (192, 768)),
        lax.dynamic_slice(exp, (1536 + shard // 2 * 384, shard % 2 * 384), (384, 384)),
    ]
    exp = [lax.dynamic_update_index_in_dim(g, o, shard, 0) for g, o in zip(got[2:], rows)]

    def places():
        here = 2 * lax.axis_index("yh") + lax.axis_index("section")
        there = [lax.rem(here + step, 4) for step in range(1, 4)]
        return [(t // 2, lax.rem(t, 2)) for t in there]

    def copies_4(ins, outs):
        there = other("core")
        out = [
            (ins[1 + k].at[pl.ds(2 * there, 2)], outs[1 + k], {"core": there}) for k in range(3)
        ]
        for step, (y, s) in enumerate(places()):
            out.append((ins[0].at[s, y], outs[0].at[step], {"yh": y, "section": s}))
        return out

    mine = (jnp.arange(2) == yh)[:, None, None]
    pairs = jnp.stack([mix, jnp.where(mine, late[None], jnp.zeros((), BF))])
    got = move(
        "last_axis",
        4,
        [pairs, *exp],
        [(3, 24, width), (2, 192, 768), (2, 192, 768), (2, 384, 384)],
        lambda: [{"yh": y, "section": s} for y, s in places()] + [{"core": other("core")}],
        copies_4,
    )
    sums = total(at(at(pairs, section, 0), yh, 0), *got[0])
    out = []
    for e, g in zip(exp, got[1:]):
        kept = lax.dynamic_slice_in_dim(e, 2 * core, 2, 0)
        low, high = jnp.where(core == 0, kept, g), jnp.where(core == 0, g, kept)
        out.append(jnp.concatenate([low, high], axis=1).astype(F32))
    return sums, out


def gather_weights(local, experts):
    rows, width = local.shape

    def kernel(*refs):
        mine, shards = refs[0], refs[1:4]
        full, late, whole = refs[4], refs[5], refs[6:9]
        stage = refs[9:12]
        sent, got, sent_x, got_e, sent_c, got_c, sent_y, sent_o, local_sem = refs[12:]
        s, yh, z, c, x = (lax.axis_index(a) for a in ("section", "yh", "z", "core", "shard"))
        place = 2 * yh + s
        ys = [lax.rem(place + k, 4) for k in (1, 2, 3)]
        ys = [{"yh": y // 2, "section": lax.rem(y, 2)} for y in ys]
        xs = [{"shard": lax.rem(x + k, 4)} for k in (1, 2, 3)]
        z_up, z_down = lax.rem(z + 1, 4), lax.rem(z + 3, 4)
        sibling, partner = {"core": 1 - c}, {"section": 1 - s}

        def piece(k, i, h):
            if k == 2:
                return shards[2].at[i, pl.ds(pl.multiple_of(h * 384, 128), 384)]
            return shards[k].at[i, pl.ds(pl.multiple_of(h * 192, 64), 192)]

        def landing(k, layer, source, half):
            if k == 2:
                return whole[2].at[layer, half, :, pl.ds(pl.multiple_of(source * 384, 128), 384)]
            return whole[k].at[layer, source, half]

        def remote(source, target, send, receive, device):
            return pltpu.make_async_remote_copy(
                src_ref=source,
                dst_ref=target,
                send_sem=send,
                recv_sem=receive,
                device_id=device,
                device_id_type=pl.DeviceIdType.MESH,
            )

        def start(copies):
            for copy in copies:
                copy.start()
            return copies

        def finish(copies):
            for copy in copies:
                copy.wait()

        has_own = x // 2 == c
        own = lax.rem(x, 2)
        staged = start(
            [pltpu.make_async_copy(piece(k, own, c), stage[k], local_sem.at[k]) for k in range(3)]
        )
        barrier = pltpu.get_barrier_semaphore()
        zs = [{"z": lax.rem(z + k, 4)} for k in (1, 2, 3)]
        x_up, x_down = xs[0]["shard"], xs[2]["shard"]
        near = ys + xs + zs + [sibling]
        near += [{"shard": lax.rem(x + k, 4), "core": 1 - c} for k in (1, 2, 3)]
        for peer in near:
            pl.semaphore_signal(
                barrier, inc=1, device_id=peer, device_id_type=pl.DeviceIdType.MESH
            )
        pl.semaphore_wait(barrier, len(near))

        here = full.at[yh, z, c, x]

        def along_y(target):
            out = [pltpu.make_async_copy(mine, target, local_sem.at[3])]
            for k, device in enumerate(ys):
                out.append(remote(mine, target, sent.at[k], got.at[k], device))
            return out

        @pl.when(s == 0)
        def _():
            start(along_y(here))

        @pl.when(s == 1)
        def _():
            start(along_y(late.at[yh, z, c, x]))

        finish(staged)

        @pl.when(has_own)
        def _():
            for k in range(3):
                remote(
                    piece(k, own, 1 - c),
                    landing(k, s, x, 1 - c),
                    sent_o.at[k],
                    got_e.at[s, x, k],
                    sibling,
                ).start()
                pltpu.make_async_copy(stage[k], landing(k, s, x, c), got_e.at[s, x, k]).start()

        def pass_on(layer, distance, to_partner):
            source = lax.rem(x + distance, 4)
            for k in range(3):
                view = landing(k, layer, source, c)
                receive = got_e.at[layer, source, k]
                remote(view, view, sent_o.at[k], receive, sibling).wait_recv()
                if to_partner:
                    remote(view, view, sent_y.at[distance, k], receive, partner).start()
                across = got_c.at[layer, source, k]
                remote(view, view, sent_c.at[layer, source, k], across, sibling).start()

        finish(along_y(here))
        view, view_late = full.at[:, z, c, x], late.at[:, z, c, x]
        along_x = start(
            [remote(view, view, sent.at[3 + k], got.at[3 + k], xs[k]) for k in range(3)]
        )
        late_z = start(
            [
                remote(view_late, view_late, sent.at[11 + k], got.at[11 + k], zs[k])
                for k in range(3)
            ]
        )
        pass_on(s, 0, True)
        finish(along_x)

        def ring(base, axis, places, up, down):
            return start(
                [
                    remote(up, up, sent.at[base], got.at[base], {axis: places[0]}),
                    remote(down, down, sent.at[base + 1], got.at[base + 1], {axis: places[1]}),
                ]
            )

        view = full.at[:, z, c]
        along_z = ring(6, "z", (z_up, z_down), view, view)
        for i in range(2):

            @pl.when(x != 2 * c + i)
            def _():
                for h in range(2):
                    for k in range(3):
                        remote(
                            piece(k, i, h),
                            landing(k, s, x, h),
                            sent_x.at[(i * 2 + h) * 3 + k],
                            got_e.at[s, x, k],
                            {"shard": 2 * c + i, "core": h},
                        ).start()

        finish(late_z)
        view = late.at[:, :, c, x]
        late_x = ring(14, "shard", (x_up, x_down), view, view)
        finish(along_z)
        along_z = ring(8, "z", (z_up, z_down), full.at[0, z_down, c], full.at[1, z_up, c])
        for distance in (1, 3, 2):
            pass_on(s, distance, True)
        finish(along_z)
        view = full.at[:, :, c]
        across = start([remote(view, view, sent.at[10], got.at[10], sibling)])
        finish(late_x)
        late_x = ring(
            16, "shard", (x_up, x_down), late.at[0, :, c, x_down], late.at[1, :, c, x_up]
        )
        for distance in (0, 1):
            pass_on(1 - s, distance, False)
        finish(late_x)
        view = late.at[:, :, c]
        across += start([remote(view, view, sent.at[18], got.at[18], sibling)])
        for distance in (3, 2):
            pass_on(1 - s, distance, False)

        finish(across)
        for i in range(2):

            @pl.when(x != 2 * c + i)
            def _():
                for h in range(2):
                    for k in range(3):
                        view = piece(k, i, h)
                        n = (i * 2 + h) * 3 + k
                        remote(view, view, sent_x.at[n], got_e.at[0, 0, k], sibling).wait_send()

        @pl.when(has_own)
        def _():
            for k in range(3):
                view = piece(k, own, 1 - c)
                remote(view, view, sent_o.at[k], got_e.at[0, 0, k], sibling).wait_send()

        for source in range(4):
            for k in range(3):
                view = landing(k, s, source, c)
                send = sent_y.at[source, k]
                remote(view, view, send, got_e.at[0, 0, k], partner).wait_send()
                for layer in range(2):
                    view = landing(k, layer, source, c)
                    arrived = landing(k, layer, source, 1 - c)
                    send, receive = sent_c.at[layer, source, k], got_c.at[layer, source, k]
                    remote(view, view, send, receive, sibling).wait_send()
                    remote(arrived, arrived, send, receive, sibling).wait_recv()

    space = pl.BlockSpec(memory_space=pltpu.HBM)
    near_space = pl.BlockSpec(memory_space=pltpu.VMEM)
    shapes = [(2, 4, 2, 4, rows, width)] * 2
    shapes += [(2, 4, 2, 192, 768), (2, 4, 2, 192, 768), (2, 2, 384, 1536)]
    dma = pltpu.SemaphoreType.DMA
    return pl.pallas_call(
        kernel,
        out_shape=[jax.ShapeDtypeStruct(shape, BF) for shape in shapes],
        in_specs=[near_space] + [space] * 3,
        out_specs=[space] * 5,
        scratch_shapes=[
            pltpu.VMEM((192, 768), BF),
            pltpu.VMEM((192, 768), BF),
            pltpu.VMEM((384, 384), BF),
            dma((19,)),
            dma((19,)),
            dma((12,)),
            dma((2, 4, 3)),
            dma((2, 4, 3)),
            dma((2, 4, 3)),
            dma((4, 3)),
            dma((3,)),
            dma((4,)),
        ],
        compiler_params=pltpu.CompilerParams(collective_id=0, has_side_effects=True),
        name="gather_weights",
    )(local, *experts)


def rank_of(route_rows):
    rows = route_rows.shape[0]
    chosen = route_rows.T[None, :, :] == jnp.arange(EXPERTS, dtype=jnp.int32)[:, None, None]
    hot = jnp.any(chosen, axis=1)
    index = jnp.arange(rows, dtype=jnp.int32)
    before = (index[:, None] < index[None, :]).astype(BF)
    return jnp.where(hot, dot(hot.astype(BF), before), -1.0)


def stacked(field):
    return jnp.concatenate(jnp.split(field, CHUNKS, axis=1), axis=0)


def unstacked(field):
    return jnp.concatenate(jnp.split(field, CHUNKS, axis=0), axis=1)


def unfold_table(sources):
    row = jnp.arange(CHUNKS * sources * EXTRA, dtype=jnp.int32)
    piece, source, extra = row // (sources * EXTRA), row // EXTRA % sources, row % EXTRA
    column = jnp.arange(sources * MAIN, dtype=jnp.int32)
    return (
        (source * MAIN + piece * EXTRA + extra)[:, None] == column[None, :]
    ).astype(BF)


def arrived_rows(message, unfold):
    width = message.shape[1] - 256
    extra = unstacked(dot(unfold, message[:, width:]).astype(BF))
    return jnp.concatenate([message[:, :width], extra], axis=0)


def fold_rows(rows, unfold, sources):
    main = rows[: sources * MAIN]
    extra = dot(unfold, stacked(rows[sources * MAIN :]), ((0,), (0,))).astype(BF)
    return jnp.concatenate([main, extra], axis=1)


def low_pair(value):
    high = value.astype(BF)
    return high, (value - high.astype(F32)).astype(BF)


OUT_COLUMNS, QKV_STEP = 1536, 512


def columns(width, place):
    return lambda rows: pl.BlockSpec((rows, width), lambda i: (0, place), memory_space=pltpu.VMEM)


OUT_BLOCK = [columns(OUT_COLUMNS, 0)]
QKV_BLOCKS = [columns(QKV_STEP, 3 + k) for k in range(4)]
NARROW_BLOCK = [columns(128, 28)]


def fused(name, body, shapes, *arrays, scratch=(), number=None):
    near = pl.BlockSpec(memory_space=pltpu.VMEM)
    specs, given = [], []
    for array in arrays:
        if isinstance(array, tuple):
            array, blocks = array
            specs += [block(array.shape[0]) for block in blocks]
            given += [array] * len(blocks)
        else:
            specs.append(near)
            given.append(array)
    return pl.pallas_call(
        body,
        grid=(1,),
        out_shape=[jax.ShapeDtypeStruct(shape, kind) for shape, kind in shapes],
        in_specs=specs,
        out_specs=[near] * len(shapes),
        scratch_shapes=list(scratch),
        compiler_params=pltpu.CompilerParams(
            vmem_limit_bytes=48 << 20, collective_id=number, has_side_effects=number is not None
        ),
        name=name,
    )(*given)


TN, NT = ((0,), (0,)), ((1,), (1,))


def slots(rank):
    count, rows = rank.shape
    place = lax.broadcasted_iota(jnp.int32, (count, MAIN, rows), 1)
    wide = jnp.broadcast_to(rank[:, None, :], (count, MAIN, rows))
    main = jnp.where(wide == place.astype(F32), 1.0, 0.0)
    extra = (MAIN + lax.rem(place, EXTRA)).astype(F32)
    extra = jnp.where((wide == extra) & (place < EXTRA * CHUNKS), 1.0, 0.0)
    return main, extra


def per_piece(table):
    piece = lax.rem(lax.broadcasted_iota(jnp.int32, table.shape, 0), MAIN) // EXTRA
    return [jnp.where(piece == j, table, 0.0) for j in range(CHUNKS)]


def flat(table):
    return table.reshape(table.shape[0] * table.shape[1], table.shape[2])


def send_table(main, extra, field):
    width = field.shape[1] // CHUNKS
    side = None
    for j, table in enumerate(per_piece(flat(extra))):
        part = dot(table.astype(BF), field[:, j * width : (j + 1) * width])
        side = part if side is None else side + part
    return dot(flat(main).astype(BF), field), side


def bring_back(main, extra, rows, exact):
    parts = low_pair if exact else (lambda t: (t.astype(BF),))
    model_width = rows.shape[1] - 256
    total_main = None
    for table in parts(main):
        part = dot(table, rows[:, :model_width], TN)
        total_main = part if total_main is None else total_main + part
    side = []
    for table in per_piece(extra):
        total_side = None
        for t in parts(table):
            part = dot(t, rows[:, model_width:], TN)
            total_side = part if total_side is None else total_side + part
        side.append(total_side)
    return total_main + jnp.concatenate(side, axis=1)


def gain_rows(narrow):
    row = lax.broadcasted_iota(jnp.int32, (8, narrow.shape[1]), 0)
    column = lax.broadcasted_iota(jnp.int32, (8, narrow.shape[1]), 1)
    pick = jnp.where(column == row + EXPERTS, 1.0, 0.0).astype(BF)
    rows = dot(pick, narrow, NT)
    return rows[0:1], rows[1:2]


def turn(field, cosine, sine):
    return field * cosine + pltpu.roll(field, HEAD_DIM // 2, 1) * sine


def turn_back(field, cosine, sine):
    return field * cosine - pltpu.roll(field, HEAD_DIM // 2, 1) * sine


def combined(x_mid, rank, gates, rows):
    main, extra = slots(rank)
    wide = jnp.broadcast_to(gates[:, None, :], main.shape)
    return x_mid + bring_back(flat(main * wide), flat(extra * wide), rows, True)


def finish_body(mid_ref, rank_ref, gates_ref, rows_ref, out_ref):
    out = combined(mid_ref[...], rank_ref[...], gates_ref[...], rows_ref[...])
    out_ref[...] = out.astype(BF)


def heads_of(kv_ref):
    kv_heads = kv_ref.shape[2] // 2 // HEAD_DIM
    parts = []
    for k in range(2 * kv_heads):
        part = kv_ref[:, :, k * HEAD_DIM : (k + 1) * HEAD_DIM]
        parts.append(part.reshape(part.shape[0] * part.shape[1], HEAD_DIM))
    return parts[:kv_heads], parts[kv_heads:]


def attention_body(combine):
    def body(*refs):
        source, refs = refs[: 4 if combine else 1], refs[4 if combine else 1 :]
        weights, refs = refs[:4], refs[4:]
        out_w, narrow, cos_ref, sin_ref, allowed_ref, rank_ref, low_ref, h_ref, q_ref = refs[:9]
        kv_ref, mid_ref, h2_ref, att_ref, probs_ref, gates_ref, out_ref, held, sent, got = refs[9:]
        here = lax.axis_index("shard")
        peers = [{"shard": x} for x in around("shard", 4)]
        barrier = pltpu.get_barrier_semaphore()
        for peer in peers:
            pl.semaphore_signal(
                barrier, inc=1, device_id=peer, device_id_type=pl.DeviceIdType.MESH
            )
        if combine:
            mid, rank, gates, rows = (ref[...] for ref in source)
            low = combined(mid, rank, gates, rows).astype(BF)
        else:
            low = source[0][...]
        low_ref[...] = low
        field = low.astype(F32)
        gain_a, gain_m = gain_rows(narrow[...])
        scale = lax.rsqrt(jnp.mean(field * field, axis=1, keepdims=True) + epsilon)
        h = (field * scale * gain_a).astype(BF)
        h_ref[...] = h
        cosine, sine = cos_ref[...], sin_ref[...]

        def projected(column, turned):
            inside = column % QKV_STEP
            part = dot(h, weights[column // QKV_STEP][:, inside : inside + 256])
            if turned:
                part = jnp.concatenate(
                    [turn(part[:, k : k + HEAD_DIM], cosine, sine) for k in (0, HEAD_DIM)], axis=1
                )
            return part.astype(BF)

        query_width, kv_width = q_ref.shape[1], kv_ref.shape[2]
        for column in range(0, kv_width, 256):
            part = projected(query_width + column, column < kv_width // 2)
            held[here, :, column : column + 256] = part
        pl.semaphore_wait(barrier, len(peers))
        copies = []
        for k, peer in enumerate(peers):
            view = held.at[here]
            copies.append(
                pltpu.make_async_remote_copy(
                    src_ref=view,
                    dst_ref=view,
                    send_sem=sent.at[k],
                    recv_sem=got.at[k],
                    device_id=peer,
                    device_id_type=pl.DeviceIdType.MESH,
                )
            )
            copies[-1].start()
        for column in range(0, query_width, 256):
            q_ref[:, column : column + 256] = projected(column, True)
        for copy in copies:
            copy.wait()

        kv_ref[...] = held[...]
        keys, values = heads_of(held)
        allowed = allowed_ref[...] > 0.0
        ratio = HEADS // len(keys)
        for head in range(HEADS):
            lanes = slice(head * HEAD_DIM, (head + 1) * HEAD_DIM)
            scores = dot(q_ref[:, lanes], keys[head // ratio], NT) * HEAD_DIM ** (-0.5)
            scores = jnp.where(allowed, scores, masked_score)
            exponent = jnp.exp(scores - jnp.max(scores, axis=1, keepdims=True))
            probs = exponent / jnp.sum(exponent, axis=1, keepdims=True)
            probs_ref[head] = probs
            att_ref[:, lanes] = dot(probs.astype(BF), values[head // ratio]).astype(BF)
        mid = field + dot(att_ref[...], out_w[...])
        mid_ref[...] = mid
        scale = lax.rsqrt(jnp.mean(mid * mid, axis=1, keepdims=True) + epsilon)
        h2 = (mid * scale * gain_m).astype(BF)
        h2_ref[...] = h2
        rank = rank_ref[...]
        logits = jnp.transpose(dot(h2, narrow[...]))[:EXPERTS]
        logits = jnp.where(rank >= 0.0, logits, masked_score)
        gate_exp = jnp.exp(logits - jnp.max(logits, axis=0, keepdims=True))
        gate_exp = jnp.where(rank >= 0.0, gate_exp, 0.0)
        gates_ref[...] = gate_exp / jnp.sum(gate_exp, axis=0, keepdims=True)
        main, side = send_table(*slots(rank), h2)
        width = main.shape[1]
        out_ref[:, :width] = main.astype(BF)
        out_ref[:, width:] = side.astype(BF)

    return body


def attention(source, weights, tables, allowed, rank, number):
    tok_rows, model_width = source[0].shape
    query_width = HEADS * HEAD_DIM
    shapes = [((tok_rows, model_width), BF)] * 2
    shapes += [
        ((tok_rows, query_width), BF),
        ((allowed.shape[1] // tok_rows, tok_rows, 4 * QKV_STEP - query_width), BF),
        ((tok_rows, model_width), F32),
        ((tok_rows, model_width), BF),
        ((tok_rows, query_width), BF),
        ((HEADS, tok_rows, allowed.shape[1]), F32),
        (rank.shape, F32),
        ((EXPERTS * MAIN, model_width + 256), BF),
    ]
    dma = pltpu.SemaphoreType.DMA
    return fused(
        "attention",
        attention_body(len(source) > 1),
        shapes,
        *source,
        (weights, QKV_BLOCKS + OUT_BLOCK + NARROW_BLOCK),
        *tables,
        allowed,
        rank,
        scratch=[pltpu.VMEM(shapes[3][0], BF), dma((3,)), dma((3,))],
        number=number,
    )


def grad_slots_body(grad_ref, rank_ref, gates_ref, rows_ref, out_ref, dlogits_ref):
    gates = gates_ref[...]
    main, extra = slots(rank_ref[...])
    wide = jnp.broadcast_to(gates[:, None, :], main.shape)
    grad_main, grad_side = send_table(main, extra, grad_ref[...])
    width = grad_main.shape[1]
    dgate = None
    for table, grad, columns in (
        (main, grad_main, slice(0, width)),
        (extra, grad_side, slice(width, width + 256)),
    ):
        slot_gate = jnp.sum(flat(table * wide), axis=1, keepdims=True)
        out_ref[:, columns] = (grad * slot_gate).astype(BF)
        slot_dgate = jnp.sum(grad * rows_ref[:, columns].astype(F32), axis=1, keepdims=True)
        part = jnp.sum((flat(table) * slot_dgate).reshape(table.shape), axis=1)
        dgate = part if dgate is None else dgate + part
    dlogits = gates * (dgate - jnp.sum(gates * dgate, axis=0, keepdims=True))
    pad = jnp.zeros((dlogits_ref.shape[1] - EXPERTS, dlogits.shape[1]), F32)
    dlogits_ref[...] = jnp.transpose(jnp.concatenate([dlogits, pad], axis=0)).astype(BF)


def grad_slots(grad, rank, gates, rows):
    shapes = [(rows.shape, BF), ((grad.shape[0], 128), BF)]
    return fused("grad_slots", grad_slots_body, shapes, grad, rank, gates, rows)


def norm_grads(field, gain, grad):
    scale = lax.rsqrt(jnp.mean(field * field, axis=1, keepdims=True) + epsilon)
    scaled = grad * gain
    centre = jnp.mean(scaled * field, axis=1, keepdims=True)
    dgain = jnp.sum(grad * field * scale, axis=0, keepdims=True)
    return scale * scaled - field * (scale * scale * scale) * centre, dgain


def grad_attend_body(
    grad_ref, rows_ref, rank_ref, dlogits_ref, weight, narrow, mid_ref, q_ref, kv_ref, probs_ref,
    cos_ref, sin_ref,
    dmid_ref, dbr_ref, dq_ref, dkv_ref, dgain_ref, datt_ref,
):
    main, extra = slots(rank_ref[...])
    dh = bring_back(flat(main), flat(extra), rows_ref[...], False)
    dh = dh + dot(dlogits_ref[...], narrow[...], NT)
    _, gain = gain_rows(narrow[...])
    dmid, dgain = norm_grads(mid_ref[...], gain, dh)
    dmid = dmid + grad_ref[...].astype(F32)
    dgain_ref[...] = dgain
    dmid_ref[...] = dmid
    dbr_ref[...] = dmid.astype(BF)
    datt_ref[...] = dot(dbr_ref[...], weight[...], NT).astype(BF)
    keys, values = heads_of(kv_ref)
    ratio = HEADS // len(keys)
    cosine, sine = cos_ref[...], sin_ref[...]
    count, tok_rows = kv_ref.shape[0], kv_ref.shape[1]
    scale = HEAD_DIM ** (-0.5)
    for k in range(len(keys)):
        dkey, dvalue = None, None
        for head in range(k * ratio, (k + 1) * ratio):
            lanes = slice(head * HEAD_DIM, (head + 1) * HEAD_DIM)
            probs, datt = probs_ref[head], datt_ref[:, lanes]
            dprobs = dot(datt, values[k], NT)
            centre = jnp.sum(dprobs * probs, axis=1, keepdims=True)
            dscores = (probs * (dprobs - centre)).astype(BF)
            part = dot(probs.astype(BF), datt, TN)
            dvalue = part if dvalue is None else dvalue + part
            part = dot(dscores, q_ref[:, lanes], TN)
            dkey = part if dkey is None else dkey + part
            dquery = dot(dscores, keys[k]) * scale
            dq_ref[:, lanes] = turn_back(dquery, cosine, sine).astype(BF)
        at_key, at_value = k * HEAD_DIM, (len(keys) + k) * HEAD_DIM
        shape = (count, tok_rows, HEAD_DIM)
        dkv_ref[:, :, at_key : at_key + HEAD_DIM] = (dkey * scale).astype(BF).reshape(shape)
        dkv_ref[:, :, at_value : at_value + HEAD_DIM] = dvalue.astype(BF).reshape(shape)


def grad_attend(grad, rows, rank, dlogits, weights, mid, q, kv, probs, tables):
    tok_rows, model_width = mid.shape
    shapes = [
        ((tok_rows, model_width), F32),
        ((tok_rows, model_width), BF),
        (q.shape, BF),
        (kv.shape, BF),
        ((1, model_width), F32),
        (q.shape, BF),
    ]
    return fused(
        "grad_attend", grad_attend_body, shapes,
        grad, rows, rank, dlogits, (weights, OUT_BLOCK + NARROW_BLOCK), mid, q, kv, probs, *tables,
    )[:5]


def grad_project_body(
    dq_ref, dkv_ref, dmid_ref, low_ref, weight_0, weight_1, weight_2, weight_3, narrow, cos_ref,
    sin_ref,
    dqkv_ref, grad_ref, dgain_ref,
):
    query_width, kv_width = dq_ref.shape[1], dkv_ref.shape[1] // 2
    cosine, sine = cos_ref[...], sin_ref[...]
    dqkv_ref[:, :query_width] = dq_ref[...]
    for k in range(0, kv_width, HEAD_DIM):
        part = turn_back(dkv_ref[:, k : k + HEAD_DIM], cosine, sine)
        dqkv_ref[:, query_width + k : query_width + k + HEAD_DIM] = part.astype(BF)
    dqkv_ref[:, query_width + kv_width :] = dkv_ref[:, kv_width:].astype(BF)
    dh = None
    for k, weight in enumerate((weight_0, weight_1, weight_2, weight_3)):
        part = dot(dqkv_ref[:, k * QKV_STEP : (k + 1) * QKV_STEP], weight[...], NT)
        dh = part if dh is None else dh + part
    gain, _ = gain_rows(narrow[...])
    dlow, dgain = norm_grads(low_ref[...].astype(F32), gain, dh)
    dgain_ref[...] = dgain
    grad_ref[...] = (dlow + dmid_ref[...]).astype(BF)


def grad_project(dq, dkv, dmid, low, weights, tables):
    tok_rows, model_width = low.shape
    shapes = [
        ((tok_rows, 4 * QKV_STEP), BF),
        ((tok_rows, model_width), BF),
        ((1, model_width), F32),
    ]
    return fused(
        "grad_project", grad_project_body, shapes,
        dq, dkv, dmid, low, (weights, QKV_BLOCKS + NARROW_BLOCK), *tables,
    )


def weight_grads_body(
    h_ref, dqkv_ref, att_ref, dbr_ref, h2_ref, dlogits_ref, dgain_a_ref, dgain_m_ref, out_ref
):
    step = 512
    place = 0
    for left, right in ((att_ref, dbr_ref), (h_ref, dqkv_ref)):
        for k in range(0, right.shape[1], step):
            part = dot(left[...], right[:, k : k + step], TN)
            out_ref[:, place : place + step] = part.astype(BF)
            place += step
    narrow = dot(h2_ref[...], dlogits_ref[...], TN)
    rows = jnp.concatenate(
        [dgain_a_ref[...], dgain_m_ref[...], jnp.zeros((126, h_ref.shape[1]), F32)], axis=0
    )
    columns = pltpu.roll(jnp.transpose(rows), EXPERTS, 1)
    out_ref[:, place:] = (narrow + columns).astype(BF)


def weight_grads(h, dqkv, att, dbr, h2, dlogits, dgain_a, dgain_m):
    columns = dqkv.shape[1] + dbr.shape[1] + 128
    return fused(
        "weight_grads", weight_grads_body, [((h.shape[1], columns), BF)],
        h, dqkv, att, dbr, h2, dlogits, dgain_a, dgain_m,
    )[0]


def greet(peers):
    barrier = pltpu.get_barrier_semaphore()
    for peer in peers:
        pl.semaphore_signal(barrier, inc=1, device_id=peer, device_id_type=pl.DeviceIdType.MESH)
    pl.semaphore_wait(barrier, len(peers))


def small_exchange(name, number, array, shape, scratch, before, after):
    def kernel(in_ref, out_ref, *rest):
        here = lax.axis_index("shard")
        held = rest[0] if scratch else out_ref
        sent, got = rest[-2:]
        peers = [{"shard": x} for x in around("shard", 4)]
        greet(peers)
        copies = []
        for k, peer in enumerate(peers):
            source, target = before(in_ref, held, here, peer["shard"], k)
            copies.append(
                pltpu.make_async_remote_copy(
                    src_ref=source,
                    dst_ref=target,
                    send_sem=sent.at[k],
                    recv_sem=got.at[k],
                    device_id=peer,
                    device_id_type=pl.DeviceIdType.MESH,
                )
            )
            copies[-1].start()
        if not scratch:
            after(in_ref, held, out_ref, here)
        for copy in copies:
            copy.wait()
        if scratch:
            after(in_ref, held, out_ref, here)

    near = pl.BlockSpec(memory_space=pltpu.VMEM)
    dma = pltpu.SemaphoreType.DMA
    return pl.pallas_call(
        kernel,
        out_shape=jax.ShapeDtypeStruct(*shape),
        in_specs=[near],
        out_specs=near,
        scratch_shapes=scratch + [dma((3,)), dma((3,))],
        compiler_params=pltpu.CompilerParams(collective_id=number, has_side_effects=True),
        name=name,
    )(array)


def sum_group(dkv, number):
    def before(in_ref, held, here, there, k):
        return in_ref.at[there], held.at[k]

    def after(in_ref, held, out_ref, here):
        out = in_ref[here].astype(F32)
        for k in range(3):
            out = out + held[k].astype(F32)
        out_ref[...] = out

    held = [pltpu.VMEM((3, *dkv.shape[1:]), BF)]
    return small_exchange("sum_group", number, dkv, (dkv.shape[1:], F32), held, before, after)


PARTNERS = [(dy, dz, (dz + k) % 4) for k in range(4) for dy in range(2) for dz in range(4)]
GROUP = 8
GROUPS = len(PARTNERS) // GROUP


def facing(n):
    k, dy, dz = n // GROUP, n // 4 % 2, n % 4
    return -k % GROUPS * GROUP + dy * 4 + -dz % 4


def partners():
    s, yh, z, x = (lax.axis_index(a) for a in ("section", "yh", "z", "shard"))
    out = []
    for dy, dz, dx in PARTNERS:
        there = {
            "section": lax.rem(s + dy, 2),
            "yh": lax.rem(yh + dy, 2),
            "z": lax.rem(z + dz, 4),
            "shard": lax.rem(x + dx, 4),
        }
        out.append((there, (there["yh"] * 4 + there["z"]) * 4 + there["shard"]))
    return out


def exchange_rows(message, returned, arrived, produced, sems, work, after, sibling=()):
    sent, got, sent_back, got_back = sems
    near = partners()
    own = near[0][1]
    greet([device for device, _ in near[1:]] + list(sibling))

    def remote(source, target, send, receive, device):
        return pltpu.make_async_remote_copy(
            src_ref=source,
            dst_ref=target,
            send_sem=send,
            recv_sem=receive,
            device_id=device,
            device_id_type=pl.DeviceIdType.MESH,
        )

    def out(n):
        device, expert = near[n]
        f = facing(n)
        return remote(message.at[expert], arrived.at[f], sent.at[n], got.at[f], device)

    def back(n):
        return remote(
            produced.at[n], returned.at[own], sent_back.at[n], got_back.at[facing(n)], near[n][0]
        )

    for k in range(GROUPS):
        for n in range(-k % GROUPS * GROUP, -k % GROUPS * GROUP + GROUP):
            if n:
                out(n).start()
    arrived[0] = message[own]
    for k in range(GROUPS):
        members = range(k * GROUP, (k + 1) * GROUP)
        for n in members:
            if n:
                remote(arrived.at[n], arrived.at[n], sent.at[n], got.at[n], near[n][0]).wait_recv()
        rows = arrived[k * GROUP : (k + 1) * GROUP]
        result = work(k, rows.reshape(GROUP * MAIN, rows.shape[2]))
        produced[k * GROUP : (k + 1) * GROUP] = result.reshape(rows.shape)
        for n in members:
            if n:
                back(n).start()
    returned[own] = produced[0]
    after()
    for n in range(1, len(near)):
        device, expert = near[n]
        out(n).wait_send()
        back(n).wait_send()
        view = returned.at[expert]
        remote(view, view, sent_back.at[n], got_back.at[n], device).wait_recv()


def exchange_call(name, number, body, inputs, shapes, message_shape, scratch):
    near = pl.BlockSpec(memory_space=pltpu.VMEM)
    dma = pltpu.SemaphoreType.DMA
    count = message_shape[0]
    return pl.pallas_call(
        body,
        out_shape=[jax.ShapeDtypeStruct(shape, kind) for shape, kind in shapes],
        in_specs=[near] * len(inputs),
        out_specs=[near] * len(shapes),
        scratch_shapes=[pltpu.VMEM(message_shape, BF), pltpu.VMEM(message_shape, BF)]
        + [dma((count,)) for _ in range(4)]
        + scratch,
        compiler_params=pltpu.CompilerParams(
            collective_id=number, has_side_effects=True, vmem_limit_bytes=56 << 20
        ),
        name=name,
    )(*inputs)


def expert_forward(message, experts, unfold, number):
    message = message.reshape(EXPERTS, MAIN, message.shape[1])
    rows = GROUP * (MAIN + EXTRA)
    depth, width = experts[0].shape

    def body(message_ref, gate_w, up_w, down_w, unfold_ref, *refs):
        returned, rows_ref, gate_ref, up_ref, hidden_ref = refs[:5]
        arrived, produced, *sems = refs[5:]

        def work(k, came):
            field = arrived_rows(came, unfold_ref[...])
            rows_ref[k] = field
            gate = dot(field, gate_w[...])
            up = dot(field, up_w[...])
            gate_ref[k] = gate
            up_ref[k] = up
            hidden = (gate / (1.0 + jnp.exp(-gate)) * up).astype(BF)
            hidden_ref[k] = hidden
            return fold_rows(dot(hidden, down_w[...]).astype(BF), unfold_ref[...], GROUP)

        exchange_rows(message_ref, returned, arrived, produced, sems, work, lambda: None)

    shapes = [
        (message.shape, BF),
        ((GROUPS, rows, depth), BF),
        ((GROUPS, rows, width), F32),
        ((GROUPS, rows, width), F32),
        ((GROUPS, rows, width), BF),
    ]
    returned, *kept = exchange_call(
        "expert_forward", number, body, [message, *experts, unfold], shapes, message.shape, []
    )
    return returned.reshape(-1, message.shape[2]), kept


def expert_backward(message, experts, kept, unfold, number):
    message = message.reshape(EXPERTS, MAIN, message.shape[1])
    rows = GROUP * (MAIN + EXTRA)
    depth, width = experts[0].shape

    shards = 4
    half, deep = depth // 8, width // 2

    def body(message_ref, gate_w, up_w, down_w, rows_ref, gate_ref, up_ref, hidden_ref, *refs):
        unfold_ref, returned, sum_ref = refs[:3]
        arrived, produced = refs[3:5]
        sems, (came_ref, dgate_ref, dup_ref) = refs[5:9], refs[9:12]
        wide_refs, (down_ref, held_gate, held_up, held_down, sent, got) = refs[12:14], refs[14:]
        core = lax.axis_index("core")
        sibling = {"core": 1 - core}

        def work(k, came):
            field = arrived_rows(came, unfold_ref[...])
            came_ref[k] = field
            dhidden = dot(field, down_w[...], NT)
            gate = gate_ref[k]
            logistic = 1.0 / (1.0 + jnp.exp(-gate))
            dgate = dhidden * up_ref[k] * (logistic * (1.0 + gate * (1.0 - logistic)))
            dgate_ref[k] = dgate.astype(BF)
            dup_ref[k] = (dhidden * (gate * logistic)).astype(BF)
            out = dot(dgate_ref[k], gate_w[...], NT) + dot(dup_ref[k], up_w[...], NT)
            return fold_rows(out.astype(BF), unfold_ref[...], GROUP)

        def to_sibling(k):
            views = [wide_refs[0].at[:, 1 - core], wide_refs[1].at[:, 1 - core]]
            views.append(down_ref.at[1 - core])
            return pltpu.make_async_remote_copy(
                src_ref=views[k],
                dst_ref=(held_gate, held_up, held_down)[k],
                send_sem=sent.at[k],
                recv_sem=got.at[k],
                device_id=sibling,
                device_id_type=pl.DeviceIdType.MESH,
            )

        def after():
            step = 256
            field = rows_ref[...].reshape(GROUPS * rows, depth)
            for k, source in enumerate((dgate_ref, dup_ref)):
                for column in range(0, width, step):
                    lanes = slice(column, column + step)
                    part = source[:, :, lanes].reshape(GROUPS * rows, step)
                    part = dot(field, part, TN).astype(BF)
                    wide_refs[k][:, :, :, lanes] = part.reshape(shards, 2, half, step)
                to_sibling(k).start()
            field = hidden_ref[...].reshape(GROUPS * rows, width)
            for column in range(0, depth, step):
                lanes = slice(column, column + step)
                part = came_ref[:, :, lanes].reshape(GROUPS * rows, step)
                part = dot(field, part, TN).astype(BF)
                down_ref[:, :, lanes] = part.reshape(2, deep, step)
            to_sibling(2).start()

        exchange_rows(
            message_ref, returned, arrived, produced, sems, work, after, (sibling,)
        )
        for k, held in enumerate((held_gate, held_up)):
            to_sibling(k).wait()
            for j in range(shards):
                part = wide_refs[k][j, core].astype(F32) + held[j].astype(F32)
                place = (k * shards + j) * half
                sum_ref[place : place + half] = part.astype(BF)
        to_sibling(2).wait()
        part = down_ref[core].astype(F32) + held_down[...].astype(F32)
        place = 2 * shards * half
        for j in range(2):
            columns_of = part[:, j * width : (j + 1) * width].astype(BF)
            sum_ref[place + j * deep : place + (j + 1) * deep] = columns_of

    shapes = [(message.shape, BF), ((3 * shards * half, width), BF)]
    dma = pltpu.SemaphoreType.DMA
    scratch = [
        pltpu.VMEM((GROUPS, rows, depth), BF),
        pltpu.VMEM((GROUPS, rows, width), BF),
        pltpu.VMEM((GROUPS, rows, width), BF),
        pltpu.VMEM((shards, 2, half, width), BF),
        pltpu.VMEM((shards, 2, half, width), BF),
        pltpu.VMEM((2, deep, depth), BF),
        pltpu.VMEM((shards, half, width), BF),
        pltpu.VMEM((shards, half, width), BF),
        pltpu.VMEM((deep, depth), BF),
        dma((3,)),
        dma((3,)),
    ]
    returned, sums = exchange_call(
        "expert_backward",
        number,
        body,
        [message, *experts, *kept, unfold],
        shapes,
        message.shape,
        scratch,
    )
    return returned.reshape(-1, message.shape[2]), sums


def forward_layer(source, weights, experts, rank, unfold, tables, allowed, numbers):
    low, h_attn, query, kv_all, x_mid, h_moe, attended, probs, gates, message = attention(
        source, weights, tables, allowed, rank, numbers[0]
    )
    returned, kept = expert_forward(message, experts, unfold, numbers[1])
    stored = {
        "low": low,
        "h_attn": h_attn,
        "query": query,
        "kv_all": kv_all,
        "probs": probs,
        "attended": attended,
        "x_mid": x_mid,
        "h_moe": h_moe,
        "gates": gates,
        "returned": returned,
        "kept": kept,
    }
    return (x_mid, rank, gates, returned), stored


def backward_layer(grad, ready, stored, weights, experts, rank, unfold, tables, numbers):
    message, dlogits = grad_slots(grad, rank, stored["gates"], stored["returned"])
    returned, half = expert_backward(message, experts, stored["kept"], unfold, numbers[0])
    kv_all = stored["kv_all"]
    dmid, dbr, dquery, dkv, dgain_m = grad_attend(
        grad, returned, rank, dlogits, weights, stored["x_mid"], stored["query"], kv_all,
        stored["probs"], tables,
    )
    dkv, *ready = lax.optimization_barrier((dkv, *ready))
    dkv = sum_group(dkv, numbers[1])
    dqkv, grad_in, dgain_a = grad_project(dquery, dkv, dmid, stored["low"], weights, tables)
    grads = weight_grads(
        stored["h_attn"], dqkv, stored["attended"], dbr, stored["h_moe"], dlogits, dgain_a, dgain_m
    )
    return grad_in, grads, half, ready


def per_device(
    tokens,
    routes,
    lengths,
    gain_attn,
    w_query,
    w_key,
    w_value,
    w_out,
    gain_moe,
    w_router,
    w_gate,
    w_up,
    w_down,
    cotangent,
):
    section, yh, z, core, shard = (
        lax.axis_index(a) for a in ("section", "yh", "z", "core", "shard")
    )
    first = section == 0
    tok_rows, model_width = tokens.shape[1:]
    group_rows = tok_rows * lax.axis_size("shard")

    def mine(a):
        return lax.dynamic_index_in_dim(a, section, 0, keepdims=False)

    def by_layer(own, other):
        return jnp.where(first, own, other), jnp.where(first, other, own)

    local = jnp.concatenate(
        [
            w_out[0],
            w_query[0],
            w_key[0],
            w_value[0],
            w_router[0],
            gain_attn[0][:, None],
            gain_moe[0][:, None],
            jnp.zeros((w_query.shape[1], 94), BF),
        ],
        axis=1,
    )
    full, late, *whole = gather_weights(local, (w_gate[0], w_up[0], w_down[0]))
    weights = [full.reshape(model_width, -1), late.reshape(model_width, -1)]
    route_other = swap(at(routes[0], 1 - section, 0), "section")
    ranks = [rank_of(r) for r in by_layer(mine(routes[0]), route_other)]
    experts = [
        (
            whole[0][layer].reshape(model_width, 768),
            whole[1][layer].reshape(model_width, 768),
            whole[2][layer].reshape(768, model_width),
        )
        for layer in range(2)
    ]
    unfold = unfold_table(GROUP)

    segment, position = document_layout(mine(lengths[:, 0]), group_rows)
    row_start = shard * tok_rows
    own_segment = lax.dynamic_slice_in_dim(segment, row_start, tok_rows)
    tables = rotary_tables(lax.dynamic_slice_in_dim(position, row_start, tok_rows), HEAD_DIM)
    query_index = row_start + jnp.arange(tok_rows, dtype=jnp.int32)
    allowed = (own_segment[:, None] == segment[None, :]) & (
        query_index[:, None] >= jnp.arange(group_rows, dtype=jnp.int32)[None, :]
    )
    allowed = allowed.astype(F32)

    source, saved = (mine(tokens),), []
    for layer in range(2):
        source, stored = forward_layer(
            source, weights[layer], experts[layer], ranks[layer], unfold, tables, allowed,
            (7 + layer, 11 + layer),
        )
        saved.append(stored)
    low = fused("finish", finish_body, [((tok_rows, model_width), BF)], *source)[0]
    grad, low = lax.optimization_barrier((mine(cotangent), low))
    away = swap(low, "section")

    sums, ready = [None, None], (away,)
    for layer in (1, 0):
        grad, mixer_grad, half, ready = backward_layer(
            grad,
            ready,
            saved[layer],
            weights[layer],
            experts[layer],
            ranks[layer],
            unfold,
            tables,
            (5 + layer, 9 + layer),
        )
        given = lax.ppermute(half, "section", [(1 - layer, layer)])
        sums[layer] = (half, given)
        if layer == 1:
            (away,), ready = ready, (given,)
            late = lax.psum_scatter(mixer_grad, DEVICES, scatter_dimension=0, tiled=True)
            late = lax.optimization_barrier(late)
    mixed = jnp.where(first, jnp.stack([low, away]), jnp.stack([away, low]))

    def finish_experts():
        return jnp.where(first, total(*sums[0]), total(sums[1][0], *ready)).astype(BF)

    mix, (grad_gate, grad_up, grad_down) = reduce_all(mixer_grad, late, finish_experts)
    return (
        mixed,
        grad[None],
        mix[:, 3616][None],
        mix[:, 1536:3072][None],
        mix[:, 3072:3328][None],
        mix[:, 3328:3584][None],
        mix[:, :1536][None],
        mix[:, 3617][None],
        mix[:, 3584:3616][None],
        grad_gate[None],
        grad_up[None],
        grad_down[None],
    )


def solution(mesh):
    fine = Mesh(mesh.devices.reshape(2, 2, 4, 2, 4), ("section", *DEVICES))
    expert = ("yh", "z", "core")
    return jax.shard_map(
        per_device,
        mesh=fine,
        in_specs=(
            P(None, DEVICES, None),
            P("section", None, DEVICES, None),
            P(None, expert, None),
            P("section", DEVICES),
            P("section", DEVICES, None),
            P("section", DEVICES, None),
            P("section", DEVICES, None),
            P("section", DEVICES, None),
            P("section", DEVICES),
            P("section", DEVICES, None),
            P("section", expert, "shard", None),
            P("section", expert, "shard", None),
            P("section", expert, None, "shard"),
            P(None, DEVICES, None),
        ),
        out_specs=(
            P(None, DEVICES, None),
            P("section", DEVICES, None),
            P("section", DEVICES),
            P("section", DEVICES, None),
            P("section", DEVICES, None),
            P("section", DEVICES, None),
            P("section", DEVICES, None),
            P("section", DEVICES),
            P("section", DEVICES, None),
            P("section", expert, "shard", None),
            P("section", expert, "shard", None),
            P("section", expert, None, "shard"),
        ),
        check_vma=False,
    )
```

```python
import jax
import jax.numpy as jnp
from jax import lax
from jax.experimental import pallas as pl
from jax.experimental.pallas import tpu as pltpu
from jax.sharding import Mesh
from jax.sharding import PartitionSpec as P

HEADS = 12
HEAD_DIM = 128
EXPERTS = 32
MAIN = 16
EXTRA = 2
CHUNKS = 6

epsilon = 1e-06
rope_base = 1000000.0
masked_score = -1e30

BF = jnp.bfloat16
F32 = jnp.float32
CHIPS = ("yh", "z", "shard")
DEVICES = ("yh", "z", "core", "shard")


def dot(a, b, dims=((1,), (0,))):
    return lax.dot_general(a, b, (dims, ((), ())), preferred_element_type=F32)


def document_layout(doc_lengths, group_rows):
    doc_ends = jnp.cumsum(doc_lengths)
    starts = doc_ends - doc_lengths
    row_index = jnp.arange(group_rows, dtype=jnp.int32)
    segment = jnp.sum((row_index[:, None] >= doc_ends[None, :]).astype(jnp.int32), axis=1)
    member = segment[:, None] == jnp.arange(doc_lengths.shape[0], dtype=jnp.int32)[None, :]
    position = row_index - jnp.sum(jnp.where(member, starts[None, :], 0), axis=1)
    return (segment, position)


def rotary_tables(position, head_size):
    half_dim = head_size // 2
    frequency = rope_base ** (-2.0 * jnp.arange(half_dim, dtype=F32) / head_size)
    angles = position.astype(F32)[:, None] * frequency[None, :]
    cosine, sine = jnp.cos(angles), jnp.sin(angles)
    return jnp.concatenate([cosine, cosine], axis=1), jnp.concatenate([-sine, sine], axis=1)


def swap(value, axis):
    return lax.ppermute(value, axis, [(0, 1), (1, 0)])


def around(axis, size):
    here = lax.axis_index(axis)
    return [lax.rem(here + step, size) for step in range(1, size)]


def move(name, number, arrays, shapes, peers, copies):
    count = len(arrays)
    total = 40

    def kernel(*refs):
        ins, outs = refs[:count], refs[count : count + len(shapes)]
        sent, got = refs[count + len(shapes) :]
        barrier = pltpu.get_barrier_semaphore()
        near = peers()
        for peer in near:
            pl.semaphore_signal(
                barrier, inc=1, device_id=peer, device_id_type=pl.DeviceIdType.MESH
            )
        pl.semaphore_wait(barrier, len(near))
        started = []
        for k, (source, target, device) in enumerate(copies(ins, outs)):
            if device is None:
                copy = pltpu.make_async_copy(source, target, got.at[k])
            else:
                copy = pltpu.make_async_remote_copy(
                    src_ref=source,
                    dst_ref=target,
                    send_sem=sent.at[k],
                    recv_sem=got.at[k],
                    device_id=device,
                    device_id_type=pl.DeviceIdType.MESH,
                )
            copy.start()
            started.append(copy)
        for copy in started:
            copy.wait()

    space = pl.BlockSpec(memory_space=pltpu.HBM)
    return pl.pallas_call(
        kernel,
        out_shape=[jax.ShapeDtypeStruct(s, BF) for s in shapes],
        in_specs=[space] * count,
        out_specs=[space] * len(shapes),
        scratch_shapes=[pltpu.SemaphoreType.DMA((total,)), pltpu.SemaphoreType.DMA((total,))],
        compiler_params=pltpu.CompilerParams(collective_id=number, has_side_effects=True),
        name=name,
    )(*arrays)


def total(*parts):
    out = parts[0].astype(F32)
    for part in parts[1:]:
        out = out + part.astype(F32)
    return out


def at(array, index, axis):
    return lax.dynamic_index_in_dim(array, index, axis, keepdims=False)


def other(axis):
    return lax.rem(lax.axis_index(axis) + 1, 2)


def reduce_all(grads, late, finish_experts):
    core, shard, z, yh, section = (
        lax.axis_index(a) for a in ("core", "shard", "z", "yh", "section")
    )
    width = grads.shape[1]
    mix = grads.reshape(8, 2, 4, 24, width)

    got = move(
        "cores",
        1,
        [mix],
        [(8, 4, 24, width)],
        lambda: [{"core": other("core")}],
        lambda ins, outs: [(ins[0].at[:, other("core")], outs[0], {"core": other("core")})],
    )[0]
    mix = total(at(mix, core, 1), got).astype(BF).reshape(2, 4, 4, 24, width)

    cut = 768
    wide = finish_experts(0)
    sizes = (cut, width - cut)

    def peers_2():
        return [{"shard": x} for x in around("shard", 4)] + [{"z": i} for i in around("z", 4)]

    def copies_2(ins, outs):
        here = lax.axis_index("shard")
        out = []
        for step, (x, i) in enumerate(zip(around("shard", 4), around("z", 4))):
            out.append((ins[0].at[:, :, x, :, pl.ds(0, cut)], outs[0].at[step], {"shard": x}))
            out.append((ins[0].at[:, i, :, :, pl.ds(cut, width - cut)], outs[1].at[step], {"z": i}))
            for k in range(2):
                rows = pl.ds(pl.multiple_of(k * 768 + x * 192, 64), 192)
                out.append((ins[1].at[rows], outs[2 + k].at[here], {"shard": x}))
        return out

    shapes = [(3, 2, 4, 24, size) for size in sizes] + [(4, 192, 768)] * 2
    *got, gate, up = move("first_axis", 2, [mix, wide], shapes, peers_2, copies_2)
    own = [
        lax.dynamic_slice(mix, (0, 0, shard, 0, 0), (2, 4, 1, 24, cut))[:, :, 0],
        lax.dynamic_slice(mix, (0, z, 0, 0, cut), (2, 1, 4, 24, width - cut))[:, 0],
    ]
    mix = [total(m, *g).astype(BF) for m, g in zip(own, got)]

    down = finish_experts(1)

    def down_shard(x):
        rows = pl.ds(pl.multiple_of(x // 2 * 384, 128), 384)
        return rows, pl.ds(pl.multiple_of(lax.rem(x, 2) * 384, 128), 384)

    def copies_3(ins, outs):
        here = lax.axis_index("shard")
        out = []
        for step, (x, i) in enumerate(zip(around("shard", 4), around("z", 4))):
            out.append((ins[0].at[:, i], outs[0].at[step], {"z": i}))
            out.append((ins[1].at[:, x], outs[1].at[step], {"shard": x}))
            out.append((ins[2].at[down_shard(x)], outs[2].at[here], {"shard": x}))
        return out

    shapes = [(3, 2, 24, size) for size in sizes] + [(4, 384, 384)]
    *got, down_got = move("other_axis", 3, [*mix, down], shapes, peers_2, copies_3)
    mix = jnp.concatenate(
        [
            total(at(mix[0], z, 1), *got[0]).astype(BF),
            total(at(mix[1], shard, 1), *got[1]).astype(BF),
        ],
        axis=-1,
    )
    rows = [
        lax.dynamic_slice(wide, (shard * 192, 0), (192, 768)),
        lax.dynamic_slice(wide, (768 + shard * 192, 0), (192, 768)),
        lax.dynamic_slice(down, (shard // 2 * 384, shard % 2 * 384), (384, 384)),
    ]
    exp = [
        lax.dynamic_update_index_in_dim(g, o, shard, 0) for g, o in zip((gate, up, down_got), rows)
    ]

    def places():
        here = 2 * lax.axis_index("yh") + lax.axis_index("section")
        there = [lax.rem(here + step, 4) for step in range(1, 4)]
        return [(t // 2, lax.rem(t, 2)) for t in there]

    def copies_4(ins, outs):
        there = other("core")
        out = [
            (ins[1 + k].at[pl.ds(2 * there, 2)], outs[1 + k], {"core": there}) for k in range(3)
        ]
        for step, (y, s) in enumerate(places()):
            out.append((ins[0].at[s, y], outs[0].at[step], {"yh": y, "section": s}))
        return out

    mine = (jnp.arange(2) == yh)[:, None, None]
    pairs = jnp.stack([mix, jnp.where(mine, late[None], jnp.zeros((), BF))])
    got = move(
        "last_axis",
        4,
        [pairs, *exp],
        [(3, 24, width), (2, 192, 768), (2, 192, 768), (2, 384, 384)],
        lambda: [{"yh": y, "section": s} for y, s in places()] + [{"core": other("core")}],
        copies_4,
    )
    sums = total(at(at(pairs, section, 0), yh, 0), *got[0])
    out = []
    for e, g in zip(exp, got[1:]):
        kept = lax.dynamic_slice_in_dim(e, 2 * core, 2, 0)
        low, high = jnp.where(core == 0, kept, g), jnp.where(core == 0, g, kept)
        out.append(jnp.concatenate([low, high], axis=1).astype(F32))
    return sums, out


def gather_weights(local, experts):
    rows, width = local.shape

    def kernel(*refs):
        mine, shards = refs[0], refs[1:4]
        full, late, whole = refs[4], refs[5], refs[6:9]
        stage = refs[9:12]
        sent, got, sent_x, got_e, sent_c, got_c, sent_y, sent_o, local_sem = refs[12:]
        s, yh, z, c, x = (lax.axis_index(a) for a in ("section", "yh", "z", "core", "shard"))
        place = 2 * yh + s
        ys = [lax.rem(place + k, 4) for k in (1, 2, 3)]
        ys = [{"yh": y // 2, "section": lax.rem(y, 2)} for y in ys]
        xs = [{"shard": lax.rem(x + k, 4)} for k in (1, 2, 3)]
        z_up, z_down = lax.rem(z + 1, 4), lax.rem(z + 3, 4)
        sibling, partner = {"core": 1 - c}, {"section": 1 - s}

        def piece(k, i, h):
            if k == 2:
                return shards[2].at[i, pl.ds(pl.multiple_of(h * 384, 128), 384)]
            return shards[k].at[i, pl.ds(pl.multiple_of(h * 192, 64), 192)]

        def landing(k, layer, source, half):
            if k == 2:
                return whole[2].at[layer, half, :, pl.ds(pl.multiple_of(source * 384, 128), 384)]
            return whole[k].at[layer, source, half]

        def remote(source, target, send, receive, device):
            return pltpu.make_async_remote_copy(
                src_ref=source,
                dst_ref=target,
                send_sem=send,
                recv_sem=receive,
                device_id=device,
                device_id_type=pl.DeviceIdType.MESH,
            )

        def start(copies):
            for copy in copies:
                copy.start()
            return copies

        def finish(copies):
            for copy in copies:
                copy.wait()

        has_own = x // 2 == c
        own = lax.rem(x, 2)
        staged = start(
            [pltpu.make_async_copy(piece(k, own, c), stage[k], local_sem.at[k]) for k in range(3)]
        )
        barrier = pltpu.get_barrier_semaphore()
        zs = [{"z": lax.rem(z + k, 4)} for k in (1, 2, 3)]
        x_up, x_down = xs[0]["shard"], xs[2]["shard"]
        near = ys + xs + zs + [sibling]
        near += [{"shard": lax.rem(x + k, 4), "core": 1 - c} for k in (1, 2, 3)]
        for peer in near:
            pl.semaphore_signal(
                barrier, inc=1, device_id=peer, device_id_type=pl.DeviceIdType.MESH
            )
        pl.semaphore_wait(barrier, len(near))

        here = full.at[yh, z, c, x]

        def along_y(target):
            out = [pltpu.make_async_copy(mine, target, local_sem.at[3])]
            for k, device in enumerate(ys):
                out.append(remote(mine, target, sent.at[k], got.at[k], device))
            return out

        @pl.when(s == 0)
        def _():
            start(along_y(here))

        @pl.when(s == 1)
        def _():
            start(along_y(late.at[yh, z, c, x]))

        finish(staged)

        @pl.when(has_own)
        def _():
            for k in range(3):
                remote(
                    piece(k, own, 1 - c),
                    landing(k, s, x, 1 - c),
                    sent_o.at[k],
                    got_e.at[s, x, k],
                    sibling,
                ).start()
                pltpu.make_async_copy(stage[k], landing(k, s, x, c), got_e.at[s, x, k]).start()

        def pass_on(layer, distance, to_partner):
            source = lax.rem(x + distance, 4)
            for k in range(3):
                view = landing(k, layer, source, c)
                receive = got_e.at[layer, source, k]
                remote(view, view, sent_o.at[k], receive, sibling).wait_recv()
                if to_partner:
                    remote(view, view, sent_y.at[distance, k], receive, partner).start()
                across = got_c.at[layer, source, k]
                remote(view, view, sent_c.at[layer, source, k], across, sibling).start()

        finish(along_y(here))
        view, view_late = full.at[:, z, c, x], late.at[:, z, c, x]
        along_x = start(
            [remote(view, view, sent.at[3 + k], got.at[3 + k], xs[k]) for k in range(3)]
        )
        late_z = start(
            [
                remote(view_late, view_late, sent.at[11 + k], got.at[11 + k], zs[k])
                for k in range(3)
            ]
        )
        pass_on(s, 0, True)
        finish(along_x)

        def ring(base, axis, places, up, down):
            return start(
                [
                    remote(up, up, sent.at[base], got.at[base], {axis: places[0]}),
                    remote(down, down, sent.at[base + 1], got.at[base + 1], {axis: places[1]}),
                ]
            )

        view = full.at[:, z, c]
        along_z = ring(6, "z", (z_up, z_down), view, view)
        for i in range(2):

            @pl.when(x != 2 * c + i)
            def _():
                for h in range(2):
                    for k in range(3):
                        remote(
                            piece(k, i, h),
                            landing(k, s, x, h),
                            sent_x.at[(i * 2 + h) * 3 + k],
                            got_e.at[s, x, k],
                            {"shard": 2 * c + i, "core": h},
                        ).start()

        finish(late_z)
        view = late.at[:, :, c, x]
        late_x = ring(14, "shard", (x_up, x_down), view, view)
        finish(along_z)
        along_z = ring(8, "z", (z_up, z_down), full.at[0, z_down, c], full.at[1, z_up, c])
        for distance in (1, 3, 2):
            pass_on(s, distance, True)
        finish(along_z)
        view = full.at[:, :, c]
        across = start([remote(view, view, sent.at[10], got.at[10], sibling)])
        finish(late_x)
        late_x = ring(
            16, "shard", (x_up, x_down), late.at[0, :, c, x_down], late.at[1, :, c, x_up]
        )
        for distance in (0, 1):
            pass_on(1 - s, distance, False)
        finish(late_x)
        view = late.at[:, :, c]
        across += start([remote(view, view, sent.at[18], got.at[18], sibling)])
        for distance in (3, 2):
            pass_on(1 - s, distance, False)

        finish(across)
        for i in range(2):

            @pl.when(x != 2 * c + i)
            def _():
                for h in range(2):
                    for k in range(3):
                        view = piece(k, i, h)
                        n = (i * 2 + h) * 3 + k
                        remote(view, view, sent_x.at[n], got_e.at[0, 0, k], sibling).wait_send()

        @pl.when(has_own)
        def _():
            for k in range(3):
                view = piece(k, own, 1 - c)
                remote(view, view, sent_o.at[k], got_e.at[0, 0, k], sibling).wait_send()

        for source in range(4):
            for k in range(3):
                view = landing(k, s, source, c)
                send = sent_y.at[source, k]
                remote(view, view, send, got_e.at[0, 0, k], partner).wait_send()
                for layer in range(2):
                    view = landing(k, layer, source, c)
                    arrived = landing(k, layer, source, 1 - c)
                    send, receive = sent_c.at[layer, source, k], got_c.at[layer, source, k]
                    remote(view, view, send, receive, sibling).wait_send()
                    remote(arrived, arrived, send, receive, sibling).wait_recv()

    space = pl.BlockSpec(memory_space=pltpu.HBM)
    near_space = pl.BlockSpec(memory_space=pltpu.VMEM)
    shapes = [(2, 4, 2, 4, rows, width)] * 2
    shapes += [(2, 4, 2, 192, 768), (2, 4, 2, 192, 768), (2, 2, 384, 1536)]
    dma = pltpu.SemaphoreType.DMA
    return pl.pallas_call(
        kernel,
        out_shape=[jax.ShapeDtypeStruct(shape, BF) for shape in shapes],
        in_specs=[near_space] + [space] * 3,
        out_specs=[space] * 5,
        scratch_shapes=[
            pltpu.VMEM((192, 768), BF),
            pltpu.VMEM((192, 768), BF),
            pltpu.VMEM((384, 384), BF),
            dma((19,)),
            dma((19,)),
            dma((12,)),
            dma((2, 4, 3)),
            dma((2, 4, 3)),
            dma((2, 4, 3)),
            dma((4, 3)),
            dma((3,)),
            dma((4,)),
        ],
        compiler_params=pltpu.CompilerParams(collective_id=0, has_side_effects=True),
        name="gather_weights",
    )(local, *experts)


def rank_of(route_rows):
    rows = route_rows.shape[0]
    chosen = route_rows.T[None, :, :] == jnp.arange(EXPERTS, dtype=jnp.int32)[:, None, None]
    hot = jnp.any(chosen, axis=1)
    index = jnp.arange(rows, dtype=jnp.int32)
    before = (index[:, None] < index[None, :]).astype(BF)
    return jnp.where(hot, dot(hot.astype(BF), before), -1.0)


def stacked(field):
    return jnp.concatenate(jnp.split(field, CHUNKS, axis=1), axis=0)


def unstacked(field):
    return jnp.concatenate(jnp.split(field, CHUNKS, axis=0), axis=1)


def unfold_table(sources):
    row = jnp.arange(CHUNKS * sources * EXTRA, dtype=jnp.int32)
    piece, source, extra = row // (sources * EXTRA), row // EXTRA % sources, row % EXTRA
    column = jnp.arange(sources * MAIN, dtype=jnp.int32)
    return (
        (source * MAIN + piece * EXTRA + extra)[:, None] == column[None, :]
    ).astype(BF)


def arrived_rows(message, unfold):
    width = message.shape[1] - 256
    extra = unstacked(dot(unfold, message[:, width:]).astype(BF))
    return jnp.concatenate([message[:, :width], extra], axis=0)


def fold_rows(rows, unfold, sources):
    main = rows[: sources * MAIN]
    extra = dot(unfold, stacked(rows[sources * MAIN :]), ((0,), (0,))).astype(BF)
    return jnp.concatenate([main, extra], axis=1)


def low_pair(value):
    high = value.astype(BF)
    return high, (value - high.astype(F32)).astype(BF)


OUT_COLUMNS, QKV_STEP = 1536, 512


def columns(width, place):
    return lambda rows: pl.BlockSpec((rows, width), lambda i: (0, place), memory_space=pltpu.VMEM)


OUT_BLOCK = [columns(OUT_COLUMNS, 0)]
QKV_BLOCKS = [columns(QKV_STEP, 3 + k) for k in range(4)]
NARROW_BLOCK = [columns(128, 28)]


def fused(name, body, shapes, *arrays, scratch=(), number=None):
    near = pl.BlockSpec(memory_space=pltpu.VMEM)
    specs, given = [], []
    for array in arrays:
        if isinstance(array, tuple):
            array, blocks = array
            specs += [block(array.shape[0]) for block in blocks]
            given += [array] * len(blocks)
        else:
            specs.append(near)
            given.append(array)
    return pl.pallas_call(
        body,
        grid=(1,),
        out_shape=[jax.ShapeDtypeStruct(shape, kind) for shape, kind in shapes],
        in_specs=specs,
        out_specs=[near] * len(shapes),
        scratch_shapes=list(scratch),
        compiler_params=pltpu.CompilerParams(
            vmem_limit_bytes=48 << 20, collective_id=number, has_side_effects=number is not None
        ),
        name=name,
    )(*given)


TN, NT = ((0,), (0,)), ((1,), (1,))


def slots(rank):
    count, rows = rank.shape
    place = lax.broadcasted_iota(jnp.int32, (count, MAIN, rows), 1)
    wide = jnp.broadcast_to(rank[:, None, :], (count, MAIN, rows))
    main = jnp.where(wide == place.astype(F32), 1.0, 0.0)
    extra = (MAIN + lax.rem(place, EXTRA)).astype(F32)
    extra = jnp.where((wide == extra) & (place < EXTRA * CHUNKS), 1.0, 0.0)
    return main, extra


def per_piece(table):
    piece = lax.rem(lax.broadcasted_iota(jnp.int32, table.shape, 0), MAIN) // EXTRA
    return [jnp.where(piece == j, table, 0.0) for j in range(CHUNKS)]


def flat(table):
    return table.reshape(table.shape[0] * table.shape[1], table.shape[2])


def send_table(main, extra, field):
    width = field.shape[1] // CHUNKS
    side = None
    for j, table in enumerate(per_piece(flat(extra))):
        part = dot(table.astype(BF), field[:, j * width : (j + 1) * width])
        side = part if side is None else side + part
    return dot(flat(main).astype(BF), field), side


def bring_back(main, extra, rows, exact):
    parts = low_pair if exact else (lambda t: (t.astype(BF),))
    model_width = rows.shape[1] - 256
    total_main = None
    for table in parts(main):
        part = dot(table, rows[:, :model_width], TN)
        total_main = part if total_main is None else total_main + part
    side = []
    for table in per_piece(extra):
        total_side = None
        for t in parts(table):
            part = dot(t, rows[:, model_width:], TN)
            total_side = part if total_side is None else total_side + part
        side.append(total_side)
    return total_main + jnp.concatenate(side, axis=1)


def gain_rows(narrow):
    row = lax.broadcasted_iota(jnp.int32, (8, narrow.shape[1]), 0)
    column = lax.broadcasted_iota(jnp.int32, (8, narrow.shape[1]), 1)
    pick = jnp.where(column == row + EXPERTS, 1.0, 0.0).astype(BF)
    rows = dot(pick, narrow, NT)
    return rows[0:1], rows[1:2]


def turn(field, cosine, sine):
    return field * cosine + pltpu.roll(field, HEAD_DIM // 2, 1) * sine


def turn_back(field, cosine, sine):
    return field * cosine - pltpu.roll(field, HEAD_DIM // 2, 1) * sine


def combined(x_mid, rank, gates, rows):
    main, extra = slots(rank)
    wide = jnp.broadcast_to(gates[:, None, :], main.shape)
    return x_mid + bring_back(flat(main * wide), flat(extra * wide), rows, True)


def finish_body(mid_ref, rank_ref, gates_ref, rows_ref, out_ref):
    out = combined(mid_ref[...], rank_ref[...], gates_ref[...], rows_ref[...])
    out_ref[...] = out.astype(BF)


def heads_of(kv_ref):
    kv_heads = kv_ref.shape[2] // 2 // HEAD_DIM
    parts = []
    for k in range(2 * kv_heads):
        part = kv_ref[:, :, k * HEAD_DIM : (k + 1) * HEAD_DIM]
        parts.append(part.reshape(part.shape[0] * part.shape[1], HEAD_DIM))
    return parts[:kv_heads], parts[kv_heads:]


def attention_body(combine):
    def body(*refs):
        source, refs = refs[: 4 if combine else 1], refs[4 if combine else 1 :]
        weights, refs = refs[:4], refs[4:]
        out_w, narrow, cos_ref, sin_ref, allowed_ref, rank_ref, low_ref, h_ref, q_ref = refs[:9]
        kv_ref, mid_ref, h2_ref, att_ref, probs_ref, gates_ref, out_ref, held, sent, got = refs[9:]
        here = lax.axis_index("shard")
        peers = [{"shard": x} for x in around("shard", 4)]
        barrier = pltpu.get_barrier_semaphore()
        for peer in peers:
            pl.semaphore_signal(
                barrier, inc=1, device_id=peer, device_id_type=pl.DeviceIdType.MESH
            )
        if combine:
            mid, rank, gates, rows = (ref[...] for ref in source)
            low = combined(mid, rank, gates, rows).astype(BF)
        else:
            low = source[0][...]
        low_ref[...] = low
        field = low.astype(F32)
        gain_a, gain_m = gain_rows(narrow[...])
        scale = lax.rsqrt(jnp.mean(field * field, axis=1, keepdims=True) + epsilon)
        h = (field * scale * gain_a).astype(BF)
        h_ref[...] = h
        cosine, sine = cos_ref[...], sin_ref[...]

        def projected(column, turned):
            inside = column % QKV_STEP
            part = dot(h, weights[column // QKV_STEP][:, inside : inside + 256])
            if turned:
                part = jnp.concatenate(
                    [turn(part[:, k : k + HEAD_DIM], cosine, sine) for k in (0, HEAD_DIM)], axis=1
                )
            return part.astype(BF)

        query_width, kv_width = q_ref.shape[1], kv_ref.shape[2]
        for column in range(0, kv_width, 256):
            part = projected(query_width + column, column < kv_width // 2)
            held[here, :, column : column + 256] = part
        pl.semaphore_wait(barrier, len(peers))
        copies = []
        for k, peer in enumerate(peers):
            view = held.at[here]
            copies.append(
                pltpu.make_async_remote_copy(
                    src_ref=view,
                    dst_ref=view,
                    send_sem=sent.at[k],
                    recv_sem=got.at[k],
                    device_id=peer,
                    device_id_type=pl.DeviceIdType.MESH,
                )
            )
            copies[-1].start()
        for column in range(0, query_width, 256):
            q_ref[:, column : column + 256] = projected(column, True)
        for copy in copies:
            copy.wait()

        kv_ref[...] = held[...]
        keys, values = heads_of(held)
        allowed = allowed_ref[...] > 0.0
        ratio = HEADS // len(keys)
        for head in range(HEADS):
            lanes = slice(head * HEAD_DIM, (head + 1) * HEAD_DIM)
            scores = dot(q_ref[:, lanes], keys[head // ratio], NT) * HEAD_DIM ** (-0.5)
            scores = jnp.where(allowed, scores, masked_score)
            exponent = jnp.exp(scores - jnp.max(scores, axis=1, keepdims=True))
            probs = exponent / jnp.sum(exponent, axis=1, keepdims=True)
            probs_ref[head] = probs
            att_ref[:, lanes] = dot(probs.astype(BF), values[head // ratio]).astype(BF)
        mid = field + dot(att_ref[...], out_w[...])
        mid_ref[...] = mid
        scale = lax.rsqrt(jnp.mean(mid * mid, axis=1, keepdims=True) + epsilon)
        h2 = (mid * scale * gain_m).astype(BF)
        h2_ref[...] = h2
        rank = rank_ref[...]
        logits = jnp.transpose(dot(h2, narrow[...]))[:EXPERTS]
        logits = jnp.where(rank >= 0.0, logits, masked_score)
        gate_exp = jnp.exp(logits - jnp.max(logits, axis=0, keepdims=True))
        gate_exp = jnp.where(rank >= 0.0, gate_exp, 0.0)
        gates_ref[...] = gate_exp / jnp.sum(gate_exp, axis=0, keepdims=True)
        main, side = send_table(*slots(rank), h2)
        width = main.shape[1]
        out_ref[:, :width] = main.astype(BF)
        out_ref[:, width:] = side.astype(BF)

    return body


def attention(source, weights, tables, allowed, rank, number):
    tok_rows, model_width = source[0].shape
    query_width = HEADS * HEAD_DIM
    shapes = [((tok_rows, model_width), BF)] * 2
    shapes += [
        ((tok_rows, query_width), BF),
        ((allowed.shape[1] // tok_rows, tok_rows, 4 * QKV_STEP - query_width), BF),
        ((tok_rows, model_width), F32),
        ((tok_rows, model_width), BF),
        ((tok_rows, query_width), BF),
        ((HEADS, tok_rows, allowed.shape[1]), F32),
        (rank.shape, F32),
        ((EXPERTS * MAIN, model_width + 256), BF),
    ]
    dma = pltpu.SemaphoreType.DMA
    return fused(
        "attention",
        attention_body(len(source) > 1),
        shapes,
        *source,
        (weights, QKV_BLOCKS + OUT_BLOCK + NARROW_BLOCK),
        *tables,
        allowed,
        rank,
        scratch=[pltpu.VMEM(shapes[3][0], BF), dma((3,)), dma((3,))],
        number=number,
    )


def grad_slots_body(grad_ref, rank_ref, gates_ref, rows_ref, out_ref, dlogits_ref):
    gates = gates_ref[...]
    main, extra = slots(rank_ref[...])
    wide = jnp.broadcast_to(gates[:, None, :], main.shape)
    grad_main, grad_side = send_table(main, extra, grad_ref[...])
    width = grad_main.shape[1]
    dgate = None
    for table, grad, columns in (
        (main, grad_main, slice(0, width)),
        (extra, grad_side, slice(width, width + 256)),
    ):
        slot_gate = jnp.sum(flat(table * wide), axis=1, keepdims=True)
        out_ref[:, columns] = (grad * slot_gate).astype(BF)
        slot_dgate = jnp.sum(grad * rows_ref[:, columns].astype(F32), axis=1, keepdims=True)
        part = jnp.sum((flat(table) * slot_dgate).reshape(table.shape), axis=1)
        dgate = part if dgate is None else dgate + part
    dlogits = gates * (dgate - jnp.sum(gates * dgate, axis=0, keepdims=True))
    pad = jnp.zeros((dlogits_ref.shape[1] - EXPERTS, dlogits.shape[1]), F32)
    dlogits_ref[...] = jnp.transpose(jnp.concatenate([dlogits, pad], axis=0)).astype(BF)


def grad_slots(grad, rank, gates, rows):
    shapes = [(rows.shape, BF), ((grad.shape[0], 128), BF)]
    return fused("grad_slots", grad_slots_body, shapes, grad, rank, gates, rows)


def norm_grads(field, gain, grad):
    scale = lax.rsqrt(jnp.mean(field * field, axis=1, keepdims=True) + epsilon)
    scaled = grad * gain
    centre = jnp.mean(scaled * field, axis=1, keepdims=True)
    dgain = jnp.sum(grad * field * scale, axis=0, keepdims=True)
    return scale * scaled - field * (scale * scale * scale) * centre, dgain


def grad_attention_body(
    grad_ref, rows_ref, rank_ref, dlogits_ref, out_w, weight_0, weight_1, weight_2, weight_3, narrow,
    mid_ref, q_ref, kv_ref, probs_ref, cos_ref, sin_ref, low_ref,
    dbr_ref, dqkv_ref, grad_out_ref, dgain_a_ref, dgain_m_ref,
    datt_ref, dkv_ref, held, sent, got,
):
    here = lax.axis_index("shard")
    peers = [{"shard": x} for x in around("shard", 4)]
    barrier = pltpu.get_barrier_semaphore()
    for peer in peers:
        pl.semaphore_signal(barrier, inc=1, device_id=peer, device_id_type=pl.DeviceIdType.MESH)
    main, extra = slots(rank_ref[...])
    dh = bring_back(flat(main), flat(extra), rows_ref[...], False)
    dh = dh + dot(dlogits_ref[...], narrow[...], NT)
    gain_a, gain_m = gain_rows(narrow[...])
    dmid, dgain = norm_grads(mid_ref[...], gain_m, dh)
    dmid = dmid + grad_ref[...].astype(F32)
    dgain_m_ref[...] = dgain
    dbr_ref[...] = dmid.astype(BF)
    datt_ref[...] = dot(dbr_ref[...], out_w[...], NT).astype(BF)
    keys, values = heads_of(kv_ref)
    ratio = HEADS // len(keys)
    cosine, sine = cos_ref[...], sin_ref[...]
    count, tok_rows, kv_columns = kv_ref.shape
    scale = HEAD_DIM ** (-0.5)
    for k in range(len(keys)):
        dkey, dvalue = None, None
        for head in range(k * ratio, (k + 1) * ratio):
            lanes = slice(head * HEAD_DIM, (head + 1) * HEAD_DIM)
            probs, datt = probs_ref[head], datt_ref[:, lanes]
            dprobs = dot(datt, values[k], NT)
            centre = jnp.sum(dprobs * probs, axis=1, keepdims=True)
            dscores = (probs * (dprobs - centre)).astype(BF)
            part = dot(probs.astype(BF), datt, TN)
            dvalue = part if dvalue is None else dvalue + part
            part = dot(dscores, q_ref[:, lanes], TN)
            dkey = part if dkey is None else dkey + part
            dquery = dot(dscores, keys[k]) * scale
            dqkv_ref[:, lanes] = turn_back(dquery, cosine, sine).astype(BF)
        at_key, at_value = k * HEAD_DIM, (len(keys) + k) * HEAD_DIM
        shape = (count, tok_rows, HEAD_DIM)
        dkv_ref[:, :, at_key : at_key + HEAD_DIM] = (dkey * scale).astype(BF).reshape(shape)
        dkv_ref[:, :, at_value : at_value + HEAD_DIM] = dvalue.astype(BF).reshape(shape)
    pl.semaphore_wait(barrier, len(peers))
    copies = []
    for k, peer in enumerate(peers):
        copies.append(
            pltpu.make_async_remote_copy(
                src_ref=dkv_ref.at[peer["shard"]],
                dst_ref=held.at[k],
                send_sem=sent.at[k],
                recv_sem=got.at[k],
                device_id=peer,
                device_id_type=pl.DeviceIdType.MESH,
            )
        )
        copies[-1].start()
    query_width = q_ref.shape[1]
    dh = None
    weights = (weight_0, weight_1, weight_2, weight_3)
    for k, weight in enumerate(weights[:-1]):
        part = dot(dqkv_ref[:, k * QKV_STEP : (k + 1) * QKV_STEP], weight[...], NT)
        dh = part if dh is None else dh + part
    for copy in copies:
        copy.wait()
    dkv = dkv_ref[here].astype(F32)
    for k in range(len(peers)):
        dkv = dkv + held[k].astype(F32)
    for k in range(0, kv_columns // 2, HEAD_DIM):
        part = turn_back(dkv[:, k : k + HEAD_DIM], cosine, sine)
        dqkv_ref[:, query_width + k : query_width + k + HEAD_DIM] = part.astype(BF)
    dqkv_ref[:, query_width + kv_columns // 2 :] = dkv[:, kv_columns // 2 :].astype(BF)
    dh = dh + dot(dqkv_ref[:, query_width:], weights[-1][...], NT)
    dlow, dgain = norm_grads(low_ref[...].astype(F32), gain_a, dh)
    dgain_a_ref[...] = dgain
    grad_out_ref[...] = (dlow + dmid).astype(BF)


def grad_attention(
    grad, rows, rank, dlogits, weights, mid, q, kv, probs, tables, low, number
):
    tok_rows, model_width = mid.shape
    shapes = [
        ((tok_rows, model_width), BF),
        ((tok_rows, 4 * QKV_STEP), BF),
        ((tok_rows, model_width), BF),
        ((1, model_width), F32),
        ((1, model_width), F32),
    ]
    dma = pltpu.SemaphoreType.DMA
    return fused(
        "grad_attention",
        grad_attention_body,
        shapes,
        grad,
        rows,
        rank,
        dlogits,
        (weights, OUT_BLOCK + QKV_BLOCKS + NARROW_BLOCK),
        mid,
        q,
        kv,
        probs,
        *tables,
        low,
        scratch=[
            pltpu.VMEM(q.shape, BF),
            pltpu.VMEM(kv.shape, BF),
            pltpu.VMEM((3, *kv.shape[1:]), BF),
            dma((3,)),
            dma((3,)),
        ],
        number=number,
    )


def weight_grads_body(
    h_ref, dqkv_ref, att_ref, dbr_ref, h2_ref, dlogits_ref, dgain_a_ref, dgain_m_ref, out_ref
):
    step = 512
    place = 0
    for left, right in ((att_ref, dbr_ref), (h_ref, dqkv_ref)):
        for k in range(0, right.shape[1], step):
            part = dot(left[...], right[:, k : k + step], TN)
            out_ref[:, place : place + step] = part.astype(BF)
            place += step
    narrow = dot(h2_ref[...], dlogits_ref[...], TN)
    rows = jnp.concatenate(
        [dgain_a_ref[...], dgain_m_ref[...], jnp.zeros((126, h_ref.shape[1]), F32)], axis=0
    )
    columns = pltpu.roll(jnp.transpose(rows), EXPERTS, 1)
    out_ref[:, place:] = (narrow + columns).astype(BF)


def weight_grads(h, dqkv, att, dbr, h2, dlogits, dgain_a, dgain_m):
    columns = dqkv.shape[1] + dbr.shape[1] + 128
    return fused(
        "weight_grads", weight_grads_body, [((h.shape[1], columns), BF)],
        h, dqkv, att, dbr, h2, dlogits, dgain_a, dgain_m,
    )[0]


def greet(peers):
    barrier = pltpu.get_barrier_semaphore()
    for peer in peers:
        pl.semaphore_signal(barrier, inc=1, device_id=peer, device_id_type=pl.DeviceIdType.MESH)
    pl.semaphore_wait(barrier, len(peers))


PARTNERS = [(dy, dz, (dz + k) % 4) for k in range(4) for dy in range(2) for dz in range(4)]
GROUP = 8
GROUPS = len(PARTNERS) // GROUP


def facing(n):
    k, dy, dz = n // GROUP, n // 4 % 2, n % 4
    return -k % GROUPS * GROUP + dy * 4 + -dz % 4


def partners():
    s, yh, z, x = (lax.axis_index(a) for a in ("section", "yh", "z", "shard"))
    out = []
    for dy, dz, dx in PARTNERS:
        there = {
            "section": lax.rem(s + dy, 2),
            "yh": lax.rem(yh + dy, 2),
            "z": lax.rem(z + dz, 4),
            "shard": lax.rem(x + dx, 4),
        }
        out.append((there, (there["yh"] * 4 + there["z"]) * 4 + there["shard"]))
    return out


def exchange_rows(message, returned, arrived, produced, sems, work, after, load, sibling=()):
    sent, got, sent_back, got_back = sems
    for copy in load:
        copy.start()
    near = partners()
    own = near[0][1]
    greet([device for device, _ in near[1:]] + list(sibling))

    def remote(source, target, send, receive, device):
        return pltpu.make_async_remote_copy(
            src_ref=source,
            dst_ref=target,
            send_sem=send,
            recv_sem=receive,
            device_id=device,
            device_id_type=pl.DeviceIdType.MESH,
        )

    def out(n):
        device, expert = near[n]
        f = facing(n)
        return remote(message.at[expert], arrived.at[f], sent.at[n], got.at[f], device)

    def back(n):
        return remote(
            produced.at[n], returned.at[own], sent_back.at[n], got_back.at[facing(n)], near[n][0]
        )

    for k in range(GROUPS):
        for n in range(-k % GROUPS * GROUP, -k % GROUPS * GROUP + GROUP):
            if n:
                out(n).start()
    arrived[0] = message[own]
    for copy in load:
        copy.wait()
    for k in range(GROUPS):
        members = range(k * GROUP, (k + 1) * GROUP)
        for n in members:
            if n:
                remote(arrived.at[n], arrived.at[n], sent.at[n], got.at[n], near[n][0]).wait_recv()
        rows = arrived[k * GROUP : (k + 1) * GROUP]
        result = work(k, rows.reshape(GROUP * MAIN, rows.shape[2]))
        produced[k * GROUP : (k + 1) * GROUP] = result.reshape(rows.shape)
        for n in members:
            if n:
                back(n).start()
    returned[own] = produced[0]
    after()
    for n in range(1, len(near)):
        device, expert = near[n]
        out(n).wait_send()
        back(n).wait_send()
        view = returned.at[expert]
        remote(view, view, sent_back.at[n], got_back.at[n], device).wait_recv()


def exchange_call(name, number, body, inputs, whole, shapes, message_shape, scratch):
    near = pl.BlockSpec(memory_space=pltpu.VMEM)
    far = pl.BlockSpec(memory_space=pltpu.HBM)
    dma = pltpu.SemaphoreType.DMA
    count = message_shape[0]
    return pl.pallas_call(
        body,
        out_shape=[jax.ShapeDtypeStruct(shape, kind) for shape, kind in shapes],
        in_specs=[far] * len(whole) + [near] * len(inputs),
        out_specs=[near] * len(shapes),
        scratch_shapes=[pltpu.VMEM(w.shape[1:], BF) for w in whole]
        + [dma((len(whole),))]
        + [pltpu.VMEM(message_shape, BF), pltpu.VMEM(message_shape, BF)]
        + [dma((count,)) for _ in range(4)]
        + scratch,
        compiler_params=pltpu.CompilerParams(
            collective_id=number, has_side_effects=True, vmem_limit_bytes=56 << 20
        ),
        name=name,
    )(*whole, *inputs)


def loads(whole, layer, held, sem):
    copies = [pltpu.make_async_copy(w.at[layer], h, sem.at[k]) for k, (w, h) in enumerate(zip(whole, held))]

    def matrix(k):
        value = held[k][...]
        return value.reshape(-1, value.shape[-1])

    return copies, matrix


def expert_forward(message, experts, layer, unfold, number):
    message = message.reshape(EXPERTS, MAIN, message.shape[1])
    rows = GROUP * (MAIN + EXTRA)
    depth, width = message.shape[2] - 256, experts[0].shape[-1]

    def body(*refs):
        whole, (message_ref, unfold_ref), refs = refs[:3], refs[3:5], refs[5:]
        returned, rows_ref, gate_ref, up_ref, hidden_ref = refs[:5]
        load, matrix = loads(whole, layer, refs[5:8], refs[8])
        arrived, produced, *sems = refs[9:]

        def work(k, came):
            field = arrived_rows(came, unfold_ref[...])
            rows_ref[k] = field
            gate = dot(field, matrix(0))
            up = dot(field, matrix(1))
            gate_ref[k] = gate
            up_ref[k] = up
            hidden = (gate / (1.0 + jnp.exp(-gate)) * up).astype(BF)
            hidden_ref[k] = hidden
            return fold_rows(dot(hidden, matrix(2)).astype(BF), unfold_ref[...], GROUP)

        exchange_rows(message_ref, returned, arrived, produced, sems, work, lambda: None, load)

    shapes = [
        (message.shape, BF),
        ((GROUPS, rows, depth), BF),
        ((GROUPS, rows, width), F32),
        ((GROUPS, rows, width), F32),
        ((GROUPS, rows, width), BF),
    ]
    returned, *kept = exchange_call(
        "expert_forward", number, body, [message, unfold], experts, shapes, message.shape, []
    )
    return returned.reshape(-1, message.shape[2]), kept


def expert_backward(message, experts, layer, kept, unfold, number):
    message = message.reshape(EXPERTS, MAIN, message.shape[1])
    rows = GROUP * (MAIN + EXTRA)
    depth, width = message.shape[2] - 256, experts[0].shape[-1]
    shards = 4
    half, deep = depth // 8, width // 2

    def body(*refs):
        whole, refs = refs[:3], refs[3:]
        message_ref, rows_ref, gate_ref, up_ref, hidden_ref, unfold_ref = refs[:6]
        returned, sum_ref, sum_down_ref = refs[6:9]
        load, matrix = loads(whole, layer, refs[9:12], refs[12])
        (arrived, produced), refs = refs[13:15], refs[15:]
        sems, (came_ref, dgate_ref, dup_ref) = refs[:4], refs[4:7]
        wide_refs, (down_ref, held_gate, held_up, held_down, sent, got) = refs[7:9], refs[9:]
        core = lax.axis_index("core")
        sibling = {"core": 1 - core}

        def work(k, came):
            field = arrived_rows(came, unfold_ref[...])
            came_ref[k] = field
            dhidden = dot(field, matrix(2), NT)
            gate = gate_ref[k]
            logistic = 1.0 / (1.0 + jnp.exp(-gate))
            dgate = dhidden * up_ref[k] * (logistic * (1.0 + gate * (1.0 - logistic)))
            dgate_ref[k] = dgate.astype(BF)
            dup_ref[k] = (dhidden * (gate * logistic)).astype(BF)
            out = dot(dgate_ref[k], matrix(0), NT) + dot(dup_ref[k], matrix(1), NT)
            return fold_rows(out.astype(BF), unfold_ref[...], GROUP)

        def to_sibling(k):
            views = [wide_refs[0].at[:, 1 - core], wide_refs[1].at[:, 1 - core]]
            views.append(down_ref.at[1 - core])
            return pltpu.make_async_remote_copy(
                src_ref=views[k],
                dst_ref=(held_gate, held_up, held_down)[k],
                send_sem=sent.at[k],
                recv_sem=got.at[k],
                device_id=sibling,
                device_id_type=pl.DeviceIdType.MESH,
            )

        def after():
            step = 256
            field = rows_ref[...].reshape(GROUPS * rows, depth)
            for k, source in enumerate((dgate_ref, dup_ref)):
                for column in range(0, width, step):
                    lanes = slice(column, column + step)
                    part = source[:, :, lanes].reshape(GROUPS * rows, step)
                    part = dot(field, part, TN).astype(BF)
                    wide_refs[k][:, :, :, lanes] = part.reshape(shards, 2, half, step)
                to_sibling(k).start()
            field = hidden_ref[...].reshape(GROUPS * rows, width)
            for column in range(0, depth, step):
                lanes = slice(column, column + step)
                part = came_ref[:, :, lanes].reshape(GROUPS * rows, step)
                part = dot(field, part, TN).astype(BF)
                down_ref[:, :, lanes] = part.reshape(2, deep, step)
            to_sibling(2).start()

        exchange_rows(
            message_ref, returned, arrived, produced, sems, work, after, load, (sibling,)
        )
        for k, held in enumerate((held_gate, held_up)):
            to_sibling(k).wait()
            for j in range(shards):
                part = wide_refs[k][j, core].astype(F32) + held[j].astype(F32)
                place = (k * shards + j) * half
                sum_ref[place : place + half] = part.astype(BF)
        to_sibling(2).wait()
        part = down_ref[core].astype(F32) + held_down[...].astype(F32)
        for j in range(2):
            columns_of = part[:, j * width : (j + 1) * width].astype(BF)
            sum_down_ref[j * deep : (j + 1) * deep] = columns_of

    shapes = [(message.shape, BF), ((2 * shards * half, width), BF), ((2 * deep, width), BF)]
    dma = pltpu.SemaphoreType.DMA
    scratch = [
        pltpu.VMEM((GROUPS, rows, depth), BF),
        pltpu.VMEM((GROUPS, rows, width), BF),
        pltpu.VMEM((GROUPS, rows, width), BF),
        pltpu.VMEM((shards, 2, half, width), BF),
        pltpu.VMEM((shards, 2, half, width), BF),
        pltpu.VMEM((2, deep, depth), BF),
        pltpu.VMEM((shards, half, width), BF),
        pltpu.VMEM((shards, half, width), BF),
        pltpu.VMEM((deep, depth), BF),
        dma((3,)),
        dma((3,)),
    ]
    returned, *sums = exchange_call(
        "expert_backward",
        number,
        body,
        [message, *kept, unfold],
        experts,
        shapes,
        message.shape,
        scratch,
    )
    return returned.reshape(-1, message.shape[2]), sums


def forward_layer(source, weights, experts, layer, rank, unfold, tables, allowed, numbers):
    low, h_attn, query, kv_all, x_mid, h_moe, attended, probs, gates, message = attention(
        source, weights, tables, allowed, rank, numbers[0]
    )
    returned, kept = expert_forward(message, experts, layer, unfold, numbers[1])
    stored = {
        "low": low,
        "h_attn": h_attn,
        "query": query,
        "kv_all": kv_all,
        "probs": probs,
        "attended": attended,
        "x_mid": x_mid,
        "h_moe": h_moe,
        "gates": gates,
        "returned": returned,
        "kept": kept,
    }
    return (x_mid, rank, gates, returned), stored


def backward_layer(grad, ready, stored, weights, experts, layer, rank, unfold, tables, numbers):
    message, dlogits = grad_slots(grad, rank, stored["gates"], stored["returned"])
    returned, halves = expert_backward(
        message, experts, layer, stored["kept"], unfold, numbers[0]
    )
    dbr, dqkv, grad_in, dgain_a, dgain_m = grad_attention(
        grad, returned, rank, dlogits, weights, stored["x_mid"], stored["query"], stored["kv_all"],
        stored["probs"], tables, stored["low"], numbers[1],
    )
    dqkv, *ready = lax.optimization_barrier((dqkv, *ready))
    grads = weight_grads(
        stored["h_attn"], dqkv, stored["attended"], dbr, stored["h_moe"], dlogits, dgain_a, dgain_m
    )
    return grad_in, grads, halves, ready


def per_device(
    tokens,
    routes,
    lengths,
    gain_attn,
    w_query,
    w_key,
    w_value,
    w_out,
    gain_moe,
    w_router,
    w_gate,
    w_up,
    w_down,
    cotangent,
):
    section, yh, z, core, shard = (
        lax.axis_index(a) for a in ("section", "yh", "z", "core", "shard")
    )
    first = section == 0
    tok_rows, model_width = tokens.shape[1:]
    group_rows = tok_rows * lax.axis_size("shard")

    def mine(a):
        return lax.dynamic_index_in_dim(a, section, 0, keepdims=False)

    def by_layer(own, other):
        return jnp.where(first, own, other), jnp.where(first, other, own)

    local = jnp.concatenate(
        [
            w_out[0],
            w_query[0],
            w_key[0],
            w_value[0],
            w_router[0],
            gain_attn[0][:, None],
            gain_moe[0][:, None],
            jnp.zeros((w_query.shape[1], 94), BF),
        ],
        axis=1,
    )
    full, late, *whole = gather_weights(local, (w_gate[0], w_up[0], w_down[0]))
    weights = [full.reshape(model_width, -1), late.reshape(model_width, -1)]
    route_other = swap(at(routes[0], 1 - section, 0), "section")
    ranks = [rank_of(r) for r in by_layer(mine(routes[0]), route_other)]
    unfold = unfold_table(GROUP)

    segment, position = document_layout(mine(lengths[:, 0]), group_rows)
    row_start = shard * tok_rows
    own_segment = lax.dynamic_slice_in_dim(segment, row_start, tok_rows)
    tables = rotary_tables(lax.dynamic_slice_in_dim(position, row_start, tok_rows), HEAD_DIM)
    query_index = row_start + jnp.arange(tok_rows, dtype=jnp.int32)
    allowed = (own_segment[:, None] == segment[None, :]) & (
        query_index[:, None] >= jnp.arange(group_rows, dtype=jnp.int32)[None, :]
    )
    allowed = allowed.astype(F32)

    source, saved = (mine(tokens),), []
    for layer in range(2):
        source, stored = forward_layer(
            source, weights[layer], whole, layer, ranks[layer], unfold, tables, allowed,
            (7 + layer, 11 + layer),
        )
        saved.append(stored)
    low = fused("finish", finish_body, [((tok_rows, model_width), BF)], *source)[0]
    grad, low = lax.optimization_barrier((mine(cotangent), low))
    away = swap(low, "section")

    sums, ready = [None, None], (away,)
    for layer in (1, 0):
        grad, mixer_grad, halves, ready = backward_layer(
            grad,
            ready,
            saved[layer],
            weights[layer],
            whole,
            layer,
            ranks[layer],
            unfold,
            tables,
            (5 + layer, 9 + layer),
        )
        given = [lax.ppermute(half, "section", [(1 - layer, layer)]) for half in halves]
        sums[layer] = list(zip(halves, given))
        if layer == 1:
            (away,), ready = ready, given
            late = lax.psum_scatter(mixer_grad, DEVICES, scatter_dimension=0, tiled=True)
            late = lax.optimization_barrier(late)
    mixed = jnp.where(first, jnp.stack([low, away]), jnp.stack([away, low]))

    def finish_experts(k):
        return jnp.where(first, total(*sums[0][k]), total(sums[1][k][0], ready[k])).astype(BF)

    mix, (grad_gate, grad_up, grad_down) = reduce_all(mixer_grad, late, finish_experts)
    return (
        mixed,
        grad[None],
        mix[:, 3616][None],
        mix[:, 1536:3072][None],
        mix[:, 3072:3328][None],
        mix[:, 3328:3584][None],
        mix[:, :1536][None],
        mix[:, 3617][None],
        mix[:, 3584:3616][None],
        grad_gate[None],
        grad_up[None],
        grad_down[None],
    )


def solution(mesh):
    fine = Mesh(mesh.devices.reshape(2, 2, 4, 2, 4), ("section", *DEVICES))
    expert = ("yh", "z", "core")
    return jax.shard_map(
        per_device,
        mesh=fine,
        in_specs=(
            P(None, DEVICES, None),
            P("section", None, DEVICES, None),
            P(None, expert, None),
            P("section", DEVICES),
            P("section", DEVICES, None),
            P("section", DEVICES, None),
            P("section", DEVICES, None),
            P("section", DEVICES, None),
            P("section", DEVICES),
            P("section", DEVICES, None),
            P("section", expert, "shard", None),
            P("section", expert, "shard", None),
            P("section", expert, None, "shard"),
            P(None, DEVICES, None),
        ),
        out_specs=(
            P(None, DEVICES, None),
            P("section", DEVICES, None),
            P("section", DEVICES),
            P("section", DEVICES, None),
            P("section", DEVICES, None),
            P("section", DEVICES, None),
            P("section", DEVICES, None),
            P("section", DEVICES),
            P("section", DEVICES, None),
            P("section", expert, "shard", None),
            P("section", expert, "shard", None),
            P("section", expert, None, "shard"),
        ),
        check_vma=False,
    )
```

```python
import jax
import jax.numpy as jnp
from jax import lax
from jax.experimental import pallas as pl
from jax.experimental.pallas import tpu as pltpu
from jax.sharding import Mesh
from jax.sharding import PartitionSpec as P

HEADS = 12
HEAD_DIM = 128
EXPERTS = 32
MAIN = 16
EXTRA = 2
CHUNKS = 6

epsilon = 1e-06
rope_base = 1000000.0
masked_score = -1e30

BF = jnp.bfloat16
F32 = jnp.float32
CHIPS = ("yh", "z", "shard")
DEVICES = ("yh", "z", "core", "shard")


def dot(a, b, dims=((1,), (0,))):
    return lax.dot_general(a, b, (dims, ((), ())), preferred_element_type=F32)


def document_layout(doc_lengths, group_rows):
    doc_ends = jnp.cumsum(doc_lengths)
    starts = doc_ends - doc_lengths
    row_index = jnp.arange(group_rows, dtype=jnp.int32)
    segment = jnp.sum((row_index[:, None] >= doc_ends[None, :]).astype(jnp.int32), axis=1)
    member = segment[:, None] == jnp.arange(doc_lengths.shape[0], dtype=jnp.int32)[None, :]
    position = row_index - jnp.sum(jnp.where(member, starts[None, :], 0), axis=1)
    return (segment, position)


def rotary_tables(position, head_size):
    half_dim = head_size // 2
    frequency = rope_base ** (-2.0 * jnp.arange(half_dim, dtype=F32) / head_size)
    angles = position.astype(F32)[:, None] * frequency[None, :]
    cosine, sine = jnp.cos(angles), jnp.sin(angles)
    return jnp.concatenate([cosine, cosine], axis=1), jnp.concatenate([-sine, sine], axis=1)


def swap(value, axis):
    return lax.ppermute(value, axis, [(0, 1), (1, 0)])


def around(axis, size):
    here = lax.axis_index(axis)
    return [lax.rem(here + step, size) for step in range(1, size)]


def move(name, number, arrays, shapes, peers, copies):
    count = len(arrays)
    total = 40

    def kernel(*refs):
        ins, outs = refs[:count], refs[count : count + len(shapes)]
        sent, got = refs[count + len(shapes) :]
        barrier = pltpu.get_barrier_semaphore()
        near = peers()
        for peer in near:
            pl.semaphore_signal(
                barrier, inc=1, device_id=peer, device_id_type=pl.DeviceIdType.MESH
            )
        pl.semaphore_wait(barrier, len(near))
        started = []
        for k, (source, target, device) in enumerate(copies(ins, outs)):
            if device is None:
                copy = pltpu.make_async_copy(source, target, got.at[k])
            else:
                copy = pltpu.make_async_remote_copy(
                    src_ref=source,
                    dst_ref=target,
                    send_sem=sent.at[k],
                    recv_sem=got.at[k],
                    device_id=device,
                    device_id_type=pl.DeviceIdType.MESH,
                )
            copy.start()
            started.append(copy)
        for copy in started:
            copy.wait()

    space = pl.BlockSpec(memory_space=pltpu.HBM)
    return pl.pallas_call(
        kernel,
        out_shape=[jax.ShapeDtypeStruct(s, BF) for s in shapes],
        in_specs=[space] * count,
        out_specs=[space] * len(shapes),
        scratch_shapes=[pltpu.SemaphoreType.DMA((total,)), pltpu.SemaphoreType.DMA((total,))],
        compiler_params=pltpu.CompilerParams(collective_id=number, has_side_effects=True),
        name=name,
    )(*arrays)


def total(*parts):
    out = parts[0].astype(F32)
    for part in parts[1:]:
        out = out + part.astype(F32)
    return out


def at(array, index, axis):
    return lax.dynamic_index_in_dim(array, index, axis, keepdims=False)


def other(axis):
    return lax.rem(lax.axis_index(axis) + 1, 2)


def reduce_all(grads, late, finish_experts, second):
    core, shard, z, yh, section = (
        lax.axis_index(a) for a in ("core", "shard", "z", "yh", "section")
    )
    width = grads.shape[1]
    mix = grads.reshape(8, 2, 4, 24, width)

    got = move(
        "cores",
        1,
        [mix],
        [(8, 4, 24, width)],
        lambda: [{"core": other("core")}],
        lambda ins, outs: [(ins[0].at[:, other("core")], outs[0], {"core": other("core")})],
    )[0]
    mix = total(at(mix, core, 1), got).astype(BF).reshape(2, 4, 4, 24, width)

    cut = 1152
    mix, after = second(mix)
    wide = finish_experts(0)
    sizes = (cut, width - cut)

    def peers_2():
        return [{"shard": x} for x in around("shard", 4)] + [{"z": i} for i in around("z", 4)]

    def wide_shard(k, x):
        return pl.ds(pl.multiple_of(k * 768 + x * 192, 64), 192)

    def copies_2(ins, outs):
        here = lax.axis_index("shard")
        out = []
        for step, (x, i) in enumerate(zip(around("shard", 4), around("z", 4))):
            out.append((ins[0].at[:, :, x, :, pl.ds(0, cut)], outs[0].at[step], {"shard": x}))
            out.append((ins[0].at[:, i, :, :, pl.ds(cut, width - cut)], outs[1].at[step], {"z": i}))
            for k in range(2):
                out.append((ins[1].at[wide_shard(k, x)], outs[2 + k].at[here], {"shard": x}))
        for k in range(2):
            out.append((ins[1].at[wide_shard(k, here)], outs[2 + k].at[here], None))
        return out

    shapes = [(3, 2, 4, 24, size) for size in sizes] + [(4, 192, 768)] * 2
    *got, gate, up = move("first_axis", 2, [mix, wide], shapes, peers_2, copies_2)
    own = [
        lax.dynamic_slice(mix, (0, 0, shard, 0, 0), (2, 4, 1, 24, cut))[:, :, 0],
        lax.dynamic_slice(mix, (0, z, 0, 0, cut), (2, 1, 4, 24, width - cut))[:, 0],
    ]
    mix = [total(m, *g).astype(BF) for m, g in zip(own, got)]

    down = finish_experts(1, after)

    def down_shard(x):
        rows = pl.ds(pl.multiple_of(x // 2 * 384, 128), 384)
        return rows, pl.ds(pl.multiple_of(lax.rem(x, 2) * 384, 128), 384)

    def copies_3(ins, outs):
        here = lax.axis_index("shard")
        out = []
        for step, (x, i) in enumerate(zip(around("shard", 4), around("z", 4))):
            out.append((ins[0].at[:, i], outs[0].at[step], {"z": i}))
            out.append((ins[1].at[:, x], outs[1].at[step], {"shard": x}))
            out.append((ins[2].at[down_shard(x)], outs[2].at[here], {"shard": x}))
        out.append((ins[2].at[down_shard(here)], outs[2].at[here], None))
        return out

    shapes = [(3, 2, 24, size) for size in sizes] + [(4, 384, 384)]
    *got, down_got = move("other_axis", 3, [*mix, down], shapes, peers_2, copies_3)
    mix = jnp.concatenate(
        [
            total(at(mix[0], z, 1), *got[0]).astype(BF),
            total(at(mix[1], shard, 1), *got[1]).astype(BF),
        ],
        axis=-1,
    )
    exp = [gate, up, down_got]

    def places():
        here = 2 * lax.axis_index("yh") + lax.axis_index("section")
        there = [lax.rem(here + step, 4) for step in range(1, 4)]
        return [(t // 2, lax.rem(t, 2)) for t in there]

    def copies_4(ins, outs):
        there = other("core")
        out = [
            (ins[1 + k].at[pl.ds(2 * there, 2)], outs[1 + k], {"core": there}) for k in range(3)
        ]
        for step, (y, s) in enumerate(places()):
            out.append((ins[0].at[s, y], outs[0].at[step], {"yh": y, "section": s}))
        return out

    mine = (jnp.arange(2) == yh)[:, None, None]
    pairs = jnp.stack([mix, jnp.where(mine, late[None], jnp.zeros((), BF))])
    got = move(
        "last_axis",
        4,
        [pairs, *exp],
        [(3, 24, width), (2, 192, 768), (2, 192, 768), (2, 384, 384)],
        lambda: [{"yh": y, "section": s} for y, s in places()] + [{"core": other("core")}],
        copies_4,
    )
    sums = total(at(at(pairs, section, 0), yh, 0), *got[0])
    out = []
    for e, g in zip(exp, got[1:]):
        kept = lax.dynamic_slice_in_dim(e, 2 * core, 2, 0)
        low, high = jnp.where(core == 0, kept, g), jnp.where(core == 0, g, kept)
        out.append(jnp.concatenate([low, high], axis=1).astype(F32))
    return sums, out


def gather_weights(local, experts):
    rows, width = local.shape

    def kernel(*refs):
        mine, shards = refs[0], refs[1:4]
        full, late, whole = refs[4], refs[5], refs[6:9]
        stage = refs[9:12]
        sent, got, sent_x, got_e, sent_c, got_c, sent_y, sent_o, local_sem = refs[12:]
        s, yh, z, c, x = (lax.axis_index(a) for a in ("section", "yh", "z", "core", "shard"))
        place = 2 * yh + s
        ys = [lax.rem(place + k, 4) for k in (1, 2, 3)]
        ys = [{"yh": y // 2, "section": lax.rem(y, 2)} for y in ys]
        xs = [{"shard": lax.rem(x + k, 4)} for k in (1, 2, 3)]
        z_up, z_down = lax.rem(z + 1, 4), lax.rem(z + 3, 4)
        sibling, partner = {"core": 1 - c}, {"section": 1 - s}

        def piece(k, i, h):
            if k == 2:
                return shards[2].at[i, pl.ds(pl.multiple_of(h * 384, 128), 384)]
            return shards[k].at[i, pl.ds(pl.multiple_of(h * 192, 64), 192)]

        def landing(k, layer, source, half):
            if k == 2:
                return whole[2].at[layer, half, :, pl.ds(pl.multiple_of(source * 384, 128), 384)]
            return whole[k].at[layer, source, half]

        def remote(source, target, send, receive, device):
            return pltpu.make_async_remote_copy(
                src_ref=source,
                dst_ref=target,
                send_sem=send,
                recv_sem=receive,
                device_id=device,
                device_id_type=pl.DeviceIdType.MESH,
            )

        def start(copies):
            for copy in copies:
                copy.start()
            return copies

        def finish(copies):
            for copy in copies:
                copy.wait()

        has_own = x // 2 == c
        own = lax.rem(x, 2)
        staged = start(
            [pltpu.make_async_copy(piece(k, own, c), stage[k], local_sem.at[k]) for k in range(3)]
        )
        barrier = pltpu.get_barrier_semaphore()
        zs = [{"z": lax.rem(z + k, 4)} for k in (1, 2, 3)]
        x_up, x_down = xs[0]["shard"], xs[2]["shard"]
        near = ys + xs + zs + [sibling]
        near += [{"shard": lax.rem(x + k, 4), "core": 1 - c} for k in (1, 2, 3)]
        for peer in near:
            pl.semaphore_signal(
                barrier, inc=1, device_id=peer, device_id_type=pl.DeviceIdType.MESH
            )
        pl.semaphore_wait(barrier, len(near))

        here = full.at[yh, z, c, x]

        def along_y(target):
            out = [pltpu.make_async_copy(mine, target, local_sem.at[3])]
            for k, device in enumerate(ys):
                out.append(remote(mine, target, sent.at[k], got.at[k], device))
            return out

        @pl.when(s == 0)
        def _():
            start(along_y(here))

        @pl.when(s == 1)
        def _():
            start(along_y(late.at[yh, z, c, x]))

        finish(staged)

        @pl.when(has_own)
        def _():
            for k in range(3):
                remote(
                    piece(k, own, 1 - c),
                    landing(k, s, x, 1 - c),
                    sent_o.at[k],
                    got_e.at[s, x, k],
                    sibling,
                ).start()
                pltpu.make_async_copy(stage[k], landing(k, s, x, c), got_e.at[s, x, k]).start()

        def pass_on(layer, distance, to_partner):
            source = lax.rem(x + distance, 4)
            for k in range(3):
                view = landing(k, layer, source, c)
                receive = got_e.at[layer, source, k]
                remote(view, view, sent_o.at[k], receive, sibling).wait_recv()
                if to_partner:
                    remote(view, view, sent_y.at[distance, k], receive, partner).start()
                across = got_c.at[layer, source, k]
                remote(view, view, sent_c.at[layer, source, k], across, sibling).start()

        finish(along_y(here))
        view, view_late = full.at[:, z, c, x], late.at[:, z, c, x]
        along_x = start(
            [remote(view, view, sent.at[3 + k], got.at[3 + k], xs[k]) for k in range(3)]
        )
        late_z = start(
            [
                remote(view_late, view_late, sent.at[11 + k], got.at[11 + k], zs[k])
                for k in range(3)
            ]
        )
        pass_on(s, 0, True)
        finish(along_x)

        def ring(base, axis, places, up, down):
            return start(
                [
                    remote(up, up, sent.at[base], got.at[base], {axis: places[0]}),
                    remote(down, down, sent.at[base + 1], got.at[base + 1], {axis: places[1]}),
                ]
            )

        view = full.at[:, z, c]
        along_z = ring(6, "z", (z_up, z_down), view, view)
        for i in range(2):

            @pl.when(x != 2 * c + i)
            def _():
                for h in range(2):
                    for k in range(3):
                        remote(
                            piece(k, i, h),
                            landing(k, s, x, h),
                            sent_x.at[(i * 2 + h) * 3 + k],
                            got_e.at[s, x, k],
                            {"shard": 2 * c + i, "core": h},
                        ).start()

        finish(late_z)
        view = late.at[:, :, c, x]
        late_x = ring(14, "shard", (x_up, x_down), view, view)
        finish(along_z)
        along_z = ring(8, "z", (z_up, z_down), full.at[0, z_down, c], full.at[1, z_up, c])
        for distance in (1, 3, 2):
            pass_on(s, distance, True)
        finish(along_z)
        view = full.at[:, :, c]
        across = start([remote(view, view, sent.at[10], got.at[10], sibling)])
        finish(late_x)
        late_x = ring(
            16, "shard", (x_up, x_down), late.at[0, :, c, x_down], late.at[1, :, c, x_up]
        )
        for distance in (0, 1):
            pass_on(1 - s, distance, False)
        finish(late_x)
        view = late.at[:, :, c]
        across += start([remote(view, view, sent.at[18], got.at[18], sibling)])
        for distance in (3, 2):
            pass_on(1 - s, distance, False)

        finish(across)
        for i in range(2):

            @pl.when(x != 2 * c + i)
            def _():
                for h in range(2):
                    for k in range(3):
                        view = piece(k, i, h)
                        n = (i * 2 + h) * 3 + k
                        remote(view, view, sent_x.at[n], got_e.at[0, 0, k], sibling).wait_send()

        @pl.when(has_own)
        def _():
            for k in range(3):
                view = piece(k, own, 1 - c)
                remote(view, view, sent_o.at[k], got_e.at[0, 0, k], sibling).wait_send()

        for source in range(4):
            for k in range(3):
                view = landing(k, s, source, c)
                send = sent_y.at[source, k]
                remote(view, view, send, got_e.at[0, 0, k], partner).wait_send()
                for layer in range(2):
                    view = landing(k, layer, source, c)
                    arrived = landing(k, layer, source, 1 - c)
                    send, receive = sent_c.at[layer, source, k], got_c.at[layer, source, k]
                    remote(view, view, send, receive, sibling).wait_send()
                    remote(arrived, arrived, send, receive, sibling).wait_recv()

    space = pl.BlockSpec(memory_space=pltpu.HBM)
    near_space = pl.BlockSpec(memory_space=pltpu.VMEM)
    shapes = [(2, 4, 2, 4, rows, width)] * 2
    shapes += [(2, 4, 2, 192, 768), (2, 4, 2, 192, 768), (2, 2, 384, 1536)]
    dma = pltpu.SemaphoreType.DMA
    return pl.pallas_call(
        kernel,
        out_shape=[jax.ShapeDtypeStruct(shape, BF) for shape in shapes],
        in_specs=[near_space] + [space] * 3,
        out_specs=[space] * 5,
        scratch_shapes=[
            pltpu.VMEM((192, 768), BF),
            pltpu.VMEM((192, 768), BF),
            pltpu.VMEM((384, 384), BF),
            dma((19,)),
            dma((19,)),
            dma((12,)),
            dma((2, 4, 3)),
            dma((2, 4, 3)),
            dma((2, 4, 3)),
            dma((4, 3)),
            dma((3,)),
            dma((4,)),
        ],
        compiler_params=pltpu.CompilerParams(collective_id=0, has_side_effects=True),
        name="gather_weights",
    )(local, *experts)


def rank_of(route_rows):
    rows = route_rows.shape[0]
    chosen = route_rows.T[None, :, :] == jnp.arange(EXPERTS, dtype=jnp.int32)[:, None, None]
    hot = jnp.any(chosen, axis=1)
    index = jnp.arange(rows, dtype=jnp.int32)
    before = (index[:, None] < index[None, :]).astype(BF)
    return jnp.where(hot, dot(hot.astype(BF), before), -1.0)


def stacked(field):
    return jnp.concatenate(jnp.split(field, CHUNKS, axis=1), axis=0)


def unstacked(field):
    return jnp.concatenate(jnp.split(field, CHUNKS, axis=0), axis=1)


def unfold_table(sources):
    row = jnp.arange(CHUNKS * sources * EXTRA, dtype=jnp.int32)
    piece, source, extra = row // (sources * EXTRA), row // EXTRA % sources, row % EXTRA
    column = jnp.arange(sources * MAIN, dtype=jnp.int32)
    return (
        (source * MAIN + piece * EXTRA + extra)[:, None] == column[None, :]
    ).astype(BF)


def arrived_rows(message, unfold):
    width = message.shape[1] - 256
    extra = unstacked(dot(unfold, message[:, width:]).astype(BF))
    return jnp.concatenate([message[:, :width], extra], axis=0)


def fold_rows(rows, unfold, sources):
    main = rows[: sources * MAIN]
    extra = dot(unfold, stacked(rows[sources * MAIN :]), ((0,), (0,))).astype(BF)
    return jnp.concatenate([main, extra], axis=1)


def low_pair(value):
    high = value.astype(BF)
    return high, (value - high.astype(F32)).astype(BF)


OUT_COLUMNS, QKV_STEP = 1536, 512


def columns(width, place):
    return lambda rows: pl.BlockSpec((rows, width), lambda i: (0, place), memory_space=pltpu.VMEM)


OUT_BLOCK = [columns(OUT_COLUMNS, 0)]
QKV_BLOCKS = [columns(QKV_STEP, 3 + k) for k in range(4)]
NARROW_BLOCK = [columns(128, 28)]


def fused(name, body, shapes, *arrays, scratch=(), number=None):
    near = pl.BlockSpec(memory_space=pltpu.VMEM)
    specs, given = [], []
    for array in arrays:
        if isinstance(array, tuple):
            array, blocks = array
            specs += [block(array.shape[0]) for block in blocks]
            given += [array] * len(blocks)
        else:
            specs.append(near)
            given.append(array)
    return pl.pallas_call(
        body,
        grid=(1,),
        out_shape=[jax.ShapeDtypeStruct(shape, kind) for shape, kind in shapes],
        in_specs=specs,
        out_specs=[near] * len(shapes),
        scratch_shapes=list(scratch),
        compiler_params=pltpu.CompilerParams(
            vmem_limit_bytes=48 << 20, collective_id=number, has_side_effects=number is not None
        ),
        name=name,
    )(*given)


TN, NT = ((0,), (0,)), ((1,), (1,))


def slots(rank):
    count, rows = rank.shape
    place = lax.broadcasted_iota(jnp.int32, (count, MAIN, rows), 1)
    wide = jnp.broadcast_to(rank[:, None, :], (count, MAIN, rows))
    main = jnp.where(wide == place.astype(F32), 1.0, 0.0)
    extra = (MAIN + lax.rem(place, EXTRA)).astype(F32)
    extra = jnp.where((wide == extra) & (place < EXTRA * CHUNKS), 1.0, 0.0)
    return main, extra


def per_piece(table):
    piece = lax.rem(lax.broadcasted_iota(jnp.int32, table.shape, 0), MAIN) // EXTRA
    return [jnp.where(piece == j, table, 0.0) for j in range(CHUNKS)]


def flat(table):
    return table.reshape(table.shape[0] * table.shape[1], table.shape[2])


def send_table(main, extra, field):
    width = field.shape[1] // CHUNKS
    side = None
    for j, table in enumerate(per_piece(flat(extra))):
        part = dot(table.astype(BF), field[:, j * width : (j + 1) * width])
        side = part if side is None else side + part
    return dot(flat(main).astype(BF), field), side


def bring_back(main, extra, rows, exact):
    parts = low_pair if exact else (lambda t: (t.astype(BF),))
    model_width = rows.shape[1] - 256
    total_main = None
    for table in parts(main):
        part = dot(table, rows[:, :model_width], TN)
        total_main = part if total_main is None else total_main + part
    side = []
    for table in per_piece(extra):
        total_side = None
        for t in parts(table):
            part = dot(t, rows[:, model_width:], TN)
            total_side = part if total_side is None else total_side + part
        side.append(total_side)
    return total_main + jnp.concatenate(side, axis=1)


def gain_rows(narrow):
    row = lax.broadcasted_iota(jnp.int32, (8, narrow.shape[1]), 0)
    column = lax.broadcasted_iota(jnp.int32, (8, narrow.shape[1]), 1)
    pick = jnp.where(column == row + EXPERTS, 1.0, 0.0).astype(BF)
    rows = dot(pick, narrow, NT)
    return rows[0:1], rows[1:2]


def turn(field, cosine, sine):
    return field * cosine + pltpu.roll(field, HEAD_DIM // 2, 1) * sine


def turn_back(field, cosine, sine):
    return field * cosine - pltpu.roll(field, HEAD_DIM // 2, 1) * sine


def combined(x_mid, rank, gates, rows):
    main, extra = slots(rank)
    wide = jnp.broadcast_to(gates[:, None, :], main.shape)
    return x_mid + bring_back(flat(main * wide), flat(extra * wide), rows, True)


def finish_body(mid_ref, rank_ref, gates_ref, rows_ref, out_ref):
    out = combined(mid_ref[...], rank_ref[...], gates_ref[...], rows_ref[...])
    out_ref[...] = out.astype(BF)


def heads_of(kv_ref):
    kv_heads = kv_ref.shape[2] // 2 // HEAD_DIM
    parts = []
    for k in range(2 * kv_heads):
        part = kv_ref[:, :, k * HEAD_DIM : (k + 1) * HEAD_DIM]
        parts.append(part.reshape(part.shape[0] * part.shape[1], HEAD_DIM))
    return parts[:kv_heads], parts[kv_heads:]


def attention_body(combine):
    def body(*refs):
        source, refs = refs[: 4 if combine else 1], refs[4 if combine else 1 :]
        weights, refs = refs[:4], refs[4:]
        out_w, narrow, cos_ref, sin_ref, allowed_ref, rank_ref, low_ref, h_ref, q_ref = refs[:9]
        kv_ref, mid_ref, h2_ref, att_ref, probs_ref, gates_ref, out_ref, held, sent, got = refs[9:]
        here = lax.axis_index("shard")
        peers = [{"shard": x} for x in around("shard", 4)]
        barrier = pltpu.get_barrier_semaphore()
        for peer in peers:
            pl.semaphore_signal(
                barrier, inc=1, device_id=peer, device_id_type=pl.DeviceIdType.MESH
            )
        if combine:
            mid, rank, gates, rows = (ref[...] for ref in source)
            low = combined(mid, rank, gates, rows).astype(BF)
        else:
            low = source[0][...]
        low_ref[...] = low
        field = low.astype(F32)
        gain_a, gain_m = gain_rows(narrow[...])
        scale = lax.rsqrt(jnp.mean(field * field, axis=1, keepdims=True) + epsilon)
        h = (field * scale * gain_a).astype(BF)
        h_ref[...] = h
        cosine, sine = cos_ref[...], sin_ref[...]

        def projected(column, turned):
            inside = column % QKV_STEP
            part = dot(h, weights[column // QKV_STEP][:, inside : inside + 256])
            if turned:
                part = jnp.concatenate(
                    [turn(part[:, k : k + HEAD_DIM], cosine, sine) for k in (0, HEAD_DIM)], axis=1
                )
            return part.astype(BF)

        query_width, kv_width = q_ref.shape[1], kv_ref.shape[2]
        for column in range(0, kv_width, 256):
            part = projected(query_width + column, column < kv_width // 2)
            held[here, :, column : column + 256] = part
        pl.semaphore_wait(barrier, len(peers))
        copies = []
        for k, peer in enumerate(peers):
            view = held.at[here]
            copies.append(
                pltpu.make_async_remote_copy(
                    src_ref=view,
                    dst_ref=view,
                    send_sem=sent.at[k],
                    recv_sem=got.at[k],
                    device_id=peer,
                    device_id_type=pl.DeviceIdType.MESH,
                )
            )
            copies[-1].start()
        for column in range(0, query_width, 256):
            q_ref[:, column : column + 256] = projected(column, True)
        for copy in copies:
            copy.wait()

        kv_ref[...] = held[...]
        keys, values = heads_of(held)
        allowed = allowed_ref[...] > 0.0
        ratio = HEADS // len(keys)
        for head in range(HEADS):
            lanes = slice(head * HEAD_DIM, (head + 1) * HEAD_DIM)
            scores = dot(q_ref[:, lanes], keys[head // ratio], NT) * HEAD_DIM ** (-0.5)
            scores = jnp.where(allowed, scores, masked_score)
            exponent = jnp.exp(scores - jnp.max(scores, axis=1, keepdims=True))
            probs = exponent / jnp.sum(exponent, axis=1, keepdims=True)
            probs_ref[head] = probs
            att_ref[:, lanes] = dot(probs.astype(BF), values[head // ratio]).astype(BF)
        mid = field + dot(att_ref[...], out_w[...])
        mid_ref[...] = mid
        scale = lax.rsqrt(jnp.mean(mid * mid, axis=1, keepdims=True) + epsilon)
        h2 = (mid * scale * gain_m).astype(BF)
        h2_ref[...] = h2
        rank = rank_ref[...]
        logits = jnp.transpose(dot(h2, narrow[...]))[:EXPERTS]
        logits = jnp.where(rank >= 0.0, logits, masked_score)
        gate_exp = jnp.exp(logits - jnp.max(logits, axis=0, keepdims=True))
        gate_exp = jnp.where(rank >= 0.0, gate_exp, 0.0)
        gates_ref[...] = gate_exp / jnp.sum(gate_exp, axis=0, keepdims=True)
        main, side = send_table(*slots(rank), h2)
        width = main.shape[1]
        out_ref[:, :width] = main.astype(BF)
        out_ref[:, width:] = side.astype(BF)

    return body


def attention(source, weights, tables, allowed, rank, number):
    tok_rows, model_width = source[0].shape
    query_width = HEADS * HEAD_DIM
    shapes = [((tok_rows, model_width), BF)] * 2
    shapes += [
        ((tok_rows, query_width), BF),
        ((allowed.shape[1] // tok_rows, tok_rows, 4 * QKV_STEP - query_width), BF),
        ((tok_rows, model_width), F32),
        ((tok_rows, model_width), BF),
        ((tok_rows, query_width), BF),
        ((HEADS, tok_rows, allowed.shape[1]), F32),
        (rank.shape, F32),
        ((EXPERTS * MAIN, model_width + 256), BF),
    ]
    dma = pltpu.SemaphoreType.DMA
    return fused(
        "attention",
        attention_body(len(source) > 1),
        shapes,
        *source,
        (weights, QKV_BLOCKS + OUT_BLOCK + NARROW_BLOCK),
        *tables,
        allowed,
        rank,
        scratch=[pltpu.VMEM(shapes[3][0], BF), dma((3,)), dma((3,))],
        number=number,
    )


def grad_slots_body(grad_ref, rank_ref, gates_ref, rows_ref, out_ref, dlogits_ref):
    gates = gates_ref[...]
    main, extra = slots(rank_ref[...])
    wide = jnp.broadcast_to(gates[:, None, :], main.shape)
    grad_main, grad_side = send_table(main, extra, grad_ref[...])
    width = grad_main.shape[1]
    dgate = None
    for table, grad, columns in (
        (main, grad_main, slice(0, width)),
        (extra, grad_side, slice(width, width + 256)),
    ):
        slot_gate = jnp.sum(flat(table * wide), axis=1, keepdims=True)
        out_ref[:, columns] = (grad * slot_gate).astype(BF)
        slot_dgate = jnp.sum(grad * rows_ref[:, columns].astype(F32), axis=1, keepdims=True)
        part = jnp.sum((flat(table) * slot_dgate).reshape(table.shape), axis=1)
        dgate = part if dgate is None else dgate + part
    dlogits = gates * (dgate - jnp.sum(gates * dgate, axis=0, keepdims=True))
    pad = jnp.zeros((dlogits_ref.shape[1] - EXPERTS, dlogits.shape[1]), F32)
    dlogits_ref[...] = jnp.transpose(jnp.concatenate([dlogits, pad], axis=0)).astype(BF)


def grad_slots(grad, rank, gates, rows):
    shapes = [(rows.shape, BF), ((grad.shape[0], 128), BF)]
    return fused("grad_slots", grad_slots_body, shapes, grad, rank, gates, rows)


def norm_grads(field, gain, grad):
    scale = lax.rsqrt(jnp.mean(field * field, axis=1, keepdims=True) + epsilon)
    scaled = grad * gain
    centre = jnp.mean(scaled * field, axis=1, keepdims=True)
    dgain = jnp.sum(grad * field * scale, axis=0, keepdims=True)
    return scale * scaled - field * (scale * scale * scale) * centre, dgain


def grad_attention_body(
    grad_ref, rows_ref, rank_ref, dlogits_ref, out_w, weight_0, weight_1, weight_2, weight_3, narrow,
    mid_ref, q_ref, kv_ref, probs_ref, cos_ref, sin_ref, low_ref,
    dbr_ref, dqkv_ref, grad_out_ref, dgain_a_ref, dgain_m_ref,
    datt_ref, dkv_ref, held, sent, got,
):
    here = lax.axis_index("shard")
    peers = [{"shard": x} for x in around("shard", 4)]
    barrier = pltpu.get_barrier_semaphore()
    for peer in peers:
        pl.semaphore_signal(barrier, inc=1, device_id=peer, device_id_type=pl.DeviceIdType.MESH)
    main, extra = slots(rank_ref[...])
    dh = bring_back(flat(main), flat(extra), rows_ref[...], False)
    dh = dh + dot(dlogits_ref[...], narrow[...], NT)
    gain_a, gain_m = gain_rows(narrow[...])
    dmid, dgain = norm_grads(mid_ref[...], gain_m, dh)
    dmid = dmid + grad_ref[...].astype(F32)
    dgain_m_ref[...] = dgain
    dbr_ref[...] = dmid.astype(BF)
    datt_ref[...] = dot(dbr_ref[...], out_w[...], NT).astype(BF)
    keys, values = heads_of(kv_ref)
    ratio = HEADS // len(keys)
    cosine, sine = cos_ref[...], sin_ref[...]
    count, tok_rows, kv_columns = kv_ref.shape
    scale = HEAD_DIM ** (-0.5)
    for k in range(len(keys)):
        dkey, dvalue = None, None
        for head in range(k * ratio, (k + 1) * ratio):
            lanes = slice(head * HEAD_DIM, (head + 1) * HEAD_DIM)
            probs, datt = probs_ref[head], datt_ref[:, lanes]
            dprobs = dot(datt, values[k], NT)
            centre = jnp.sum(dprobs * probs, axis=1, keepdims=True)
            dscores = (probs * (dprobs - centre)).astype(BF)
            part = dot(probs.astype(BF), datt, TN)
            dvalue = part if dvalue is None else dvalue + part
            part = dot(dscores, q_ref[:, lanes], TN)
            dkey = part if dkey is None else dkey + part
            dquery = dot(dscores, keys[k]) * scale
            dqkv_ref[:, lanes] = turn_back(dquery, cosine, sine).astype(BF)
        at_key, at_value = k * HEAD_DIM, (len(keys) + k) * HEAD_DIM
        shape = (count, tok_rows, HEAD_DIM)
        dkv_ref[:, :, at_key : at_key + HEAD_DIM] = (dkey * scale).astype(BF).reshape(shape)
        dkv_ref[:, :, at_value : at_value + HEAD_DIM] = dvalue.astype(BF).reshape(shape)
    pl.semaphore_wait(barrier, len(peers))
    copies = []
    for k, peer in enumerate(peers):
        copies.append(
            pltpu.make_async_remote_copy(
                src_ref=dkv_ref.at[peer["shard"]],
                dst_ref=held.at[k],
                send_sem=sent.at[k],
                recv_sem=got.at[k],
                device_id=peer,
                device_id_type=pl.DeviceIdType.MESH,
            )
        )
        copies[-1].start()
    query_width = q_ref.shape[1]
    dh = None
    weights = (weight_0, weight_1, weight_2, weight_3)
    for k, weight in enumerate(weights[:-1]):
        part = dot(dqkv_ref[:, k * QKV_STEP : (k + 1) * QKV_STEP], weight[...], NT)
        dh = part if dh is None else dh + part
    for copy in copies:
        copy.wait()
    dkv = dkv_ref[here].astype(F32)
    for k in range(len(peers)):
        dkv = dkv + held[k].astype(F32)
    for k in range(0, kv_columns // 2, HEAD_DIM):
        part = turn_back(dkv[:, k : k + HEAD_DIM], cosine, sine)
        dqkv_ref[:, query_width + k : query_width + k + HEAD_DIM] = part.astype(BF)
    dqkv_ref[:, query_width + kv_columns // 2 :] = dkv[:, kv_columns // 2 :].astype(BF)
    dh = dh + dot(dqkv_ref[:, query_width:], weights[-1][...], NT)
    dlow, dgain = norm_grads(low_ref[...].astype(F32), gain_a, dh)
    dgain_a_ref[...] = dgain
    grad_out_ref[...] = (dlow + dmid).astype(BF)


def grad_attention(
    grad, rows, rank, dlogits, weights, mid, q, kv, probs, tables, low, number
):
    tok_rows, model_width = mid.shape
    shapes = [
        ((tok_rows, model_width), BF),
        ((tok_rows, 4 * QKV_STEP), BF),
        ((tok_rows, model_width), BF),
        ((1, model_width), F32),
        ((1, model_width), F32),
    ]
    dma = pltpu.SemaphoreType.DMA
    return fused(
        "grad_attention",
        grad_attention_body,
        shapes,
        grad,
        rows,
        rank,
        dlogits,
        (weights, OUT_BLOCK + QKV_BLOCKS + NARROW_BLOCK),
        mid,
        q,
        kv,
        probs,
        *tables,
        low,
        scratch=[
            pltpu.VMEM(q.shape, BF),
            pltpu.VMEM(kv.shape, BF),
            pltpu.VMEM((3, *kv.shape[1:]), BF),
            dma((3,)),
            dma((3,)),
        ],
        number=number,
    )


def weight_grads_body(
    h_ref, dqkv_ref, att_ref, dbr_ref, h2_ref, dlogits_ref, dgain_a_ref, dgain_m_ref, out_ref
):
    step = 512
    place = 0
    for left, right in ((att_ref, dbr_ref), (h_ref, dqkv_ref)):
        for k in range(0, right.shape[1], step):
            part = dot(left[...], right[:, k : k + step], TN)
            out_ref[:, place : place + step] = part.astype(BF)
            place += step
    narrow = dot(h2_ref[...], dlogits_ref[...], TN)
    rows = jnp.concatenate(
        [dgain_a_ref[...], dgain_m_ref[...], jnp.zeros((126, h_ref.shape[1]), F32)], axis=0
    )
    columns = pltpu.roll(jnp.transpose(rows), EXPERTS, 1)
    out_ref[:, place:] = (narrow + columns).astype(BF)


def weight_grads(h, dqkv, att, dbr, h2, dlogits, dgain_a, dgain_m):
    columns = dqkv.shape[1] + dbr.shape[1] + 128
    return fused(
        "weight_grads", weight_grads_body, [((h.shape[1], columns), BF)],
        h, dqkv, att, dbr, h2, dlogits, dgain_a, dgain_m,
    )[0]


def greet(peers):
    barrier = pltpu.get_barrier_semaphore()
    for peer in peers:
        pl.semaphore_signal(barrier, inc=1, device_id=peer, device_id_type=pl.DeviceIdType.MESH)
    pl.semaphore_wait(barrier, len(peers))


PARTNERS = [(dy, dz, (dz + k) % 4) for k in range(4) for dy in range(2) for dz in range(4)]
GROUP = 8
GROUPS = len(PARTNERS) // GROUP


def facing(n):
    k, dy, dz = n // GROUP, n // 4 % 2, n % 4
    return -k % GROUPS * GROUP + dy * 4 + -dz % 4


def partners():
    s, yh, z, x = (lax.axis_index(a) for a in ("section", "yh", "z", "shard"))
    out = []
    for dy, dz, dx in PARTNERS:
        there = {
            "section": lax.rem(s + dy, 2),
            "yh": lax.rem(yh + dy, 2),
            "z": lax.rem(z + dz, 4),
            "shard": lax.rem(x + dx, 4),
        }
        out.append((there, (there["yh"] * 4 + there["z"]) * 4 + there["shard"]))
    return out


def exchange_rows(message, returned, arrived, produced, sems, work, after, load, sibling=()):
    sent, got, sent_back, got_back = sems
    for copy in load:
        copy.start()
    near = partners()
    own = near[0][1]
    greet([device for device, _ in near[1:]] + list(sibling))

    def remote(source, target, send, receive, device):
        return pltpu.make_async_remote_copy(
            src_ref=source,
            dst_ref=target,
            send_sem=send,
            recv_sem=receive,
            device_id=device,
            device_id_type=pl.DeviceIdType.MESH,
        )

    def out(n):
        device, expert = near[n]
        f = facing(n)
        return remote(message.at[expert], arrived.at[f], sent.at[n], got.at[f], device)

    def back(n):
        return remote(
            produced.at[n], returned.at[own], sent_back.at[n], got_back.at[facing(n)], near[n][0]
        )

    for k in range(GROUPS):
        for n in range(-k % GROUPS * GROUP, -k % GROUPS * GROUP + GROUP):
            if n:
                out(n).start()
    arrived[0] = message[own]
    for copy in load:
        copy.wait()
    for k in range(GROUPS):
        members = range(k * GROUP, (k + 1) * GROUP)
        for n in members:
            if n:
                remote(arrived.at[n], arrived.at[n], sent.at[n], got.at[n], near[n][0]).wait_recv()
        rows = arrived[k * GROUP : (k + 1) * GROUP]
        result = work(k, rows.reshape(GROUP * MAIN, rows.shape[2]))
        produced[k * GROUP : (k + 1) * GROUP] = result.reshape(rows.shape)
        for n in members:
            if n:
                back(n).start()
    returned[own] = produced[0]
    after()
    for n in range(1, len(near)):
        device, expert = near[n]
        out(n).wait_send()
        back(n).wait_send()
        view = returned.at[expert]
        remote(view, view, sent_back.at[n], got_back.at[n], device).wait_recv()


def exchange_call(name, number, body, inputs, whole, shapes, message_shape, scratch):
    near = pl.BlockSpec(memory_space=pltpu.VMEM)
    far = pl.BlockSpec(memory_space=pltpu.HBM)
    dma = pltpu.SemaphoreType.DMA
    count = message_shape[0]
    return pl.pallas_call(
        body,
        out_shape=[jax.ShapeDtypeStruct(shape, kind) for shape, kind in shapes],
        in_specs=[far] * len(whole) + [near] * len(inputs),
        out_specs=[near] * len(shapes),
        scratch_shapes=[pltpu.VMEM(w.shape[1:], BF) for w in whole]
        + [dma((len(whole),))]
        + [pltpu.VMEM(message_shape, BF), pltpu.VMEM(message_shape, BF)]
        + [dma((count,)) for _ in range(4)]
        + scratch,
        compiler_params=pltpu.CompilerParams(
            collective_id=number, has_side_effects=True, vmem_limit_bytes=56 << 20
        ),
        name=name,
    )(*whole, *inputs)


def loads(whole, layer, held, sem):
    copies = [pltpu.make_async_copy(w.at[layer], h, sem.at[k]) for k, (w, h) in enumerate(zip(whole, held))]

    def matrix(k):
        value = held[k][...]
        return value.reshape(-1, value.shape[-1])

    return copies, matrix


def expert_forward(message, experts, layer, unfold, number):
    message = message.reshape(EXPERTS, MAIN, message.shape[1])
    rows = GROUP * (MAIN + EXTRA)
    depth, width = message.shape[2] - 256, experts[0].shape[-1]

    def body(*refs):
        whole, (message_ref, unfold_ref), refs = refs[:3], refs[3:5], refs[5:]
        returned, rows_ref, gate_ref, up_ref, hidden_ref = refs[:5]
        load, matrix = loads(whole, layer, refs[5:8], refs[8])
        arrived, produced, *sems = refs[9:]

        def work(k, came):
            field = arrived_rows(came, unfold_ref[...])
            rows_ref[k] = field
            gate = dot(field, matrix(0))
            up = dot(field, matrix(1))
            gate_ref[k] = gate
            up_ref[k] = up
            hidden = (gate / (1.0 + jnp.exp(-gate)) * up).astype(BF)
            hidden_ref[k] = hidden
            return fold_rows(dot(hidden, matrix(2)).astype(BF), unfold_ref[...], GROUP)

        exchange_rows(message_ref, returned, arrived, produced, sems, work, lambda: None, load)

    shapes = [
        (message.shape, BF),
        ((GROUPS, rows, depth), BF),
        ((GROUPS, rows, width), F32),
        ((GROUPS, rows, width), F32),
        ((GROUPS, rows, width), BF),
    ]
    returned, *kept = exchange_call(
        "expert_forward", number, body, [message, unfold], experts, shapes, message.shape, []
    )
    return returned.reshape(-1, message.shape[2]), kept


def expert_backward(message, experts, layer, kept, unfold, number):
    message = message.reshape(EXPERTS, MAIN, message.shape[1])
    rows = GROUP * (MAIN + EXTRA)
    depth, width = message.shape[2] - 256, experts[0].shape[-1]
    shards = 4
    half, deep = depth // 8, width // 2

    def body(*refs):
        whole, refs = refs[:3], refs[3:]
        message_ref, rows_ref, gate_ref, up_ref, hidden_ref, unfold_ref = refs[:6]
        returned, sum_ref, sum_down_ref = refs[6:9]
        load, matrix = loads(whole, layer, refs[9:12], refs[12])
        (arrived, produced), refs = refs[13:15], refs[15:]
        sems, (came_ref, dgate_ref, dup_ref) = refs[:4], refs[4:7]
        wide_refs, (down_ref, held_gate, held_up, held_down, sent, got) = refs[7:9], refs[9:]
        core = lax.axis_index("core")
        sibling = {"core": 1 - core}

        def work(k, came):
            field = arrived_rows(came, unfold_ref[...])
            came_ref[k] = field
            dhidden = dot(field, matrix(2), NT)
            gate = gate_ref[k]
            logistic = 1.0 / (1.0 + jnp.exp(-gate))
            dgate = dhidden * up_ref[k] * (logistic * (1.0 + gate * (1.0 - logistic)))
            dgate_ref[k] = dgate.astype(BF)
            dup_ref[k] = (dhidden * (gate * logistic)).astype(BF)
            out = dot(dgate_ref[k], matrix(0), NT) + dot(dup_ref[k], matrix(1), NT)
            return fold_rows(out.astype(BF), unfold_ref[...], GROUP)

        def to_sibling(k):
            views = [wide_refs[0].at[:, 1 - core], wide_refs[1].at[:, 1 - core]]
            views.append(down_ref.at[1 - core])
            return pltpu.make_async_remote_copy(
                src_ref=views[k],
                dst_ref=(held_gate, held_up, held_down)[k],
                send_sem=sent.at[k],
                recv_sem=got.at[k],
                device_id=sibling,
                device_id_type=pl.DeviceIdType.MESH,
            )

        def after():
            step = 256
            field = rows_ref[...].reshape(GROUPS * rows, depth)
            for k, source in enumerate((dgate_ref, dup_ref)):
                for column in range(0, width, step):
                    lanes = slice(column, column + step)
                    part = source[:, :, lanes].reshape(GROUPS * rows, step)
                    part = dot(field, part, TN).astype(BF)
                    wide_refs[k][:, :, :, lanes] = part.reshape(shards, 2, half, step)
                to_sibling(k).start()
            field = hidden_ref[...].reshape(GROUPS * rows, width)
            for column in range(0, depth, step):
                lanes = slice(column, column + step)
                part = came_ref[:, :, lanes].reshape(GROUPS * rows, step)
                part = dot(field, part, TN).astype(BF)
                down_ref[:, :, lanes] = part.reshape(2, deep, step)
            to_sibling(2).start()

        exchange_rows(
            message_ref, returned, arrived, produced, sems, work, after, load, (sibling,)
        )
        for k, held in enumerate((held_gate, held_up)):
            to_sibling(k).wait()
            for j in range(shards):
                part = wide_refs[k][j, core].astype(F32) + held[j].astype(F32)
                place = (k * shards + j) * half
                sum_ref[place : place + half] = part.astype(BF)
        to_sibling(2).wait()
        part = down_ref[core].astype(F32) + held_down[...].astype(F32)
        for j in range(2):
            columns_of = part[:, j * width : (j + 1) * width].astype(BF)
            sum_down_ref[j * deep : (j + 1) * deep] = columns_of

    shapes = [(message.shape, BF), ((2 * shards * half, width), BF), ((2 * deep, width), BF)]
    dma = pltpu.SemaphoreType.DMA
    scratch = [
        pltpu.VMEM((GROUPS, rows, depth), BF),
        pltpu.VMEM((GROUPS, rows, width), BF),
        pltpu.VMEM((GROUPS, rows, width), BF),
        pltpu.VMEM((shards, 2, half, width), BF),
        pltpu.VMEM((shards, 2, half, width), BF),
        pltpu.VMEM((2, deep, depth), BF),
        pltpu.VMEM((shards, half, width), BF),
        pltpu.VMEM((shards, half, width), BF),
        pltpu.VMEM((deep, depth), BF),
        dma((3,)),
        dma((3,)),
    ]
    returned, *sums = exchange_call(
        "expert_backward",
        number,
        body,
        [message, *kept, unfold],
        experts,
        shapes,
        message.shape,
        scratch,
    )
    return returned.reshape(-1, message.shape[2]), sums


def forward_layer(source, weights, experts, layer, rank, unfold, tables, allowed, numbers):
    low, h_attn, query, kv_all, x_mid, h_moe, attended, probs, gates, message = attention(
        source, weights, tables, allowed, rank, numbers[0]
    )
    returned, kept = expert_forward(message, experts, layer, unfold, numbers[1])
    stored = {
        "low": low,
        "h_attn": h_attn,
        "query": query,
        "kv_all": kv_all,
        "probs": probs,
        "attended": attended,
        "x_mid": x_mid,
        "h_moe": h_moe,
        "gates": gates,
        "returned": returned,
        "kept": kept,
    }
    return (x_mid, rank, gates, returned), stored


def backward_layer(grad, ready, stored, weights, experts, layer, rank, unfold, tables, numbers):
    message, dlogits = grad_slots(grad, rank, stored["gates"], stored["returned"])
    returned, halves = expert_backward(
        message, experts, layer, stored["kept"], unfold, numbers[0]
    )
    dbr, dqkv, grad_in, dgain_a, dgain_m = grad_attention(
        grad, returned, rank, dlogits, weights, stored["x_mid"], stored["query"], stored["kv_all"],
        stored["probs"], tables, stored["low"], numbers[1],
    )
    dqkv, *ready = lax.optimization_barrier((dqkv, *ready))
    grads = weight_grads(
        stored["h_attn"], dqkv, stored["attended"], dbr, stored["h_moe"], dlogits, dgain_a, dgain_m
    )
    return grad_in, grads, halves, ready


def per_device(
    tokens,
    routes,
    lengths,
    gain_attn,
    w_query,
    w_key,
    w_value,
    w_out,
    gain_moe,
    w_router,
    w_gate,
    w_up,
    w_down,
    cotangent,
):
    section, yh, z, core, shard = (
        lax.axis_index(a) for a in ("section", "yh", "z", "core", "shard")
    )
    first = section == 0
    tok_rows, model_width = tokens.shape[1:]
    group_rows = tok_rows * lax.axis_size("shard")

    def mine(a):
        return lax.dynamic_index_in_dim(a, section, 0, keepdims=False)

    def by_layer(own, other):
        return jnp.where(first, own, other), jnp.where(first, other, own)

    local = jnp.concatenate(
        [
            w_out[0],
            w_query[0],
            w_key[0],
            w_value[0],
            w_router[0],
            gain_attn[0][:, None],
            gain_moe[0][:, None],
            jnp.zeros((w_query.shape[1], 94), BF),
        ],
        axis=1,
    )
    full, late, *whole = gather_weights(local, (w_gate[0], w_up[0], w_down[0]))
    weights = [full.reshape(model_width, -1), late.reshape(model_width, -1)]
    route_other = swap(at(routes[0], 1 - section, 0), "section")
    ranks = [rank_of(r) for r in by_layer(mine(routes[0]), route_other)]
    unfold = unfold_table(GROUP)

    segment, position = document_layout(mine(lengths[:, 0]), group_rows)
    row_start = shard * tok_rows
    own_segment = lax.dynamic_slice_in_dim(segment, row_start, tok_rows)
    tables = rotary_tables(lax.dynamic_slice_in_dim(position, row_start, tok_rows), HEAD_DIM)
    query_index = row_start + jnp.arange(tok_rows, dtype=jnp.int32)
    allowed = (own_segment[:, None] == segment[None, :]) & (
        query_index[:, None] >= jnp.arange(group_rows, dtype=jnp.int32)[None, :]
    )
    allowed = allowed.astype(F32)

    source, saved = (mine(tokens),), []
    for layer in range(2):
        source, stored = forward_layer(
            source, weights[layer], whole, layer, ranks[layer], unfold, tables, allowed,
            (7 + layer, 11 + layer),
        )
        saved.append(stored)
    low = fused("finish", finish_body, [((tok_rows, model_width), BF)], *source)[0]
    grad, low = lax.optimization_barrier((mine(cotangent), low))
    away = swap(low, "section")

    sums, ready = [None, None], (away,)

    def across(half, layer):
        return lax.ppermute(half, "section", [(1 - layer, layer)])

    for layer in (1, 0):
        grad, mixer_grad, halves, ready = backward_layer(
            grad,
            ready,
            saved[layer],
            weights[layer],
            whole,
            layer,
            ranks[layer],
            unfold,
            tables,
            (5 + layer, 9 + layer),
        )
        sums[layer] = [(half, across(half, layer)) for half in halves[: 1 + layer]]
        if layer == 1:
            (away,), ready = ready, [given for _, given in sums[1]]
            late = lax.psum_scatter(mixer_grad, DEVICES, scatter_dimension=0, tiled=True)
            late = lax.optimization_barrier(late)
    mixed = jnp.where(first, jnp.stack([low, away]), jnp.stack([away, low]))

    def finish_experts(k, after=None):
        if after is None:
            own, given = sums[0][0]
        else:
            own, given = after
        return jnp.where(first, total(own, given), total(sums[1][k][0], ready[k])).astype(BF)

    def second(mix):
        mix, given, own = lax.optimization_barrier((mix, sums[0][0][1], halves[1]))
        sums[0][0] = (sums[0][0][0], given)
        return mix, (own, across(own, 0))

    mix, (grad_gate, grad_up, grad_down) = reduce_all(mixer_grad, late, finish_experts, second)
    return (
        mixed,
        grad[None],
        mix[:, 3616][None],
        mix[:, 1536:3072][None],
        mix[:, 3072:3328][None],
        mix[:, 3328:3584][None],
        mix[:, :1536][None],
        mix[:, 3617][None],
        mix[:, 3584:3616][None],
        grad_gate[None],
        grad_up[None],
        grad_down[None],
    )


def solution(mesh):
    fine = Mesh(mesh.devices.reshape(2, 2, 4, 2, 4), ("section", *DEVICES))
    expert = ("yh", "z", "core")
    return jax.shard_map(
        per_device,
        mesh=fine,
        in_specs=(
            P(None, DEVICES, None),
            P("section", None, DEVICES, None),
            P(None, expert, None),
            P("section", DEVICES),
            P("section", DEVICES, None),
            P("section", DEVICES, None),
            P("section", DEVICES, None),
            P("section", DEVICES, None),
            P("section", DEVICES),
            P("section", DEVICES, None),
            P("section", expert, "shard", None),
            P("section", expert, "shard", None),
            P("section", expert, None, "shard"),
            P(None, DEVICES, None),
        ),
        out_specs=(
            P(None, DEVICES, None),
            P("section", DEVICES, None),
            P("section", DEVICES),
            P("section", DEVICES, None),
            P("section", DEVICES, None),
            P("section", DEVICES, None),
            P("section", DEVICES, None),
            P("section", DEVICES),
            P("section", DEVICES, None),
            P("section", expert, "shard", None),
            P("section", expert, "shard", None),
            P("section", expert, None, "shard"),
        ),
        check_vma=False,
    )
```

```python
import jax
import jax.numpy as jnp
from jax import lax
from jax.experimental import pallas as pl
from jax.experimental.pallas import tpu as pltpu
from jax.sharding import Mesh
from jax.sharding import PartitionSpec as P

HEADS = 12
HEAD_DIM = 128
EXPERTS = 32
MAIN = 16
EXTRA = 2
CHUNKS = 6

epsilon = 1e-06
rope_base = 1000000.0
masked_score = -1e30

BF = jnp.bfloat16
F32 = jnp.float32
CHIPS = ("yh", "z", "shard")
DEVICES = ("yh", "z", "core", "shard")


def dot(a, b, dims=((1,), (0,))):
    return lax.dot_general(a, b, (dims, ((), ())), preferred_element_type=F32)


def document_layout(doc_lengths, group_rows):
    doc_ends = jnp.cumsum(doc_lengths)
    starts = doc_ends - doc_lengths
    row_index = jnp.arange(group_rows, dtype=jnp.int32)
    segment = jnp.sum((row_index[:, None] >= doc_ends[None, :]).astype(jnp.int32), axis=1)
    member = segment[:, None] == jnp.arange(doc_lengths.shape[0], dtype=jnp.int32)[None, :]
    position = row_index - jnp.sum(jnp.where(member, starts[None, :], 0), axis=1)
    return (segment, position)


def rotary_tables(position, head_size):
    half_dim = head_size // 2
    frequency = rope_base ** (-2.0 * jnp.arange(half_dim, dtype=F32) / head_size)
    angles = position.astype(F32)[:, None] * frequency[None, :]
    cosine, sine = jnp.cos(angles), jnp.sin(angles)
    return jnp.concatenate([cosine, cosine], axis=1), jnp.concatenate([-sine, sine], axis=1)


def swap(value, axis):
    return lax.ppermute(value, axis, [(0, 1), (1, 0)])


def around(axis, size):
    here = lax.axis_index(axis)
    return [lax.rem(here + step, size) for step in range(1, size)]


def move(name, number, arrays, shapes, peers, copies):
    count = len(arrays)
    total = 40

    def kernel(*refs):
        ins, outs = refs[:count], refs[count : count + len(shapes)]
        sent, got = refs[count + len(shapes) :]
        barrier = pltpu.get_barrier_semaphore()
        near = peers()
        for peer in near:
            pl.semaphore_signal(
                barrier, inc=1, device_id=peer, device_id_type=pl.DeviceIdType.MESH
            )
        pl.semaphore_wait(barrier, len(near))
        started = []
        for k, (source, target, device) in enumerate(copies(ins, outs)):
            if device is None:
                copy = pltpu.make_async_copy(source, target, got.at[k])
            else:
                copy = pltpu.make_async_remote_copy(
                    src_ref=source,
                    dst_ref=target,
                    send_sem=sent.at[k],
                    recv_sem=got.at[k],
                    device_id=device,
                    device_id_type=pl.DeviceIdType.MESH,
                )
            copy.start()
            started.append(copy)
        for copy in started:
            copy.wait()

    space = pl.BlockSpec(memory_space=pltpu.HBM)
    return pl.pallas_call(
        kernel,
        out_shape=[jax.ShapeDtypeStruct(s, BF) for s in shapes],
        in_specs=[space] * count,
        out_specs=[space] * len(shapes),
        scratch_shapes=[pltpu.SemaphoreType.DMA((total,)), pltpu.SemaphoreType.DMA((total,))],
        compiler_params=pltpu.CompilerParams(collective_id=number, has_side_effects=True),
        name=name,
    )(*arrays)


def total(*parts):
    out = parts[0].astype(F32)
    for part in parts[1:]:
        out = out + part.astype(F32)
    return out


def at(array, index, axis):
    return lax.dynamic_index_in_dim(array, index, axis, keepdims=False)


def other(axis):
    return lax.rem(lax.axis_index(axis) + 1, 2)


def reduce_all(grads, late, finish_experts):
    core, shard, z, yh, section = (
        lax.axis_index(a) for a in ("core", "shard", "z", "yh", "section")
    )
    width = grads.shape[1]
    mix = grads.reshape(8, 2, 4, 24, width)

    got = move(
        "cores",
        1,
        [mix],
        [(8, 4, 24, width)],
        lambda: [{"core": other("core")}],
        lambda ins, outs: [(ins[0].at[:, other("core")], outs[0], {"core": other("core")})],
    )[0]
    mix = total(at(mix, core, 1), got).astype(BF).reshape(2, 4, 4, 24, width)

    cut = 1792
    sizes = (cut, width - cut)

    def peers_2():
        return [{"shard": x} for x in around("shard", 4)] + [{"z": i} for i in around("z", 4)]

    def copies_2(ins, outs):
        out = []
        for step, (x, i) in enumerate(zip(around("shard", 4), around("z", 4))):
            out.append((ins[0].at[:, :, x, :, pl.ds(0, cut)], outs[0].at[step], {"shard": x}))
            out.append((ins[0].at[:, i, :, :, pl.ds(cut, width - cut)], outs[1].at[step], {"z": i}))
        return out

    shapes = [(3, 2, 4, 24, size) for size in sizes]
    got = move("first_axis", 2, [mix], shapes, peers_2, copies_2)
    own = [
        lax.dynamic_slice(mix, (0, 0, shard, 0, 0), (2, 4, 1, 24, cut))[:, :, 0],
        lax.dynamic_slice(mix, (0, z, 0, 0, cut), (2, 1, 4, 24, width - cut))[:, 0],
    ]
    mix = [total(m, *g).astype(BF) for m, g in zip(own, got)]

    exp = finish_experts()

    def shards_of(ref, x):
        down = ref.at[
            pl.ds(pl.multiple_of(1536 + x // 2 * 384, 128), 384),
            pl.ds(pl.multiple_of(lax.rem(x, 2) * 384, 128), 384),
        ]
        gate = ref.at[pl.ds(pl.multiple_of(x * 192, 64), 192)]
        up = ref.at[pl.ds(pl.multiple_of(768 + x * 192, 64), 192)]
        return gate, up, down

    def copies_3(ins, outs):
        here = lax.axis_index("shard")
        out = []
        for step, (x, i) in enumerate(zip(around("shard", 4), around("z", 4))):
            out.append((ins[0].at[:, i], outs[0].at[step], {"z": i}))
            out.append((ins[1].at[:, x], outs[1].at[step], {"shard": x}))
            for k, source in enumerate(shards_of(ins[2], x)):
                out.append((source, outs[2 + k].at[here], {"shard": x}))
        for k, source in enumerate(shards_of(ins[2], here)):
            out.append((source, outs[2 + k].at[here], None))
        return out

    shapes = [(3, 2, 24, size) for size in sizes] + [(4, 192, 768), (4, 192, 768), (4, 384, 384)]
    got = move("other_axis", 3, [*mix, exp], shapes, peers_2, copies_3)
    mix = jnp.concatenate(
        [
            total(at(mix[0], z, 1), *got[0]).astype(BF),
            total(at(mix[1], shard, 1), *got[1]).astype(BF),
        ],
        axis=-1,
    )
    exp = got[2:]

    def places():
        here = 2 * lax.axis_index("yh") + lax.axis_index("section")
        there = [lax.rem(here + step, 4) for step in range(1, 4)]
        return [(t // 2, lax.rem(t, 2)) for t in there]

    def copies_4(ins, outs):
        there = other("core")
        out = [
            (ins[1 + k].at[pl.ds(2 * there, 2)], outs[1 + k], {"core": there}) for k in range(3)
        ]
        for step, (y, s) in enumerate(places()):
            out.append((ins[0].at[s, y], outs[0].at[step], {"yh": y, "section": s}))
        return out

    mine = (jnp.arange(2) == yh)[:, None, None]
    pairs = jnp.stack([mix, jnp.where(mine, late[None], jnp.zeros((), BF))])
    got = move(
        "last_axis",
        4,
        [pairs, *exp],
        [(3, 24, width), (2, 192, 768), (2, 192, 768), (2, 384, 384)],
        lambda: [{"yh": y, "section": s} for y, s in places()] + [{"core": other("core")}],
        copies_4,
    )
    sums = total(at(at(pairs, section, 0), yh, 0), *got[0])
    out = []
    for e, g in zip(exp, got[1:]):
        kept = lax.dynamic_slice_in_dim(e, 2 * core, 2, 0)
        low, high = jnp.where(core == 0, kept, g), jnp.where(core == 0, g, kept)
        out.append(jnp.concatenate([low, high], axis=1).astype(F32))
    return sums, out


def gather_weights(local, experts):
    rows, width = local.shape

    def kernel(*refs):
        mine, shards = refs[0], refs[1:4]
        full, late, whole = refs[4], refs[5], refs[6:9]
        stage = refs[9:12]
        sent, got, sent_x, got_e, sent_c, got_c, sent_y, sent_o, local_sem = refs[12:]
        s, yh, z, c, x = (lax.axis_index(a) for a in ("section", "yh", "z", "core", "shard"))
        place = 2 * yh + s
        ys = [lax.rem(place + k, 4) for k in (1, 2, 3)]
        ys = [{"yh": y // 2, "section": lax.rem(y, 2)} for y in ys]
        xs = [{"shard": lax.rem(x + k, 4)} for k in (1, 2, 3)]
        z_up, z_down = lax.rem(z + 1, 4), lax.rem(z + 3, 4)
        sibling, partner = {"core": 1 - c}, {"section": 1 - s}

        def piece(k, i, h):
            if k == 2:
                return shards[2].at[i, pl.ds(pl.multiple_of(h * 384, 128), 384)]
            return shards[k].at[i, pl.ds(pl.multiple_of(h * 192, 64), 192)]

        def landing(k, layer, source, half):
            if k == 2:
                return whole[2].at[layer, half, :, pl.ds(pl.multiple_of(source * 384, 128), 384)]
            return whole[k].at[layer, source, half]

        def remote(source, target, send, receive, device):
            return pltpu.make_async_remote_copy(
                src_ref=source,
                dst_ref=target,
                send_sem=send,
                recv_sem=receive,
                device_id=device,
                device_id_type=pl.DeviceIdType.MESH,
            )

        def start(copies):
            for copy in copies:
                copy.start()
            return copies

        def finish(copies):
            for copy in copies:
                copy.wait()

        has_own = x // 2 == c
        own = lax.rem(x, 2)
        staged = start(
            [pltpu.make_async_copy(piece(k, own, c), stage[k], local_sem.at[k]) for k in range(3)]
        )
        barrier = pltpu.get_barrier_semaphore()
        zs = [{"z": lax.rem(z + k, 4)} for k in (1, 2, 3)]
        x_up, x_down = xs[0]["shard"], xs[2]["shard"]
        near = ys + xs + zs + [sibling]
        near += [{"shard": lax.rem(x + k, 4), "core": 1 - c} for k in (1, 2, 3)]
        for peer in near:
            pl.semaphore_signal(
                barrier, inc=1, device_id=peer, device_id_type=pl.DeviceIdType.MESH
            )
        pl.semaphore_wait(barrier, len(near))

        here = full.at[yh, z, c, x]

        def along_y(target):
            out = [pltpu.make_async_copy(mine, target, local_sem.at[3])]
            for k, device in enumerate(ys):
                out.append(remote(mine, target, sent.at[k], got.at[k], device))
            return out

        @pl.when(s == 0)
        def _():
            start(along_y(here))

        @pl.when(s == 1)
        def _():
            start(along_y(late.at[yh, z, c, x]))

        finish(staged)

        @pl.when(has_own)
        def _():
            for k in range(3):
                remote(
                    piece(k, own, 1 - c),
                    landing(k, s, x, 1 - c),
                    sent_o.at[k],
                    got_e.at[s, x, k],
                    sibling,
                ).start()
                pltpu.make_async_copy(stage[k], landing(k, s, x, c), got_e.at[s, x, k]).start()

        def pass_on(layer, distance, to_partner):
            source = lax.rem(x + distance, 4)
            for k in range(3):
                view = landing(k, layer, source, c)
                receive = got_e.at[layer, source, k]
                remote(view, view, sent_o.at[k], receive, sibling).wait_recv()
                if to_partner:
                    remote(view, view, sent_y.at[distance, k], receive, partner).start()
                across = got_c.at[layer, source, k]
                remote(view, view, sent_c.at[layer, source, k], across, sibling).start()

        finish(along_y(here))
        view, view_late = full.at[:, z, c, x], late.at[:, z, c, x]
        along_x = start(
            [remote(view, view, sent.at[3 + k], got.at[3 + k], xs[k]) for k in range(3)]
        )
        late_z = start(
            [
                remote(view_late, view_late, sent.at[11 + k], got.at[11 + k], zs[k])
                for k in range(3)
            ]
        )
        pass_on(s, 0, True)
        finish(along_x)

        def ring(base, axis, places, up, down):
            return start(
                [
                    remote(up, up, sent.at[base], got.at[base], {axis: places[0]}),
                    remote(down, down, sent.at[base + 1], got.at[base + 1], {axis: places[1]}),
                ]
            )

        view = full.at[:, z, c]
        along_z = ring(6, "z", (z_up, z_down), view, view)
        for i in range(2):

            @pl.when(x != 2 * c + i)
            def _():
                for h in range(2):
                    for k in range(3):
                        remote(
                            piece(k, i, h),
                            landing(k, s, x, h),
                            sent_x.at[(i * 2 + h) * 3 + k],
                            got_e.at[s, x, k],
                            {"shard": 2 * c + i, "core": h},
                        ).start()

        finish(late_z)
        view = late.at[:, :, c, x]
        late_x = ring(14, "shard", (x_up, x_down), view, view)
        finish(along_z)
        along_z = ring(8, "z", (z_up, z_down), full.at[0, z_down, c], full.at[1, z_up, c])
        for distance in (1, 3, 2):
            pass_on(s, distance, True)
        finish(along_z)
        view = full.at[:, :, c]
        across = start([remote(view, view, sent.at[10], got.at[10], sibling)])
        finish(late_x)
        late_x = ring(
            16, "shard", (x_up, x_down), late.at[0, :, c, x_down], late.at[1, :, c, x_up]
        )
        for distance in (0, 1):
            pass_on(1 - s, distance, False)
        finish(late_x)
        view = late.at[:, :, c]
        across += start([remote(view, view, sent.at[18], got.at[18], sibling)])
        for distance in (3, 2):
            pass_on(1 - s, distance, False)

        finish(across)
        for i in range(2):

            @pl.when(x != 2 * c + i)
            def _():
                for h in range(2):
                    for k in range(3):
                        view = piece(k, i, h)
                        n = (i * 2 + h) * 3 + k
                        remote(view, view, sent_x.at[n], got_e.at[0, 0, k], sibling).wait_send()

        @pl.when(has_own)
        def _():
            for k in range(3):
                view = piece(k, own, 1 - c)
                remote(view, view, sent_o.at[k], got_e.at[0, 0, k], sibling).wait_send()

        for source in range(4):
            for k in range(3):
                view = landing(k, s, source, c)
                send = sent_y.at[source, k]
                remote(view, view, send, got_e.at[0, 0, k], partner).wait_send()
                for layer in range(2):
                    view = landing(k, layer, source, c)
                    arrived = landing(k, layer, source, 1 - c)
                    send, receive = sent_c.at[layer, source, k], got_c.at[layer, source, k]
                    remote(view, view, send, receive, sibling).wait_send()
                    remote(arrived, arrived, send, receive, sibling).wait_recv()

    space = pl.BlockSpec(memory_space=pltpu.HBM)
    near_space = pl.BlockSpec(memory_space=pltpu.VMEM)
    shapes = [(2, 4, 2, 4, rows, width)] * 2
    shapes += [(2, 4, 2, 192, 768), (2, 4, 2, 192, 768), (2, 2, 384, 1536)]
    dma = pltpu.SemaphoreType.DMA
    return pl.pallas_call(
        kernel,
        out_shape=[jax.ShapeDtypeStruct(shape, BF) for shape in shapes],
        in_specs=[near_space] + [space] * 3,
        out_specs=[space] * 5,
        scratch_shapes=[
            pltpu.VMEM((192, 768), BF),
            pltpu.VMEM((192, 768), BF),
            pltpu.VMEM((384, 384), BF),
            dma((19,)),
            dma((19,)),
            dma((12,)),
            dma((2, 4, 3)),
            dma((2, 4, 3)),
            dma((2, 4, 3)),
            dma((4, 3)),
            dma((3,)),
            dma((4,)),
        ],
        compiler_params=pltpu.CompilerParams(collective_id=0, has_side_effects=True),
        name="gather_weights",
    )(local, *experts)


def rank_of(route_rows):
    rows = route_rows.shape[0]
    chosen = route_rows.T[None, :, :] == jnp.arange(EXPERTS, dtype=jnp.int32)[:, None, None]
    hot = jnp.any(chosen, axis=1)
    index = jnp.arange(rows, dtype=jnp.int32)
    before = (index[:, None] < index[None, :]).astype(BF)
    return jnp.where(hot, dot(hot.astype(BF), before), -1.0)


def stacked(field):
    return jnp.concatenate(jnp.split(field, CHUNKS, axis=1), axis=0)


def unstacked(field):
    return jnp.concatenate(jnp.split(field, CHUNKS, axis=0), axis=1)


def unfold_table(sources):
    row = jnp.arange(CHUNKS * sources * EXTRA, dtype=jnp.int32)
    piece, source, extra = row // (sources * EXTRA), row // EXTRA % sources, row % EXTRA
    column = jnp.arange(sources * MAIN, dtype=jnp.int32)
    return (
        (source * MAIN + piece * EXTRA + extra)[:, None] == column[None, :]
    ).astype(BF)


def arrived_rows(message, unfold):
    width = message.shape[1] - 256
    extra = unstacked(dot(unfold, message[:, width:]).astype(BF))
    return jnp.concatenate([message[:, :width], extra], axis=0)


def fold_rows(rows, unfold, sources):
    main = rows[: sources * MAIN]
    extra = dot(unfold, stacked(rows[sources * MAIN :]), ((0,), (0,))).astype(BF)
    return jnp.concatenate([main, extra], axis=1)


def low_pair(value):
    high = value.astype(BF)
    return high, (value - high.astype(F32)).astype(BF)


OUT_COLUMNS, QKV_STEP = 1536, 512


def columns(width, place):
    return lambda rows: pl.BlockSpec((rows, width), lambda i: (0, place), memory_space=pltpu.VMEM)


OUT_BLOCK = [columns(OUT_COLUMNS, 0)]
QKV_BLOCKS = [columns(QKV_STEP, 3 + k) for k in range(4)]
NARROW_BLOCK = [columns(128, 28)]


def fused(name, body, shapes, *arrays, scratch=(), number=None):
    near = pl.BlockSpec(memory_space=pltpu.VMEM)
    specs, given = [], []
    for array in arrays:
        if isinstance(array, tuple):
            array, blocks = array
            specs += [block(array.shape[0]) for block in blocks]
            given += [array] * len(blocks)
        else:
            specs.append(near)
            given.append(array)
    return pl.pallas_call(
        body,
        grid=(1,),
        out_shape=[jax.ShapeDtypeStruct(shape, kind) for shape, kind in shapes],
        in_specs=specs,
        out_specs=[near] * len(shapes),
        scratch_shapes=list(scratch),
        compiler_params=pltpu.CompilerParams(
            vmem_limit_bytes=48 << 20, collective_id=number, has_side_effects=number is not None
        ),
        name=name,
    )(*given)


TN, NT = ((0,), (0,)), ((1,), (1,))


def slots(rank):
    count, rows = rank.shape
    place = lax.broadcasted_iota(jnp.int32, (count, MAIN, rows), 1)
    wide = jnp.broadcast_to(rank[:, None, :], (count, MAIN, rows))
    main = jnp.where(wide == place.astype(F32), 1.0, 0.0)
    extra = (MAIN + lax.rem(place, EXTRA)).astype(F32)
    extra = jnp.where((wide == extra) & (place < EXTRA * CHUNKS), 1.0, 0.0)
    return main, extra


def per_piece(table):
    piece = lax.rem(lax.broadcasted_iota(jnp.int32, table.shape, 0), MAIN) // EXTRA
    return [jnp.where(piece == j, table, 0.0) for j in range(CHUNKS)]


def flat(table):
    return table.reshape(table.shape[0] * table.shape[1], table.shape[2])


def send_table(main, extra, field):
    width = field.shape[1] // CHUNKS
    side = None
    for j, table in enumerate(per_piece(flat(extra))):
        part = dot(table.astype(BF), field[:, j * width : (j + 1) * width])
        side = part if side is None else side + part
    return dot(flat(main).astype(BF), field), side


def bring_back(main, extra, rows, exact):
    parts = low_pair if exact else (lambda t: (t.astype(BF),))
    model_width = rows.shape[1] - 256
    total_main = None
    for table in parts(main):
        part = dot(table, rows[:, :model_width], TN)
        total_main = part if total_main is None else total_main + part
    side = []
    for table in per_piece(extra):
        total_side = None
        for t in parts(table):
            part = dot(t, rows[:, model_width:], TN)
            total_side = part if total_side is None else total_side + part
        side.append(total_side)
    return total_main + jnp.concatenate(side, axis=1)


def gain_rows(narrow):
    row = lax.broadcasted_iota(jnp.int32, (8, narrow.shape[1]), 0)
    column = lax.broadcasted_iota(jnp.int32, (8, narrow.shape[1]), 1)
    pick = jnp.where(column == row + EXPERTS, 1.0, 0.0).astype(BF)
    rows = dot(pick, narrow, NT)
    return rows[0:1], rows[1:2]


def turn(field, cosine, sine):
    return field * cosine + pltpu.roll(field, HEAD_DIM // 2, 1) * sine


def turn_back(field, cosine, sine):
    return field * cosine - pltpu.roll(field, HEAD_DIM // 2, 1) * sine


def combined(x_mid, rank, gates, rows):
    main, extra = slots(rank)
    wide = jnp.broadcast_to(gates[:, None, :], main.shape)
    return x_mid + bring_back(flat(main * wide), flat(extra * wide), rows, True)


def finish_body(mid_ref, rank_ref, gates_ref, rows_ref, out_ref):
    out = combined(mid_ref[...], rank_ref[...], gates_ref[...], rows_ref[...])
    out_ref[...] = out.astype(BF)


def heads_of(kv_ref):
    kv_heads = kv_ref.shape[2] // 2 // HEAD_DIM
    parts = []
    for k in range(2 * kv_heads):
        part = kv_ref[:, :, k * HEAD_DIM : (k + 1) * HEAD_DIM]
        parts.append(part.reshape(part.shape[0] * part.shape[1], HEAD_DIM))
    return parts[:kv_heads], parts[kv_heads:]


def attention_body(combine):
    def body(*refs):
        source, refs = refs[: 4 if combine else 1], refs[4 if combine else 1 :]
        weights, refs = refs[:4], refs[4:]
        out_w, narrow, cos_ref, sin_ref, allowed_ref, rank_ref, low_ref, h_ref, q_ref = refs[:9]
        kv_ref, mid_ref, h2_ref, att_ref, probs_ref, gates_ref, out_ref, held, sent, got = refs[9:]
        here = lax.axis_index("shard")
        peers = [{"shard": x} for x in around("shard", 4)]
        barrier = pltpu.get_barrier_semaphore()
        for peer in peers:
            pl.semaphore_signal(
                barrier, inc=1, device_id=peer, device_id_type=pl.DeviceIdType.MESH
            )
        if combine:
            mid, rank, gates, rows = (ref[...] for ref in source)
            low = combined(mid, rank, gates, rows).astype(BF)
        else:
            low = source[0][...]
        low_ref[...] = low
        field = low.astype(F32)
        gain_a, gain_m = gain_rows(narrow[...])
        scale = lax.rsqrt(jnp.mean(field * field, axis=1, keepdims=True) + epsilon)
        h = (field * scale * gain_a).astype(BF)
        h_ref[...] = h
        cosine, sine = cos_ref[...], sin_ref[...]

        def projected(column, turned):
            inside = column % QKV_STEP
            part = dot(h, weights[column // QKV_STEP][:, inside : inside + 256])
            if turned:
                part = jnp.concatenate(
                    [turn(part[:, k : k + HEAD_DIM], cosine, sine) for k in (0, HEAD_DIM)], axis=1
                )
            return part.astype(BF)

        query_width, kv_width = q_ref.shape[1], kv_ref.shape[2]
        for column in range(0, kv_width, 256):
            part = projected(query_width + column, column < kv_width // 2)
            held[here, :, column : column + 256] = part
        pl.semaphore_wait(barrier, len(peers))
        copies = []
        for k, peer in enumerate(peers):
            view = held.at[here]
            copies.append(
                pltpu.make_async_remote_copy(
                    src_ref=view,
                    dst_ref=view,
                    send_sem=sent.at[k],
                    recv_sem=got.at[k],
                    device_id=peer,
                    device_id_type=pl.DeviceIdType.MESH,
                )
            )
            copies[-1].start()
        for column in range(0, query_width, 256):
            q_ref[:, column : column + 256] = projected(column, True)
        for copy in copies:
            copy.wait()

        kv_ref[...] = held[...]
        keys, values = heads_of(held)
        allowed = allowed_ref[...] > 0.0
        ratio = HEADS // len(keys)
        for head in range(HEADS):
            lanes = slice(head * HEAD_DIM, (head + 1) * HEAD_DIM)
            scores = dot(q_ref[:, lanes], keys[head // ratio], NT) * HEAD_DIM ** (-0.5)
            scores = jnp.where(allowed, scores, masked_score)
            exponent = jnp.exp(scores - jnp.max(scores, axis=1, keepdims=True))
            probs = exponent / jnp.sum(exponent, axis=1, keepdims=True)
            probs_ref[head] = probs
            att_ref[:, lanes] = dot(probs.astype(BF), values[head // ratio]).astype(BF)
        mid = field + dot(att_ref[...], out_w[...])
        mid_ref[...] = mid
        scale = lax.rsqrt(jnp.mean(mid * mid, axis=1, keepdims=True) + epsilon)
        h2 = (mid * scale * gain_m).astype(BF)
        h2_ref[...] = h2
        rank = rank_ref[...]
        logits = jnp.transpose(dot(h2, narrow[...]))[:EXPERTS]
        logits = jnp.where(rank >= 0.0, logits, masked_score)
        gate_exp = jnp.exp(logits - jnp.max(logits, axis=0, keepdims=True))
        gate_exp = jnp.where(rank >= 0.0, gate_exp, 0.0)
        gates_ref[...] = gate_exp / jnp.sum(gate_exp, axis=0, keepdims=True)
        main, side = send_table(*slots(rank), h2)
        width = main.shape[1]
        out_ref[:, :width] = main.astype(BF)
        out_ref[:, width:] = side.astype(BF)

    return body


def attention(source, weights, tables, allowed, rank, number):
    tok_rows, model_width = source[0].shape
    query_width = HEADS * HEAD_DIM
    shapes = [((tok_rows, model_width), BF)] * 2
    shapes += [
        ((tok_rows, query_width), BF),
        ((allowed.shape[1] // tok_rows, tok_rows, 4 * QKV_STEP - query_width), BF),
        ((tok_rows, model_width), F32),
        ((tok_rows, model_width), BF),
        ((tok_rows, query_width), BF),
        ((HEADS, tok_rows, allowed.shape[1]), F32),
        (rank.shape, F32),
        ((EXPERTS * MAIN, model_width + 256), BF),
    ]
    dma = pltpu.SemaphoreType.DMA
    return fused(
        "attention",
        attention_body(len(source) > 1),
        shapes,
        *source,
        (weights, QKV_BLOCKS + OUT_BLOCK + NARROW_BLOCK),
        *tables,
        allowed,
        rank,
        scratch=[pltpu.VMEM(shapes[3][0], BF), dma((3,)), dma((3,))],
        number=number,
    )


def grad_slots_body(grad_ref, rank_ref, gates_ref, rows_ref, out_ref, dlogits_ref):
    gates = gates_ref[...]
    main, extra = slots(rank_ref[...])
    wide = jnp.broadcast_to(gates[:, None, :], main.shape)
    grad_main, grad_side = send_table(main, extra, grad_ref[...])
    width = grad_main.shape[1]
    dgate = None
    for table, grad, columns in (
        (main, grad_main, slice(0, width)),
        (extra, grad_side, slice(width, width + 256)),
    ):
        slot_gate = jnp.sum(flat(table * wide), axis=1, keepdims=True)
        out_ref[:, columns] = (grad * slot_gate).astype(BF)
        slot_dgate = jnp.sum(grad * rows_ref[:, columns].astype(F32), axis=1, keepdims=True)
        part = jnp.sum((flat(table) * slot_dgate).reshape(table.shape), axis=1)
        dgate = part if dgate is None else dgate + part
    dlogits = gates * (dgate - jnp.sum(gates * dgate, axis=0, keepdims=True))
    pad = jnp.zeros((dlogits_ref.shape[1] - EXPERTS, dlogits.shape[1]), F32)
    dlogits_ref[...] = jnp.transpose(jnp.concatenate([dlogits, pad], axis=0)).astype(BF)


def grad_slots(grad, rank, gates, rows):
    shapes = [(rows.shape, BF), ((grad.shape[0], 128), BF)]
    return fused("grad_slots", grad_slots_body, shapes, grad, rank, gates, rows)


def norm_grads(field, gain, grad):
    scale = lax.rsqrt(jnp.mean(field * field, axis=1, keepdims=True) + epsilon)
    scaled = grad * gain
    centre = jnp.mean(scaled * field, axis=1, keepdims=True)
    dgain = jnp.sum(grad * field * scale, axis=0, keepdims=True)
    return scale * scaled - field * (scale * scale * scale) * centre, dgain


def grad_attention_body(
    grad_ref, rows_ref, rank_ref, dlogits_ref, out_w, weight_0, weight_1, weight_2, weight_3, narrow,
    mid_ref, q_ref, kv_ref, probs_ref, cos_ref, sin_ref, low_ref,
    dbr_ref, dqkv_ref, grad_out_ref, dgain_a_ref, dgain_m_ref,
    datt_ref, dkv_ref, held, sent, got,
):
    here = lax.axis_index("shard")
    peers = [{"shard": x} for x in around("shard", 4)]
    barrier = pltpu.get_barrier_semaphore()
    for peer in peers:
        pl.semaphore_signal(barrier, inc=1, device_id=peer, device_id_type=pl.DeviceIdType.MESH)
    main, extra = slots(rank_ref[...])
    dh = bring_back(flat(main), flat(extra), rows_ref[...], False)
    dh = dh + dot(dlogits_ref[...], narrow[...], NT)
    gain_a, gain_m = gain_rows(narrow[...])
    dmid, dgain = norm_grads(mid_ref[...], gain_m, dh)
    dmid = dmid + grad_ref[...].astype(F32)
    dgain_m_ref[...] = dgain
    dbr_ref[...] = dmid.astype(BF)
    datt_ref[...] = dot(dbr_ref[...], out_w[...], NT).astype(BF)
    keys, values = heads_of(kv_ref)
    ratio = HEADS // len(keys)
    cosine, sine = cos_ref[...], sin_ref[...]
    count, tok_rows, kv_columns = kv_ref.shape
    scale = HEAD_DIM ** (-0.5)
    for k in range(len(keys)):
        dkey, dvalue = None, None
        for head in range(k * ratio, (k + 1) * ratio):
            lanes = slice(head * HEAD_DIM, (head + 1) * HEAD_DIM)
            probs, datt = probs_ref[head], datt_ref[:, lanes]
            dprobs = dot(datt, values[k], NT)
            centre = jnp.sum(dprobs * probs, axis=1, keepdims=True)
            dscores = (probs * (dprobs - centre)).astype(BF)
            part = dot(probs.astype(BF), datt, TN)
            dvalue = part if dvalue is None else dvalue + part
            part = dot(dscores, q_ref[:, lanes], TN)
            dkey = part if dkey is None else dkey + part
            dquery = dot(dscores, keys[k]) * scale
            dqkv_ref[:, lanes] = turn_back(dquery, cosine, sine).astype(BF)
        at_key, at_value = k * HEAD_DIM, (len(keys) + k) * HEAD_DIM
        shape = (count, tok_rows, HEAD_DIM)
        dkv_ref[:, :, at_key : at_key + HEAD_DIM] = (dkey * scale).astype(BF).reshape(shape)
        dkv_ref[:, :, at_value : at_value + HEAD_DIM] = dvalue.astype(BF).reshape(shape)
    pl.semaphore_wait(barrier, len(peers))
    copies = []
    for k, peer in enumerate(peers):
        copies.append(
            pltpu.make_async_remote_copy(
                src_ref=dkv_ref.at[peer["shard"]],
                dst_ref=held.at[k],
                send_sem=sent.at[k],
                recv_sem=got.at[k],
                device_id=peer,
                device_id_type=pl.DeviceIdType.MESH,
            )
        )
        copies[-1].start()
    query_width = q_ref.shape[1]
    dh = None
    weights = (weight_0, weight_1, weight_2, weight_3)
    for k, weight in enumerate(weights[:-1]):
        part = dot(dqkv_ref[:, k * QKV_STEP : (k + 1) * QKV_STEP], weight[...], NT)
        dh = part if dh is None else dh + part
    for copy in copies:
        copy.wait()
    dkv = dkv_ref[here].astype(F32)
    for k in range(len(peers)):
        dkv = dkv + held[k].astype(F32)
    for k in range(0, kv_columns // 2, HEAD_DIM):
        part = turn_back(dkv[:, k : k + HEAD_DIM], cosine, sine)
        dqkv_ref[:, query_width + k : query_width + k + HEAD_DIM] = part.astype(BF)
    dqkv_ref[:, query_width + kv_columns // 2 :] = dkv[:, kv_columns // 2 :].astype(BF)
    dh = dh + dot(dqkv_ref[:, query_width:], weights[-1][...], NT)
    dlow, dgain = norm_grads(low_ref[...].astype(F32), gain_a, dh)
    dgain_a_ref[...] = dgain
    grad_out_ref[...] = (dlow + dmid).astype(BF)


def grad_attention(
    grad, rows, rank, dlogits, weights, mid, q, kv, probs, tables, low, number
):
    tok_rows, model_width = mid.shape
    shapes = [
        ((tok_rows, model_width), BF),
        ((tok_rows, 4 * QKV_STEP), BF),
        ((tok_rows, model_width), BF),
        ((1, model_width), F32),
        ((1, model_width), F32),
    ]
    dma = pltpu.SemaphoreType.DMA
    return fused(
        "grad_attention",
        grad_attention_body,
        shapes,
        grad,
        rows,
        rank,
        dlogits,
        (weights, OUT_BLOCK + QKV_BLOCKS + NARROW_BLOCK),
        mid,
        q,
        kv,
        probs,
        *tables,
        low,
        scratch=[
            pltpu.VMEM(q.shape, BF),
            pltpu.VMEM(kv.shape, BF),
            pltpu.VMEM((3, *kv.shape[1:]), BF),
            dma((3,)),
            dma((3,)),
        ],
        number=number,
    )


def weight_grads_body(
    h_ref, dqkv_ref, att_ref, dbr_ref, h2_ref, dlogits_ref, dgain_a_ref, dgain_m_ref, out_ref
):
    step = 512
    place = 0
    for left, right in ((att_ref, dbr_ref), (h_ref, dqkv_ref)):
        for k in range(0, right.shape[1], step):
            part = dot(left[...], right[:, k : k + step], TN)
            out_ref[:, place : place + step] = part.astype(BF)
            place += step
    narrow = dot(h2_ref[...], dlogits_ref[...], TN)
    rows = jnp.concatenate(
        [dgain_a_ref[...], dgain_m_ref[...], jnp.zeros((126, h_ref.shape[1]), F32)], axis=0
    )
    columns = pltpu.roll(jnp.transpose(rows), EXPERTS, 1)
    out_ref[:, place:] = (narrow + columns).astype(BF)


def weight_grads(h, dqkv, att, dbr, h2, dlogits, dgain_a, dgain_m):
    columns = dqkv.shape[1] + dbr.shape[1] + 128
    return fused(
        "weight_grads", weight_grads_body, [((h.shape[1], columns), BF)],
        h, dqkv, att, dbr, h2, dlogits, dgain_a, dgain_m,
    )[0]


def greet(peers):
    barrier = pltpu.get_barrier_semaphore()
    for peer in peers:
        pl.semaphore_signal(barrier, inc=1, device_id=peer, device_id_type=pl.DeviceIdType.MESH)
    pl.semaphore_wait(barrier, len(peers))


PARTNERS = [(dy, dz, (dz + k) % 4) for k in range(4) for dy in range(2) for dz in range(4)]
GROUP = 8
GROUPS = len(PARTNERS) // GROUP


def facing(n):
    k, dy, dz = n // GROUP, n // 4 % 2, n % 4
    return -k % GROUPS * GROUP + dy * 4 + -dz % 4


def partners():
    s, yh, z, x = (lax.axis_index(a) for a in ("section", "yh", "z", "shard"))
    out = []
    for dy, dz, dx in PARTNERS:
        there = {
            "section": lax.rem(s + dy, 2),
            "yh": lax.rem(yh + dy, 2),
            "z": lax.rem(z + dz, 4),
            "shard": lax.rem(x + dx, 4),
        }
        out.append((there, (there["yh"] * 4 + there["z"]) * 4 + there["shard"]))
    return out


def exchange_rows(message, returned, arrived, produced, sems, work, after, load, sibling=()):
    sent, got, sent_back, got_back = sems
    for copy in load:
        copy.start()
    near = partners()
    own = near[0][1]
    greet([device for device, _ in near[1:]] + list(sibling))

    def remote(source, target, send, receive, device):
        return pltpu.make_async_remote_copy(
            src_ref=source,
            dst_ref=target,
            send_sem=send,
            recv_sem=receive,
            device_id=device,
            device_id_type=pl.DeviceIdType.MESH,
        )

    def out(n):
        device, expert = near[n]
        f = facing(n)
        return remote(message.at[expert], arrived.at[f], sent.at[n], got.at[f], device)

    def back(n):
        return remote(
            produced.at[n], returned.at[own], sent_back.at[n], got_back.at[facing(n)], near[n][0]
        )

    for k in range(GROUPS):
        for n in range(-k % GROUPS * GROUP, -k % GROUPS * GROUP + GROUP):
            if n:
                out(n).start()
    arrived[0] = message[own]
    for copy in load:
        copy.wait()
    for k in range(GROUPS):
        members = range(k * GROUP, (k + 1) * GROUP)
        for n in members:
            if n:
                remote(arrived.at[n], arrived.at[n], sent.at[n], got.at[n], near[n][0]).wait_recv()
        rows = arrived[k * GROUP : (k + 1) * GROUP]
        result = work(k, rows.reshape(GROUP * MAIN, rows.shape[2]))
        produced[k * GROUP : (k + 1) * GROUP] = result.reshape(rows.shape)
        for n in members:
            if n:
                back(n).start()
    returned[own] = produced[0]
    after()
    for n in range(1, len(near)):
        device, expert = near[n]
        out(n).wait_send()
        back(n).wait_send()
        view = returned.at[expert]
        remote(view, view, sent_back.at[n], got_back.at[n], device).wait_recv()


def exchange_call(name, number, body, inputs, whole, shapes, message_shape, scratch):
    near = pl.BlockSpec(memory_space=pltpu.VMEM)
    far = pl.BlockSpec(memory_space=pltpu.HBM)
    dma = pltpu.SemaphoreType.DMA
    count = message_shape[0]
    return pl.pallas_call(
        body,
        out_shape=[jax.ShapeDtypeStruct(shape, kind) for shape, kind in shapes],
        in_specs=[far] * len(whole) + [near] * len(inputs),
        out_specs=[near] * len(shapes),
        scratch_shapes=[pltpu.VMEM(w.shape[1:], BF) for w in whole]
        + [dma((len(whole),))]
        + [pltpu.VMEM(message_shape, BF), pltpu.VMEM(message_shape, BF)]
        + [dma((count,)) for _ in range(4)]
        + scratch,
        compiler_params=pltpu.CompilerParams(
            collective_id=number, has_side_effects=True, vmem_limit_bytes=56 << 20
        ),
        name=name,
    )(*whole, *inputs)


def loads(whole, layer, held, sem):
    copies = [pltpu.make_async_copy(w.at[layer], h, sem.at[k]) for k, (w, h) in enumerate(zip(whole, held))]

    def matrix(k):
        value = held[k][...]
        return value.reshape(-1, value.shape[-1])

    return copies, matrix


def expert_forward(message, experts, layer, unfold, number):
    message = message.reshape(EXPERTS, MAIN, message.shape[1])
    rows = GROUP * (MAIN + EXTRA)
    depth, width = message.shape[2] - 256, experts[0].shape[-1]

    def body(*refs):
        whole, (message_ref, unfold_ref), refs = refs[:3], refs[3:5], refs[5:]
        returned, rows_ref, gate_ref, up_ref, hidden_ref = refs[:5]
        load, matrix = loads(whole, layer, refs[5:8], refs[8])
        arrived, produced, *sems = refs[9:]

        def work(k, came):
            field = arrived_rows(came, unfold_ref[...])
            rows_ref[k] = field
            gate = dot(field, matrix(0))
            up = dot(field, matrix(1))
            gate_ref[k] = gate
            up_ref[k] = up
            hidden = (gate / (1.0 + jnp.exp(-gate)) * up).astype(BF)
            hidden_ref[k] = hidden
            return fold_rows(dot(hidden, matrix(2)).astype(BF), unfold_ref[...], GROUP)

        exchange_rows(message_ref, returned, arrived, produced, sems, work, lambda: None, load)

    shapes = [
        (message.shape, BF),
        ((GROUPS, rows, depth), BF),
        ((GROUPS, rows, width), F32),
        ((GROUPS, rows, width), F32),
        ((GROUPS, rows, width), BF),
    ]
    returned, *kept = exchange_call(
        "expert_forward", number, body, [message, unfold], experts, shapes, message.shape, []
    )
    return returned.reshape(-1, message.shape[2]), kept


def expert_backward(message, experts, layer, kept, unfold, number):
    message = message.reshape(EXPERTS, MAIN, message.shape[1])
    rows = GROUP * (MAIN + EXTRA)
    depth, width = message.shape[2] - 256, experts[0].shape[-1]
    shards = 4
    half, deep = depth // 8, width // 2

    def body(*refs):
        whole, refs = refs[:3], refs[3:]
        message_ref, rows_ref, gate_ref, up_ref, hidden_ref, unfold_ref = refs[:6]
        returned, sum_ref = refs[6:8]
        load, matrix = loads(whole, layer, refs[8:11], refs[11])
        (arrived, produced), refs = refs[12:14], refs[14:]
        sems, (came_ref, dgate_ref, dup_ref) = refs[:4], refs[4:7]
        wide_refs, (down_ref, held_gate, held_up, held_down, sent, got) = refs[7:9], refs[9:]
        core = lax.axis_index("core")
        sibling = {"core": 1 - core}

        def work(k, came):
            field = arrived_rows(came, unfold_ref[...])
            came_ref[k] = field
            dhidden = dot(field, matrix(2), NT)
            gate = gate_ref[k]
            logistic = 1.0 / (1.0 + jnp.exp(-gate))
            dgate = dhidden * up_ref[k] * (logistic * (1.0 + gate * (1.0 - logistic)))
            dgate_ref[k] = dgate.astype(BF)
            dup_ref[k] = (dhidden * (gate * logistic)).astype(BF)
            out = dot(dgate_ref[k], matrix(0), NT) + dot(dup_ref[k], matrix(1), NT)
            return fold_rows(out.astype(BF), unfold_ref[...], GROUP)

        def to_sibling(k):
            views = [wide_refs[0].at[:, 1 - core], wide_refs[1].at[:, 1 - core]]
            views.append(down_ref.at[1 - core])
            return pltpu.make_async_remote_copy(
                src_ref=views[k],
                dst_ref=(held_gate, held_up, held_down)[k],
                send_sem=sent.at[k],
                recv_sem=got.at[k],
                device_id=sibling,
                device_id_type=pl.DeviceIdType.MESH,
            )

        def after():
            step = 256
            field = rows_ref[...].reshape(GROUPS * rows, depth)
            for k, source in enumerate((dgate_ref, dup_ref)):
                for column in range(0, width, step):
                    lanes = slice(column, column + step)
                    part = source[:, :, lanes].reshape(GROUPS * rows, step)
                    part = dot(field, part, TN).astype(BF)
                    wide_refs[k][:, :, :, lanes] = part.reshape(shards, 2, half, step)
                to_sibling(k).start()
            field = hidden_ref[...].reshape(GROUPS * rows, width)
            for column in range(0, depth, step):
                lanes = slice(column, column + step)
                part = came_ref[:, :, lanes].reshape(GROUPS * rows, step)
                part = dot(field, part, TN).astype(BF)
                down_ref[:, :, lanes] = part.reshape(2, deep, step)
            to_sibling(2).start()

        exchange_rows(
            message_ref, returned, arrived, produced, sems, work, after, load, (sibling,)
        )
        for k, held in enumerate((held_gate, held_up)):
            to_sibling(k).wait()
            for j in range(shards):
                part = wide_refs[k][j, core].astype(F32) + held[j].astype(F32)
                place = (k * shards + j) * half
                sum_ref[place : place + half] = part.astype(BF)
        to_sibling(2).wait()
        part = down_ref[core].astype(F32) + held_down[...].astype(F32)
        place = 2 * shards * half
        for j in range(2):
            columns_of = part[:, j * width : (j + 1) * width].astype(BF)
            sum_ref[place + j * deep : place + (j + 1) * deep] = columns_of

    shapes = [(message.shape, BF), ((3 * shards * half, width), BF)]
    dma = pltpu.SemaphoreType.DMA
    scratch = [
        pltpu.VMEM((GROUPS, rows, depth), BF),
        pltpu.VMEM((GROUPS, rows, width), BF),
        pltpu.VMEM((GROUPS, rows, width), BF),
        pltpu.VMEM((shards, 2, half, width), BF),
        pltpu.VMEM((shards, 2, half, width), BF),
        pltpu.VMEM((2, deep, depth), BF),
        pltpu.VMEM((shards, half, width), BF),
        pltpu.VMEM((shards, half, width), BF),
        pltpu.VMEM((deep, depth), BF),
        dma((3,)),
        dma((3,)),
    ]
    returned, sums = exchange_call(
        "expert_backward",
        number,
        body,
        [message, *kept, unfold],
        experts,
        shapes,
        message.shape,
        scratch,
    )
    return returned.reshape(-1, message.shape[2]), sums


def forward_layer(source, weights, experts, layer, rank, unfold, tables, allowed, numbers):
    low, h_attn, query, kv_all, x_mid, h_moe, attended, probs, gates, message = attention(
        source, weights, tables, allowed, rank, numbers[0]
    )
    returned, kept = expert_forward(message, experts, layer, unfold, numbers[1])
    stored = {
        "low": low,
        "h_attn": h_attn,
        "query": query,
        "kv_all": kv_all,
        "probs": probs,
        "attended": attended,
        "x_mid": x_mid,
        "h_moe": h_moe,
        "gates": gates,
        "returned": returned,
        "kept": kept,
    }
    return (x_mid, rank, gates, returned), stored


def backward_layer(grad, ready, stored, weights, experts, layer, rank, unfold, tables, numbers):
    message, dlogits = grad_slots(grad, rank, stored["gates"], stored["returned"])
    returned, half = expert_backward(
        message, experts, layer, stored["kept"], unfold, numbers[0]
    )
    dbr, dqkv, grad_in, dgain_a, dgain_m = grad_attention(
        grad, returned, rank, dlogits, weights, stored["x_mid"], stored["query"], stored["kv_all"],
        stored["probs"], tables, stored["low"], numbers[1],
    )
    dqkv, *ready = lax.optimization_barrier((dqkv, *ready))
    grads = weight_grads(
        stored["h_attn"], dqkv, stored["attended"], dbr, stored["h_moe"], dlogits, dgain_a, dgain_m
    )
    return grad_in, grads, half, ready


def per_device(
    tokens,
    routes,
    lengths,
    gain_attn,
    w_query,
    w_key,
    w_value,
    w_out,
    gain_moe,
    w_router,
    w_gate,
    w_up,
    w_down,
    cotangent,
):
    section, yh, z, core, shard = (
        lax.axis_index(a) for a in ("section", "yh", "z", "core", "shard")
    )
    first = section == 0
    tok_rows, model_width = tokens.shape[1:]
    group_rows = tok_rows * lax.axis_size("shard")

    def mine(a):
        return lax.dynamic_index_in_dim(a, section, 0, keepdims=False)

    def by_layer(own, other):
        return jnp.where(first, own, other), jnp.where(first, other, own)

    local = jnp.concatenate(
        [
            w_out[0],
            w_query[0],
            w_key[0],
            w_value[0],
            w_router[0],
            gain_attn[0][:, None],
            gain_moe[0][:, None],
            jnp.zeros((w_query.shape[1], 94), BF),
        ],
        axis=1,
    )
    full, late, *whole = gather_weights(local, (w_gate[0], w_up[0], w_down[0]))
    weights = [full.reshape(model_width, -1), late.reshape(model_width, -1)]
    route_other = swap(at(routes[0], 1 - section, 0), "section")
    ranks = [rank_of(r) for r in by_layer(mine(routes[0]), route_other)]
    unfold = unfold_table(GROUP)

    segment, position = document_layout(mine(lengths[:, 0]), group_rows)
    row_start = shard * tok_rows
    own_segment = lax.dynamic_slice_in_dim(segment, row_start, tok_rows)
    tables = rotary_tables(lax.dynamic_slice_in_dim(position, row_start, tok_rows), HEAD_DIM)
    query_index = row_start + jnp.arange(tok_rows, dtype=jnp.int32)
    allowed = (own_segment[:, None] == segment[None, :]) & (
        query_index[:, None] >= jnp.arange(group_rows, dtype=jnp.int32)[None, :]
    )
    allowed = allowed.astype(F32)

    source, saved = (mine(tokens),), []
    for layer in range(2):
        source, stored = forward_layer(
            source, weights[layer], whole, layer, ranks[layer], unfold, tables, allowed,
            (7 + layer, 11 + layer),
        )
        saved.append(stored)
    low = fused("finish", finish_body, [((tok_rows, model_width), BF)], *source)[0]
    grad, low = lax.optimization_barrier((mine(cotangent), low))
    away = swap(low, "section")

    sums, ready = [None, None], (away,)
    for layer in (1, 0):
        grad, mixer_grad, half, ready = backward_layer(
            grad,
            ready,
            saved[layer],
            weights[layer],
            whole,
            layer,
            ranks[layer],
            unfold,
            tables,
            (5 + layer, 9 + layer),
        )
        given = lax.ppermute(half, "section", [(1 - layer, layer)])
        sums[layer] = (half, given)
        if layer == 1:
            (away,), ready = ready, (given,)
            late = lax.psum_scatter(mixer_grad, DEVICES, scatter_dimension=0, tiled=True)
            late = lax.optimization_barrier(late)
    mixed = jnp.where(first, jnp.stack([low, away]), jnp.stack([away, low]))

    def finish_experts():
        return jnp.where(first, total(*sums[0]), total(sums[1][0], *ready)).astype(BF)

    mix, (grad_gate, grad_up, grad_down) = reduce_all(mixer_grad, late, finish_experts)
    return (
        mixed,
        grad[None],
        mix[:, 3616][None],
        mix[:, 1536:3072][None],
        mix[:, 3072:3328][None],
        mix[:, 3328:3584][None],
        mix[:, :1536][None],
        mix[:, 3617][None],
        mix[:, 3584:3616][None],
        grad_gate[None],
        grad_up[None],
        grad_down[None],
    )


def solution(mesh):
    fine = Mesh(mesh.devices.reshape(2, 2, 4, 2, 4), ("section", *DEVICES))
    expert = ("yh", "z", "core")
    return jax.shard_map(
        per_device,
        mesh=fine,
        in_specs=(
            P(None, DEVICES, None),
            P("section", None, DEVICES, None),
            P(None, expert, None),
            P("section", DEVICES),
            P("section", DEVICES, None),
            P("section", DEVICES, None),
            P("section", DEVICES, None),
            P("section", DEVICES, None),
            P("section", DEVICES),
            P("section", DEVICES, None),
            P("section", expert, "shard", None),
            P("section", expert, "shard", None),
            P("section", expert, None, "shard"),
            P(None, DEVICES, None),
        ),
        out_specs=(
            P(None, DEVICES, None),
            P("section", DEVICES, None),
            P("section", DEVICES),
            P("section", DEVICES, None),
            P("section", DEVICES, None),
            P("section", DEVICES, None),
            P("section", DEVICES, None),
            P("section", DEVICES),
            P("section", DEVICES, None),
            P("section", expert, "shard", None),
            P("section", expert, "shard", None),
            P("section", expert, None, "shard"),
        ),
        check_vma=False,
    )
```

```python
import jax
import jax.numpy as jnp
from jax import lax
from jax.experimental import pallas as pl
from jax.experimental.pallas import tpu as pltpu
from jax.sharding import Mesh
from jax.sharding import PartitionSpec as P

HEADS = 12
HEAD_DIM = 128
EXPERTS = 32
MAIN = 16
EXTRA = 2
CHUNKS = 6

epsilon = 1e-06
rope_base = 1000000.0
masked_score = -1e30

BF = jnp.bfloat16
F32 = jnp.float32
CHIPS = ("yh", "z", "shard")
DEVICES = ("yh", "z", "core", "shard")


def dot(a, b, dims=((1,), (0,))):
    return lax.dot_general(a, b, (dims, ((), ())), preferred_element_type=F32)


def document_layout(doc_lengths, group_rows):
    doc_ends = jnp.cumsum(doc_lengths)
    starts = doc_ends - doc_lengths
    row_index = jnp.arange(group_rows, dtype=jnp.int32)
    segment = jnp.sum((row_index[:, None] >= doc_ends[None, :]).astype(jnp.int32), axis=1)
    member = segment[:, None] == jnp.arange(doc_lengths.shape[0], dtype=jnp.int32)[None, :]
    position = row_index - jnp.sum(jnp.where(member, starts[None, :], 0), axis=1)
    return (segment, position)


def rotary_tables(position, head_size):
    half_dim = head_size // 2
    frequency = rope_base ** (-2.0 * jnp.arange(half_dim, dtype=F32) / head_size)
    angles = position.astype(F32)[:, None] * frequency[None, :]
    cosine, sine = jnp.cos(angles), jnp.sin(angles)
    return jnp.concatenate([cosine, cosine], axis=1), jnp.concatenate([-sine, sine], axis=1)


def swap(value, axis):
    return lax.ppermute(value, axis, [(0, 1), (1, 0)])


def around(axis, size):
    here = lax.axis_index(axis)
    return [lax.rem(here + step, size) for step in range(1, size)]


def move(name, number, arrays, shapes, peers, copies):
    count = len(arrays)
    total = 40

    def kernel(*refs):
        ins, outs = refs[:count], refs[count : count + len(shapes)]
        sent, got = refs[count + len(shapes) :]
        barrier = pltpu.get_barrier_semaphore()
        near = peers()
        for peer in near:
            pl.semaphore_signal(
                barrier, inc=1, device_id=peer, device_id_type=pl.DeviceIdType.MESH
            )
        pl.semaphore_wait(barrier, len(near))
        started = []
        for k, (source, target, device) in enumerate(copies(ins, outs)):
            if device is None:
                copy = pltpu.make_async_copy(source, target, got.at[k])
            else:
                copy = pltpu.make_async_remote_copy(
                    src_ref=source,
                    dst_ref=target,
                    send_sem=sent.at[k],
                    recv_sem=got.at[k],
                    device_id=device,
                    device_id_type=pl.DeviceIdType.MESH,
                )
            copy.start()
            started.append(copy)
        for copy in started:
            copy.wait()

    space = pl.BlockSpec(memory_space=pltpu.HBM)
    return pl.pallas_call(
        kernel,
        out_shape=[jax.ShapeDtypeStruct(s, BF) for s in shapes],
        in_specs=[space] * count,
        out_specs=[space] * len(shapes),
        scratch_shapes=[pltpu.SemaphoreType.DMA((total,)), pltpu.SemaphoreType.DMA((total,))],
        compiler_params=pltpu.CompilerParams(collective_id=number, has_side_effects=True),
        name=name,
    )(*arrays)


def total(*parts):
    out = parts[0].astype(F32)
    for part in parts[1:]:
        out = out + part.astype(F32)
    return out


def at(array, index, axis):
    return lax.dynamic_index_in_dim(array, index, axis, keepdims=False)


def other(axis):
    return lax.rem(lax.axis_index(axis) + 1, 2)


def reduce_all(grads, late, finish_experts):
    core, shard, z, yh, section = (
        lax.axis_index(a) for a in ("core", "shard", "z", "yh", "section")
    )
    width = grads.shape[2]
    mix = grads.reshape(2, 4, 4, 24, width)

    cut = 1792
    sizes = (cut, width - cut)

    def peers_2():
        return [{"shard": x} for x in around("shard", 4)] + [{"z": i} for i in around("z", 4)]

    def copies_2(ins, outs):
        out = []
        for step, (x, i) in enumerate(zip(around("shard", 4), around("z", 4))):
            out.append((ins[0].at[:, :, x, :, pl.ds(0, cut)], outs[0].at[step], {"shard": x}))
            out.append((ins[0].at[:, i, :, :, pl.ds(cut, width - cut)], outs[1].at[step], {"z": i}))
        return out

    shapes = [(3, 2, 4, 24, size) for size in sizes]
    got = move("first_axis", 2, [mix], shapes, peers_2, copies_2)
    own = [
        lax.dynamic_slice(mix, (0, 0, shard, 0, 0), (2, 4, 1, 24, cut))[:, :, 0],
        lax.dynamic_slice(mix, (0, z, 0, 0, cut), (2, 1, 4, 24, width - cut))[:, 0],
    ]
    mix = [total(m, *g).astype(BF) for m, g in zip(own, got)]

    exp = finish_experts()

    def shards_of(ref, x):
        down = ref.at[
            pl.ds(pl.multiple_of(1536 + x // 2 * 384, 128), 384),
            pl.ds(pl.multiple_of(lax.rem(x, 2) * 384, 128), 384),
        ]
        gate = ref.at[pl.ds(pl.multiple_of(x * 192, 64), 192)]
        up = ref.at[pl.ds(pl.multiple_of(768 + x * 192, 64), 192)]
        return gate, up, down

    def copies_3(ins, outs):
        here = lax.axis_index("shard")
        out = []
        for step, (x, i) in enumerate(zip(around("shard", 4), around("z", 4))):
            out.append((ins[0].at[:, i], outs[0].at[step], {"z": i}))
            out.append((ins[1].at[:, x], outs[1].at[step], {"shard": x}))
            for k, source in enumerate(shards_of(ins[2], x)):
                out.append((source, outs[2 + k].at[here], {"shard": x}))
        for k, source in enumerate(shards_of(ins[2], here)):
            out.append((source, outs[2 + k].at[here], None))
        return out

    shapes = [(3, 2, 24, size) for size in sizes] + [(4, 192, 768), (4, 192, 768), (4, 384, 384)]
    got = move("other_axis", 3, [*mix, exp], shapes, peers_2, copies_3)
    mix = jnp.concatenate(
        [
            total(at(mix[0], z, 1), *got[0]).astype(BF),
            total(at(mix[1], shard, 1), *got[1]).astype(BF),
        ],
        axis=-1,
    )
    exp = got[2:]

    def places():
        here = 2 * lax.axis_index("yh") + lax.axis_index("section")
        there = [lax.rem(here + step, 4) for step in range(1, 4)]
        return [(t // 2, lax.rem(t, 2)) for t in there]

    def copies_4(ins, outs):
        there = other("core")
        out = [
            (ins[1 + k].at[pl.ds(2 * there, 2)], outs[1 + k], {"core": there}) for k in range(3)
        ]
        for step, (y, s) in enumerate(places()):
            out.append((ins[0].at[s, y], outs[0].at[step], {"yh": y, "section": s}))
        return out

    mine = (jnp.arange(2) == yh)[:, None, None]
    pairs = jnp.stack([mix, jnp.where(mine, late[None], jnp.zeros((), BF))])
    got = move(
        "last_axis",
        4,
        [pairs, *exp],
        [(3, 24, width), (2, 192, 768), (2, 192, 768), (2, 384, 384)],
        lambda: [{"yh": y, "section": s} for y, s in places()] + [{"core": other("core")}],
        copies_4,
    )
    sums = total(at(at(pairs, section, 0), yh, 0), *got[0])
    out = []
    for e, g in zip(exp, got[1:]):
        kept = lax.dynamic_slice_in_dim(e, 2 * core, 2, 0)
        low, high = jnp.where(core == 0, kept, g), jnp.where(core == 0, g, kept)
        out.append(jnp.concatenate([low, high], axis=1).astype(F32))
    return sums, out


def gather_weights(local, experts):
    rows, width = local.shape

    def kernel(*refs):
        mine, shards = refs[0], refs[1:4]
        full, late, whole = refs[4], refs[5], refs[6:9]
        stage = refs[9:12]
        sent, got, sent_x, got_e, sent_c, got_c, sent_y, sent_o, local_sem = refs[12:]
        s, yh, z, c, x = (lax.axis_index(a) for a in ("section", "yh", "z", "core", "shard"))
        place = 2 * yh + s
        ys = [lax.rem(place + k, 4) for k in (1, 2, 3)]
        ys = [{"yh": y // 2, "section": lax.rem(y, 2)} for y in ys]
        xs = [{"shard": lax.rem(x + k, 4)} for k in (1, 2, 3)]
        z_up, z_down = lax.rem(z + 1, 4), lax.rem(z + 3, 4)
        sibling, partner = {"core": 1 - c}, {"section": 1 - s}

        def piece(k, i, h):
            if k == 2:
                return shards[2].at[i, pl.ds(pl.multiple_of(h * 384, 128), 384)]
            return shards[k].at[i, pl.ds(pl.multiple_of(h * 192, 64), 192)]

        def landing(k, layer, source, half):
            if k == 2:
                return whole[2].at[layer, half, :, pl.ds(pl.multiple_of(source * 384, 128), 384)]
            return whole[k].at[layer, source, half]

        def remote(source, target, send, receive, device):
            return pltpu.make_async_remote_copy(
                src_ref=source,
                dst_ref=target,
                send_sem=send,
                recv_sem=receive,
                device_id=device,
                device_id_type=pl.DeviceIdType.MESH,
            )

        def start(copies):
            for copy in copies:
                copy.start()
            return copies

        def finish(copies):
            for copy in copies:
                copy.wait()

        has_own = x // 2 == c
        own = lax.rem(x, 2)
        staged = start(
            [pltpu.make_async_copy(piece(k, own, c), stage[k], local_sem.at[k]) for k in range(3)]
        )
        barrier = pltpu.get_barrier_semaphore()
        zs = [{"z": lax.rem(z + k, 4)} for k in (1, 2, 3)]
        x_up, x_down = xs[0]["shard"], xs[2]["shard"]
        near = ys + xs + zs + [sibling]
        near += [{"shard": lax.rem(x + k, 4), "core": 1 - c} for k in (1, 2, 3)]
        for peer in near:
            pl.semaphore_signal(
                barrier, inc=1, device_id=peer, device_id_type=pl.DeviceIdType.MESH
            )
        pl.semaphore_wait(barrier, len(near))

        here = full.at[yh, z, c, x]

        def along_y(target):
            out = [pltpu.make_async_copy(mine, target, local_sem.at[3])]
            for k, device in enumerate(ys):
                out.append(remote(mine, target, sent.at[k], got.at[k], device))
            return out

        @pl.when(s == 0)
        def _():
            start(along_y(here))

        @pl.when(s == 1)
        def _():
            start(along_y(late.at[yh, z, c, x]))

        finish(staged)

        @pl.when(has_own)
        def _():
            for k in range(3):
                remote(
                    piece(k, own, 1 - c),
                    landing(k, s, x, 1 - c),
                    sent_o.at[k],
                    got_e.at[s, x, k],
                    sibling,
                ).start()
                pltpu.make_async_copy(stage[k], landing(k, s, x, c), got_e.at[s, x, k]).start()

        def pass_on(layer, distance, to_partner):
            source = lax.rem(x + distance, 4)
            for k in range(3):
                view = landing(k, layer, source, c)
                receive = got_e.at[layer, source, k]
                remote(view, view, sent_o.at[k], receive, sibling).wait_recv()
                if to_partner:
                    remote(view, view, sent_y.at[distance, k], receive, partner).start()
                across = got_c.at[layer, source, k]
                remote(view, view, sent_c.at[layer, source, k], across, sibling).start()

        finish(along_y(here))
        view, view_late = full.at[:, z, c, x], late.at[:, z, c, x]
        along_x = start(
            [remote(view, view, sent.at[3 + k], got.at[3 + k], xs[k]) for k in range(3)]
        )
        late_z = start(
            [
                remote(view_late, view_late, sent.at[11 + k], got.at[11 + k], zs[k])
                for k in range(3)
            ]
        )
        pass_on(s, 0, True)
        finish(along_x)

        def ring(base, axis, places, up, down):
            return start(
                [
                    remote(up, up, sent.at[base], got.at[base], {axis: places[0]}),
                    remote(down, down, sent.at[base + 1], got.at[base + 1], {axis: places[1]}),
                ]
            )

        view = full.at[:, z, c]
        along_z = ring(6, "z", (z_up, z_down), view, view)
        for i in range(2):

            @pl.when(x != 2 * c + i)
            def _():
                for h in range(2):
                    for k in range(3):
                        remote(
                            piece(k, i, h),
                            landing(k, s, x, h),
                            sent_x.at[(i * 2 + h) * 3 + k],
                            got_e.at[s, x, k],
                            {"shard": 2 * c + i, "core": h},
                        ).start()

        finish(late_z)
        view = late.at[:, :, c, x]
        late_x = ring(14, "shard", (x_up, x_down), view, view)
        finish(along_z)
        along_z = ring(8, "z", (z_up, z_down), full.at[0, z_down, c], full.at[1, z_up, c])
        for distance in (1, 3, 2):
            pass_on(s, distance, True)
        finish(along_z)
        view = full.at[:, :, c]
        across = start([remote(view, view, sent.at[10], got.at[10], sibling)])
        finish(late_x)
        late_x = ring(
            16, "shard", (x_up, x_down), late.at[0, :, c, x_down], late.at[1, :, c, x_up]
        )
        for distance in (0, 1):
            pass_on(1 - s, distance, False)
        finish(late_x)
        view = late.at[:, :, c]
        across += start([remote(view, view, sent.at[18], got.at[18], sibling)])
        for distance in (3, 2):
            pass_on(1 - s, distance, False)

        finish(across)
        for i in range(2):

            @pl.when(x != 2 * c + i)
            def _():
                for h in range(2):
                    for k in range(3):
                        view = piece(k, i, h)
                        n = (i * 2 + h) * 3 + k
                        remote(view, view, sent_x.at[n], got_e.at[0, 0, k], sibling).wait_send()

        @pl.when(has_own)
        def _():
            for k in range(3):
                view = piece(k, own, 1 - c)
                remote(view, view, sent_o.at[k], got_e.at[0, 0, k], sibling).wait_send()

        for source in range(4):
            for k in range(3):
                view = landing(k, s, source, c)
                send = sent_y.at[source, k]
                remote(view, view, send, got_e.at[0, 0, k], partner).wait_send()
                for layer in range(2):
                    view = landing(k, layer, source, c)
                    arrived = landing(k, layer, source, 1 - c)
                    send, receive = sent_c.at[layer, source, k], got_c.at[layer, source, k]
                    remote(view, view, send, receive, sibling).wait_send()
                    remote(arrived, arrived, send, receive, sibling).wait_recv()

    space = pl.BlockSpec(memory_space=pltpu.HBM)
    near_space = pl.BlockSpec(memory_space=pltpu.VMEM)
    shapes = [(2, 4, 2, 4, rows, width)] * 2
    shapes += [(2, 4, 2, 192, 768), (2, 4, 2, 192, 768), (2, 2, 384, 1536)]
    dma = pltpu.SemaphoreType.DMA
    return pl.pallas_call(
        kernel,
        out_shape=[jax.ShapeDtypeStruct(shape, BF) for shape in shapes],
        in_specs=[near_space] + [space] * 3,
        out_specs=[space] * 5,
        scratch_shapes=[
            pltpu.VMEM((192, 768), BF),
            pltpu.VMEM((192, 768), BF),
            pltpu.VMEM((384, 384), BF),
            dma((19,)),
            dma((19,)),
            dma((12,)),
            dma((2, 4, 3)),
            dma((2, 4, 3)),
            dma((2, 4, 3)),
            dma((4, 3)),
            dma((3,)),
            dma((4,)),
        ],
        compiler_params=pltpu.CompilerParams(collective_id=0, has_side_effects=True),
        name="gather_weights",
    )(local, *experts)


def rank_of(route_rows):
    rows = route_rows.shape[0]
    chosen = route_rows.T[None, :, :] == jnp.arange(EXPERTS, dtype=jnp.int32)[:, None, None]
    hot = jnp.any(chosen, axis=1)
    index = jnp.arange(rows, dtype=jnp.int32)
    before = (index[:, None] < index[None, :]).astype(BF)
    return jnp.where(hot, dot(hot.astype(BF), before), -1.0)


def stacked(field):
    return jnp.concatenate(jnp.split(field, CHUNKS, axis=1), axis=0)


def unstacked(field):
    return jnp.concatenate(jnp.split(field, CHUNKS, axis=0), axis=1)


def unfold_table(sources):
    row = jnp.arange(CHUNKS * sources * EXTRA, dtype=jnp.int32)
    piece, source, extra = row // (sources * EXTRA), row // EXTRA % sources, row % EXTRA
    column = jnp.arange(sources * MAIN, dtype=jnp.int32)
    return (
        (source * MAIN + piece * EXTRA + extra)[:, None] == column[None, :]
    ).astype(BF)


def arrived_rows(message, unfold):
    width = message.shape[1] - 256
    extra = unstacked(dot(unfold, message[:, width:]).astype(BF))
    return jnp.concatenate([message[:, :width], extra], axis=0)


def fold_rows(rows, unfold, sources):
    main = rows[: sources * MAIN]
    extra = dot(unfold, stacked(rows[sources * MAIN :]), ((0,), (0,))).astype(BF)
    return jnp.concatenate([main, extra], axis=1)


def low_pair(value):
    high = value.astype(BF)
    return high, (value - high.astype(F32)).astype(BF)


OUT_COLUMNS, QKV_STEP = 1536, 512


def columns(width, place):
    return lambda rows: pl.BlockSpec((rows, width), lambda i: (0, place), memory_space=pltpu.VMEM)


OUT_BLOCK = [columns(OUT_COLUMNS, 0)]
QKV_BLOCKS = [columns(QKV_STEP, 3 + k) for k in range(4)]
NARROW_BLOCK = [columns(128, 28)]


def fused(name, body, shapes, *arrays, scratch=(), number=None):
    near = pl.BlockSpec(memory_space=pltpu.VMEM)
    specs, given = [], []
    for array in arrays:
        if isinstance(array, tuple):
            array, blocks = array
            specs += [block(array.shape[0]) for block in blocks]
            given += [array] * len(blocks)
        else:
            specs.append(near)
            given.append(array)
    return pl.pallas_call(
        body,
        grid=(1,),
        out_shape=[jax.ShapeDtypeStruct(shape, kind) for shape, kind in shapes],
        in_specs=specs,
        out_specs=[near] * len(shapes),
        scratch_shapes=list(scratch),
        compiler_params=pltpu.CompilerParams(
            vmem_limit_bytes=48 << 20, collective_id=number, has_side_effects=number is not None
        ),
        name=name,
    )(*given)


TN, NT = ((0,), (0,)), ((1,), (1,))


def slots(rank):
    count, rows = rank.shape
    place = lax.broadcasted_iota(jnp.int32, (count, MAIN, rows), 1)
    wide = jnp.broadcast_to(rank[:, None, :], (count, MAIN, rows))
    main = jnp.where(wide == place.astype(F32), 1.0, 0.0)
    extra = (MAIN + lax.rem(place, EXTRA)).astype(F32)
    extra = jnp.where((wide == extra) & (place < EXTRA * CHUNKS), 1.0, 0.0)
    return main, extra


def per_piece(table):
    piece = lax.rem(lax.broadcasted_iota(jnp.int32, table.shape, 0), MAIN) // EXTRA
    return [jnp.where(piece == j, table, 0.0) for j in range(CHUNKS)]


def flat(table):
    return table.reshape(table.shape[0] * table.shape[1], table.shape[2])


def send_table(main, extra, field):
    width = field.shape[1] // CHUNKS
    side = None
    for j, table in enumerate(per_piece(flat(extra))):
        part = dot(table.astype(BF), field[:, j * width : (j + 1) * width])
        side = part if side is None else side + part
    return dot(flat(main).astype(BF), field), side


def bring_back(main, extra, rows, exact):
    parts = low_pair if exact else (lambda t: (t.astype(BF),))
    model_width = rows.shape[1] - 256
    total_main = None
    for table in parts(main):
        part = dot(table, rows[:, :model_width], TN)
        total_main = part if total_main is None else total_main + part
    side = []
    for table in per_piece(extra):
        total_side = None
        for t in parts(table):
            part = dot(t, rows[:, model_width:], TN)
            total_side = part if total_side is None else total_side + part
        side.append(total_side)
    return total_main + jnp.concatenate(side, axis=1)


def gain_rows(narrow):
    row = lax.broadcasted_iota(jnp.int32, (8, narrow.shape[1]), 0)
    column = lax.broadcasted_iota(jnp.int32, (8, narrow.shape[1]), 1)
    pick = jnp.where(column == row + EXPERTS, 1.0, 0.0).astype(BF)
    rows = dot(pick, narrow, NT)
    return rows[0:1], rows[1:2]


def turn(field, cosine, sine):
    return field * cosine + pltpu.roll(field, HEAD_DIM // 2, 1) * sine


def turn_back(field, cosine, sine):
    return field * cosine - pltpu.roll(field, HEAD_DIM // 2, 1) * sine


def combined(x_mid, rank, gates, rows):
    main, extra = slots(rank)
    wide = jnp.broadcast_to(gates[:, None, :], main.shape)
    return x_mid + bring_back(flat(main * wide), flat(extra * wide), rows, True)


def finish_body(mid_ref, rank_ref, gates_ref, rows_ref, out_ref):
    out = combined(mid_ref[...], rank_ref[...], gates_ref[...], rows_ref[...])
    out_ref[...] = out.astype(BF)


def heads_of(kv_ref):
    kv_heads = kv_ref.shape[2] // 2 // HEAD_DIM
    parts = []
    for k in range(2 * kv_heads):
        part = kv_ref[:, :, k * HEAD_DIM : (k + 1) * HEAD_DIM]
        parts.append(part.reshape(part.shape[0] * part.shape[1], HEAD_DIM))
    return parts[:kv_heads], parts[kv_heads:]


def attention_body(combine):
    def body(*refs):
        source, refs = refs[: 4 if combine else 1], refs[4 if combine else 1 :]
        weights, refs = refs[:4], refs[4:]
        out_w, narrow, cos_ref, sin_ref, allowed_ref, rank_ref, low_ref, h_ref, q_ref = refs[:9]
        kv_ref, mid_ref, h2_ref, att_ref, probs_ref, gates_ref, out_ref, held, sent, got = refs[9:]
        here = lax.axis_index("shard")
        peers = [{"shard": x} for x in around("shard", 4)]
        barrier = pltpu.get_barrier_semaphore()
        for peer in peers:
            pl.semaphore_signal(
                barrier, inc=1, device_id=peer, device_id_type=pl.DeviceIdType.MESH
            )
        if combine:
            mid, rank, gates, rows = (ref[...] for ref in source)
            low = combined(mid, rank, gates, rows).astype(BF)
        else:
            low = source[0][...]
        low_ref[...] = low
        field = low.astype(F32)
        gain_a, gain_m = gain_rows(narrow[...])
        scale = lax.rsqrt(jnp.mean(field * field, axis=1, keepdims=True) + epsilon)
        h = (field * scale * gain_a).astype(BF)
        h_ref[...] = h
        cosine, sine = cos_ref[...], sin_ref[...]

        def projected(column, turned):
            inside = column % QKV_STEP
            part = dot(h, weights[column // QKV_STEP][:, inside : inside + 256])
            if turned:
                part = jnp.concatenate(
                    [turn(part[:, k : k + HEAD_DIM], cosine, sine) for k in (0, HEAD_DIM)], axis=1
                )
            return part.astype(BF)

        query_width, kv_width = q_ref.shape[1], kv_ref.shape[2]
        for column in range(0, kv_width, 256):
            part = projected(query_width + column, column < kv_width // 2)
            held[here, :, column : column + 256] = part
        pl.semaphore_wait(barrier, len(peers))
        copies = []
        for k, peer in enumerate(peers):
            view = held.at[here]
            copies.append(
                pltpu.make_async_remote_copy(
                    src_ref=view,
                    dst_ref=view,
                    send_sem=sent.at[k],
                    recv_sem=got.at[k],
                    device_id=peer,
                    device_id_type=pl.DeviceIdType.MESH,
                )
            )
            copies[-1].start()
        for column in range(0, query_width, 256):
            q_ref[:, column : column + 256] = projected(column, True)
        for copy in copies:
            copy.wait()

        kv_ref[...] = held[...]
        keys, values = heads_of(held)
        allowed = allowed_ref[...] > 0.0
        ratio = HEADS // len(keys)
        for head in range(HEADS):
            lanes = slice(head * HEAD_DIM, (head + 1) * HEAD_DIM)
            scores = dot(q_ref[:, lanes], keys[head // ratio], NT) * HEAD_DIM ** (-0.5)
            scores = jnp.where(allowed, scores, masked_score)
            exponent = jnp.exp(scores - jnp.max(scores, axis=1, keepdims=True))
            probs = exponent / jnp.sum(exponent, axis=1, keepdims=True)
            probs_ref[head] = probs
            att_ref[:, lanes] = dot(probs.astype(BF), values[head // ratio]).astype(BF)
        mid = field + dot(att_ref[...], out_w[...])
        mid_ref[...] = mid
        scale = lax.rsqrt(jnp.mean(mid * mid, axis=1, keepdims=True) + epsilon)
        h2 = (mid * scale * gain_m).astype(BF)
        h2_ref[...] = h2
        rank = rank_ref[...]
        logits = jnp.transpose(dot(h2, narrow[...]))[:EXPERTS]
        logits = jnp.where(rank >= 0.0, logits, masked_score)
        gate_exp = jnp.exp(logits - jnp.max(logits, axis=0, keepdims=True))
        gate_exp = jnp.where(rank >= 0.0, gate_exp, 0.0)
        gates_ref[...] = gate_exp / jnp.sum(gate_exp, axis=0, keepdims=True)
        main, side = send_table(*slots(rank), h2)
        width = main.shape[1]
        out_ref[:, :width] = main.astype(BF)
        out_ref[:, width:] = side.astype(BF)

    return body


def attention(source, weights, tables, allowed, rank, number):
    tok_rows, model_width = source[0].shape
    query_width = HEADS * HEAD_DIM
    shapes = [((tok_rows, model_width), BF)] * 2
    shapes += [
        ((tok_rows, query_width), BF),
        ((allowed.shape[1] // tok_rows, tok_rows, 4 * QKV_STEP - query_width), BF),
        ((tok_rows, model_width), F32),
        ((tok_rows, model_width), BF),
        ((tok_rows, query_width), BF),
        ((HEADS, tok_rows, allowed.shape[1]), F32),
        (rank.shape, F32),
        ((EXPERTS * MAIN, model_width + 256), BF),
    ]
    dma = pltpu.SemaphoreType.DMA
    return fused(
        "attention",
        attention_body(len(source) > 1),
        shapes,
        *source,
        (weights, QKV_BLOCKS + OUT_BLOCK + NARROW_BLOCK),
        *tables,
        allowed,
        rank,
        scratch=[pltpu.VMEM(shapes[3][0], BF), dma((3,)), dma((3,))],
        number=number,
    )


def grad_slots_body(grad_ref, rank_ref, gates_ref, rows_ref, out_ref, dlogits_ref):
    gates = gates_ref[...]
    main, extra = slots(rank_ref[...])
    wide = jnp.broadcast_to(gates[:, None, :], main.shape)
    grad_main, grad_side = send_table(main, extra, grad_ref[...])
    width = grad_main.shape[1]
    dgate = None
    for table, grad, columns in (
        (main, grad_main, slice(0, width)),
        (extra, grad_side, slice(width, width + 256)),
    ):
        slot_gate = jnp.sum(flat(table * wide), axis=1, keepdims=True)
        out_ref[:, columns] = (grad * slot_gate).astype(BF)
        slot_dgate = jnp.sum(grad * rows_ref[:, columns].astype(F32), axis=1, keepdims=True)
        part = jnp.sum((flat(table) * slot_dgate).reshape(table.shape), axis=1)
        dgate = part if dgate is None else dgate + part
    dlogits = gates * (dgate - jnp.sum(gates * dgate, axis=0, keepdims=True))
    pad = jnp.zeros((dlogits_ref.shape[1] - EXPERTS, dlogits.shape[1]), F32)
    dlogits_ref[...] = jnp.transpose(jnp.concatenate([dlogits, pad], axis=0)).astype(BF)


def grad_slots(grad, rank, gates, rows):
    shapes = [(rows.shape, BF), ((grad.shape[0], 128), BF)]
    return fused("grad_slots", grad_slots_body, shapes, grad, rank, gates, rows)


def norm_grads(field, gain, grad):
    scale = lax.rsqrt(jnp.mean(field * field, axis=1, keepdims=True) + epsilon)
    scaled = grad * gain
    centre = jnp.mean(scaled * field, axis=1, keepdims=True)
    dgain = jnp.sum(grad * field * scale, axis=0, keepdims=True)
    return scale * scaled - field * (scale * scale * scale) * centre, dgain


def grad_attention_body(
    grad_ref, rows_ref, rank_ref, dlogits_ref, out_w, weight_0, weight_1, weight_2, weight_3, narrow,
    mid_ref, q_ref, kv_ref, probs_ref, cos_ref, sin_ref, low_ref,
    dbr_ref, dqkv_ref, grad_out_ref, dgain_a_ref, dgain_m_ref,
    datt_ref, dkv_ref, held, sent, got,
):
    here = lax.axis_index("shard")
    peers = [{"shard": x} for x in around("shard", 4)]
    barrier = pltpu.get_barrier_semaphore()
    for peer in peers:
        pl.semaphore_signal(barrier, inc=1, device_id=peer, device_id_type=pl.DeviceIdType.MESH)
    main, extra = slots(rank_ref[...])
    dh = bring_back(flat(main), flat(extra), rows_ref[...], False)
    dh = dh + dot(dlogits_ref[...], narrow[...], NT)
    gain_a, gain_m = gain_rows(narrow[...])
    dmid, dgain = norm_grads(mid_ref[...], gain_m, dh)
    dmid = dmid + grad_ref[...].astype(F32)
    dgain_m_ref[...] = dgain
    dbr_ref[...] = dmid.astype(BF)
    datt_ref[...] = dot(dbr_ref[...], out_w[...], NT).astype(BF)
    keys, values = heads_of(kv_ref)
    ratio = HEADS // len(keys)
    cosine, sine = cos_ref[...], sin_ref[...]
    count, tok_rows, kv_columns = kv_ref.shape
    scale = HEAD_DIM ** (-0.5)
    for k in range(len(keys)):
        dkey, dvalue = None, None
        for head in range(k * ratio, (k + 1) * ratio):
            lanes = slice(head * HEAD_DIM, (head + 1) * HEAD_DIM)
            probs, datt = probs_ref[head], datt_ref[:, lanes]
            dprobs = dot(datt, values[k], NT)
            centre = jnp.sum(dprobs * probs, axis=1, keepdims=True)
            dscores = (probs * (dprobs - centre)).astype(BF)
            part = dot(probs.astype(BF), datt, TN)
            dvalue = part if dvalue is None else dvalue + part
            part = dot(dscores, q_ref[:, lanes], TN)
            dkey = part if dkey is None else dkey + part
            dquery = dot(dscores, keys[k]) * scale
            dqkv_ref[:, lanes] = turn_back(dquery, cosine, sine).astype(BF)
        at_key, at_value = k * HEAD_DIM, (len(keys) + k) * HEAD_DIM
        shape = (count, tok_rows, HEAD_DIM)
        dkv_ref[:, :, at_key : at_key + HEAD_DIM] = (dkey * scale).astype(BF).reshape(shape)
        dkv_ref[:, :, at_value : at_value + HEAD_DIM] = dvalue.astype(BF).reshape(shape)
    pl.semaphore_wait(barrier, len(peers))
    copies = []
    for k, peer in enumerate(peers):
        copies.append(
            pltpu.make_async_remote_copy(
                src_ref=dkv_ref.at[peer["shard"]],
                dst_ref=held.at[k],
                send_sem=sent.at[k],
                recv_sem=got.at[k],
                device_id=peer,
                device_id_type=pl.DeviceIdType.MESH,
            )
        )
        copies[-1].start()
    query_width = q_ref.shape[1]
    dh = None
    weights = (weight_0, weight_1, weight_2, weight_3)
    for k, weight in enumerate(weights[:-1]):
        part = dot(dqkv_ref[:, k * QKV_STEP : (k + 1) * QKV_STEP], weight[...], NT)
        dh = part if dh is None else dh + part
    for copy in copies:
        copy.wait()
    dkv = dkv_ref[here].astype(F32)
    for k in range(len(peers)):
        dkv = dkv + held[k].astype(F32)
    for k in range(0, kv_columns // 2, HEAD_DIM):
        part = turn_back(dkv[:, k : k + HEAD_DIM], cosine, sine)
        dqkv_ref[:, query_width + k : query_width + k + HEAD_DIM] = part.astype(BF)
    dqkv_ref[:, query_width + kv_columns // 2 :] = dkv[:, kv_columns // 2 :].astype(BF)
    dh = dh + dot(dqkv_ref[:, query_width:], weights[-1][...], NT)
    dlow, dgain = norm_grads(low_ref[...].astype(F32), gain_a, dh)
    dgain_a_ref[...] = dgain
    grad_out_ref[...] = (dlow + dmid).astype(BF)


def grad_attention(
    grad, rows, rank, dlogits, weights, mid, q, kv, probs, tables, low, number
):
    tok_rows, model_width = mid.shape
    shapes = [
        ((tok_rows, model_width), BF),
        ((tok_rows, 4 * QKV_STEP), BF),
        ((tok_rows, model_width), BF),
        ((1, model_width), F32),
        ((1, model_width), F32),
    ]
    dma = pltpu.SemaphoreType.DMA
    return fused(
        "grad_attention",
        grad_attention_body,
        shapes,
        grad,
        rows,
        rank,
        dlogits,
        (weights, OUT_BLOCK + QKV_BLOCKS + NARROW_BLOCK),
        mid,
        q,
        kv,
        probs,
        *tables,
        low,
        scratch=[
            pltpu.VMEM(q.shape, BF),
            pltpu.VMEM(kv.shape, BF),
            pltpu.VMEM((3, *kv.shape[1:]), BF),
            dma((3,)),
            dma((3,)),
        ],
        number=number,
    )


def weight_grads_body(
    h_ref, dqkv_ref, att_ref, dbr_ref, h2_ref, dlogits_ref, dgain_a_ref, dgain_m_ref, out_ref
):
    step = 512
    place = 0
    for left, right in ((att_ref, dbr_ref), (h_ref, dqkv_ref)):
        for k in range(0, right.shape[1], step):
            part = dot(left[...], right[:, k : k + step], TN)
            out_ref[:, place : place + step] = part.astype(BF)
            place += step
    narrow = dot(h2_ref[...], dlogits_ref[...], TN)
    rows = jnp.concatenate(
        [dgain_a_ref[...], dgain_m_ref[...], jnp.zeros((126, h_ref.shape[1]), F32)], axis=0
    )
    columns = pltpu.roll(jnp.transpose(rows), EXPERTS, 1)
    out_ref[:, place:] = (narrow + columns).astype(BF)


def weight_grads(h, dqkv, att, dbr, h2, dlogits, dgain_a, dgain_m):
    columns = dqkv.shape[1] + dbr.shape[1] + 128
    return fused(
        "weight_grads", weight_grads_body, [((h.shape[1], columns), BF)],
        h, dqkv, att, dbr, h2, dlogits, dgain_a, dgain_m,
    )[0]


def greet(peers):
    barrier = pltpu.get_barrier_semaphore()
    for peer in peers:
        pl.semaphore_signal(barrier, inc=1, device_id=peer, device_id_type=pl.DeviceIdType.MESH)
    pl.semaphore_wait(barrier, len(peers))


def weight_grads_half(*arrays, number):
    model_width = arrays[0].shape[1]
    width = arrays[1].shape[1] + arrays[3].shape[1] + 128
    shape = (8, 2, model_width // 16, width)

    def body(h_ref, dqkv_ref, att_ref, dbr_ref, h2_ref, dlogits_ref, dgain_a, dgain_m, *refs):
        out_ref, all_ref, held, sent, got = refs
        core = lax.axis_index("core")
        sibling = {"core": 1 - core}
        greet([sibling])
        copies = []

        def put(place, part):
            columns_of = pl.ds(place, part.shape[1])
            all_ref[:, :, :, columns_of] = part.astype(BF).reshape(*shape[:3], part.shape[1])
            k = len(copies)
            copy = pltpu.make_async_remote_copy(
                src_ref=all_ref.at[:, 1 - core, :, columns_of],
                dst_ref=held.at[:, :, columns_of],
                send_sem=sent.at[k],
                recv_sem=got.at[k],
                device_id=sibling,
                device_id_type=pl.DeviceIdType.MESH,
            )
            copy.start()
            copies.append((copy, columns_of))

        step, place = 512, 0
        for left, right in ((att_ref, dbr_ref), (h_ref, dqkv_ref)):
            for k in range(0, right.shape[1], step):
                put(place, dot(left[...], right[:, k : k + step], TN))
                place += step
        narrow = dot(h2_ref[...], dlogits_ref[...], TN)
        rows = jnp.concatenate(
            [dgain_a[...], dgain_m[...], jnp.zeros((126, model_width), F32)], axis=0
        )
        put(place, narrow + pltpu.roll(jnp.transpose(rows), EXPERTS, 1))
        for copy, columns_of in copies:
            copy.wait()
            own = all_ref[:, core, :, columns_of].astype(F32)
            out_ref[:, :, columns_of] = (own + held[:, :, columns_of].astype(F32)).astype(BF)

    half = (shape[0], shape[2], width)
    dma = pltpu.SemaphoreType.DMA
    return fused(
        "weight_grads_half",
        body,
        [(half, BF)],
        *arrays,
        scratch=[pltpu.VMEM(shape, BF), pltpu.VMEM(half, BF), dma((8,)), dma((8,))],
        number=number,
    )[0]


PARTNERS = [(dy, dz, (dz + k) % 4) for k in range(4) for dy in range(2) for dz in range(4)]
GROUP = 8
GROUPS = len(PARTNERS) // GROUP


def facing(n):
    k, dy, dz = n // GROUP, n // 4 % 2, n % 4
    return -k % GROUPS * GROUP + dy * 4 + -dz % 4


def partners():
    s, yh, z, x = (lax.axis_index(a) for a in ("section", "yh", "z", "shard"))
    out = []
    for dy, dz, dx in PARTNERS:
        there = {
            "section": lax.rem(s + dy, 2),
            "yh": lax.rem(yh + dy, 2),
            "z": lax.rem(z + dz, 4),
            "shard": lax.rem(x + dx, 4),
        }
        out.append((there, (there["yh"] * 4 + there["z"]) * 4 + there["shard"]))
    return out


def exchange_rows(message, returned, arrived, produced, sems, work, after, load, sibling=()):
    sent, got, sent_back, got_back = sems
    for copy in load:
        copy.start()
    near = partners()
    own = near[0][1]
    greet([device for device, _ in near[1:]] + list(sibling))

    def remote(source, target, send, receive, device):
        return pltpu.make_async_remote_copy(
            src_ref=source,
            dst_ref=target,
            send_sem=send,
            recv_sem=receive,
            device_id=device,
            device_id_type=pl.DeviceIdType.MESH,
        )

    def out(n):
        device, expert = near[n]
        f = facing(n)
        return remote(message.at[expert], arrived.at[f], sent.at[n], got.at[f], device)

    def back(n):
        return remote(
            produced.at[n], returned.at[own], sent_back.at[n], got_back.at[facing(n)], near[n][0]
        )

    for k in range(GROUPS):
        for n in range(-k % GROUPS * GROUP, -k % GROUPS * GROUP + GROUP):
            if n:
                out(n).start()
    arrived[0] = message[own]
    for copy in load:
        copy.wait()
    for k in range(GROUPS):
        members = range(k * GROUP, (k + 1) * GROUP)
        for n in members:
            if n:
                remote(arrived.at[n], arrived.at[n], sent.at[n], got.at[n], near[n][0]).wait_recv()
        rows = arrived[k * GROUP : (k + 1) * GROUP]
        result = work(k, rows.reshape(GROUP * MAIN, rows.shape[2]))
        produced[k * GROUP : (k + 1) * GROUP] = result.reshape(rows.shape)
        for n in members:
            if n:
                back(n).start()
    returned[own] = produced[0]
    after()
    for n in range(1, len(near)):
        device, expert = near[n]
        out(n).wait_send()
        back(n).wait_send()
        view = returned.at[expert]
        remote(view, view, sent_back.at[n], got_back.at[n], device).wait_recv()


def exchange_call(name, number, body, inputs, whole, shapes, message_shape, scratch):
    near = pl.BlockSpec(memory_space=pltpu.VMEM)
    far = pl.BlockSpec(memory_space=pltpu.HBM)
    dma = pltpu.SemaphoreType.DMA
    count = message_shape[0]
    return pl.pallas_call(
        body,
        out_shape=[jax.ShapeDtypeStruct(shape, kind) for shape, kind in shapes],
        in_specs=[far] * len(whole) + [near] * len(inputs),
        out_specs=[near] * len(shapes),
        scratch_shapes=[pltpu.VMEM(w.shape[1:], BF) for w in whole]
        + [dma((len(whole),))]
        + [pltpu.VMEM(message_shape, BF), pltpu.VMEM(message_shape, BF)]
        + [dma((count,)) for _ in range(4)]
        + scratch,
        compiler_params=pltpu.CompilerParams(
            collective_id=number, has_side_effects=True, vmem_limit_bytes=56 << 20
        ),
        name=name,
    )(*whole, *inputs)


def loads(whole, layer, held, sem):
    copies = [pltpu.make_async_copy(w.at[layer], h, sem.at[k]) for k, (w, h) in enumerate(zip(whole, held))]

    def matrix(k):
        value = held[k][...]
        return value.reshape(-1, value.shape[-1])

    return copies, matrix


def expert_forward(message, experts, layer, unfold, number):
    message = message.reshape(EXPERTS, MAIN, message.shape[1])
    rows = GROUP * (MAIN + EXTRA)
    depth, width = message.shape[2] - 256, experts[0].shape[-1]

    def body(*refs):
        whole, (message_ref, unfold_ref), refs = refs[:3], refs[3:5], refs[5:]
        returned, rows_ref, gate_ref, up_ref, hidden_ref = refs[:5]
        load, matrix = loads(whole, layer, refs[5:8], refs[8])
        arrived, produced, *sems = refs[9:]

        def work(k, came):
            field = arrived_rows(came, unfold_ref[...])
            rows_ref[k] = field
            gate = dot(field, matrix(0))
            up = dot(field, matrix(1))
            gate_ref[k] = gate
            up_ref[k] = up
            hidden = (gate / (1.0 + jnp.exp(-gate)) * up).astype(BF)
            hidden_ref[k] = hidden
            return fold_rows(dot(hidden, matrix(2)).astype(BF), unfold_ref[...], GROUP)

        exchange_rows(message_ref, returned, arrived, produced, sems, work, lambda: None, load)

    shapes = [
        (message.shape, BF),
        ((GROUPS, rows, depth), BF),
        ((GROUPS, rows, width), F32),
        ((GROUPS, rows, width), F32),
        ((GROUPS, rows, width), BF),
    ]
    returned, *kept = exchange_call(
        "expert_forward", number, body, [message, unfold], experts, shapes, message.shape, []
    )
    return returned.reshape(-1, message.shape[2]), kept


def expert_backward(message, experts, layer, kept, unfold, number):
    message = message.reshape(EXPERTS, MAIN, message.shape[1])
    rows = GROUP * (MAIN + EXTRA)
    depth, width = message.shape[2] - 256, experts[0].shape[-1]
    shards = 4
    half, deep = depth // 8, width // 2

    def body(*refs):
        whole, refs = refs[:3], refs[3:]
        message_ref, rows_ref, gate_ref, up_ref, hidden_ref, unfold_ref = refs[:6]
        returned, sum_ref = refs[6:8]
        load, matrix = loads(whole, layer, refs[8:11], refs[11])
        (arrived, produced), refs = refs[12:14], refs[14:]
        sems, (came_ref, dgate_ref, dup_ref) = refs[:4], refs[4:7]
        wide_refs, (down_ref, held_gate, held_up, held_down, sent, got) = refs[7:9], refs[9:]
        core = lax.axis_index("core")
        sibling = {"core": 1 - core}

        def work(k, came):
            field = arrived_rows(came, unfold_ref[...])
            came_ref[k] = field
            dhidden = dot(field, matrix(2), NT)
            gate = gate_ref[k]
            logistic = 1.0 / (1.0 + jnp.exp(-gate))
            dgate = dhidden * up_ref[k] * (logistic * (1.0 + gate * (1.0 - logistic)))
            dgate_ref[k] = dgate.astype(BF)
            dup_ref[k] = (dhidden * (gate * logistic)).astype(BF)
            out = dot(dgate_ref[k], matrix(0), NT) + dot(dup_ref[k], matrix(1), NT)
            return fold_rows(out.astype(BF), unfold_ref[...], GROUP)

        def to_sibling(k):
            views = [wide_refs[0].at[:, 1 - core], wide_refs[1].at[:, 1 - core]]
            views.append(down_ref.at[1 - core])
            return pltpu.make_async_remote_copy(
                src_ref=views[k],
                dst_ref=(held_gate, held_up, held_down)[k],
                send_sem=sent.at[k],
                recv_sem=got.at[k],
                device_id=sibling,
                device_id_type=pl.DeviceIdType.MESH,
            )

        def after():
            step = 256
            field = rows_ref[...].reshape(GROUPS * rows, depth)
            for k, source in enumerate((dgate_ref, dup_ref)):
                for column in range(0, width, step):
                    lanes = slice(column, column + step)
                    part = source[:, :, lanes].reshape(GROUPS * rows, step)
                    part = dot(field, part, TN).astype(BF)
                    wide_refs[k][:, :, :, lanes] = part.reshape(shards, 2, half, step)
                to_sibling(k).start()
            field = hidden_ref[...].reshape(GROUPS * rows, width)
            for column in range(0, depth, step):
                lanes = slice(column, column + step)
                part = came_ref[:, :, lanes].reshape(GROUPS * rows, step)
                part = dot(field, part, TN).astype(BF)
                down_ref[:, :, lanes] = part.reshape(2, deep, step)
            to_sibling(2).start()

        exchange_rows(
            message_ref, returned, arrived, produced, sems, work, after, load, (sibling,)
        )
        for k, held in enumerate((held_gate, held_up)):
            to_sibling(k).wait()
            for j in range(shards):
                part = wide_refs[k][j, core].astype(F32) + held[j].astype(F32)
                place = (k * shards + j) * half
                sum_ref[place : place + half] = part.astype(BF)
        to_sibling(2).wait()
        part = down_ref[core].astype(F32) + held_down[...].astype(F32)
        place = 2 * shards * half
        for j in range(2):
            columns_of = part[:, j * width : (j + 1) * width].astype(BF)
            sum_ref[place + j * deep : place + (j + 1) * deep] = columns_of

    shapes = [(message.shape, BF), ((3 * shards * half, width), BF)]
    dma = pltpu.SemaphoreType.DMA
    scratch = [
        pltpu.VMEM((GROUPS, rows, depth), BF),
        pltpu.VMEM((GROUPS, rows, width), BF),
        pltpu.VMEM((GROUPS, rows, width), BF),
        pltpu.VMEM((shards, 2, half, width), BF),
        pltpu.VMEM((shards, 2, half, width), BF),
        pltpu.VMEM((2, deep, depth), BF),
        pltpu.VMEM((shards, half, width), BF),
        pltpu.VMEM((shards, half, width), BF),
        pltpu.VMEM((deep, depth), BF),
        dma((3,)),
        dma((3,)),
    ]
    returned, sums = exchange_call(
        "expert_backward",
        number,
        body,
        [message, *kept, unfold],
        experts,
        shapes,
        message.shape,
        scratch,
    )
    return returned.reshape(-1, message.shape[2]), sums


def forward_layer(source, weights, experts, layer, rank, unfold, tables, allowed, numbers):
    low, h_attn, query, kv_all, x_mid, h_moe, attended, probs, gates, message = attention(
        source, weights, tables, allowed, rank, numbers[0]
    )
    returned, kept = expert_forward(message, experts, layer, unfold, numbers[1])
    stored = {
        "low": low,
        "h_attn": h_attn,
        "query": query,
        "kv_all": kv_all,
        "probs": probs,
        "attended": attended,
        "x_mid": x_mid,
        "h_moe": h_moe,
        "gates": gates,
        "returned": returned,
        "kept": kept,
    }
    return (x_mid, rank, gates, returned), stored


def backward_layer(grad, ready, stored, weights, experts, layer, rank, unfold, tables, numbers):
    message, dlogits = grad_slots(grad, rank, stored["gates"], stored["returned"])
    returned, half = expert_backward(
        message, experts, layer, stored["kept"], unfold, numbers[0]
    )
    dbr, dqkv, grad_in, dgain_a, dgain_m = grad_attention(
        grad, returned, rank, dlogits, weights, stored["x_mid"], stored["query"], stored["kv_all"],
        stored["probs"], tables, stored["low"], numbers[1],
    )
    dqkv, *ready = lax.optimization_barrier((dqkv, *ready))
    arrays = (
        stored["h_attn"], dqkv, stored["attended"], dbr, stored["h_moe"], dlogits, dgain_a, dgain_m
    )
    grads = weight_grads(*arrays) if layer else weight_grads_half(*arrays, number=1)
    return grad_in, grads, half, ready


def per_device(
    tokens,
    routes,
    lengths,
    gain_attn,
    w_query,
    w_key,
    w_value,
    w_out,
    gain_moe,
    w_router,
    w_gate,
    w_up,
    w_down,
    cotangent,
):
    section, yh, z, core, shard = (
        lax.axis_index(a) for a in ("section", "yh", "z", "core", "shard")
    )
    first = section == 0
    tok_rows, model_width = tokens.shape[1:]
    group_rows = tok_rows * lax.axis_size("shard")

    def mine(a):
        return lax.dynamic_index_in_dim(a, section, 0, keepdims=False)

    def by_layer(own, other):
        return jnp.where(first, own, other), jnp.where(first, other, own)

    local = jnp.concatenate(
        [
            w_out[0],
            w_query[0],
            w_key[0],
            w_value[0],
            w_router[0],
            gain_attn[0][:, None],
            gain_moe[0][:, None],
            jnp.zeros((w_query.shape[1], 94), BF),
        ],
        axis=1,
    )
    full, late, *whole = gather_weights(local, (w_gate[0], w_up[0], w_down[0]))
    weights = [full.reshape(model_width, -1), late.reshape(model_width, -1)]
    route_other = swap(at(routes[0], 1 - section, 0), "section")
    ranks = [rank_of(r) for r in by_layer(mine(routes[0]), route_other)]
    unfold = unfold_table(GROUP)

    segment, position = document_layout(mine(lengths[:, 0]), group_rows)
    row_start = shard * tok_rows
    own_segment = lax.dynamic_slice_in_dim(segment, row_start, tok_rows)
    tables = rotary_tables(lax.dynamic_slice_in_dim(position, row_start, tok_rows), HEAD_DIM)
    query_index = row_start + jnp.arange(tok_rows, dtype=jnp.int32)
    allowed = (own_segment[:, None] == segment[None, :]) & (
        query_index[:, None] >= jnp.arange(group_rows, dtype=jnp.int32)[None, :]
    )
    allowed = allowed.astype(F32)

    source, saved = (mine(tokens),), []
    for layer in range(2):
        source, stored = forward_layer(
            source, weights[layer], whole, layer, ranks[layer], unfold, tables, allowed,
            (7 + layer, 11 + layer),
        )
        saved.append(stored)
    low = fused("finish", finish_body, [((tok_rows, model_width), BF)], *source)[0]
    grad, low = lax.optimization_barrier((mine(cotangent), low))
    away = swap(low, "section")

    sums, ready = [None, None], (away,)
    for layer in (1, 0):
        grad, mixer_grad, half, ready = backward_layer(
            grad,
            ready,
            saved[layer],
            weights[layer],
            whole,
            layer,
            ranks[layer],
            unfold,
            tables,
            (5 + layer, 9 + layer),
        )
        given = lax.ppermute(half, "section", [(1 - layer, layer)])
        sums[layer] = (half, given)
        if layer == 1:
            (away,), ready = ready, (given,)
            late = lax.psum_scatter(mixer_grad, DEVICES, scatter_dimension=0, tiled=True)
            late = lax.optimization_barrier(late)
    mixed = jnp.where(first, jnp.stack([low, away]), jnp.stack([away, low]))

    def finish_experts():
        return jnp.where(first, total(*sums[0]), total(sums[1][0], *ready)).astype(BF)

    mix, (grad_gate, grad_up, grad_down) = reduce_all(mixer_grad, late, finish_experts)
    return (
        mixed,
        grad[None],
        mix[:, 3616][None],
        mix[:, 1536:3072][None],
        mix[:, 3072:3328][None],
        mix[:, 3328:3584][None],
        mix[:, :1536][None],
        mix[:, 3617][None],
        mix[:, 3584:3616][None],
        grad_gate[None],
        grad_up[None],
        grad_down[None],
    )


def solution(mesh):
    fine = Mesh(mesh.devices.reshape(2, 2, 4, 2, 4), ("section", *DEVICES))
    expert = ("yh", "z", "core")
    return jax.shard_map(
        per_device,
        mesh=fine,
        in_specs=(
            P(None, DEVICES, None),
            P("section", None, DEVICES, None),
            P(None, expert, None),
            P("section", DEVICES),
            P("section", DEVICES, None),
            P("section", DEVICES, None),
            P("section", DEVICES, None),
            P("section", DEVICES, None),
            P("section", DEVICES),
            P("section", DEVICES, None),
            P("section", expert, "shard", None),
            P("section", expert, "shard", None),
            P("section", expert, None, "shard"),
            P(None, DEVICES, None),
        ),
        out_specs=(
            P(None, DEVICES, None),
            P("section", DEVICES, None),
            P("section", DEVICES),
            P("section", DEVICES, None),
            P("section", DEVICES, None),
            P("section", DEVICES, None),
            P("section", DEVICES, None),
            P("section", DEVICES),
            P("section", DEVICES, None),
            P("section", expert, "shard", None),
            P("section", expert, "shard", None),
            P("section", expert, None, "shard"),
        ),
        check_vma=False,
    )
```

```python
import jax
import jax.numpy as jnp
from jax import lax
from jax.experimental import pallas as pl
from jax.experimental.pallas import tpu as pltpu
from jax.sharding import Mesh
from jax.sharding import PartitionSpec as P

HEADS = 12
HEAD_DIM = 128
EXPERTS = 32
MAIN = 16
EXTRA = 2
CHUNKS = 6

epsilon = 1e-06
rope_base = 1000000.0
masked_score = -1e30

BF = jnp.bfloat16
F32 = jnp.float32
CHIPS = ("yh", "z", "shard")
DEVICES = ("yh", "z", "core", "shard")


def dot(a, b, dims=((1,), (0,))):
    return lax.dot_general(a, b, (dims, ((), ())), preferred_element_type=F32)


def document_layout(doc_lengths, group_rows):
    doc_ends = jnp.cumsum(doc_lengths)
    starts = doc_ends - doc_lengths
    row_index = jnp.arange(group_rows, dtype=jnp.int32)
    segment = jnp.sum((row_index[:, None] >= doc_ends[None, :]).astype(jnp.int32), axis=1)
    member = segment[:, None] == jnp.arange(doc_lengths.shape[0], dtype=jnp.int32)[None, :]
    position = row_index - jnp.sum(jnp.where(member, starts[None, :], 0), axis=1)
    return (segment, position)


def rotary_tables(position, head_size):
    half_dim = head_size // 2
    frequency = rope_base ** (-2.0 * jnp.arange(half_dim, dtype=F32) / head_size)
    angles = position.astype(F32)[:, None] * frequency[None, :]
    cosine, sine = jnp.cos(angles), jnp.sin(angles)
    return jnp.concatenate([cosine, cosine], axis=1), jnp.concatenate([-sine, sine], axis=1)


def swap(value, axis):
    return lax.ppermute(value, axis, [(0, 1), (1, 0)])


def around(axis, size):
    here = lax.axis_index(axis)
    return [lax.rem(here + step, size) for step in range(1, size)]


def move(name, number, arrays, shapes, peers, copies):
    count = len(arrays)
    total = 40

    def kernel(*refs):
        ins, outs = refs[:count], refs[count : count + len(shapes)]
        sent, got = refs[count + len(shapes) :]
        barrier = pltpu.get_barrier_semaphore()
        near = peers()
        for peer in near:
            pl.semaphore_signal(
                barrier, inc=1, device_id=peer, device_id_type=pl.DeviceIdType.MESH
            )
        pl.semaphore_wait(barrier, len(near))
        started = []
        for k, (source, target, device) in enumerate(copies(ins, outs)):
            if device is None:
                copy = pltpu.make_async_copy(source, target, got.at[k])
            else:
                copy = pltpu.make_async_remote_copy(
                    src_ref=source,
                    dst_ref=target,
                    send_sem=sent.at[k],
                    recv_sem=got.at[k],
                    device_id=device,
                    device_id_type=pl.DeviceIdType.MESH,
                )
            copy.start()
            started.append(copy)
        for copy in started:
            copy.wait()

    space = pl.BlockSpec(memory_space=pltpu.HBM)
    return pl.pallas_call(
        kernel,
        out_shape=[jax.ShapeDtypeStruct(s, BF) for s in shapes],
        in_specs=[space] * count,
        out_specs=[space] * len(shapes),
        scratch_shapes=[pltpu.SemaphoreType.DMA((total,)), pltpu.SemaphoreType.DMA((total,))],
        compiler_params=pltpu.CompilerParams(collective_id=number, has_side_effects=True),
        name=name,
    )(*arrays)


def total(*parts):
    out = parts[0].astype(F32)
    for part in parts[1:]:
        out = out + part.astype(F32)
    return out


def at(array, index, axis):
    return lax.dynamic_index_in_dim(array, index, axis, keepdims=False)


def other(axis):
    return lax.rem(lax.axis_index(axis) + 1, 2)


def reduce_all(grads, late, finish_experts):
    core, shard, z, yh, section = (
        lax.axis_index(a) for a in ("core", "shard", "z", "yh", "section")
    )
    width = grads.shape[2]
    mix = grads.reshape(2, 4, 4, 24, width)

    cut = 1792
    sizes = (cut, width - cut)

    def peers_2():
        return [{"shard": x} for x in around("shard", 4)] + [{"z": i} for i in around("z", 4)]

    def copies_2(ins, outs):
        out = []
        for step, (x, i) in enumerate(zip(around("shard", 4), around("z", 4))):
            out.append((ins[0].at[:, :, x, :, pl.ds(0, cut)], outs[0].at[step], {"shard": x}))
            out.append((ins[0].at[:, i, :, :, pl.ds(cut, width - cut)], outs[1].at[step], {"z": i}))
        return out

    shapes = [(3, 2, 4, 24, size) for size in sizes]
    got = move("first_axis", 2, [mix], shapes, peers_2, copies_2)
    own = [
        lax.dynamic_slice(mix, (0, 0, shard, 0, 0), (2, 4, 1, 24, cut))[:, :, 0],
        lax.dynamic_slice(mix, (0, z, 0, 0, cut), (2, 1, 4, 24, width - cut))[:, 0],
    ]
    mix = [total(m, *g).astype(BF) for m, g in zip(own, got)]


    def shards_of(ref, x):
        down = ref.at[
            pl.ds(pl.multiple_of(1536 + x // 2 * 384, 128), 384),
            pl.ds(pl.multiple_of(lax.rem(x, 2) * 384, 128), 384),
        ]
        gate = ref.at[pl.ds(pl.multiple_of(x * 192, 64), 192)]
        up = ref.at[pl.ds(pl.multiple_of(768 + x * 192, 64), 192)]
        return gate, up, down

    def copies_3(ins, outs):
        here = lax.axis_index("shard")
        out = []
        for step, (x, i) in enumerate(zip(around("shard", 4), around("z", 4))):
            out.append((ins[0].at[:, i], outs[0].at[step], {"z": i}))
            out.append((ins[1].at[:, x], outs[1].at[step], {"shard": x}))
        return out

    shapes = [(3, 2, 24, size) for size in sizes]
    got = move("other_axis", 3, mix, shapes, peers_2, copies_3)
    mix = jnp.concatenate(
        [
            total(at(mix[0], z, 1), *got[0]).astype(BF),
            total(at(mix[1], shard, 1), *got[1]).astype(BF),
        ],
        axis=-1,
    )
    def places():
        here = 2 * lax.axis_index("yh") + lax.axis_index("section")
        there = [lax.rem(here + step, 4) for step in range(1, 4)]
        return [(t // 2, lax.rem(t, 2)) for t in there]

    def copies_4(ins, outs):
        here = lax.axis_index("shard")
        out = []
        for step, (y, s) in enumerate(places()):
            out.append((ins[0].at[s, y], outs[0].at[step], {"yh": y, "section": s}))
        for x in around("shard", 4):
            for k, source in enumerate(shards_of(ins[1], x)):
                out.append((source, outs[1 + k].at[here], {"shard": x}))
        for k, source in enumerate(shards_of(ins[1], here)):
            out.append((source, outs[1 + k].at[here], None))
        return out

    def copies_5(ins, outs):
        there = other("core")
        return [(r.at[pl.ds(2 * there, 2)], o, {"core": there}) for r, o in zip(ins, outs)]

    mine = (jnp.arange(2) == yh)[:, None, None]
    pairs = jnp.stack([mix, jnp.where(mine, late[None], jnp.zeros((), BF))])
    pairs = lax.optimization_barrier(pairs)
    got = move(
        "last_axis",
        4,
        [pairs, finish_experts()],
        [(3, 24, width), (4, 192, 768), (4, 192, 768), (4, 384, 384)],
        lambda: [{"yh": y, "section": s} for y, s in places()]
        + [{"shard": x} for x in around("shard", 4)],
        copies_4,
    )
    exp = got[1:]
    back = move(
        "owner_cores",
        13,
        list(exp),
        [(2, 192, 768), (2, 192, 768), (2, 384, 384)],
        lambda: [{"core": other("core")}],
        copies_5,
    )
    got = [got[0], *back]
    sums = total(at(at(pairs, section, 0), yh, 0), *got[0])
    out = []
    for e, g in zip(exp, got[1:]):
        kept = lax.dynamic_slice_in_dim(e, 2 * core, 2, 0)
        low, high = jnp.where(core == 0, kept, g), jnp.where(core == 0, g, kept)
        out.append(jnp.concatenate([low, high], axis=1).astype(F32))
    return sums, out


def gather_weights(local, experts):
    rows, width = local.shape

    def kernel(*refs):
        mine, shards = refs[0], refs[1:4]
        full, late, whole = refs[4], refs[5], refs[6:9]
        stage = refs[9:12]
        sent, got, sent_x, got_e, sent_c, got_c, sent_y, sent_o, local_sem = refs[12:]
        s, yh, z, c, x = (lax.axis_index(a) for a in ("section", "yh", "z", "core", "shard"))
        place = 2 * yh + s
        ys = [lax.rem(place + k, 4) for k in (1, 2, 3)]
        ys = [{"yh": y // 2, "section": lax.rem(y, 2)} for y in ys]
        xs = [{"shard": lax.rem(x + k, 4)} for k in (1, 2, 3)]
        z_up, z_down = lax.rem(z + 1, 4), lax.rem(z + 3, 4)
        sibling, partner = {"core": 1 - c}, {"section": 1 - s}

        def piece(k, i, h):
            if k == 2:
                return shards[2].at[i, pl.ds(pl.multiple_of(h * 384, 128), 384)]
            return shards[k].at[i, pl.ds(pl.multiple_of(h * 192, 64), 192)]

        def landing(k, layer, source, half):
            if k == 2:
                return whole[2].at[layer, half, :, pl.ds(pl.multiple_of(source * 384, 128), 384)]
            return whole[k].at[layer, source, half]

        def remote(source, target, send, receive, device):
            return pltpu.make_async_remote_copy(
                src_ref=source,
                dst_ref=target,
                send_sem=send,
                recv_sem=receive,
                device_id=device,
                device_id_type=pl.DeviceIdType.MESH,
            )

        def start(copies):
            for copy in copies:
                copy.start()
            return copies

        def finish(copies):
            for copy in copies:
                copy.wait()

        has_own = x // 2 == c
        own = lax.rem(x, 2)
        staged = start(
            [pltpu.make_async_copy(piece(k, own, c), stage[k], local_sem.at[k]) for k in range(3)]
        )
        barrier = pltpu.get_barrier_semaphore()
        zs = [{"z": lax.rem(z + k, 4)} for k in (1, 2, 3)]
        x_up, x_down = xs[0]["shard"], xs[2]["shard"]
        near = ys + xs + zs + [sibling]
        near += [{"shard": lax.rem(x + k, 4), "core": 1 - c} for k in (1, 2, 3)]
        for peer in near:
            pl.semaphore_signal(
                barrier, inc=1, device_id=peer, device_id_type=pl.DeviceIdType.MESH
            )
        pl.semaphore_wait(barrier, len(near))

        here = full.at[yh, z, c, x]

        def along_y(target):
            out = [pltpu.make_async_copy(mine, target, local_sem.at[3])]
            for k, device in enumerate(ys):
                out.append(remote(mine, target, sent.at[k], got.at[k], device))
            return out

        @pl.when(s == 0)
        def _():
            start(along_y(here))

        @pl.when(s == 1)
        def _():
            start(along_y(late.at[yh, z, c, x]))

        finish(staged)

        @pl.when(has_own)
        def _():
            for k in range(3):
                remote(
                    piece(k, own, 1 - c),
                    landing(k, s, x, 1 - c),
                    sent_o.at[k],
                    got_e.at[s, x, k],
                    sibling,
                ).start()
                pltpu.make_async_copy(stage[k], landing(k, s, x, c), got_e.at[s, x, k]).start()

        def pass_on(layer, distance, to_partner):
            source = lax.rem(x + distance, 4)
            for k in range(3):
                view = landing(k, layer, source, c)
                receive = got_e.at[layer, source, k]
                remote(view, view, sent_o.at[k], receive, sibling).wait_recv()
                if to_partner:
                    remote(view, view, sent_y.at[distance, k], receive, partner).start()
                across = got_c.at[layer, source, k]
                remote(view, view, sent_c.at[layer, source, k], across, sibling).start()

        finish(along_y(here))
        view, view_late = full.at[:, z, c, x], late.at[:, z, c, x]
        along_x = start(
            [remote(view, view, sent.at[3 + k], got.at[3 + k], xs[k]) for k in range(3)]
        )
        late_z = start(
            [
                remote(view_late, view_late, sent.at[11 + k], got.at[11 + k], zs[k])
                for k in range(3)
            ]
        )
        pass_on(s, 0, True)
        finish(along_x)

        def ring(base, axis, places, up, down):
            return start(
                [
                    remote(up, up, sent.at[base], got.at[base], {axis: places[0]}),
                    remote(down, down, sent.at[base + 1], got.at[base + 1], {axis: places[1]}),
                ]
            )

        view = full.at[:, z, c]
        along_z = ring(6, "z", (z_up, z_down), view, view)
        for i in range(2):

            @pl.when(x != 2 * c + i)
            def _():
                for h in range(2):
                    for k in range(3):
                        remote(
                            piece(k, i, h),
                            landing(k, s, x, h),
                            sent_x.at[(i * 2 + h) * 3 + k],
                            got_e.at[s, x, k],
                            {"shard": 2 * c + i, "core": h},
                        ).start()

        finish(late_z)
        view = late.at[:, :, c, x]
        late_x = ring(14, "shard", (x_up, x_down), view, view)
        finish(along_z)
        along_z = ring(8, "z", (z_up, z_down), full.at[0, z_down, c], full.at[1, z_up, c])
        for distance in (1, 3, 2):
            pass_on(s, distance, True)
        finish(along_z)
        view = full.at[:, :, c]
        across = start([remote(view, view, sent.at[10], got.at[10], sibling)])
        finish(late_x)
        late_x = ring(
            16, "shard", (x_up, x_down), late.at[0, :, c, x_down], late.at[1, :, c, x_up]
        )
        for distance in (0, 1):
            pass_on(1 - s, distance, False)
        finish(late_x)
        view = late.at[:, :, c]
        across += start([remote(view, view, sent.at[18], got.at[18], sibling)])
        for distance in (3, 2):
            pass_on(1 - s, distance, False)

        finish(across)
        for i in range(2):

            @pl.when(x != 2 * c + i)
            def _():
                for h in range(2):
                    for k in range(3):
                        view = piece(k, i, h)
                        n = (i * 2 + h) * 3 + k
                        remote(view, view, sent_x.at[n], got_e.at[0, 0, k], sibling).wait_send()

        @pl.when(has_own)
        def _():
            for k in range(3):
                view = piece(k, own, 1 - c)
                remote(view, view, sent_o.at[k], got_e.at[0, 0, k], sibling).wait_send()

        for source in range(4):
            for k in range(3):
                view = landing(k, s, source, c)
                send = sent_y.at[source, k]
                remote(view, view, send, got_e.at[0, 0, k], partner).wait_send()
                for layer in range(2):
                    view = landing(k, layer, source, c)
                    arrived = landing(k, layer, source, 1 - c)
                    send, receive = sent_c.at[layer, source, k], got_c.at[layer, source, k]
                    remote(view, view, send, receive, sibling).wait_send()
                    remote(arrived, arrived, send, receive, sibling).wait_recv()

    space = pl.BlockSpec(memory_space=pltpu.HBM)
    near_space = pl.BlockSpec(memory_space=pltpu.VMEM)
    shapes = [(2, 4, 2, 4, rows, width)] * 2
    shapes += [(2, 4, 2, 192, 768), (2, 4, 2, 192, 768), (2, 2, 384, 1536)]
    dma = pltpu.SemaphoreType.DMA
    return pl.pallas_call(
        kernel,
        out_shape=[jax.ShapeDtypeStruct(shape, BF) for shape in shapes],
        in_specs=[near_space] + [space] * 3,
        out_specs=[space] * 5,
        scratch_shapes=[
            pltpu.VMEM((192, 768), BF),
            pltpu.VMEM((192, 768), BF),
            pltpu.VMEM((384, 384), BF),
            dma((19,)),
            dma((19,)),
            dma((12,)),
            dma((2, 4, 3)),
            dma((2, 4, 3)),
            dma((2, 4, 3)),
            dma((4, 3)),
            dma((3,)),
            dma((4,)),
        ],
        compiler_params=pltpu.CompilerParams(collective_id=0, has_side_effects=True),
        name="gather_weights",
    )(local, *experts)


def rank_of(route_rows):
    rows = route_rows.shape[0]
    chosen = route_rows.T[None, :, :] == jnp.arange(EXPERTS, dtype=jnp.int32)[:, None, None]
    hot = jnp.any(chosen, axis=1)
    index = jnp.arange(rows, dtype=jnp.int32)
    before = (index[:, None] < index[None, :]).astype(BF)
    return jnp.where(hot, dot(hot.astype(BF), before), -1.0)


def stacked(field):
    return jnp.concatenate(jnp.split(field, CHUNKS, axis=1), axis=0)


def unstacked(field):
    return jnp.concatenate(jnp.split(field, CHUNKS, axis=0), axis=1)


def unfold_table(sources):
    row = jnp.arange(CHUNKS * sources * EXTRA, dtype=jnp.int32)
    piece, source, extra = row // (sources * EXTRA), row // EXTRA % sources, row % EXTRA
    column = jnp.arange(sources * MAIN, dtype=jnp.int32)
    return (
        (source * MAIN + piece * EXTRA + extra)[:, None] == column[None, :]
    ).astype(BF)


def arrived_rows(message, unfold):
    width = message.shape[1] - 256
    extra = unstacked(dot(unfold, message[:, width:]).astype(BF))
    return jnp.concatenate([message[:, :width], extra], axis=0)


def fold_rows(rows, unfold, sources):
    main = rows[: sources * MAIN]
    extra = dot(unfold, stacked(rows[sources * MAIN :]), ((0,), (0,))).astype(BF)
    return jnp.concatenate([main, extra], axis=1)


def low_pair(value):
    high = value.astype(BF)
    return high, (value - high.astype(F32)).astype(BF)


OUT_COLUMNS, QKV_STEP = 1536, 512


def columns(width, place):
    return lambda rows: pl.BlockSpec((rows, width), lambda i: (0, place), memory_space=pltpu.VMEM)


OUT_BLOCK = [columns(OUT_COLUMNS, 0)]
QKV_BLOCKS = [columns(QKV_STEP, 3 + k) for k in range(4)]
NARROW_BLOCK = [columns(128, 28)]


def fused(name, body, shapes, *arrays, scratch=(), number=None):
    near = pl.BlockSpec(memory_space=pltpu.VMEM)
    specs, given = [], []
    for array in arrays:
        if isinstance(array, tuple):
            array, blocks = array
            specs += [block(array.shape[0]) for block in blocks]
            given += [array] * len(blocks)
        else:
            specs.append(near)
            given.append(array)
    return pl.pallas_call(
        body,
        grid=(1,),
        out_shape=[jax.ShapeDtypeStruct(shape, kind) for shape, kind in shapes],
        in_specs=specs,
        out_specs=[near] * len(shapes),
        scratch_shapes=list(scratch),
        compiler_params=pltpu.CompilerParams(
            vmem_limit_bytes=48 << 20, collective_id=number, has_side_effects=number is not None
        ),
        name=name,
    )(*given)


TN, NT = ((0,), (0,)), ((1,), (1,))


def slots(rank):
    count, rows = rank.shape
    place = lax.broadcasted_iota(jnp.int32, (count, MAIN, rows), 1)
    wide = jnp.broadcast_to(rank[:, None, :], (count, MAIN, rows))
    main = jnp.where(wide == place.astype(F32), 1.0, 0.0)
    extra = (MAIN + lax.rem(place, EXTRA)).astype(F32)
    extra = jnp.where((wide == extra) & (place < EXTRA * CHUNKS), 1.0, 0.0)
    return main, extra


def per_piece(table):
    piece = lax.rem(lax.broadcasted_iota(jnp.int32, table.shape, 0), MAIN) // EXTRA
    return [jnp.where(piece == j, table, 0.0) for j in range(CHUNKS)]


def flat(table):
    return table.reshape(table.shape[0] * table.shape[1], table.shape[2])


def send_table(main, extra, field):
    width = field.shape[1] // CHUNKS
    side = None
    for j, table in enumerate(per_piece(flat(extra))):
        part = dot(table.astype(BF), field[:, j * width : (j + 1) * width])
        side = part if side is None else side + part
    return dot(flat(main).astype(BF), field), side


def bring_back(main, extra, rows, exact):
    parts = low_pair if exact else (lambda t: (t.astype(BF),))
    model_width = rows.shape[1] - 256
    total_main = None
    for table in parts(main):
        part = dot(table, rows[:, :model_width], TN)
        total_main = part if total_main is None else total_main + part
    side = []
    for table in per_piece(extra):
        total_side = None
        for t in parts(table):
            part = dot(t, rows[:, model_width:], TN)
            total_side = part if total_side is None else total_side + part
        side.append(total_side)
    return total_main + jnp.concatenate(side, axis=1)


def gain_rows(narrow):
    row = lax.broadcasted_iota(jnp.int32, (8, narrow.shape[1]), 0)
    column = lax.broadcasted_iota(jnp.int32, (8, narrow.shape[1]), 1)
    pick = jnp.where(column == row + EXPERTS, 1.0, 0.0).astype(BF)
    rows = dot(pick, narrow, NT)
    return rows[0:1], rows[1:2]


def turn(field, cosine, sine):
    return field * cosine + pltpu.roll(field, HEAD_DIM // 2, 1) * sine


def turn_back(field, cosine, sine):
    return field * cosine - pltpu.roll(field, HEAD_DIM // 2, 1) * sine


def combined(x_mid, rank, gates, rows):
    main, extra = slots(rank)
    wide = jnp.broadcast_to(gates[:, None, :], main.shape)
    return x_mid + bring_back(flat(main * wide), flat(extra * wide), rows, True)


def finish_body(mid_ref, rank_ref, gates_ref, rows_ref, out_ref):
    out = combined(mid_ref[...], rank_ref[...], gates_ref[...], rows_ref[...])
    out_ref[...] = out.astype(BF)


def heads_of(kv_ref):
    kv_heads = kv_ref.shape[2] // 2 // HEAD_DIM
    parts = []
    for k in range(2 * kv_heads):
        part = kv_ref[:, :, k * HEAD_DIM : (k + 1) * HEAD_DIM]
        parts.append(part.reshape(part.shape[0] * part.shape[1], HEAD_DIM))
    return parts[:kv_heads], parts[kv_heads:]


def attention_body(combine):
    def body(*refs):
        source, refs = refs[: 4 if combine else 1], refs[4 if combine else 1 :]
        weights, refs = refs[:4], refs[4:]
        out_w, narrow, cos_ref, sin_ref, allowed_ref, rank_ref, low_ref, h_ref, q_ref = refs[:9]
        kv_ref, mid_ref, h2_ref, att_ref, probs_ref, gates_ref, out_ref, held, sent, got = refs[9:]
        here = lax.axis_index("shard")
        peers = [{"shard": x} for x in around("shard", 4)]
        barrier = pltpu.get_barrier_semaphore()
        for peer in peers:
            pl.semaphore_signal(
                barrier, inc=1, device_id=peer, device_id_type=pl.DeviceIdType.MESH
            )
        if combine:
            mid, rank, gates, rows = (ref[...] for ref in source)
            low = combined(mid, rank, gates, rows).astype(BF)
        else:
            low = source[0][...]
        low_ref[...] = low
        field = low.astype(F32)
        gain_a, gain_m = gain_rows(narrow[...])
        scale = lax.rsqrt(jnp.mean(field * field, axis=1, keepdims=True) + epsilon)
        h = (field * scale * gain_a).astype(BF)
        h_ref[...] = h
        cosine, sine = cos_ref[...], sin_ref[...]

        def projected(column, turned):
            inside = column % QKV_STEP
            part = dot(h, weights[column // QKV_STEP][:, inside : inside + 256])
            if turned:
                part = jnp.concatenate(
                    [turn(part[:, k : k + HEAD_DIM], cosine, sine) for k in (0, HEAD_DIM)], axis=1
                )
            return part.astype(BF)

        query_width, kv_width = q_ref.shape[1], kv_ref.shape[2]
        for column in range(0, kv_width, 256):
            part = projected(query_width + column, column < kv_width // 2)
            held[here, :, column : column + 256] = part
        pl.semaphore_wait(barrier, len(peers))
        copies = []
        for k, peer in enumerate(peers):
            view = held.at[here]
            copies.append(
                pltpu.make_async_remote_copy(
                    src_ref=view,
                    dst_ref=view,
                    send_sem=sent.at[k],
                    recv_sem=got.at[k],
                    device_id=peer,
                    device_id_type=pl.DeviceIdType.MESH,
                )
            )
            copies[-1].start()
        for column in range(0, query_width, 256):
            q_ref[:, column : column + 256] = projected(column, True)
        for copy in copies:
            copy.wait()

        kv_ref[...] = held[...]
        keys, values = heads_of(held)
        allowed = allowed_ref[...] > 0.0
        ratio = HEADS // len(keys)
        for head in range(HEADS):
            lanes = slice(head * HEAD_DIM, (head + 1) * HEAD_DIM)
            scores = dot(q_ref[:, lanes], keys[head // ratio], NT) * HEAD_DIM ** (-0.5)
            scores = jnp.where(allowed, scores, masked_score)
            exponent = jnp.exp(scores - jnp.max(scores, axis=1, keepdims=True))
            probs = exponent / jnp.sum(exponent, axis=1, keepdims=True)
            probs_ref[head] = probs
            att_ref[:, lanes] = dot(probs.astype(BF), values[head // ratio]).astype(BF)
        mid = field + dot(att_ref[...], out_w[...])
        mid_ref[...] = mid
        scale = lax.rsqrt(jnp.mean(mid * mid, axis=1, keepdims=True) + epsilon)
        h2 = (mid * scale * gain_m).astype(BF)
        h2_ref[...] = h2
        rank = rank_ref[...]
        logits = jnp.transpose(dot(h2, narrow[...]))[:EXPERTS]
        logits = jnp.where(rank >= 0.0, logits, masked_score)
        gate_exp = jnp.exp(logits - jnp.max(logits, axis=0, keepdims=True))
        gate_exp = jnp.where(rank >= 0.0, gate_exp, 0.0)
        gates_ref[...] = gate_exp / jnp.sum(gate_exp, axis=0, keepdims=True)
        main, side = send_table(*slots(rank), h2)
        width = main.shape[1]
        out_ref[:, :width] = main.astype(BF)
        out_ref[:, width:] = side.astype(BF)

    return body


def attention(source, weights, tables, allowed, rank, number):
    tok_rows, model_width = source[0].shape
    query_width = HEADS * HEAD_DIM
    shapes = [((tok_rows, model_width), BF)] * 2
    shapes += [
        ((tok_rows, query_width), BF),
        ((allowed.shape[1] // tok_rows, tok_rows, 4 * QKV_STEP - query_width), BF),
        ((tok_rows, model_width), F32),
        ((tok_rows, model_width), BF),
        ((tok_rows, query_width), BF),
        ((HEADS, tok_rows, allowed.shape[1]), F32),
        (rank.shape, F32),
        ((EXPERTS * MAIN, model_width + 256), BF),
    ]
    dma = pltpu.SemaphoreType.DMA
    return fused(
        "attention",
        attention_body(len(source) > 1),
        shapes,
        *source,
        (weights, QKV_BLOCKS + OUT_BLOCK + NARROW_BLOCK),
        *tables,
        allowed,
        rank,
        scratch=[pltpu.VMEM(shapes[3][0], BF), dma((3,)), dma((3,))],
        number=number,
    )


def grad_slots_body(grad_ref, rank_ref, gates_ref, rows_ref, out_ref, dlogits_ref):
    gates = gates_ref[...]
    main, extra = slots(rank_ref[...])
    wide = jnp.broadcast_to(gates[:, None, :], main.shape)
    grad_main, grad_side = send_table(main, extra, grad_ref[...])
    width = grad_main.shape[1]
    dgate = None
    for table, grad, columns in (
        (main, grad_main, slice(0, width)),
        (extra, grad_side, slice(width, width + 256)),
    ):
        slot_gate = jnp.sum(flat(table * wide), axis=1, keepdims=True)
        out_ref[:, columns] = (grad * slot_gate).astype(BF)
        slot_dgate = jnp.sum(grad * rows_ref[:, columns].astype(F32), axis=1, keepdims=True)
        part = jnp.sum((flat(table) * slot_dgate).reshape(table.shape), axis=1)
        dgate = part if dgate is None else dgate + part
    dlogits = gates * (dgate - jnp.sum(gates * dgate, axis=0, keepdims=True))
    pad = jnp.zeros((dlogits_ref.shape[1] - EXPERTS, dlogits.shape[1]), F32)
    dlogits_ref[...] = jnp.transpose(jnp.concatenate([dlogits, pad], axis=0)).astype(BF)


def grad_slots(grad, rank, gates, rows):
    shapes = [(rows.shape, BF), ((grad.shape[0], 128), BF)]
    return fused("grad_slots", grad_slots_body, shapes, grad, rank, gates, rows)


def norm_grads(field, gain, grad):
    scale = lax.rsqrt(jnp.mean(field * field, axis=1, keepdims=True) + epsilon)
    scaled = grad * gain
    centre = jnp.mean(scaled * field, axis=1, keepdims=True)
    dgain = jnp.sum(grad * field * scale, axis=0, keepdims=True)
    return scale * scaled - field * (scale * scale * scale) * centre, dgain


def grad_attention_body(
    grad_ref, rows_ref, rank_ref, dlogits_ref, out_w, weight_0, weight_1, weight_2, weight_3, narrow,
    mid_ref, q_ref, kv_ref, probs_ref, cos_ref, sin_ref, low_ref,
    dbr_ref, dqkv_ref, grad_out_ref, dgain_a_ref, dgain_m_ref,
    datt_ref, dkv_ref, held, sent, got,
):
    here = lax.axis_index("shard")
    peers = [{"shard": x} for x in around("shard", 4)]
    barrier = pltpu.get_barrier_semaphore()
    for peer in peers:
        pl.semaphore_signal(barrier, inc=1, device_id=peer, device_id_type=pl.DeviceIdType.MESH)
    main, extra = slots(rank_ref[...])
    dh = bring_back(flat(main), flat(extra), rows_ref[...], False)
    dh = dh + dot(dlogits_ref[...], narrow[...], NT)
    gain_a, gain_m = gain_rows(narrow[...])
    dmid, dgain = norm_grads(mid_ref[...], gain_m, dh)
    dmid = dmid + grad_ref[...].astype(F32)
    dgain_m_ref[...] = dgain
    dbr_ref[...] = dmid.astype(BF)
    datt_ref[...] = dot(dbr_ref[...], out_w[...], NT).astype(BF)
    keys, values = heads_of(kv_ref)
    ratio = HEADS // len(keys)
    cosine, sine = cos_ref[...], sin_ref[...]
    count, tok_rows, kv_columns = kv_ref.shape
    scale = HEAD_DIM ** (-0.5)
    for k in range(len(keys)):
        dkey, dvalue = None, None
        for head in range(k * ratio, (k + 1) * ratio):
            lanes = slice(head * HEAD_DIM, (head + 1) * HEAD_DIM)
            probs, datt = probs_ref[head], datt_ref[:, lanes]
            dprobs = dot(datt, values[k], NT)
            centre = jnp.sum(dprobs * probs, axis=1, keepdims=True)
            dscores = (probs * (dprobs - centre)).astype(BF)
            part = dot(probs.astype(BF), datt, TN)
            dvalue = part if dvalue is None else dvalue + part
            part = dot(dscores, q_ref[:, lanes], TN)
            dkey = part if dkey is None else dkey + part
            dquery = dot(dscores, keys[k]) * scale
            dqkv_ref[:, lanes] = turn_back(dquery, cosine, sine).astype(BF)
        at_key, at_value = k * HEAD_DIM, (len(keys) + k) * HEAD_DIM
        shape = (count, tok_rows, HEAD_DIM)
        dkv_ref[:, :, at_key : at_key + HEAD_DIM] = (dkey * scale).astype(BF).reshape(shape)
        dkv_ref[:, :, at_value : at_value + HEAD_DIM] = dvalue.astype(BF).reshape(shape)
    pl.semaphore_wait(barrier, len(peers))
    copies = []
    for k, peer in enumerate(peers):
        copies.append(
            pltpu.make_async_remote_copy(
                src_ref=dkv_ref.at[peer["shard"]],
                dst_ref=held.at[k],
                send_sem=sent.at[k],
                recv_sem=got.at[k],
                device_id=peer,
                device_id_type=pl.DeviceIdType.MESH,
            )
        )
        copies[-1].start()
    query_width = q_ref.shape[1]
    dh = None
    weights = (weight_0, weight_1, weight_2, weight_3)
    for k, weight in enumerate(weights[:-1]):
        part = dot(dqkv_ref[:, k * QKV_STEP : (k + 1) * QKV_STEP], weight[...], NT)
        dh = part if dh is None else dh + part
    for copy in copies:
        copy.wait()
    dkv = dkv_ref[here].astype(F32)
    for k in range(len(peers)):
        dkv = dkv + held[k].astype(F32)
    for k in range(0, kv_columns // 2, HEAD_DIM):
        part = turn_back(dkv[:, k : k + HEAD_DIM], cosine, sine)
        dqkv_ref[:, query_width + k : query_width + k + HEAD_DIM] = part.astype(BF)
    dqkv_ref[:, query_width + kv_columns // 2 :] = dkv[:, kv_columns // 2 :].astype(BF)
    dh = dh + dot(dqkv_ref[:, query_width:], weights[-1][...], NT)
    dlow, dgain = norm_grads(low_ref[...].astype(F32), gain_a, dh)
    dgain_a_ref[...] = dgain
    grad_out_ref[...] = (dlow + dmid).astype(BF)


def grad_attention(
    grad, rows, rank, dlogits, weights, mid, q, kv, probs, tables, low, number
):
    tok_rows, model_width = mid.shape
    shapes = [
        ((tok_rows, model_width), BF),
        ((tok_rows, 4 * QKV_STEP), BF),
        ((tok_rows, model_width), BF),
        ((1, model_width), F32),
        ((1, model_width), F32),
    ]
    dma = pltpu.SemaphoreType.DMA
    return fused(
        "grad_attention",
        grad_attention_body,
        shapes,
        grad,
        rows,
        rank,
        dlogits,
        (weights, OUT_BLOCK + QKV_BLOCKS + NARROW_BLOCK),
        mid,
        q,
        kv,
        probs,
        *tables,
        low,
        scratch=[
            pltpu.VMEM(q.shape, BF),
            pltpu.VMEM(kv.shape, BF),
            pltpu.VMEM((3, *kv.shape[1:]), BF),
            dma((3,)),
            dma((3,)),
        ],
        number=number,
    )


def weight_grads_body(
    h_ref, dqkv_ref, att_ref, dbr_ref, h2_ref, dlogits_ref, dgain_a_ref, dgain_m_ref, out_ref
):
    step = 512
    place = 0
    for left, right in ((att_ref, dbr_ref), (h_ref, dqkv_ref)):
        for k in range(0, right.shape[1], step):
            part = dot(left[...], right[:, k : k + step], TN)
            out_ref[:, place : place + step] = part.astype(BF)
            place += step
    narrow = dot(h2_ref[...], dlogits_ref[...], TN)
    rows = jnp.concatenate(
        [dgain_a_ref[...], dgain_m_ref[...], jnp.zeros((126, h_ref.shape[1]), F32)], axis=0
    )
    columns = pltpu.roll(jnp.transpose(rows), EXPERTS, 1)
    out_ref[:, place:] = (narrow + columns).astype(BF)


def weight_grads(h, dqkv, att, dbr, h2, dlogits, dgain_a, dgain_m):
    columns = dqkv.shape[1] + dbr.shape[1] + 128
    return fused(
        "weight_grads", weight_grads_body, [((h.shape[1], columns), BF)],
        h, dqkv, att, dbr, h2, dlogits, dgain_a, dgain_m,
    )[0]


def greet(peers):
    barrier = pltpu.get_barrier_semaphore()
    for peer in peers:
        pl.semaphore_signal(barrier, inc=1, device_id=peer, device_id_type=pl.DeviceIdType.MESH)
    pl.semaphore_wait(barrier, len(peers))


def weight_grads_half(*arrays, number):
    model_width = arrays[0].shape[1]
    width = arrays[1].shape[1] + arrays[3].shape[1] + 128
    shape = (8, 2, model_width // 16, width)

    def body(h_ref, dqkv_ref, att_ref, dbr_ref, h2_ref, dlogits_ref, dgain_a, dgain_m, *refs):
        out_ref, all_ref, held, sent, got = refs
        core = lax.axis_index("core")
        sibling = {"core": 1 - core}
        greet([sibling])
        copies = []

        def put(place, part):
            columns_of = pl.ds(place, part.shape[1])
            all_ref[:, :, :, columns_of] = part.astype(BF).reshape(*shape[:3], part.shape[1])
            k = len(copies)
            copy = pltpu.make_async_remote_copy(
                src_ref=all_ref.at[:, 1 - core, :, columns_of],
                dst_ref=held.at[:, :, columns_of],
                send_sem=sent.at[k],
                recv_sem=got.at[k],
                device_id=sibling,
                device_id_type=pl.DeviceIdType.MESH,
            )
            copy.start()
            copies.append((copy, columns_of))

        step, place = 512, 0
        for left, right in ((att_ref, dbr_ref), (h_ref, dqkv_ref)):
            for k in range(0, right.shape[1], step):
                put(place, dot(left[...], right[:, k : k + step], TN))
                place += step
        narrow = dot(h2_ref[...], dlogits_ref[...], TN)
        rows = jnp.concatenate(
            [dgain_a[...], dgain_m[...], jnp.zeros((126, model_width), F32)], axis=0
        )
        put(place, narrow + pltpu.roll(jnp.transpose(rows), EXPERTS, 1))
        for copy, columns_of in copies:
            copy.wait()
            own = all_ref[:, core, :, columns_of].astype(F32)
            out_ref[:, :, columns_of] = (own + held[:, :, columns_of].astype(F32)).astype(BF)

    half = (shape[0], shape[2], width)
    dma = pltpu.SemaphoreType.DMA
    return fused(
        "weight_grads_half",
        body,
        [(half, BF)],
        *arrays,
        scratch=[pltpu.VMEM(shape, BF), pltpu.VMEM(half, BF), dma((8,)), dma((8,))],
        number=number,
    )[0]


PARTNERS = [(dy, dz, (dz + k) % 4) for k in range(4) for dy in range(2) for dz in range(4)]
GROUP = 8
GROUPS = len(PARTNERS) // GROUP


def facing(n):
    k, dy, dz = n // GROUP, n // 4 % 2, n % 4
    return -k % GROUPS * GROUP + dy * 4 + -dz % 4


def partners():
    s, yh, z, x = (lax.axis_index(a) for a in ("section", "yh", "z", "shard"))
    out = []
    for dy, dz, dx in PARTNERS:
        there = {
            "section": lax.rem(s + dy, 2),
            "yh": lax.rem(yh + dy, 2),
            "z": lax.rem(z + dz, 4),
            "shard": lax.rem(x + dx, 4),
        }
        out.append((there, (there["yh"] * 4 + there["z"]) * 4 + there["shard"]))
    return out


def exchange_rows(message, returned, arrived, produced, sems, work, after, load, sibling=()):
    sent, got, sent_back, got_back = sems
    for copy in load:
        copy.start()
    near = partners()
    own = near[0][1]
    greet([device for device, _ in near[1:]] + list(sibling))

    def remote(source, target, send, receive, device):
        return pltpu.make_async_remote_copy(
            src_ref=source,
            dst_ref=target,
            send_sem=send,
            recv_sem=receive,
            device_id=device,
            device_id_type=pl.DeviceIdType.MESH,
        )

    def out(n):
        device, expert = near[n]
        f = facing(n)
        return remote(message.at[expert], arrived.at[f], sent.at[n], got.at[f], device)

    def back(n):
        return remote(
            produced.at[n], returned.at[own], sent_back.at[n], got_back.at[facing(n)], near[n][0]
        )

    for k in range(GROUPS):
        for n in range(-k % GROUPS * GROUP, -k % GROUPS * GROUP + GROUP):
            if n:
                out(n).start()
    arrived[0] = message[own]
    for copy in load:
        copy.wait()
    for k in range(GROUPS):
        members = range(k * GROUP, (k + 1) * GROUP)
        for n in members:
            if n:
                remote(arrived.at[n], arrived.at[n], sent.at[n], got.at[n], near[n][0]).wait_recv()
        rows = arrived[k * GROUP : (k + 1) * GROUP]
        result = work(k, rows.reshape(GROUP * MAIN, rows.shape[2]))
        produced[k * GROUP : (k + 1) * GROUP] = result.reshape(rows.shape)
        for n in members:
            if n:
                back(n).start()
    returned[own] = produced[0]
    after()
    for n in range(1, len(near)):
        device, expert = near[n]
        out(n).wait_send()
        back(n).wait_send()
        view = returned.at[expert]
        remote(view, view, sent_back.at[n], got_back.at[n], device).wait_recv()


def exchange_call(name, number, body, inputs, whole, shapes, message_shape, scratch):
    near = pl.BlockSpec(memory_space=pltpu.VMEM)
    far = pl.BlockSpec(memory_space=pltpu.HBM)
    dma = pltpu.SemaphoreType.DMA
    count = message_shape[0]
    return pl.pallas_call(
        body,
        out_shape=[jax.ShapeDtypeStruct(shape, kind) for shape, kind in shapes],
        in_specs=[far] * len(whole) + [near] * len(inputs),
        out_specs=[near] * len(shapes),
        scratch_shapes=[pltpu.VMEM(w.shape[1:], BF) for w in whole]
        + [dma((len(whole),))]
        + [pltpu.VMEM(message_shape, BF), pltpu.VMEM(message_shape, BF)]
        + [dma((count,)) for _ in range(4)]
        + scratch,
        compiler_params=pltpu.CompilerParams(
            collective_id=number, has_side_effects=True, vmem_limit_bytes=56 << 20
        ),
        name=name,
    )(*whole, *inputs)


def loads(whole, layer, held, sem):
    copies = [pltpu.make_async_copy(w.at[layer], h, sem.at[k]) for k, (w, h) in enumerate(zip(whole, held))]

    def matrix(k):
        value = held[k][...]
        return value.reshape(-1, value.shape[-1])

    return copies, matrix


def expert_forward(message, experts, layer, unfold, number):
    message = message.reshape(EXPERTS, MAIN, message.shape[1])
    rows = GROUP * (MAIN + EXTRA)
    depth, width = message.shape[2] - 256, experts[0].shape[-1]

    def body(*refs):
        whole, (message_ref, unfold_ref), refs = refs[:3], refs[3:5], refs[5:]
        returned, rows_ref, gate_ref, up_ref, hidden_ref = refs[:5]
        load, matrix = loads(whole, layer, refs[5:8], refs[8])
        arrived, produced, *sems = refs[9:]

        def work(k, came):
            field = arrived_rows(came, unfold_ref[...])
            rows_ref[k] = field
            gate = dot(field, matrix(0))
            up = dot(field, matrix(1))
            gate_ref[k] = gate
            up_ref[k] = up
            hidden = (gate / (1.0 + jnp.exp(-gate)) * up).astype(BF)
            hidden_ref[k] = hidden
            return fold_rows(dot(hidden, matrix(2)).astype(BF), unfold_ref[...], GROUP)

        exchange_rows(message_ref, returned, arrived, produced, sems, work, lambda: None, load)

    shapes = [
        (message.shape, BF),
        ((GROUPS, rows, depth), BF),
        ((GROUPS, rows, width), F32),
        ((GROUPS, rows, width), F32),
        ((GROUPS, rows, width), BF),
    ]
    returned, *kept = exchange_call(
        "expert_forward", number, body, [message, unfold], experts, shapes, message.shape, []
    )
    return returned.reshape(-1, message.shape[2]), kept


def expert_backward(message, experts, layer, kept, unfold, number):
    message = message.reshape(EXPERTS, MAIN, message.shape[1])
    rows = GROUP * (MAIN + EXTRA)
    depth, width = message.shape[2] - 256, experts[0].shape[-1]
    shards = 4
    half, deep = depth // 8, width // 2

    def body(*refs):
        whole, refs = refs[:3], refs[3:]
        message_ref, rows_ref, gate_ref, up_ref, hidden_ref, unfold_ref = refs[:6]
        returned, sum_ref = refs[6:8]
        load, matrix = loads(whole, layer, refs[8:11], refs[11])
        (arrived, produced), refs = refs[12:14], refs[14:]
        sems, (came_ref, dgate_ref, dup_ref) = refs[:4], refs[4:7]
        wide_refs, (down_ref, held_gate, held_up, held_down, sent, got) = refs[7:9], refs[9:]
        core = lax.axis_index("core")
        sibling = {"core": 1 - core}

        def work(k, came):
            field = arrived_rows(came, unfold_ref[...])
            came_ref[k] = field
            dhidden = dot(field, matrix(2), NT)
            gate = gate_ref[k]
            logistic = 1.0 / (1.0 + jnp.exp(-gate))
            dgate = dhidden * up_ref[k] * (logistic * (1.0 + gate * (1.0 - logistic)))
            dgate_ref[k] = dgate.astype(BF)
            dup_ref[k] = (dhidden * (gate * logistic)).astype(BF)
            out = dot(dgate_ref[k], matrix(0), NT) + dot(dup_ref[k], matrix(1), NT)
            return fold_rows(out.astype(BF), unfold_ref[...], GROUP)

        def to_sibling(k):
            views = [wide_refs[0].at[:, 1 - core], wide_refs[1].at[:, 1 - core]]
            views.append(down_ref.at[1 - core])
            return pltpu.make_async_remote_copy(
                src_ref=views[k],
                dst_ref=(held_gate, held_up, held_down)[k],
                send_sem=sent.at[k],
                recv_sem=got.at[k],
                device_id=sibling,
                device_id_type=pl.DeviceIdType.MESH,
            )

        def after():
            step = 256
            field = rows_ref[...].reshape(GROUPS * rows, depth)
            for k, source in enumerate((dgate_ref, dup_ref)):
                for column in range(0, width, step):
                    lanes = slice(column, column + step)
                    part = source[:, :, lanes].reshape(GROUPS * rows, step)
                    part = dot(field, part, TN).astype(BF)
                    wide_refs[k][:, :, :, lanes] = part.reshape(shards, 2, half, step)
                to_sibling(k).start()
            field = hidden_ref[...].reshape(GROUPS * rows, width)
            for column in range(0, depth, step):
                lanes = slice(column, column + step)
                part = came_ref[:, :, lanes].reshape(GROUPS * rows, step)
                part = dot(field, part, TN).astype(BF)
                down_ref[:, :, lanes] = part.reshape(2, deep, step)
            to_sibling(2).start()

        exchange_rows(
            message_ref, returned, arrived, produced, sems, work, after, load, (sibling,)
        )
        for k, held in enumerate((held_gate, held_up)):
            to_sibling(k).wait()
            for j in range(shards):
                part = wide_refs[k][j, core].astype(F32) + held[j].astype(F32)
                place = (k * shards + j) * half
                sum_ref[place : place + half] = part.astype(BF)
        to_sibling(2).wait()
        part = down_ref[core].astype(F32) + held_down[...].astype(F32)
        place = 2 * shards * half
        for j in range(2):
            columns_of = part[:, j * width : (j + 1) * width].astype(BF)
            sum_ref[place + j * deep : place + (j + 1) * deep] = columns_of

    shapes = [(message.shape, BF), ((3 * shards * half, width), BF)]
    dma = pltpu.SemaphoreType.DMA
    scratch = [
        pltpu.VMEM((GROUPS, rows, depth), BF),
        pltpu.VMEM((GROUPS, rows, width), BF),
        pltpu.VMEM((GROUPS, rows, width), BF),
        pltpu.VMEM((shards, 2, half, width), BF),
        pltpu.VMEM((shards, 2, half, width), BF),
        pltpu.VMEM((2, deep, depth), BF),
        pltpu.VMEM((shards, half, width), BF),
        pltpu.VMEM((shards, half, width), BF),
        pltpu.VMEM((deep, depth), BF),
        dma((3,)),
        dma((3,)),
    ]
    returned, sums = exchange_call(
        "expert_backward",
        number,
        body,
        [message, *kept, unfold],
        experts,
        shapes,
        message.shape,
        scratch,
    )
    return returned.reshape(-1, message.shape[2]), sums


def forward_layer(source, weights, experts, layer, rank, unfold, tables, allowed, numbers):
    low, h_attn, query, kv_all, x_mid, h_moe, attended, probs, gates, message = attention(
        source, weights, tables, allowed, rank, numbers[0]
    )
    returned, kept = expert_forward(message, experts, layer, unfold, numbers[1])
    stored = {
        "low": low,
        "h_attn": h_attn,
        "query": query,
        "kv_all": kv_all,
        "probs": probs,
        "attended": attended,
        "x_mid": x_mid,
        "h_moe": h_moe,
        "gates": gates,
        "returned": returned,
        "kept": kept,
    }
    return (x_mid, rank, gates, returned), stored


def backward_layer(grad, ready, stored, weights, experts, layer, rank, unfold, tables, numbers):
    message, dlogits = grad_slots(grad, rank, stored["gates"], stored["returned"])
    returned, half = expert_backward(
        message, experts, layer, stored["kept"], unfold, numbers[0]
    )
    dbr, dqkv, grad_in, dgain_a, dgain_m = grad_attention(
        grad, returned, rank, dlogits, weights, stored["x_mid"], stored["query"], stored["kv_all"],
        stored["probs"], tables, stored["low"], numbers[1],
    )
    dqkv, *ready = lax.optimization_barrier((dqkv, *ready))
    arrays = (
        stored["h_attn"], dqkv, stored["attended"], dbr, stored["h_moe"], dlogits, dgain_a, dgain_m
    )
    grads = weight_grads(*arrays) if layer else weight_grads_half(*arrays, number=1)
    return grad_in, grads, half, ready


def per_device(
    tokens,
    routes,
    lengths,
    gain_attn,
    w_query,
    w_key,
    w_value,
    w_out,
    gain_moe,
    w_router,
    w_gate,
    w_up,
    w_down,
    cotangent,
):
    section, yh, z, core, shard = (
        lax.axis_index(a) for a in ("section", "yh", "z", "core", "shard")
    )
    first = section == 0
    tok_rows, model_width = tokens.shape[1:]
    group_rows = tok_rows * lax.axis_size("shard")

    def mine(a):
        return lax.dynamic_index_in_dim(a, section, 0, keepdims=False)

    def by_layer(own, other):
        return jnp.where(first, own, other), jnp.where(first, other, own)

    local = jnp.concatenate(
        [
            w_out[0],
            w_query[0],
            w_key[0],
            w_value[0],
            w_router[0],
            gain_attn[0][:, None],
            gain_moe[0][:, None],
            jnp.zeros((w_query.shape[1], 94), BF),
        ],
        axis=1,
    )
    full, late, *whole = gather_weights(local, (w_gate[0], w_up[0], w_down[0]))
    weights = [full.reshape(model_width, -1), late.reshape(model_width, -1)]
    route_other = swap(at(routes[0], 1 - section, 0), "section")
    ranks = [rank_of(r) for r in by_layer(mine(routes[0]), route_other)]
    unfold = unfold_table(GROUP)

    segment, position = document_layout(mine(lengths[:, 0]), group_rows)
    row_start = shard * tok_rows
    own_segment = lax.dynamic_slice_in_dim(segment, row_start, tok_rows)
    tables = rotary_tables(lax.dynamic_slice_in_dim(position, row_start, tok_rows), HEAD_DIM)
    query_index = row_start + jnp.arange(tok_rows, dtype=jnp.int32)
    allowed = (own_segment[:, None] == segment[None, :]) & (
        query_index[:, None] >= jnp.arange(group_rows, dtype=jnp.int32)[None, :]
    )
    allowed = allowed.astype(F32)

    source, saved = (mine(tokens),), []
    for layer in range(2):
        source, stored = forward_layer(
            source, weights[layer], whole, layer, ranks[layer], unfold, tables, allowed,
            (7 + layer, 11 + layer),
        )
        saved.append(stored)
    low = fused("finish", finish_body, [((tok_rows, model_width), BF)], *source)[0]
    grad, low = lax.optimization_barrier((mine(cotangent), low))
    away = swap(low, "section")

    sums, ready = [None, None], (away,)
    for layer in (1, 0):
        grad, mixer_grad, half, ready = backward_layer(
            grad,
            ready,
            saved[layer],
            weights[layer],
            whole,
            layer,
            ranks[layer],
            unfold,
            tables,
            (5 + layer, 9 + layer),
        )
        given = lax.ppermute(half, "section", [(1 - layer, layer)])
        sums[layer] = (half, given)
        if layer == 1:
            (away,), ready = ready, (given,)
            late = lax.psum_scatter(mixer_grad, DEVICES, scatter_dimension=0, tiled=True)
            late = lax.optimization_barrier(late)
    mixed = jnp.where(first, jnp.stack([low, away]), jnp.stack([away, low]))

    def finish_experts():
        return jnp.where(first, total(*sums[0]), total(sums[1][0], *ready)).astype(BF)

    mix, (grad_gate, grad_up, grad_down) = reduce_all(mixer_grad, late, finish_experts)
    return (
        mixed,
        grad[None],
        mix[:, 3616][None],
        mix[:, 1536:3072][None],
        mix[:, 3072:3328][None],
        mix[:, 3328:3584][None],
        mix[:, :1536][None],
        mix[:, 3617][None],
        mix[:, 3584:3616][None],
        grad_gate[None],
        grad_up[None],
        grad_down[None],
    )


def solution(mesh):
    fine = Mesh(mesh.devices.reshape(2, 2, 4, 2, 4), ("section", *DEVICES))
    expert = ("yh", "z", "core")
    return jax.shard_map(
        per_device,
        mesh=fine,
        in_specs=(
            P(None, DEVICES, None),
            P("section", None, DEVICES, None),
            P(None, expert, None),
            P("section", DEVICES),
            P("section", DEVICES, None),
            P("section", DEVICES, None),
            P("section", DEVICES, None),
            P("section", DEVICES, None),
            P("section", DEVICES),
            P("section", DEVICES, None),
            P("section", expert, "shard", None),
            P("section", expert, "shard", None),
            P("section", expert, None, "shard"),
            P(None, DEVICES, None),
        ),
        out_specs=(
            P(None, DEVICES, None),
            P("section", DEVICES, None),
            P("section", DEVICES),
            P("section", DEVICES, None),
            P("section", DEVICES, None),
            P("section", DEVICES, None),
            P("section", DEVICES, None),
            P("section", DEVICES),
            P("section", DEVICES, None),
            P("section", expert, "shard", None),
            P("section", expert, "shard", None),
            P("section", expert, None, "shard"),
        ),
        check_vma=False,
    )
```
